32 devices in a mesh: batch: 4 (over y, core), rows: 8 (over z, x).
Axes of the slice: x: 2, y: 2, z: 4, core: 2. Of those that a mesh axis runs over, the one named last changes fastest.
Arguments:
- params: float32 [8527872], P(('batch', 'rows')), as said below
- moment1: float32 [8527872], P(('batch', 'rows')), as said below
- moment2: float32 [8527872], P(('batch', 'rows')), as said below
- images: float32 [32, 3, 64, 64], P('batch', None, 'rows'), may hold values from -1 to 1
- noise: float32 [32, 3, 64, 64], P('batch', None, 'rows'), may hold values from -6 to 6
- timesteps: int32 [32], P('batch'), may hold values from 2 to 2999
- masks: int32 [32, 64, 64], P('batch', 'rows'), may hold values from 0 to 1, as said below
- weight_index: int32 [32], P('batch'), may hold values from 0 to 3
Outputs:
- params_new: float32 [8527872], P(('batch', 'rows'))
- moment1_new: float32 [8527872], P(('batch', 'rows'))
- moment2_new: float32 [8527872], P(('batch', 'rows'))
- params_low: bfloat16 [8527872], P(('batch', 'rows'))
- loss_sum: float32 [], replicated
- loss_vlb: float32 [], replicated
- count: float32 [], replicated
- grad_norm: float32 [], replicated
The draws below stay inside these ranges and needn't reach their ends.
Inputs may be any that keep to these rules, and one draw needn't show every extreme that they name: `masks`: 1 marks a valid pixel. `params`: parameters at the usual initial scales. `moment1`: both signs. `moment2`: positive.
All inputs are finite; a program needn't handle non-finite values.
Results may differ from the reference program's by a relative error of at most 0.0019.
The reference program's roundings to bfloat16 on the way (of `weights`, `noisy`, `embed` and `skip`) count: a program that leaves them out, or rounds other values in their place, can miss the bound.
Values may be sent and summed in bfloat16 or wider, within the bound.
No kernel may reach another device: no remote copies, remote signals or barrier semaphores. Data moves between devices by JAX's collectives and lax.ppermute only.
A program may use at most 384 MiB of HBM per device.

```python
import math
import jax
import jax.numpy as jnp
from jax import lax

IN_CH = 3
C0 = 192
CH = 384
TEMB = 768
HEADS = 4
HEAD_DIM = 96
GROUPS = 32
IMG = 64
OUT_CH = 6
DIFF_STEPS = 4000
BLOCKS = 2
STEP = 10
IMAGES = 32
RAW = 8526342
PARAM = 8527872


clip_limit = 0.05


def segments_drawn():
    return [('stem_w', (3, 3, IN_CH, C0), 9 * IN_CH), ('stem_b', (C0,), 0), ('time1_w', (C0, TEMB), C0), ('time1_b', (TEMB,), 0), ('time2_w', (TEMB, TEMB), TEMB), ('time2_b', (TEMB,), 0), ('down_w', (3, 3, C0, CH), 9 * C0), ('down_b', (CH,), 0), ('res_w', (BLOCKS, 2, 3, 3, CH, CH), 9 * CH), ('res_b', (BLOCKS, 2, CH), 0), ('emb_w', (BLOCKS, TEMB, 2 * CH), TEMB), ('emb_b', (BLOCKS, 2 * CH), 0), ('res_gain', (BLOCKS, 2, CH), -1), ('res_shift', (BLOCKS, 2, CH), 0), ('attn_gain', (CH,), -1), ('attn_shift', (CH,), 0), ('qkv_w', (CH, 3 * CH), CH), ('qv_b', (2 * CH,), 0), ('proj_w', (CH, CH), 8), ('proj_b', (CH,), 0), ('head_gain', (C0 + CH,), -1), ('head_shift', (C0 + CH,), 0), ('head_w', (3, 3, C0 + CH, OUT_CH), 9 * (C0 + CH)), ('head_b', (OUT_CH,), 0)]


def entry_scale():
    pieces = []
    for name, shape, fan in segments_drawn():
        pieces.append(jnp.full((math.prod(shape),), 1.0 if fan > 0 else 5.0, jnp.float32))
    pieces.append(jnp.ones((PARAM - RAW,), jnp.float32))
    return jnp.concatenate(pieces) * (clip_limit / math.sqrt(PARAM))


def draw_params(key, part):
    key = jax.random.fold_in(key, 11)
    pieces = []
    for name, shape, fan in segments_drawn():
        amount = math.prod(shape)
        normal = jnp.clip(jax.random.normal(jax.random.fold_in(key, len(pieces)), (amount,), jnp.float32), -4.0, 4.0)
        if fan > 0:
            pieces.append(normal * fan ** (-0.5))
        elif fan == 0:
            pieces.append(0.1 * normal)
        else:
            pieces.append(1.0 + 0.1 * normal)
    pieces.append(jnp.zeros((PARAM - RAW,), jnp.float32))
    return jnp.concatenate(pieces)


def draw_moment1(key, part):
    key = jax.random.fold_in(key, 21)
    normal = jnp.clip(jax.random.normal(key, (PARAM,), jnp.float32), -4.0, 4.0)
    return 0.11 * entry_scale() * normal


def draw_moment2(key, part):
    key = jax.random.fold_in(key, 31)
    spread = jnp.exp(jax.random.uniform(key, (PARAM,), jnp.float32, math.log(0.5), math.log(8.0)))
    gradient = entry_scale()
    return 0.001 * gradient * gradient * spread


def draw_masks(key, part):
    key = jax.random.fold_in(key, 5)
    rows = jnp.arange(IMG)[None, :, None]
    image = jnp.arange(IMAGES)[:, None, None]
    limit = (IMG - 1 + 2 * rows) * (IMAGES + image)
    drawn = jax.random.randint(key, (IMAGES, IMG, IMG), 0, 6 * (IMG - 1) * IMAGES)
    return (drawn < limit).astype(jnp.int32)


def place_ends(entries, own_key, smallest, largest):
    spot = [jax.random.randint(jax.random.fold_in(own_key, axis), (), 0, length) for axis, length in enumerate(entries.shape)]
    main_axis = entries.shape.index(max(entries.shape))
    neighbour = spot[:main_axis] + [(spot[main_axis] + 1) % entries.shape[main_axis]] + spot[main_axis + 1:]
    return entries.at[tuple(spot)].set(smallest).at[tuple(neighbour)].set(largest)


def steps_of(key, dims, shards, low, high):
    def one(position, shards_of):
        heights = jax.random.uniform(jax.random.fold_in(jax.random.fold_in(key, 6), position), (shards_of,), jnp.float32, low / len(shards), high / len(shards))
        return jnp.repeat(jnp.exp(heights), dims[position] // shards_of).reshape((-1,) + (1,) * (len(dims) - position - 1))

    level = one(*shards[0])
    for cut in shards[1:]:
        level = level * one(*cut)
    return level


def gaussian(own_key, shape, deviation, most, split=(), kind=jnp.bfloat16):
    values = jax.random.normal(own_key, shape, jnp.float32) * deviation
    if len(split) > 0:
        values = steps_of(own_key, shape, split, -0.22, 0.18) * values
    return jnp.clip(values, min=-most, max=most).astype(kind)


def setup_inputs(seed: int = 0) -> dict:
    splits = jax.random.split(jax.random.key(seed), 9)
    params = draw_params(jax.random.fold_in(splits[8], 71), 0)
    moment1 = draw_moment1(jax.random.fold_in(splits[8], 71), 0)
    moment2 = draw_moment2(jax.random.fold_in(splits[8], 71), 0)
    images = jnp.clip(jax.random.uniform(splits[3], (IMAGES, IN_CH, IMG, IMG), jnp.float32, -1.0, 1.0) * steps_of(splits[3], (IMAGES, IN_CH, IMG, IMG), ((0, 4), (2, 8)), -0.4, 0.0), -1.0, 1.0)
    noise = gaussian(splits[4], (IMAGES, IN_CH, IMG, IMG), 1.0, 6.0, ((0, 4), (2, 8)), jnp.float32)
    timesteps = place_ends(jax.random.randint(splits[5], (IMAGES,), 2, 3 * DIFF_STEPS // 4), jax.random.fold_in(splits[5], 1), 2, (3 * DIFF_STEPS // 4) - 1).astype(jnp.int32)
    masks = draw_masks(jax.random.fold_in(splits[8], 71), 0)
    weight_index = place_ends(jax.random.randint(splits[7], (IMAGES,), 0, 4), jax.random.fold_in(splits[7], 1), 0, 3).astype(jnp.int32)
    return {"params": params, "moment1": moment1, "moment2": moment2, "images": images, "noise": noise, "timesteps": timesteps, "masks": masks, "weight_index": weight_index}


@jax.custom_vjp
def low(v):
    return lax.optimization_barrier(v.astype(jnp.bfloat16)).astype(jnp.float32)

@jax.custom_vjp
def low_back(v):
    return v

def low_keep(v):
    return (low(v), None)

def low_pass(kept, grad):
    return (grad,)

def back_keep(v):
    return (v, None)

def back_low(kept, grad):
    return (low(grad),)
low.defvjp(low_keep, low_pass)
low_back.defvjp(back_keep, back_low)
highest = lax.Precision.HIGHEST
cosine_offset = 0.008
kl_weight = 0.001
clip_limit = 0.05
learn_rate = 0.05
decay_first = 0.9
decay_second = 0.999
weight_decay = 0.01

def segments():
    return [('stem_w', (3, 3, IN_CH, C0)), ('stem_b', (C0,)), ('time1_w', (C0, TEMB)), ('time1_b', (TEMB,)), ('time2_w', (TEMB, TEMB)), ('time2_b', (TEMB,)), ('down_w', (3, 3, C0, CH)), ('down_b', (CH,)), ('res_w', (BLOCKS, 2, 3, 3, CH, CH)), ('res_b', (BLOCKS, 2, CH)), ('emb_w', (BLOCKS, TEMB, 2 * CH)), ('emb_b', (BLOCKS, 2 * CH)), ('res_gain', (BLOCKS, 2, CH)), ('res_shift', (BLOCKS, 2, CH)), ('attn_gain', (CH,)), ('attn_shift', (CH,)), ('qkv_w', (CH, 3 * CH)), ('qv_b', (2 * CH,)), ('proj_w', (CH, CH)), ('proj_b', (CH,)), ('head_gain', (C0 + CH,)), ('head_shift', (C0 + CH,)), ('head_w', (3, 3, C0 + CH, OUT_CH)), ('head_b', (OUT_CH,))]

def unpack(flat):
    table = {}
    offset = 0
    for name, shape in segments():
        amount = math.prod(shape)
        table[name] = flat[offset:offset + amount].reshape(shape)
        offset = offset + amount
    return table

def plan(steps):
    timef = steps.astype(jnp.float32)
    angle = math.pi / 2.0 / (1.0 + cosine_offset)
    theta = (timef / DIFF_STEPS + cosine_offset) * angle
    before = ((timef - 1.0) / DIFF_STEPS + cosine_offset) * angle
    anchor = cosine_offset * angle
    base = math.cos(anchor) ** 2
    signal = jnp.cos(theta) ** 2 / base
    one_minus = jnp.sin(theta + anchor) * jnp.sin(timef / DIFF_STEPS * angle) / base
    one_prev = jnp.sin(before + anchor) * jnp.sin((timef - 1.0) / DIFF_STEPS * angle) / base
    beta = jnp.sin(theta + before) * math.sin(angle / DIFF_STEPS) / jnp.cos(before) ** 2
    alpha = 1.0 - beta
    tilde = beta * one_prev / one_minus
    return (signal, one_minus, beta, alpha, tilde)

def silu(value):
    return value * jax.nn.sigmoid(value)

def matmul(left, right):
    return jnp.dot(left, right, precision=highest)

def conv(inputs, kernel, stride):
    return lax.conv_general_dilated(inputs[None], kernel, (stride, stride), ((1, 1), (1, 1)), dimension_numbers=('NHWC', 'HWIO', 'NHWC'), precision=highest)[0]

def group_norm(values, gain, shift):
    height, width, chans = values.shape
    grouped = values.reshape(height, width, GROUPS, chans // GROUPS)
    mean = lax.optimization_barrier(jnp.mean(grouped, axis=(0, 1, 3), keepdims=True))
    spread = lax.optimization_barrier(jnp.mean(grouped * grouped, axis=(0, 1, 3), keepdims=True)) - mean * mean
    normed = ((grouped - mean) * lax.rsqrt(spread + 1e-05)).reshape(height, width, chans)
    return normed * gain + shift

def image_loss(weights, clean, noise, step, mask, sample_weight):
    signal, one_minus, beta, alpha, tilde = plan(step)
    noisy = low(jnp.sqrt(signal) * clean + jnp.sqrt(one_minus) * noise)
    half = C0 // 2
    freqs = jnp.exp(-math.log(10000.0) * jnp.arange(half).astype(jnp.float32) / half)
    angles = step.astype(jnp.float32) * freqs
    sinus = low(jnp.concatenate([jnp.cos(angles), jnp.sin(angles)]))
    hidden = low(silu(matmul(sinus, weights['time1_w']) + weights['time1_b']))
    embed = low(silu(matmul(hidden, weights['time2_w']) + weights['time2_b']))
    skip = low(low_back(conv(noisy, weights['stem_w'], 1) + weights['stem_b']))
    state = low_back(conv(skip, weights['down_w'], 2) + weights['down_b'])
    for index in range(BLOCKS):
        modulate = matmul(embed, weights['emb_w'][index]) + weights['emb_b'][index]
        act = low(silu(group_norm(state, weights['res_gain'][index, 0], weights['res_shift'][index, 0])))
        inner = low_back(conv(act, weights['res_w'][index, 0], 1) + weights['res_b'][index, 0])
        inner = group_norm(inner, weights['res_gain'][index, 1], weights['res_shift'][index, 1])
        act = low(silu(inner * (1.0 + modulate[:CH]) + modulate[CH:]))
        state = state + low_back(conv(act, weights['res_w'][index, 1], 1) + weights['res_b'][index, 1])
    height, width = (state.shape[0], state.shape[1])
    normed = low(group_norm(state, weights['attn_gain'], weights['attn_shift']).reshape(height * width, CH))
    bias = jnp.concatenate([weights['qv_b'][:CH], jnp.zeros((CH,), jnp.float32), weights['qv_b'][CH:]])
    project = low(low_back(matmul(normed, weights['qkv_w']) + bias))
    query = project[:, :CH].reshape(-1, HEADS, HEAD_DIM)
    keys = project[:, CH:2 * CH].reshape(-1, HEADS, HEAD_DIM)
    values = project[:, 2 * CH:].reshape(-1, HEADS, HEAD_DIM)
    scores = low_back(jnp.einsum('qhd,khd->hqk', query, keys, precision=highest) / math.sqrt(HEAD_DIM))
    probs = low(jax.nn.softmax(scores, axis=-1))
    mixed = jnp.einsum('hqk,khd->qhd', probs, values, precision=highest).reshape(-1, CH)
    mixed = low(low_back(mixed))
    branch = low_back(matmul(mixed, weights['proj_w']) + weights['proj_b'])
    state = state + branch.reshape(height, width, CH)
    upsampled = jnp.repeat(jnp.repeat(state, 2, axis=0), 2, axis=1)
    joined = jnp.concatenate([upsampled, skip], axis=-1)
    act = low(silu(group_norm(joined, weights['head_gain'], weights['head_shift'])))
    out = low_back(conv(act, weights['head_w'], 1) + weights['head_b'])
    error = out[..., :IN_CH] - noise
    fraction = (out[..., IN_CH:] + 1.0) / 2.0
    log_beta = jnp.log(beta)
    log_tilde = jnp.log(tilde)
    log_var = fraction * log_beta + (1.0 - fraction) * log_tilde
    coefficient = beta * beta / (alpha * one_minus)
    divergence = 0.5 * (-1.0 + log_var - log_tilde + jnp.exp(log_tilde - log_var) + coefficient * error * error * jnp.exp(-log_var))
    each = lax.optimization_barrier(jnp.sum(error * error + kl_weight * divergence, axis=-1))
    weight = sample_weight * mask.astype(jnp.float32)
    vlb = jnp.sum(weight * kl_weight * lax.optimization_barrier(jnp.sum(divergence, axis=-1)))
    return (jnp.sum(weight * each), vlb)

def reference(params, moment1, moment2, images, noise, timesteps, masks, weight_index):
    rounded = params.astype(jnp.bfloat16).astype(jnp.float32)
    clean_all = jnp.transpose(images, (0, 2, 3, 1))
    noise_all = jnp.transpose(noise, (0, 2, 3, 1))
    sample_weights = 0.5 + 0.5 * weight_index.astype(jnp.float32)
    checked = jax.checkpoint(image_loss)

    def total_loss(flat):
        weights = unpack(flat)

        def accumulate(carry, item):
            total, vlb = checked(weights, *item)
            return ((carry[0] + total, carry[1] + vlb), None)
        zero = jnp.zeros((), jnp.float32)
        (result, vlb_sum), unused = lax.scan(accumulate, (zero, zero), (clean_all, noise_all, timesteps, masks, sample_weights))
        return (result, vlb_sum)
    loss_sum, backward, loss_vlb = jax.vjp(total_loss, rounded, has_aux=True)
    gradient, = backward(jnp.ones_like(loss_sum))
    count = jnp.sum(masks).astype(jnp.float32)
    scaled = gradient / count
    grad_norm = jnp.sqrt(jnp.sum(scaled * scaled))
    clipped = scaled * jnp.minimum(1.0, clip_limit / (grad_norm + 1e-06))
    first = decay_first * moment1 + (1.0 - decay_first) * clipped
    second = decay_second * moment2 + (1.0 - decay_second) * clipped * clipped
    first_hat = first / (1.0 - decay_first ** STEP)
    second_hat = second / (1.0 - decay_second ** STEP)
    updated = params - learn_rate * (first_hat / (jnp.sqrt(second_hat) + 1e-08) + weight_decay * params)
    return (updated, first, second, updated.astype(jnp.bfloat16), loss_sum, loss_vlb, count, grad_norm)
```

```python
import math

import jax
import jax.numpy as jnp
from jax import lax
from jax.sharding import PartitionSpec as P

IN_CH = 3
C0 = 192
CH = 384
TEMB = 768
HEADS = 4
HEAD_DIM = 96
GROUPS = 32
OUT_CH = 6
DIFF_STEPS = 4000
BLOCKS = 2
WIDE = 384
STEP = 10


cosine_offset = 0.008
kl_weight = 0.001
clip_limit = 0.05
learn_rate = 0.05
decay_first = 0.9
decay_second = 0.999
weight_decay = 0.01
narrow = jnp.bfloat16


def with_halo(value):
    return jnp.pad(value, ((0, 0), (1, 1), (0, 0), (0, 0)))


def segments():
    return [
        ("stem_w", (3, 3, IN_CH, C0)),
        ("stem_b", (C0,)),
        ("time1_w", (C0, TEMB)),
        ("time1_b", (TEMB,)),
        ("time2_w", (TEMB, TEMB)),
        ("time2_b", (TEMB,)),
        ("down_w", (3, 3, C0, CH)),
        ("down_b", (CH,)),
        ("res_w", (BLOCKS, 2, 3, 3, CH, CH)),
        ("res_b", (BLOCKS, 2, CH)),
        ("emb_w", (BLOCKS, TEMB, 2 * CH)),
        ("emb_b", (BLOCKS, 2 * CH)),
        ("res_gain", (BLOCKS, 2, CH)),
        ("res_shift", (BLOCKS, 2, CH)),
        ("attn_gain", (CH,)),
        ("attn_shift", (CH,)),
        ("qkv_w", (CH, 3 * CH)),
        ("qv_b", (2 * CH,)),
        ("proj_w", (CH, CH)),
        ("proj_b", (CH,)),
        ("head_gain", (C0 + CH,)),
        ("head_shift", (C0 + CH,)),
        ("head_w", (3, 3, C0 + CH, OUT_CH)),
        ("head_b", (OUT_CH,)),
    ]


def unpack(whole):
    table = {}
    offset = 0
    for name, shape in segments():
        amount = math.prod(shape)
        first, last = offset // WIDE, -(-(offset + amount) // WIDE)
        part = whole[first:last].reshape(-1)
        table[name] = part[offset - first * WIDE : offset - first * WIDE + amount].reshape(shape)
        offset = offset + amount
    return table


def pack(table, rows):
    pieces, pending = [], []
    for name, shape in segments():
        flat = table[name].reshape(-1)
        pending.append(flat)
        held = sum(piece.shape[0] for piece in pending)
        if held % WIDE == 0:
            joined = pending[0] if len(pending) == 1 else jnp.concatenate(pending)
            pieces.append(joined.reshape(-1, WIDE))
            pending = []
    used = sum(piece.shape[0] for piece in pieces)
    held = sum(piece.shape[0] for piece in pending)
    pending.append(jnp.zeros(((rows - used) * WIDE - held,), jnp.float32))
    pieces.append(jnp.concatenate(pending).reshape(-1, WIDE))
    return jnp.concatenate(pieces)


def plan(steps):
    timef = steps.astype(jnp.float32)
    angle = math.pi / 2.0 / (1.0 + cosine_offset)
    theta = (timef / DIFF_STEPS + cosine_offset) * angle
    before = ((timef - 1.0) / DIFF_STEPS + cosine_offset) * angle
    anchor = cosine_offset * angle
    base = math.cos(anchor) ** 2
    signal = jnp.cos(theta) ** 2 / base
    one_minus = jnp.sin(theta + anchor) * jnp.sin(timef / DIFF_STEPS * angle) / base
    one_prev = jnp.sin(before + anchor) * jnp.sin((timef - 1.0) / DIFF_STEPS * angle) / base
    beta = jnp.sin(theta + before) * math.sin(angle / DIFF_STEPS) / jnp.cos(before) ** 2
    alpha = 1.0 - beta
    tilde = beta * one_prev / one_minus
    return (signal, one_minus, beta, alpha, tilde)


def silu(value):
    return value * jax.nn.sigmoid(value)


def silu_grad(value):
    gate = jax.nn.sigmoid(value)
    return gate * (1.0 + value * (1.0 - gate))


def column_sum(tensor):
    return jnp.sum(tensor.astype(jnp.float32), axis=(0, 1, 2))


def precise(left, right):
    return jnp.dot(left, right, precision=lax.Precision.HIGHEST)


def per_image(value):
    return value[:, None, None, None]


def conv_apply(padded, kernel, stride):
    return lax.conv_general_dilated(
        padded,
        kernel,
        (stride, stride),
        "VALID",
        dimension_numbers=("NHWC", "HWIO", "NHWC"),
        preferred_element_type=jnp.float32,
    )


def widen(tensor):
    return jnp.pad(tensor, ((0, 0), (0, 0), (1, 1), (0, 0)))


def flipped(kernel):
    return jnp.transpose(kernel[::-1, ::-1], (0, 1, 3, 2))


def kernel_grad(padded, grad, stride):
    batch, rows, cols, outs = grad.shape
    parts = []
    for top in range(3):
        for left in range(3):
            window = lax.slice(
                padded,
                (0, top, left, 0),
                (
                    batch,
                    top + stride * (rows - 1) + 1,
                    left + stride * (cols - 1) + 1,
                    padded.shape[3],
                ),
                (1, stride, stride, 1),
            )
            parts.append(
                jnp.einsum("brci,brco->io", window, grad, preferred_element_type=jnp.float32)
            )
    return jnp.stack(parts).reshape(3, 3, padded.shape[3], outs)


def conv_same(inputs, kernel, bias):
    padded = widen(with_halo(inputs))
    return (conv_apply(padded, kernel, 1) + bias.astype(jnp.float32), padded)


def conv_same_back(padded, kernel, grad):
    grad_padded = widen(with_halo(grad))
    return (conv_apply(grad_padded, flipped(kernel), 1), kernel_grad(padded, grad, 1))


def conv_down(inputs, kernel, bias):
    padded = widen(jnp.pad(inputs, ((0, 0), (1, 0), (0, 0), (0, 0))))
    return (conv_apply(padded, kernel, 2) + bias.astype(jnp.float32), padded)


def conv_down_back(padded, kernel, grad):
    spread = lax.conv_general_dilated(
        grad,
        flipped(kernel),
        (1, 1),
        ((2, 2), (2, 3)),
        lhs_dilation=(2, 2),
        dimension_numbers=("NHWC", "HWIO", "NHWC"),
        preferred_element_type=jnp.float32,
    )
    inputs_grad = spread[:, 1:, 1:-1]
    return (inputs_grad, kernel_grad(padded, grad, 2))


def norm_forward(values, gain, shift):
    batch, rows, cols, chans = values.shape
    grouped = values.reshape(batch, rows, cols, GROUPS, chans // GROUPS)
    totals = jnp.sum(grouped, axis=(1, 2, 4))
    squares = jnp.sum(grouped * grouped, axis=(1, 2, 4))
    amount = rows * cols * (chans // GROUPS)
    mean = totals / amount
    inverse = lax.rsqrt(squares / amount - mean * mean + 1e-05)
    normed = ((grouped - mean[:, None, None, :, None]) * inverse[:, None, None, :, None]).reshape(
        values.shape
    )
    return (normed * gain + shift, (normed, inverse))


def norm_back(grad, kept, gain):
    normed, inverse = kept
    batch, rows, cols, chans = grad.shape
    gain_grad = jnp.sum(grad * normed, axis=(0, 1, 2))
    shift_grad = jnp.sum(grad, axis=(0, 1, 2))
    shape = (batch, rows, cols, GROUPS, chans // GROUPS)
    scaled = (grad * gain).reshape(shape)
    normed = normed.reshape(shape)
    first = jnp.sum(scaled, axis=(1, 2, 4))
    second = jnp.sum(scaled * normed, axis=(1, 2, 4))
    amount = rows * cols * (chans // GROUPS)
    inputs_grad = (
        scaled
        - first[:, None, None, :, None] / amount
        - normed * second[:, None, None, :, None] / amount
    ) * inverse[:, None, None, :, None]
    return (inputs_grad.reshape(grad.shape), gain_grad, shift_grad)


def time_forward(steps, weights):
    half = C0 // 2
    freqs = jnp.exp(-math.log(10000.0) * jnp.arange(half).astype(jnp.float32) / half)
    angles = steps.astype(jnp.float32)[:, None] * freqs
    sinus = jnp.concatenate([jnp.cos(angles), jnp.sin(angles)], axis=-1).astype(narrow)
    hidden_pre = (
        jnp.dot(sinus, weights["time1_w"], preferred_element_type=jnp.float32) + weights["time1_b"]
    )
    hidden = silu(hidden_pre).astype(narrow)
    outer_pre = (
        jnp.dot(hidden, weights["time2_w"], preferred_element_type=jnp.float32) + weights["time2_b"]
    )
    return (silu(outer_pre).astype(narrow), (sinus, hidden_pre, hidden, outer_pre))


def time_back(embed_grad, weights, kept):
    sinus, hidden_pre, hidden, outer_pre = kept
    outer_grad = embed_grad * silu_grad(outer_pre)
    hidden_grad = precise(outer_grad, weights["time2_w"].astype(jnp.float32).T) * silu_grad(
        hidden_pre
    )
    return {
        "time2_w": precise(hidden.astype(jnp.float32).T, outer_grad),
        "time2_b": jnp.sum(outer_grad, axis=0),
        "time1_w": precise(sinus.astype(jnp.float32).T, hidden_grad),
        "time1_b": jnp.sum(hidden_grad, axis=0),
    }


def block_forward(state, weights, embed, index):
    modulate = (
        jnp.dot(embed, weights["emb_w"][index], preferred_element_type=jnp.float32)
        + weights["emb_b"][index]
    )
    scale = 1.0 + modulate[:, None, None, :CH]
    offset = modulate[:, None, None, CH:]
    normed_one, saved_one = norm_forward(
        state, weights["res_gain"][index, 0], weights["res_shift"][index, 0]
    )
    inner, padded_one = conv_same(
        silu(normed_one).astype(narrow), weights["res_w"][index, 0], weights["res_b"][index, 0]
    )
    normed_two, saved_two = norm_forward(
        inner, weights["res_gain"][index, 1], weights["res_shift"][index, 1]
    )
    before = normed_two * scale + offset
    outer, padded_two = conv_same(
        silu(before).astype(narrow), weights["res_w"][index, 1], weights["res_b"][index, 1]
    )
    return (
        state + outer,
        (normed_one, saved_one, padded_one, normed_two, saved_two, before, padded_two, scale),
    )


def block_back(grad, weights, embed, index, kept):
    normed_one, saved_one, padded_one, normed_two, saved_two, before, padded_two, scale = kept
    outer_grad = grad.astype(narrow)
    act_two, kernel_two = conv_same_back(padded_two, weights["res_w"][index, 1], outer_grad)
    before_grad = act_two * silu_grad(before)
    modulate_grad = jnp.concatenate(
        [jnp.sum(before_grad * normed_two, axis=(1, 2)), jnp.sum(before_grad, axis=(1, 2))], axis=-1
    )
    inner_grad, gain_two, shift_two = norm_back(
        before_grad * scale, saved_two, weights["res_gain"][index, 1]
    )
    inner_low = inner_grad.astype(narrow)
    act_one, kernel_one = conv_same_back(padded_one, weights["res_w"][index, 0], inner_low)
    state_grad, gain_one, shift_one = norm_back(
        act_one * silu_grad(normed_one), saved_one, weights["res_gain"][index, 0]
    )
    result = {
        "res_w": jnp.stack([kernel_one, kernel_two]),
        "res_b": jnp.stack([column_sum(inner_low), column_sum(outer_grad)]),
        "emb_w": precise(embed.astype(jnp.float32).T, modulate_grad),
        "emb_b": jnp.sum(modulate_grad, axis=0),
        "res_gain": jnp.stack([gain_one, gain_two]),
        "res_shift": jnp.stack([shift_one, shift_two]),
    }
    embed_grad = precise(modulate_grad, weights["emb_w"][index].astype(jnp.float32).T)
    return (grad + state_grad, result, embed_grad)


def to_heads(tensor, thirds):
    batch, places, width = tensor.shape
    split = tensor.reshape(batch, places, thirds, HEADS, HEAD_DIM)
    return jnp.transpose(split, (0, 3, 1, 2, 4)).reshape(batch * HEADS, places, thirds * HEAD_DIM)


def from_heads(tensor, batch, thirds):
    items, places, width = tensor.shape
    split = tensor.reshape(batch, HEADS, places, thirds, HEAD_DIM)
    return jnp.transpose(split, (0, 2, 3, 1, 4)).reshape(batch, places, thirds * CH)


def head_scores(query, keys):
    return jnp.einsum("kqd,kpd->kqp", query, keys, preferred_element_type=jnp.float32) / math.sqrt(
        HEAD_DIM
    )


def attention_forward(state, weights):
    batch, rows, cols, chans = state.shape
    normed, saved = norm_forward(state, weights["attn_gain"], weights["attn_shift"])
    normed_low = normed.astype(narrow).reshape(batch, rows * cols, CH)
    bias = jnp.concatenate([weights["qv_b"][:CH], jnp.zeros((CH,), narrow), weights["qv_b"][CH:]])
    project = (
        jnp.einsum("bpc,cf->bpf", normed_low, weights["qkv_w"], preferred_element_type=jnp.float32)
        + bias
    ).astype(narrow)
    spread = to_heads(project, 3)
    query = spread[..., :HEAD_DIM]
    keys = spread[..., HEAD_DIM : 2 * HEAD_DIM]
    values = spread[..., 2 * HEAD_DIM :]
    scores = head_scores(query, keys)
    top = jnp.max(scores, axis=-1, keepdims=True)
    log_total = top + jnp.log(jnp.sum(jnp.exp(scores - top), axis=-1, keepdims=True))
    probs = jnp.exp(scores - log_total).astype(narrow)
    mixed = jnp.einsum("kqp,kpd->kqd", probs, values, preferred_element_type=jnp.float32).astype(
        narrow
    )
    mixed_local = from_heads(mixed, batch, 1)
    out = (
        jnp.einsum(
            "bpc,cf->bpf", mixed_local, weights["proj_w"], preferred_element_type=jnp.float32
        )
        + weights["proj_b"]
    )
    return (state + out.reshape(state.shape), (normed_low, saved, spread, log_total, mixed_local))


def attention_back(grad, weights, kept):
    normed_low, saved, spread, log_total, mixed_local = kept
    batch, rows, cols, chans = grad.shape
    out_grad = grad.reshape(batch, rows * cols, CH).astype(narrow)
    proj_w_grad = jnp.einsum(
        "bpc,bpf->cf", mixed_local, out_grad, preferred_element_type=jnp.float32
    )
    mixed_grad = jnp.einsum(
        "bpf,cf->bpc", out_grad, weights["proj_w"], preferred_element_type=jnp.float32
    )
    mixed_grad = to_heads(mixed_grad.astype(narrow), 1)
    query = spread[..., :HEAD_DIM]
    keys = spread[..., HEAD_DIM : 2 * HEAD_DIM]
    values = spread[..., 2 * HEAD_DIM :]
    probs = jnp.exp(head_scores(query, keys) - log_total)
    values_grad = jnp.einsum(
        "kqp,kqd->kpd", probs.astype(narrow), mixed_grad, preferred_element_type=jnp.float32
    )
    probs_grad = jnp.einsum("kqd,kpd->kqp", mixed_grad, values, preferred_element_type=jnp.float32)
    score_grad = (
        probs * (probs_grad - jnp.sum(probs_grad * probs, axis=-1, keepdims=True))
    ).astype(narrow)
    query_grad = jnp.einsum(
        "kqp,kpd->kqd", score_grad, keys, preferred_element_type=jnp.float32
    ) / math.sqrt(HEAD_DIM)
    keys_grad = jnp.einsum(
        "kqp,kqd->kpd", score_grad, query, preferred_element_type=jnp.float32
    ) / math.sqrt(HEAD_DIM)
    item_grad = jnp.concatenate([query_grad, keys_grad, values_grad], axis=-1).astype(narrow)
    project_grad = from_heads(item_grad, batch, 3)
    bias_grad = jnp.sum(project_grad.astype(jnp.float32), axis=(0, 1))
    normed_grad = jnp.einsum(
        "bpf,cf->bpc", project_grad, weights["qkv_w"], preferred_element_type=jnp.float32
    )
    state_grad, gain_grad, shift_grad = norm_back(
        normed_grad.reshape(grad.shape), saved, weights["attn_gain"]
    )
    result = {
        "proj_w": proj_w_grad,
        "proj_b": jnp.sum(out_grad.astype(jnp.float32), axis=(0, 1)),
        "qkv_w": jnp.einsum(
            "bpc,bpf->cf", normed_low, project_grad, preferred_element_type=jnp.float32
        ),
        "qv_b": jnp.concatenate([bias_grad[:CH], bias_grad[2 * CH :]]),
        "attn_gain": gain_grad,
        "attn_shift": shift_grad,
    }
    return (grad + state_grad, result)


def head_forward(state, skip, weights):
    upsampled = jnp.repeat(jnp.repeat(state, 2, axis=1), 2, axis=2)
    joined = jnp.concatenate([upsampled, skip.astype(jnp.float32)], axis=-1)
    normed, saved = norm_forward(joined, weights["head_gain"], weights["head_shift"])
    out, padded = conv_same(silu(normed).astype(narrow), weights["head_w"], weights["head_b"])
    return (out, (normed, saved, padded))


def head_back(out_grad, weights, kept):
    normed, saved, padded = kept
    out_low = out_grad.astype(narrow)
    act_grad, kernel = conv_same_back(padded, weights["head_w"], out_low)
    joined_grad, gain_grad, shift_grad = norm_back(
        act_grad * silu_grad(normed), saved, weights["head_gain"]
    )
    batch, rows, cols, chans = joined_grad.shape
    upper = joined_grad[..., :CH].reshape(batch, rows // 2, 2, cols // 2, 2, CH).sum(axis=(2, 4))
    result = {
        "head_w": kernel,
        "head_b": column_sum(out_low),
        "head_gain": gain_grad,
        "head_shift": shift_grad,
    }
    return (upper, joined_grad[..., CH:], result)


def loss_terms(out, noise, mask, sample_weight, beta, alpha, one_minus, tilde):
    error = out[..., :IN_CH] - noise
    fraction = (out[..., IN_CH:] + 1.0) / 2.0
    log_beta = per_image(jnp.log(beta))
    log_tilde = per_image(jnp.log(tilde))
    log_var = fraction * log_beta + (1.0 - fraction) * log_tilde
    coefficient = per_image(beta * beta / (alpha * one_minus))
    inverse = jnp.exp(-log_var)
    ratio = jnp.exp(log_tilde - log_var)
    divergence = 0.5 * (-1.0 + log_var - log_tilde + ratio + coefficient * error * error * inverse)
    each = jnp.sum(error * error + kl_weight * divergence, axis=-1)
    weight = sample_weight[:, None, None] * mask.astype(jnp.float32)
    total = jnp.sum(weight * each)
    vlb = jnp.sum(weight * kl_weight * jnp.sum(divergence, axis=-1))
    weight = weight[..., None]
    predict_grad = weight * (2.0 * error + kl_weight * coefficient * error * inverse)
    spread_grad = (
        weight
        * kl_weight
        * 0.5
        * (1.0 - ratio - coefficient * error * error * inverse)
        * (log_beta - log_tilde)
        / 2.0
    )
    return (total, vlb, jnp.concatenate([predict_grad, spread_grad], axis=-1))


def micro_step(weights, clean, noise, steps, mask, sample_weight):
    clean = jnp.transpose(clean, (0, 2, 3, 1))
    noise = jnp.transpose(noise, (0, 2, 3, 1))
    signal, one_minus, beta, alpha, tilde = plan(steps)
    noisy = jnp.sqrt(per_image(signal)) * clean + jnp.sqrt(per_image(one_minus)) * noise
    embed, time_kept = time_forward(steps, weights)
    stem_out, stem_padded = conv_same(noisy.astype(narrow), weights["stem_w"], weights["stem_b"])
    skip = stem_out.astype(narrow)
    state, down_padded = conv_down(skip, weights["down_w"], weights["down_b"])
    block_kept = []
    for index in range(BLOCKS):
        state, kept = block_forward(state, weights, embed, index)
        block_kept.append(kept)
    state, attention_kept = attention_forward(state, weights)
    out, head_kept = head_forward(state, skip, weights)
    loss, vlb, out_grad = loss_terms(out, noise, mask, sample_weight, beta, alpha, one_minus, tilde)
    state_grad, skip_grad, grads = head_back(out_grad, weights, head_kept)
    state_grad, attention_grads = attention_back(state_grad, weights, attention_kept)
    grads.update(attention_grads)
    embed_grad = jnp.zeros((steps.shape[0], TEMB), jnp.float32)
    block_grads = [None] * BLOCKS
    for index in reversed(range(BLOCKS)):
        state_grad, block_grads[index], part = block_back(
            state_grad, weights, embed, index, block_kept[index]
        )
        embed_grad = embed_grad + part
    for name in block_grads[0]:
        grads[name] = jnp.stack([entry[name] for entry in block_grads])
    down_low = state_grad.astype(narrow)
    skip_more, down_kernel = conv_down_back(down_padded, weights["down_w"], down_low)
    stem_low = (skip_grad + skip_more).astype(narrow)
    grads.update(
        {
            "down_w": down_kernel,
            "down_b": column_sum(down_low),
            "stem_w": kernel_grad(stem_padded, stem_low, 1),
            "stem_b": column_sum(stem_low),
        }
    )
    grads.update(time_back(embed_grad, weights, time_kept))
    return (loss, vlb, grads)


def whole_images(value):
    return lax.all_to_all(value, "rows", split_axis=0, concat_axis=2, tiled=True)


def shards(params, moment1, moment2, images, noise, timesteps, masks, weight_index):
    shard = params.shape[0]
    params, moment1, moment2 = (
        value.reshape(-1, WIDE) for value in (params, moment1, moment2)
    )
    total_rows = params.shape[0] * lax.axis_size("batch") * lax.axis_size("rows")
    whole = lax.all_gather(params.astype(narrow), ("batch", "rows"), axis=0, tiled=True)
    weights = unpack(whole)
    group = images.shape[0] // lax.axis_size("rows")
    place = lax.axis_index("rows") * group
    count = lax.psum(jnp.sum(masks).astype(jnp.float32), ("batch", "rows"))
    own = whole_images(
        jnp.concatenate([images, noise, masks.astype(jnp.float32)[:, None]], axis=1)
    )
    steps = lax.dynamic_slice_in_dim(timesteps, place, group)
    sample_weight = 0.5 + 0.5 * lax.dynamic_slice_in_dim(weight_index, place, group).astype(
        jnp.float32
    )
    loss_local, vlb_local, grads = micro_step(
        weights, own[:, :IN_CH], own[:, IN_CH : 2 * IN_CH], steps, own[:, 2 * IN_CH], sample_weight
    )
    summed = pack(grads, total_rows)
    summed = lax.psum_scatter(summed, ("batch", "rows"), scatter_dimension=0, tiled=True)
    scaled = summed / count
    squares, loss_sum, loss_vlb = lax.psum(
        (jnp.sum(scaled * scaled), loss_local, vlb_local), ("batch", "rows")
    )
    grad_norm = jnp.sqrt(squares)
    clipped = scaled * jnp.minimum(1.0, clip_limit / (grad_norm + 1e-06))
    first = decay_first * moment1 + (1.0 - decay_first) * clipped
    second = decay_second * moment2 + (1.0 - decay_second) * clipped * clipped
    first_hat = first / (1.0 - decay_first**STEP)
    second_hat = second / (1.0 - decay_second**STEP)
    updated = params - learn_rate * (
        first_hat / (jnp.sqrt(second_hat) + 1e-08) + weight_decay * params
    )
    arrays = (value.reshape(shard) for value in (updated, first, second, updated.astype(narrow)))
    return (*arrays, loss_sum, loss_vlb, count, grad_norm)


def solution(mesh):
    return jax.shard_map(
        shards,
        mesh=mesh,
        in_specs=(
            P(("batch", "rows")),
            P(("batch", "rows")),
            P(("batch", "rows")),
            P("batch", None, "rows", None),
            P("batch", None, "rows", None),
            P("batch"),
            P("batch", "rows", None),
            P("batch"),
        ),
        out_specs=(
            P(("batch", "rows")),
            P(("batch", "rows")),
            P(("batch", "rows")),
            P(("batch", "rows")),
            P(),
            P(),
            P(),
            P(),
        ),
        check_vma=False,
    )
```

```python
import functools
import math

import jax
import jax.numpy as jnp
from jax import lax
from jax.experimental import pallas as pl
from jax.experimental.pallas import tpu as pltpu
from jax.sharding import Mesh
from jax.sharding import PartitionSpec as P

IN_CH = 3
C0 = 192
CH = 384
TEMB = 768
HEADS = 4
HEAD_DIM = 96
GROUPS = 32
OUT_CH = 6
DIFF_STEPS = 4000
BLOCKS = 2
STEP = 10

cosine_offset = 0.008
kl_weight = 0.001
clip_limit = 0.05
learn_rate = 0.05
decay_first = 0.9
decay_second = 0.999
weight_decay = 0.01
narrow = jnp.bfloat16
f32 = jnp.float32


def segments():
    return [
        ("stem_w", (3, 3, IN_CH, C0)),
        ("stem_b", (C0,)),
        ("time1_w", (C0, TEMB)),
        ("time1_b", (TEMB,)),
        ("time2_w", (TEMB, TEMB)),
        ("time2_b", (TEMB,)),
        ("down_w", (3, 3, C0, CH)),
        ("down_b", (CH,)),
        ("res_w", (BLOCKS, 2, 3, 3, CH, CH)),
        ("res_b", (BLOCKS, 2, CH)),
        ("emb_w", (BLOCKS, TEMB, 2 * CH)),
        ("emb_b", (BLOCKS, 2 * CH)),
        ("res_gain", (BLOCKS, 2, CH)),
        ("res_shift", (BLOCKS, 2, CH)),
        ("attn_gain", (CH,)),
        ("attn_shift", (CH,)),
        ("qkv_w", (CH, 3 * CH)),
        ("qv_b", (2 * CH,)),
        ("proj_w", (CH, CH)),
        ("proj_b", (CH,)),
        ("head_gain", (C0 + CH,)),
        ("head_shift", (C0 + CH,)),
        ("head_w", (3, 3, C0 + CH, OUT_CH)),
        ("head_b", (OUT_CH,)),
    ]


WIDE = 384
TILE = 16
LEAD = 13
ROW = {}
offset = 0
for name, shape in segments():
    ROW[name] = offset // WIDE
    offset += math.prod(shape)
RES = ROW["res_w"]+LEAD
TAIL = ROW["res_b"]


def plan(steps):
    timef = steps.astype(jnp.float32)
    angle = math.pi / 2.0 / (1.0 + cosine_offset)
    theta = (timef / DIFF_STEPS + cosine_offset) * angle
    before = ((timef - 1.0) / DIFF_STEPS + cosine_offset) * angle
    anchor = cosine_offset * angle
    base = math.cos(anchor) ** 2
    signal = jnp.cos(theta) ** 2 / base
    one_minus = jnp.sin(theta + anchor) * jnp.sin(timef / DIFF_STEPS * angle) / base
    one_prev = jnp.sin(before + anchor) * jnp.sin((timef - 1.0) / DIFF_STEPS * angle) / base
    beta = jnp.sin(theta + before) * math.sin(angle / DIFF_STEPS) / jnp.cos(before) ** 2
    alpha = 1.0 - beta
    tilde = beta * one_prev / one_minus
    return (signal, one_minus, beta, alpha, tilde)


def silu(value):
    return value * jax.nn.sigmoid(value)


def silu_grad(value):
    gate = jax.nn.sigmoid(value)
    return gate * (1.0 + value * (1.0 - gate))


def precise(left, right):
    return jnp.dot(left, right, precision=lax.Precision.HIGHEST)


SIDE=32; PIX=SIDE*SIDE
LIMIT=60*1024*1024
VM=pltpu.VMEM

def call(kernel, ins, outs, scratch, flops, away=(), away_out=(), alias={}):
    spec = pl.BlockSpec(memory_space=VM)
    places = [pl.BlockSpec(memory_space=pl.ANY) if i in away else spec for i in range(len(ins))]
    moved = sum(a.size*a.dtype.itemsize for a in ins) + sum(math.prod(o.shape)*o.dtype.itemsize for o in outs)
    return pl.pallas_call(
        kernel, out_shape=outs, in_specs=places,
        out_specs=[pl.BlockSpec(memory_space=pl.ANY) if i in away_out else spec for i in range(len(outs))],
        scratch_shapes=scratch, input_output_aliases=alias,
        compiler_params=pltpu.CompilerParams(vmem_limit_bytes=LIMIT),
        cost_estimate=pl.CostEstimate(flops=flops, bytes_accessed=moved, transcendentals=0),
    )(*ins)

def sds(shape, dtype=f32): return jax.ShapeDtypeStruct(shape, dtype)

def dot(a, b): return jnp.dot(a, b, preferred_element_type=f32)
def dot_nt(a, b): return lax.dot_general(a, b, (((1,), (1,)), ((), ())), preferred_element_type=f32)

def sigmoid(v): return 1.0 / (1.0 + jnp.exp(-v))

def membership(chans, per, first=0):
    c = lax.broadcasted_iota(jnp.int32, (chans, 128), 0) + first
    g = lax.broadcasted_iota(jnp.int32, (chans, 128), 1)
    return ((c >= g*per) & (c < (g+1)*per)).astype(f32).astype(narrow)

def three(v):
    hi = v.astype(narrow); rest = v - hi.astype(f32)
    mid = rest.astype(narrow); low = (rest - mid.astype(f32)).astype(narrow)
    return hi, mid, low

def exact(v, ones):
    return sum(dot(p, ones) for p in three(v))
def exact_nt(v, ones):
    return sum(dot_nt(p, ones) for p in three(v))

def group_totals(stats, member):
    return exact_nt(exact(stats, member), member)

def fold(v):
    return jnp.sum(v.reshape(-1, 8, v.shape[-1]), axis=0)

def rows_of(*rows):
    r = jnp.concatenate(rows, axis=0)
    return jnp.concatenate([r, jnp.zeros((8-r.shape[0], r.shape[1]), f32)], axis=0)

def norm_stats(s1, s2, member, amount):
    stats = rows_of(jnp.sum(s1, axis=0, keepdims=True), jnp.sum(s2, axis=0, keepdims=True))
    tot = group_totals(stats, member) / amount
    mean = tot[0:1]
    return mean, lax.rsqrt(tot[1:2] - mean*mean + 1e-05)

EL=128
def steps(n, body, init=None):
    return lax.fori_loop(0, n, body, init)

def pixel_column(rows, width):
    return lax.broadcasted_iota(jnp.int32, (rows, width), 0) % SIDE

def spread(pad_ref, out_ref, width, backward):
    zero = jnp.zeros((SIDE, 3*width), narrow)
    out_ref[0:SIDE, :] = zero
    out_ref[SIDE+PIX:SIDE+PIX+SIDE, :] = zero
    col = pixel_column(EL, width)
    for r in range(0, PIX, EL):
        before = jnp.where(col == 0, 0.0, pad_ref[r+7:r+7+EL, :]).astype(narrow)
        after = jnp.where(col == SIDE-1, 0.0, pad_ref[r+9:r+9+EL, :]).astype(narrow)
        mid = pad_ref[r+8:r+8+EL, :].astype(narrow)
        first, last = (after, before) if backward else (before, after)
        out_ref[r+SIDE:r+SIDE+EL, 0:width] = first
        out_ref[r+SIDE:r+SIDE+EL, width:2*width] = mid
        out_ref[r+SIDE:r+SIDE+EL, 2*width:3*width] = last

MC=1024
def conv_rows(xs_ref, w_ref, base, r):
    acc = dot(xs_ref[pl.ds(r, MC), :], w_ref[base:base+3*CH, :])
    acc += dot(xs_ref[pl.ds(r+SIDE, MC), :], w_ref[base+3*CH:base+6*CH, :])
    return acc + dot(xs_ref[pl.ds(r+2*SIDE, MC), :], w_ref[base+6*CH:base+9*CH, :])

TAPS=9*CH
def fetch(whole_ref, base, w_ref, sems, order):
    copies = []
    for i in order:
        copy = pltpu.make_async_copy(whole_ref.at[base+i*TAPS:base+(i+1)*TAPS, :], w_ref.at[i*TAPS:(i+1)*TAPS, :], sems.at[i])
        copy.start()
        copies.append(copy)
    return copies

def block_forward_kernel(base, state_ref, whole_ref, vec_ref, out_ref, inner_ref, stat_ref, pad_ref, xs_ref, w_ref, sems):
    first_in, second_in = fetch(whole_ref, base, w_ref, sems, (0, 1))
    bias1, bias2, gain1, shift1, gain2, shift2, scale, offset = (vec_ref[i:i+1, :] for i in range(8))
    member = membership(CH, CH//GROUPS)
    amount = PIX*(CH//GROUPS)
    def sums(i, c):
        v = state_ref[pl.ds(pl.multiple_of(i*EL, EL), EL), :]
        return c[0]+fold(v), c[1]+fold(v*v)
    z = jnp.zeros((8, CH), f32)
    mean1, inv1 = norm_stats(*steps(PIX//EL, sums, (z, z)), member, amount)
    def act1(i, _):
        r = pl.multiple_of(i*EL, EL)
        v = (state_ref[pl.ds(r, EL), :] - mean1)*inv1*gain1 + shift1
        pad_ref[pl.ds(r+8, EL), :] = v*sigmoid(v)
        return _
    steps(PIX//EL, act1, 0)
    spread(pad_ref, xs_ref, CH, False)
    first_in.wait()
    def conv1(i, c):
        r = pl.multiple_of(i*MC, MC)
        v = conv_rows(xs_ref, w_ref, 0, r) + bias1
        inner_ref[pl.ds(r, MC), :] = v
        return c[0]+fold(v), c[1]+fold(v*v)
    mean2, inv2 = norm_stats(*steps(PIX//MC, conv1, (z, z)), member, amount)
    def act2(i, _):
        r = pl.multiple_of(i*EL, EL)
        v = (inner_ref[pl.ds(r, EL), :] - mean2)*inv2*gain2 + shift2
        v = v*scale + offset
        pad_ref[pl.ds(r+8, EL), :] = v*sigmoid(v)
        return _
    steps(PIX//EL, act2, 0)
    spread(pad_ref, xs_ref, CH, False)
    second_in.wait()
    def conv2(i, _):
        r = pl.multiple_of(i*MC, MC)
        out_ref[pl.ds(r, MC), :] = state_ref[pl.ds(r, MC), :] + (conv_rows(xs_ref, w_ref, TAPS, r) + bias2)
        return _
    steps(PIX//MC, conv2, 0)
    stat_ref[...] = rows_of(mean1, inv1, mean2, inv2)

def block_forward(state, whole, base, vectors):
    return call(functools.partial(block_forward_kernel, base), [state, whole, vectors],
        [sds((PIX, CH)), sds((PIX, CH)), sds((8, CH))],
        [pltpu.VMEM((PIX+16, CH), f32), pltpu.VMEM((PIX+2*SIDE, 3*CH), narrow), pltpu.VMEM((2*TAPS, CH), narrow),
         pltpu.SemaphoreType.DMA((2,))], 2*2*PIX*TAPS*CH, away=(1,))

def back_taps(gs_ref, w_ref, base, r):
    acc = None
    for dy in range(3):
        for dx in range(3):
            part = dot_nt(gs_ref[pl.ds(r+SIDE*(2-dy), MC), dx*CH:(dx+1)*CH],
                          w_ref[base+(3*dy+dx)*CH:base+(3*dy+dx+1)*CH, :])
            acc = part if acc is None else acc+part
    return acc

def kernel_grads(xt_ref, gs_ref, dw_ref, base):
    def body(dy, _):
        r = pl.multiple_of(SIDE*(2-dy), SIDE)
        for dx in range(3):
            at = (base+(3*dy+dx)*CH)//TILE
            value = dot(xt_ref[...], gs_ref[pl.ds(r, PIX), dx*CH:(dx+1)*CH])
            dw_ref[pl.ds(at, CH//TILE)] = value.astype(dw_ref.dtype).reshape(CH//TILE, TILE, CH)
        return _
    steps(3, body, 0)

def block_back_kernel(base, grad_ref, state_ref, inner_ref, stat_ref, whole_ref, vec_ref, large_in_ref, out_ref, large_ref, small_ref,
                      pad_ref, gs_ref, xt_ref, keep_ref, w_ref, dw_ref, sems):
    second_in, first_in = fetch(whole_ref, base, w_ref, sems, (1, 0))
    bias1, bias2, gain1, shift1, gain2, shift2, scale, offset = (vec_ref[i:i+1, :] for i in range(8))
    mean1, inv1, mean2, inv2 = (stat_ref[i:i+1, :] for i in range(4))
    member = membership(CH, CH//GROUPS)
    amount = PIX*(CH//GROUPS)
    z = jnp.zeros((8, CH), f32)
    def low(i, c):
        r = pl.multiple_of(i*EL, EL)
        g = grad_ref[pl.ds(r, EL), :].astype(narrow).astype(f32)
        pad_ref[pl.ds(r+8, EL), :] = g
        return c+fold(g)
    bias2_grad = steps(PIX//EL, low, z)
    spread(pad_ref, gs_ref, CH, True)
    for i in range(PIX//EL):
        r = i*EL
        v = (inner_ref[r:r+EL, :] - mean2)*inv2*gain2 + shift2
        v = v*scale + offset
        xt_ref[:, r:r+EL] = jnp.transpose(v*sigmoid(v)).astype(narrow)
    kernel_grads(xt_ref, gs_ref, dw_ref, TAPS)
    half = TAPS//TILE
    second_out = pltpu.make_async_copy(dw_ref.at[half:2*half], large_ref.at[base//TILE+half:base//TILE+2*half], sems.at[2])
    second_out.start()
    second_in.wait()
    def back2(i, c):
        r = pl.multiple_of(i*MC, MC)
        d = back_taps(gs_ref, w_ref, TAPS, r)
        n = (inner_ref[pl.ds(r, MC), :] - mean2)*inv2
        nt = n*gain2 + shift2
        v = nt*scale + offset
        s = sigmoid(v)
        d = d*(s*(1.0+v*(1.0-s)))
        keep_ref[pl.ds(r, MC), :] = d
        return c[0]+fold(d*nt), c[1]+fold(d), c[2]+fold(d*n)
    mod_scale, mod_offset, dn = steps(PIX//MC, back2, (z, z, z))
    one = lambda v: jnp.sum(v, axis=0, keepdims=True)
    mod_scale, mod_offset, dn = one(mod_scale), one(mod_offset), one(dn)
    tot = group_totals(rows_of(mod_offset*scale*gain2, dn*scale*gain2), member)/amount
    first, second = tot[0:1], tot[1:2]
    def inner_back(i, c):
        r = pl.multiple_of(i*EL, EL)
        n = (inner_ref[pl.ds(r, EL), :] - mean2)*inv2
        g = (keep_ref[pl.ds(r, EL), :]*scale*gain2 - first - n*second)*inv2
        g = g.astype(narrow).astype(f32)
        pad_ref[pl.ds(r+8, EL), :] = g
        return c+fold(g)
    bias1_grad = steps(PIX//EL, inner_back, z)
    spread(pad_ref, gs_ref, CH, True)
    for i in range(PIX//EL):
        r = i*EL
        v = (state_ref[r:r+EL, :] - mean1)*inv1*gain1 + shift1
        xt_ref[:, r:r+EL] = jnp.transpose(v*sigmoid(v)).astype(narrow)
    kernel_grads(xt_ref, gs_ref, dw_ref, 0)
    first_out = pltpu.make_async_copy(dw_ref.at[0:half], large_ref.at[base//TILE:base//TILE+half], sems.at[3])
    first_out.start()
    first_in.wait()
    def back1(i, c):
        r = pl.multiple_of(i*MC, MC)
        d = back_taps(gs_ref, w_ref, 0, r)
        n = (state_ref[pl.ds(r, MC), :] - mean1)*inv1
        v = n*gain1 + shift1
        s = sigmoid(v)
        d = d*(s*(1.0+v*(1.0-s)))
        keep_ref[pl.ds(r, MC), :] = d
        return c[0]+fold(d), c[1]+fold(d*n)
    shift1_grad, gain1_grad = (one(v) for v in steps(PIX//MC, back1, (z, z)))
    tot = group_totals(rows_of(shift1_grad*gain1, gain1_grad*gain1), member)/amount
    first1, second1 = tot[0:1], tot[1:2]
    def state_back(i, _):
        r = pl.multiple_of(i*EL, EL)
        n = (state_ref[pl.ds(r, EL), :] - mean1)*inv1
        out_ref[pl.ds(r, EL), :] = grad_ref[pl.ds(r, EL), :] + (keep_ref[pl.ds(r, EL), :]*gain1 - first1 - n*second1)*inv1
        return _
    steps(PIX//EL, state_back, 0)
    first_out.wait()
    second_out.wait()
    small_ref[...] = jnp.concatenate([one(bias1_grad), one(bias2_grad), gain1_grad, dn*scale, shift1_grad, mod_offset*scale, mod_scale, mod_offset], axis=0)

def block_back(grad, state, inner, stat, whole, base, vectors, large):
    return call(functools.partial(block_back_kernel, base), [grad, state, inner, stat, whole, vectors, large],
        [sds((PIX, CH)), sds(large.shape, narrow), sds((8, CH))],
        [pltpu.VMEM((PIX+16, CH), f32), pltpu.VMEM((PIX+2*SIDE, 3*CH), narrow), pltpu.VMEM((CH, PIX), narrow),
         pltpu.VMEM((PIX, CH), f32), pltpu.VMEM((2*TAPS, CH), narrow), pltpu.VMEM((2*TAPS//TILE, TILE, CH), narrow),
         pltpu.SemaphoreType.DMA((4,))], 2*4*PIX*TAPS*CH, away=(4, 6), away_out=(1,), alias={6: 1})

PHASES = [(0, 0), (0, 1), (1, 0), (1, 1)]
OFFSETS = [(dy, dx) for dy in (-1, 0, 1) for dx in (-1, 0, 1)]

def source(a, b, dy, dx):
    return 2*((a+dy) % 2) + (b+dx) % 2, (a+dy)//2, (b+dx)//2

def shift_lanes(v, di, dj):
    if di == 0 and dj == 0:
        return v
    moved = pltpu.roll(v, (-(SIDE*di+dj)) % PIX, 1)
    p = lax.broadcasted_iota(jnp.int32, v.shape, 1)
    i, j = p // SIDE + di, p % SIDE + dj
    return jnp.where((i >= 0) & (i < SIDE) & (j >= 0) & (j < SIDE), moved, 0.0)

def stack(phases, a, b, sign):
    rows = []
    for dy, dx in OFFSETS:
        at, di, dj = source(a, b, sign*dy, sign*dx)
        rows.append(shift_lanes(phases[at], di, dj))
    rows.append(jnp.zeros((128-72, PIX), f32))
    return jnp.concatenate(rows, axis=0)

def stem_down_kernel(noisy_ref, sw_ref, sb_ref, dw_ref, db_ref, skip_ref, state_ref, pad_ref, xs_ref):
    phases = [noisy_ref[i] for i in range(4)]
    col = pixel_column(EL, C0)
    xs_ref[:, 0:SIDE, :] = jnp.zeros((6, SIDE, C0), narrow)
    for a, b in PHASES:
        rows = jnp.transpose(stack(phases, a, b, 1)).astype(narrow)
        v = (dot(rows, sw_ref[...]) + sb_ref[...]).astype(narrow)
        skip_ref[2*a+b] = v
        if b == 0:
            xs_ref[3*a+1, SIDE:SIDE+PIX, :] = v
        else:
            xs_ref[3*a+2, SIDE:SIDE+PIX, :] = v
            pad_ref[8:8+PIX, :] = v.astype(f32)
            for r in range(0, PIX, EL):
                xs_ref[3*a, SIDE+r:SIDE+r+EL, :] = jnp.where(col == 0, 0.0, pad_ref[r+7:r+7+EL, :]).astype(narrow)
    acc = None
    for t, (dy, dx) in enumerate(OFFSETS):
        top = 0 if dy == -1 else SIDE
        part = dot(xs_ref[3*(dy % 2)+dx+1, top:top+PIX, :], dw_ref[t*C0:(t+1)*C0, :])
        acc = part if acc is None else acc+part
    state_ref[...] = acc + db_ref[...]

def stem_down(noisy, stem_w, stem_b, down_w, down_b):
    return call(stem_down_kernel, [noisy, stem_w, stem_b, down_w, down_b],
        [sds((4, PIX, C0), narrow), sds((PIX, CH))],
        [pltpu.VMEM((PIX+16, C0), f32), pltpu.VMEM((6, PIX+SIDE, C0), narrow)], 2*PIX*9*C0*CH)

def down_stem_back_kernel(grad_ref, skip_ref, more_ref, dw_ref, noisy_ref, large_in_ref, large_ref, sdw_ref, small_ref, small_s_ref,
                          pad_ref, gs_ref, ddw_ref, low_ref, sems):
    top_row = ROW["down_w"]+LEAD
    spare = top_row % TILE
    ddw_ref[0:TILE, :] = jnp.zeros((TILE, CH), f32)
    ddw_ref[9*C0:9*C0+TILE, :] = jnp.zeros((TILE, CH), f32)
    z = jnp.zeros((8, CH), f32)
    gs_ref[:, PIX:PIX+SIDE, :] = jnp.zeros((2, SIDE, CH), narrow)
    col = pixel_column(EL, CH)
    total = z
    pad_ref[PIX:PIX+16, :] = jnp.zeros((16, CH), f32)
    for r in range(0, PIX, EL):
        g = grad_ref[r:r+EL, :].astype(narrow)
        gs_ref[0, r:r+EL, :] = g
        g = g.astype(f32)
        pad_ref[r:r+EL, :] = g
        total += fold(g)
    for r in range(0, PIX, EL):
        gs_ref[1, r:r+EL, :] = jnp.where(col == SIDE-1, 0.0, pad_ref[r+1:r+1+EL, :]).astype(narrow)
    small_ref[...] = rows_of(jnp.sum(total, axis=0, keepdims=True))
    def shifted(dy, dx):
        top = SIDE if dy == -1 else 0
        return gs_ref[1 if dx == -1 else 0, top:top+PIX, :]
    phases = [noisy_ref[i] for i in range(4)]
    stem_grad, stem_bias = None, None
    for a, b in PHASES:
        turned = jnp.transpose(skip_ref[2*a+b].astype(f32)).astype(narrow)
        more = more_ref[2*a+b]
        for t, (dy, dx) in enumerate(OFFSETS):
            if (dy % 2, dx % 2) == (a, b):
                g = shifted(dy, dx)
                ddw_ref[spare+t*C0:spare+(t+1)*C0, :] = dot(turned, g)
                more += dot_nt(g, dw_ref[t*C0:(t+1)*C0, :])
        low = more.astype(narrow)
        part = dot(stack(phases, a, b, 1).astype(narrow), low)
        stem_grad = part if stem_grad is None else stem_grad+part
        part = fold(low.astype(f32))
        stem_bias = part if stem_bias is None else stem_bias+part
    for r in range(0, 9*C0+TILE, 16*TILE):
        end = min(r+16*TILE, 9*C0+TILE)
        low_ref[r//TILE:end//TILE] = ddw_ref[r:end, :].astype(narrow).reshape((end-r)//TILE, TILE, CH)
    copy = pltpu.make_async_copy(low_ref, large_ref.at[top_row//TILE:top_row//TILE+9*C0//TILE+1], sems.at[0])
    copy.start()
    copy.wait()
    sdw_ref[...] = stem_grad
    small_s_ref[...] = rows_of(jnp.sum(stem_bias, axis=0, keepdims=True))

def down_stem_back(grad, skip, more, down_w, noisy, large):
    return call(down_stem_back_kernel, [grad, skip, more, down_w, noisy, large],
        [sds(large.shape, narrow), sds((128, C0)), sds((8, CH)), sds((8, C0))],
        [pltpu.VMEM((PIX+16, CH), f32), pltpu.VMEM((2, PIX+SIDE, CH), narrow), pltpu.VMEM((9*C0+TILE, CH), f32),
         pltpu.VMEM((9*C0//TILE+1, TILE, CH), narrow), pltpu.SemaphoreType.DMA((1,))],
        2*2*PIX*9*C0*CH, away=(5,), away_out=(0,), alias={5: 0})

HEAD_PER = (C0+CH)//GROUPS
def silu_slope(v):
    s = sigmoid(v)
    return s*(1.0+v*(1.0-s))

KL = 0.001
def head_kernel(num_ref, state_ref, skip_ref, wu_ref, ws_ref, vu_ref, vs_ref, bias_ref, noise_ref, mask_ref,
                state_grad_ref, skip_grad_ref, gu_ref, gs_ref, small_u_ref, small_s_ref, gb_ref, loss_ref,
                up_ref, side_ref, q_ref):
    log_beta, log_tilde, coefficient, sample = (num_ref[i] for i in range(4))
    gain_u, shift_u = vu_ref[0:1, :], vu_ref[1:2, :]
    gain_s, shift_s = vs_ref[0:1, :], vs_ref[1:2, :]
    mu, ms = membership(CH, HEAD_PER), membership(C0, HEAD_PER, CH)
    amount = 4*PIX*HEAD_PER
    one = lambda v: jnp.sum(v, axis=0, keepdims=True)
    zu, zs = jnp.zeros((8, CH), f32), jnp.zeros((8, C0), f32)
    def sums_u(i, c):
        v = state_ref[pl.ds(pl.multiple_of(i*EL, EL), EL), :]
        return c[0]+fold(v), c[1]+fold(v*v)
    u1, u2 = steps(PIX//EL, sums_u, (zu, zu))
    s1, s2 = zs, zs
    for k in range(4):
        def sums_s(i, c):
            v = skip_ref[k, pl.ds(pl.multiple_of(i*EL, EL), EL), :].astype(f32)
            return c[0]+fold(v), c[1]+fold(v*v)
        s1, s2 = steps(PIX//EL, sums_s, (s1, s2))
    tot = (exact(rows_of(4.0*one(u1), 4.0*one(u2)), mu) + exact(rows_of(one(s1), one(s2)), ms))/amount
    tot_u, tot_s = exact_nt(tot, mu), exact_nt(tot, ms)
    mean_u, inv_u = tot_u[0:1], lax.rsqrt(tot_u[1:2]-tot_u[0:1]*tot_u[0:1]+1e-05)
    mean_s, inv_s = tot_s[0:1], lax.rsqrt(tot_s[1:2]-tot_s[0:1]*tot_s[0:1]+1e-05)
    def act_u(i, _):
        r = pl.ds(pl.multiple_of(i*EL, EL), EL)
        v = (state_ref[r, :]-mean_u)*inv_u*gain_u+shift_u
        up_ref[r, :] = (v*sigmoid(v)).astype(narrow)
        return _
    steps(PIX//EL, act_u, 0)
    for k in range(4):
        def act_s(i, _):
            r = pl.ds(pl.multiple_of(i*EL, EL), EL)
            v = (skip_ref[k, r, :].astype(f32)-mean_s)*inv_s*gain_s+shift_s
            side_ref[k, r, :] = (v*sigmoid(v)).astype(narrow)
            return _
        steps(PIX//EL, act_s, 0)
    from_up = dot_nt(wu_ref[...], up_ref[...])
    for k in range(4):
        q_ref[k] = from_up + dot_nt(ws_ref[...], side_ref[k])
    row = lax.broadcasted_iota(jnp.int32, (8, PIX), 0)
    loss, vlb, outs, bias_grad = jnp.zeros((1, PIX), f32), jnp.zeros((1, PIX), f32), [], jnp.zeros((8, PIX), f32)
    for a, b in PHASES:
        out = jnp.zeros((8, PIX), f32)
        for t, (dy, dx) in enumerate(OFFSETS):
            at, di, dj = source(a, b, dy, dx)
            out += shift_lanes(q_ref[at, 8*t:8*t+8, :], di, dj)
        out += bias_ref[:, 0:1]
        k = 2*a+b
        error = jnp.where(row < 3, out - noise_ref[k], 0.0)
        fraction = jnp.where(row < 3, (pltpu.roll(out, 5, 0)+1.0)/2.0, 0.0)
        log_var = fraction*log_beta + (1.0-fraction)*log_tilde
        inverse = jnp.exp(-log_var)
        ratio = jnp.exp(log_tilde-log_var)
        divergence = 0.5*(-1.0+log_var-log_tilde+ratio+coefficient*error*error*inverse)
        divergence = jnp.where(row < 3, divergence, 0.0)
        weight = sample*mask_ref[k]
        loss += weight*jnp.sum(error*error+KL*divergence, axis=0, keepdims=True)
        vlb += weight*KL*jnp.sum(divergence, axis=0, keepdims=True)
        predict = weight*(2.0*error+KL*coefficient*error*inverse)
        var_grad = weight*KL*0.5*(1.0-ratio-coefficient*error*error*inverse)*(log_beta-log_tilde)/2.0
        og = jnp.where(row < 3, predict, jnp.where(row < 6, pltpu.roll(var_grad, 3, 0), 0.0))
        og = og.astype(narrow).astype(f32)
        bias_grad += og
        outs.append(og)
    gb_ref[...] = jnp.broadcast_to(jnp.sum(bias_grad, axis=1, keepdims=True), (8, 128))
    loss_ref[...] = jnp.concatenate([jnp.broadcast_to(jnp.sum(loss, axis=1, keepdims=True), (1, 128)),
        jnp.broadcast_to(jnp.sum(vlb, axis=1, keepdims=True), (1, 128)), jnp.zeros((6, 128), f32)], axis=0)
    nine_sum, gs_total = None, None
    d1, d2 = zs, zs
    for a, b in PHASES:
        k = 2*a+b
        nine = stack(outs, a, b, -1)
        nine_sum = nine if nine_sum is None else nine_sum+nine
        part = dot(nine.astype(narrow), side_ref[k])
        gs_total = part if gs_total is None else gs_total+part
        d = dot(jnp.transpose(nine).astype(narrow), ws_ref[...])
        n = (skip_ref[k].astype(f32)-mean_s)*inv_s
        d = d*silu_slope(n*gain_s+shift_s)
        skip_grad_ref[k] = d
        d1, d2 = d1+fold(d), d2+fold(d*n)
    gs_ref[...] = gs_total
    hi = nine_sum.astype(narrow); lo = (nine_sum-hi.astype(f32)).astype(narrow)
    gu_ref[...] = dot(hi, up_ref[...])+dot(lo, up_ref[...])
    turned = jnp.transpose(nine_sum)
    hi = turned.astype(narrow); lo = (turned-hi.astype(f32)).astype(narrow)
    d = dot(hi, wu_ref[...])+dot(lo, wu_ref[...])
    n = (state_ref[...]-mean_u)*inv_u
    d = d*silu_slope(n*gain_u+shift_u)
    state_grad_ref[...] = d
    e1, e2 = one(fold(d)), one(fold(d*n))
    d1, d2 = one(d1), one(d2)
    small_u_ref[...] = rows_of(e2, e1)
    small_s_ref[...] = rows_of(d2, d1)
    tot = (exact(rows_of(e1*gain_u, e2*gain_u), mu)+exact(rows_of(d1*gain_s, d2*gain_s), ms))/amount
    tot_u, tot_s = exact_nt(tot, mu), exact_nt(tot, ms)
    def back_u(i, _):
        r = pl.ds(pl.multiple_of(i*EL, EL), EL)
        n = (state_ref[r, :]-mean_u)*inv_u
        state_grad_ref[r, :] = (state_grad_ref[r, :]*gain_u-4.0*tot_u[0:1]-4.0*n*tot_u[1:2])*inv_u
        return _
    steps(PIX//EL, back_u, 0)
    for k in range(4):
        def back_s(i, _):
            r = pl.ds(pl.multiple_of(i*EL, EL), EL)
            n = (skip_ref[k, r, :].astype(f32)-mean_s)*inv_s
            skip_grad_ref[k, r, :] = (skip_grad_ref[k, r, :]*gain_s-tot_s[0:1]-n*tot_s[1:2])*inv_s
            return _
        steps(PIX//EL, back_s, 0)

def head(numbers, state, skip, wu, ws, vu, vs, bias, noise, mask):
    spec = pl.BlockSpec(memory_space=VM)
    ins = [numbers, state, skip, wu, ws, vu, vs, bias, noise, mask]
    outs = [sds((PIX, CH)), sds((4, PIX, C0)), sds((128, CH)), sds((128, C0)), sds((8, CH)), sds((8, C0)), sds((8, 128)), sds((8, 128))]
    return pl.pallas_call(head_kernel, out_shape=outs,
        in_specs=[pl.BlockSpec(memory_space=pltpu.SMEM)]+[spec]*(len(ins)-1), out_specs=[spec]*len(outs),
        scratch_shapes=[pltpu.VMEM((PIX, CH), narrow), pltpu.VMEM((4, PIX, C0), narrow), pltpu.VMEM((4, 128, PIX), f32)],
        compiler_params=pltpu.CompilerParams(vmem_limit_bytes=LIMIT),
        cost_estimate=pl.CostEstimate(flops=4*2*PIX*128*(4*C0+CH), bytes_accessed=12*2**20, transcendentals=0))(*ins)

HP = 128
QW = HEADS*HP
SCALE = 1.0/math.sqrt(HEAD_DIM)
QC = 256
ATTN_FIRST = (ROW["attn_gain"]+LEAD)//TILE
ATTN_TILES = -(-(ROW["proj_b"]+LEAD+1)//TILE)-ATTN_FIRST
ATTN = {name: ROW[name]+LEAD-ATTN_FIRST*TILE for name in ("attn_gain", "attn_shift", "qkv_w", "qv_b", "proj_w", "proj_b")}

def get_rows(ref, at):
    return jnp.concatenate([ref[i, at, :] for i in range(3)], axis=1)

def put_rows(ref, at, value):
    for i in range(3):
        ref[i, at, :] = value[:, i*128:(i+1)*128]

def attention_forward_kernel(state_ref, whole_ref, out_ref, qkv_ref, log_ref, mixed_t_ref, stat_ref, wp_ref, wo_ref, vec_ref,
                             mixed_ref, vt_ref, bp_ref, rows_ref, wide_ref, sems):
    copy = pltpu.make_async_copy(whole_ref.at[ATTN_FIRST*TILE:(ATTN_FIRST+ATTN_TILES)*TILE, :], rows_ref, sems.at[0])
    copy.start()
    copy.wait()
    for r in range(0, ATTN_TILES*TILE, 16*TILE):
        end = min(r+16*TILE, ATTN_TILES*TILE)
        put_rows(wide_ref, slice(r, end), rows_ref[r:end, :].astype(f32))
    one_row = lambda name, i=0: get_rows(wide_ref, slice(ATTN[name]+i, ATTN[name]+i+1))
    gain, shift, bias = one_row("attn_gain"), one_row("attn_shift"), one_row("proj_b")
    vec_ref[...] = rows_of(gain, shift)
    nothing = jnp.zeros((CH, HP-HEAD_DIM), f32)
    for j in range(3):
        third = get_rows(wide_ref, pl.ds(ATTN["qkv_w"]+j, CH, stride=3))
        third_bias = one_row("qv_b", j//2) if j != 1 else jnp.zeros((1, CH), f32)
        for h in range(HEADS):
            to = slice(j*QW+h*HP, j*QW+(h+1)*HP)
            wp_ref[:, to] = jnp.concatenate([third[:, h*HEAD_DIM:(h+1)*HEAD_DIM], nothing], axis=1).astype(narrow)
            bp_ref[:, to] = jnp.concatenate([third_bias[:, h*HEAD_DIM:(h+1)*HEAD_DIM], nothing[0:1]], axis=1)
    for h in range(HEADS):
        at = ATTN["proj_w"]+h*HEAD_DIM
        wo_ref[h*HP:h*HP+HEAD_DIM, :] = get_rows(wide_ref, slice(at, at+HEAD_DIM)).astype(narrow)
        wo_ref[h*HP+HEAD_DIM:(h+1)*HP, :] = jnp.zeros((HP-HEAD_DIM, CH), narrow)
    member = membership(CH, CH//GROUPS)
    def sums(i, c):
        v = state_ref[pl.ds(pl.multiple_of(i*EL, EL), EL), :]
        return c[0]+fold(v), c[1]+fold(v*v)
    z = jnp.zeros((8, CH), f32)
    mean, inv = norm_stats(*steps(PIX//EL, sums, (z, z)), member, PIX*(CH//GROUPS))
    stat_ref[...] = rows_of(mean, inv)
    def project(i, _):
        r = pl.ds(pl.multiple_of(i*256, 256), 256)
        n = ((state_ref[r, :]-mean)*inv*gain+shift).astype(narrow)
        qkv_ref[r, :] = (dot(n, wp_ref[...])+bp_ref[...]).astype(narrow)
        return _
    steps(PIX//256, project, 0)
    for h in range(HEADS):
        vt_ref[...] = jnp.transpose(qkv_ref[:, 2*QW+h*HP:2*QW+(h+1)*HP].astype(f32)).astype(narrow)
        for c in range(0, PIX, QC):
            s = dot_nt(qkv_ref[:, QW+h*HP:QW+(h+1)*HP], qkv_ref[c:c+QC, h*HP:(h+1)*HP])*SCALE
            top = jnp.max(s, axis=0, keepdims=True)
            e = jnp.exp(s-top)
            total = jnp.sum(e, axis=0, keepdims=True)
            log_ref[h:h+1, c:c+QC] = top+jnp.log(total)
            p = (e*(1.0/total)).astype(narrow)
            m = dot(vt_ref[...], p).astype(narrow)
            mixed_t_ref[h*HP:(h+1)*HP, c:c+QC] = m
            mixed_ref[c:c+QC, h*HP:(h+1)*HP] = jnp.transpose(m.astype(f32)).astype(narrow)
    log_ref[HEADS:8, :] = jnp.zeros((8-HEADS, PIX), f32)
    def finish(i, _):
        r = pl.ds(pl.multiple_of(i*256, 256), 256)
        out_ref[r, :] = state_ref[r, :]+(dot(mixed_ref[r, :], wo_ref[...])+bias)
        return _
    steps(PIX//256, finish, 0)

def attention_forward(state, whole):
    return call(attention_forward_kernel, [state, whole],
        [sds((PIX, CH)), sds((PIX, 3*QW), narrow), sds((8, PIX)), sds((QW, PIX), narrow), sds((8, CH)),
         sds((CH, 3*QW), narrow), sds((QW, CH), narrow), sds((8, CH))],
        [pltpu.VMEM((PIX, QW), narrow), pltpu.VMEM((HP, PIX), narrow), pltpu.VMEM((1, 3*QW), f32),
         pltpu.VMEM((ATTN_TILES*TILE, CH), narrow), pltpu.VMEM((3, ATTN_TILES*TILE, 128), f32), pltpu.SemaphoreType.DMA((1,))],
        2*PIX*(CH*4*QW+2*PIX*QW), away=(1,))

def attention_back_kernel(grad_ref, state_ref, stat_ref, qkv_ref, log_ref, mixed_t_ref, wp_ref, wo_ref, vec_ref,
                          out_ref, large_ref, small_ref, bias_ref, dm_ref, pg_ref, kt_ref, dv_ref, dk_ref, nt_ref, keep_ref,
                          wide_ref, rows_ref, sems):
    gain, shift = vec_ref[0:1, :], vec_ref[1:2, :]
    mean, inv = stat_ref[0:1, :], stat_ref[1:2, :]
    member = membership(CH, CH//GROUPS)
    z = jnp.zeros((8, CH), f32)
    one = lambda v: jnp.sum(v, axis=0, keepdims=True)
    def start(i, c):
        r = pl.ds(pl.multiple_of(i*256, 256), 256)
        g = grad_ref[r, :].astype(narrow)
        keep_ref[r, :] = g
        dm_ref[r, :] = dot_nt(g, wo_ref[...]).astype(narrow)
        return c+fold(g.astype(f32))
    proj_bias = steps(PIX//256, start, z)
    for name, after in (("attn_gain", ATTN["qkv_w"]), ("qv_b", ATTN["proj_w"]), ("proj_b", ATTN_TILES*TILE)):
        put_rows(wide_ref, slice(ATTN[name], after), jnp.zeros((after-ATTN[name], CH), f32))
    wo_grad = dot(mixed_t_ref[...], keep_ref[...])
    for h in range(HEADS):
        at = ATTN["proj_w"]+h*HEAD_DIM
        put_rows(wide_ref, slice(at, at+HEAD_DIM), wo_grad[h*HP:h*HP+HEAD_DIM, :])
    for h in range(HEADS):
        q0, k0, v0 = h*HP, QW+h*HP, 2*QW+h*HP
        kt_ref[...] = jnp.transpose(qkv_ref[:, k0:k0+HP].astype(f32)).astype(narrow)
        for c in range(0, PIX, QC):
            q, dm = qkv_ref[c:c+QC, q0:q0+HP], dm_ref[c:c+QC, h*HP:(h+1)*HP]
            s = dot_nt(qkv_ref[:, k0:k0+HP], q)*SCALE
            p = jnp.exp(s-log_ref[h:h+1, c:c+QC])
            dp = dot_nt(qkv_ref[:, v0:v0+HP], dm)
            delta = jnp.sum(dp*p, axis=0, keepdims=True)
            ds = (p*(dp-delta)).astype(narrow)
            dv = dot(p.astype(narrow), dm)
            dk = dot(ds, q)
            if c == 0:
                dv_ref[...] = dv
                dk_ref[...] = dk
            else:
                dv_ref[...] += dv
                dk_ref[...] += dk
            dq = dot(kt_ref[...], ds)
            pg_ref[c:c+QC, q0:q0+HP] = jnp.transpose(dq*SCALE).astype(narrow)
        pg_ref[:, k0:k0+HP] = (dk_ref[...]*SCALE).astype(narrow)
        pg_ref[:, v0:v0+HP] = dv_ref[...].astype(narrow)
    for r in range(0, PIX, 256):
        nt_ref[:, r:r+256] = jnp.transpose((state_ref[r:r+256, :]-mean)*inv*gain+shift).astype(narrow)
    for j in range(3):
        third = dot(nt_ref[...], pg_ref[:, j*QW:(j+1)*QW])
        third = jnp.concatenate([third[:, h*HP:h*HP+HEAD_DIM] for h in range(HEADS)], axis=1)
        put_rows(wide_ref, pl.ds(ATTN["qkv_w"]+j, CH, stride=3), third)
    for r in range(0, ATTN_TILES, 16):
        end = min(r+16, ATTN_TILES)
        rows_ref[r:end] = get_rows(wide_ref, slice(r*TILE, end*TILE)).astype(narrow).reshape(end-r, TILE, CH)
    copy = pltpu.make_async_copy(rows_ref, large_ref.at[ATTN_FIRST:ATTN_FIRST+ATTN_TILES], sems.at[0])
    copy.start()
    zb = jnp.zeros((8, 3*QW), f32)
    def norm_grad(i, c):
        r = pl.ds(pl.multiple_of(i*256, 256), 256)
        d = dot_nt(pg_ref[r, :], wp_ref[...])
        n = (state_ref[r, :]-mean)*inv
        out_ref[r, :] = d
        return c[0]+fold(d), c[1]+fold(d*n), c[2]+fold(pg_ref[r, :].astype(f32))
    shift_grad, gain_grad, bias_grad = (one(v) for v in steps(PIX//256, norm_grad, (z, z, zb)))
    bias_ref[...] = rows_of(bias_grad)
    tot = group_totals(rows_of(shift_grad*gain, gain_grad*gain), member)/(PIX*(CH//GROUPS))
    first, second = tot[0:1], tot[1:2]
    def finish(i, _):
        r = pl.ds(pl.multiple_of(i*EL, EL), EL)
        n = (state_ref[r, :]-mean)*inv
        out_ref[r, :] = grad_ref[r, :]+(out_ref[r, :]*gain-first-n*second)*inv
        return _
    steps(PIX//EL, finish, 0)
    small_ref[...] = rows_of(gain_grad, shift_grad, one(proj_bias))
    copy.wait()

def attention_back(grad, state, stat, qkv, log, mixed_t, wp, wo, vec, tiles):
    return call(attention_back_kernel, [grad, state, stat, qkv, log, mixed_t, wp, wo, vec],
        [sds((PIX, CH)), sds((tiles, TILE, CH), narrow), sds((8, CH)), sds((8, 3*QW))],
        [pltpu.VMEM((PIX, QW), narrow), pltpu.VMEM((PIX, 3*QW), narrow), pltpu.VMEM((HP, PIX), narrow), pltpu.VMEM((PIX, HP), f32),
         pltpu.VMEM((PIX, HP), f32), pltpu.VMEM((CH, PIX), narrow), pltpu.VMEM((PIX, CH), narrow),
         pltpu.VMEM((3, ATTN_TILES*TILE, 128), f32), pltpu.VMEM((ATTN_TILES, TILE, CH), narrow), pltpu.SemaphoreType.DMA((1,))],
        2*PIX*(CH*8*QW+5*PIX*QW), away_out=(1,))


def to_phases(v):
    c = v.shape[0]
    return jnp.transpose(v.reshape(c, SIDE, 2, SIDE, 2), (2, 4, 0, 1, 3)).reshape(4, c, PIX)


def pad_rows8(v):
    return jnp.pad(v, ((0, 0), (0, 8-v.shape[1]), (0, 0)))


def taps_rows(v):
    v = jnp.pad(v, ((0, 0), (0, 8-v.shape[1]), (0, 0))).reshape(72, v.shape[2])
    return jnp.pad(v, ((0, 128-72), (0, 0)))


def heads_unpad(v):
    v = v.reshape(v.shape[:-1]+(-1, HP))[..., :HEAD_DIM]
    return v.reshape(v.shape[:-2]+(-1,))


class Place:
    def __init__(self, sizes, share):
        self.sizes = sizes
        self.share = share
        self.total = sizes["y"]*sizes["c"]*sizes["z"]*sizes["x"]
        firsts = [(share*d+LEAD)//TILE for d in range(self.total)]
        lasts = [-(-(share*(d+1)+LEAD)//TILE) for d in range(self.total)]
        self.block = max(last-first for first, last in zip(firsts, lasts))
        self.tiles = max(first+self.block for first in firsts)
        self.tiles = -(-self.tiles//TILE)*TILE
        self.at = {axis: lax.axis_index(axis) for axis in sizes}

    def device(self, y, c, z, x):
        s = self.sizes
        return ((y*s["c"]+c)*s["z"]+z)*s["x"]+x

    def first(self, device):
        return (self.share*device+LEAD)//TILE

    def me(self):
        a = self.at
        return self.device(a["y"], a["c"], a["z"], a["x"])


def turn(value, axis, size, distance):
    return lax.ppermute(value, axis, [(i, (i+distance) % size) for i in range(size)])


def add_everywhere(value, place):
    for axis in ("c", "x", "y", "z"):
        size, step = place.sizes[axis], 1
        while step < size:
            value = value+lax.ppermute(value, axis, [(i, i ^ step) for i in range(size)])
            step *= 2
    return value


def cut_kernel(count, size, starts_ref, large_ref, out_ref, sems):
    copies = [pltpu.make_async_copy(large_ref.at[pl.ds(starts_ref[i], size)], out_ref.at[i], sems.at[i]) for i in range(count)]
    for copy in copies:
        copy.start()
    for copy in copies:
        copy.wait()


def cut(large, starts, size):
    count = starts.shape[0]
    return pl.pallas_call(
        functools.partial(cut_kernel, count, size),
        out_shape=sds((count, size, TILE, WIDE), narrow),
        in_specs=[pl.BlockSpec(memory_space=pltpu.SMEM), pl.BlockSpec(memory_space=pl.ANY)],
        out_specs=pl.BlockSpec(memory_space=VM),
        scratch_shapes=[pltpu.SemaphoreType.DMA((count,))],
        compiler_params=pltpu.CompilerParams(vmem_limit_bytes=LIMIT),
        cost_estimate=pl.CostEstimate(flops=0, bytes_accessed=4*count*size*TILE*WIDE, transcendentals=0),
    )(starts, large)


def merge_kernel(coords, sends, count, size, starts_ref, large_ref, arrived_ref, *refs):
    outs, (held_ref, sems) = refs[:-2], refs[-2:]
    copies = [pltpu.make_async_copy(large_ref.at[pl.ds(starts_ref[i], size)], held_ref.at[i], sems.at[i]) for i in range(count)]
    for copy in copies:
        copy.start()
    for i in range(count):
        copies[i].wait()
        which, at = sends[i]
        def body(t, _):
            outs[which][at, t] = (held_ref[i, t].astype(f32)+arrived_ref[i, t].astype(f32)).astype(outs[which].dtype)
            return _
        lax.fori_loop(0, size, body, 0)


def share_out(large, place, parts):
    s, a, block = place.sizes, place.at, place.block
    half = (s["z"]+1)//2
    coords = [(y, z, x) for y in range(s["y"]) for z in range(s["z"]) for x in range(s["x"])]

    def starts(core):
        return jnp.stack([
            place.first(place.device((a["y"]+y) % s["y"], core, (a["z"]+z) % s["z"], (a["x"]+x) % s["x"])) for y, z, x in coords
        ]).astype(jnp.int32)

    other, mine = starts(1-a["c"]), starts(a["c"])
    bounds = [block*i//parts for i in range(parts+1)]
    groups = [("y", [(0, z, x) for z in range(half) for x in range(s["x"])])]
    groups += [("y%d" % k, [(k, z, x) for z in range(half) for x in range(s["x"])]) for k in range(1, s["y"])]
    groups += [("x", [(y, z, 0) for z in range(half, s["z"]) for y in range(s["y"])])]
    groups += [("x%d" % k, [(y, z, k) for z in range(half, s["z"]) for y in range(s["y"])]) for k in range(1, s["x"])]
    names = [name for name, members in groups]
    sends = [None]*len(coords)
    for g, (name, members) in enumerate(groups):
        for at, member in enumerate(members):
            sends[coords.index(member)] = (g, at)
    results = []
    for part in range(parts):
        begin, size = bounds[part], bounds[part+1]-bounds[part]
        arrived = turn(cut(large, other+begin, size), "c", 2, 1)
        outs = [sds((len(members), size, TILE, WIDE), f32 if name in ("y", "x") else narrow) for name, members in groups]
        merged = pl.pallas_call(
            functools.partial(merge_kernel, coords, sends, len(coords), size),
            out_shape=outs,
            in_specs=[pl.BlockSpec(memory_space=pltpu.SMEM), pl.BlockSpec(memory_space=pl.ANY), pl.BlockSpec(memory_space=VM)],
            out_specs=[pl.BlockSpec(memory_space=VM)]*len(outs),
            scratch_shapes=[pltpu.VMEM((len(coords), size, TILE, WIDE), narrow), pltpu.SemaphoreType.DMA((len(coords),))],
            compiler_params=pltpu.CompilerParams(vmem_limit_bytes=LIMIT),
            cost_estimate=pl.CostEstimate(flops=0, bytes_accessed=8*len(coords)*size*TILE*WIDE, transcendentals=0),
        )(mine+begin, large, arrived)
        merged = dict(zip(names, merged))
        near, far = merged["y"], merged["x"]
        near = near+sum(turn(merged["y%d" % k], "y", s["y"], k).astype(f32) for k in range(1, s["y"]))
        far = far+sum(turn(merged["x%d" % k], "x", s["x"], k).astype(f32) for k in range(1, s["x"]))
        near = near.reshape((half, s["x"])+near.shape[1:])
        far = far.reshape((s["z"]-half, s["y"])+far.shape[1:])
        near = near[:, 0]+sum(turn(near[:, k].astype(narrow), "x", s["x"], k).astype(f32) for k in range(1, s["x"]))
        far = far[:, 0]+sum(turn(far[:, k].astype(narrow), "y", s["y"], k).astype(f32) for k in range(1, s["y"]))
        total = near[0]
        for z in range(1, s["z"]):
            value = near[z] if z < half else far[z-half]
            total = total+turn(value.astype(narrow), "z", s["z"], z).astype(f32)
        results.append(total)
    return jnp.concatenate(results, axis=0)


def assemble_kernel(share, count, block, pieces_ref, out_ref, held_ref, sems):
    firsts = [(share*d+LEAD)//TILE for d in range(count)]
    firsts.append(firsts[-1]+block)
    arriving, leaving = [], []
    for d in range(count):
        copy = pltpu.make_async_copy(pieces_ref.at[d], held_ref.at[d], sems.at[0, d])
        copy.start()
        arriving.append(copy)
    for d in range(count):
        arriving[d].wait()
        if d:
            held_ref[d, 0] = held_ref[d, 0]+held_ref[d-1, firsts[d]-firsts[d-1]]
        size = firsts[d+1]-firsts[d]
        copy = pltpu.make_async_copy(held_ref.at[d, 0:size], out_ref.at[firsts[d]:firsts[d]+size], sems.at[1, d])
        copy.start()
        leaving.append(copy)
    for copy in leaving:
        copy.wait()


def assemble(pieces, place):
    count, block = place.total, place.block
    anywhere = pl.BlockSpec(memory_space=pl.ANY)
    return pl.pallas_call(
        functools.partial(assemble_kernel, place.share, count, block),
        out_shape=sds((place.tiles, TILE, WIDE), narrow),
        in_specs=[anywhere],
        out_specs=anywhere,
        scratch_shapes=[pltpu.VMEM((count, block, TILE, WIDE), narrow), pltpu.SemaphoreType.DMA((2, count))],
        compiler_params=pltpu.CompilerParams(vmem_limit_bytes=LIMIT),
        cost_estimate=pl.CostEstimate(flops=0, bytes_accessed=4*count*block*TILE*WIDE, transcendentals=0),
    )(pieces)


SPOTS = (
    list(range(14))
    + [ROW["time1_b"], ROW["time1_b"]+1, ROW["time2_b"], ROW["time2_b"]+1, ROW["down_b"]]
    + [ROW["res_b"]+i for i in range(4)]
    + [ROW["emb_b"]+i for i in range(4)]
    + [ROW["res_gain"]+i for i in range(4)]
    + [ROW["res_shift"]+i for i in range(4)]
    + [ROW["attn_gain"], ROW["attn_shift"], ROW["qv_b"], ROW["qv_b"]+1, ROW["proj_b"]]
    + [ROW["head_gain"]+i for i in range(85)]
)


def time_forward(steps, w1, b1, w2, b2):
    half = C0 // 2
    freqs = jnp.exp(-math.log(10000.0) * jnp.arange(half).astype(f32) / half)
    angles = steps[:, None] * freqs
    sinus = jnp.concatenate([jnp.cos(angles), jnp.sin(angles)], axis=-1).astype(narrow)
    hidden_pre = dot(sinus, w1) + b1
    hidden = silu(hidden_pre).astype(narrow)
    outer_pre = dot(hidden, w2) + b2
    return silu(outer_pre).astype(narrow), (sinus, hidden_pre, hidden, outer_pre)


def rank_one_share(place, kept, embed, hidden_grad, outer_grad, moved, small):
    share, n = place.share, place.total
    sinus, hidden_pre, hidden, outer_pre = kept
    row = share*place.me()+jnp.arange(share)

    def left(parts, first):
        length = sum(part.shape[0] for part in parts)
        table = jnp.concatenate([jnp.zeros((share, n), f32)]+parts+[jnp.zeros((share, n), f32)])
        return lax.dynamic_slice_in_dim(table, jnp.clip(share*place.me()-first+share, 0, length+share), share)

    def twice(value):
        return jnp.repeat(value.astype(f32).T, 2, axis=0)

    time_left = left([twice(sinus), jnp.zeros((2, n), f32), twice(hidden)], ROW["time1_w"])
    emb_left = left([twice(embed), twice(embed)], ROW["emb_w"])
    time_left = time_left+emb_left
    columns, right = [], []
    for begin, length, value in (
        (ROW["time1_w"], 2*C0, hidden_grad),
        (ROW["time2_w"], 2*TEMB, outer_grad),
        (ROW["emb_w"], 2*TEMB, moved[:, :2*CH]),
        (ROW["emb_w"]+2*TEMB, 2*TEMB, moved[:, 2*CH:]),
    ):
        for part in range(2):
            held = (row >= begin) & (row < begin+length) & ((row-begin) % 2 == part)
            columns.append(jnp.where(held[:, None], time_left, 0.0))
            right.append(value[:, part*CH:(part+1)*CH])
    spots = jnp.array(SPOTS+[-1]*(128-len(SPOTS)))
    columns.append((row[:, None] == spots[None]).astype(f32))
    right.append(small)
    return precise(jnp.concatenate(columns, axis=1), jnp.concatenate(right))


def step(sizes, params, moment1, moment2, images, noise, timesteps, masks, weight_index):
    flat = params.shape[0]
    share = flat // WIDE
    params, moment1, moment2 = (value.reshape(share, WIDE) for value in (params, moment1, moment2))
    place = Place(sizes, share)
    a, me = place.at, place.me()
    spare = (share*me+LEAD) % TILE
    piece = jnp.zeros((place.block*TILE, WIDE), narrow)
    piece = lax.dynamic_update_slice_in_dim(piece, params.astype(narrow), spare, axis=0)
    pieces = lax.all_gather(piece.reshape(place.block, TILE, WIDE), ("y", "c", "z", "x"), axis=0)

    own = jnp.concatenate([images, noise, masks.astype(f32)[:, None]], axis=1)
    own = lax.all_to_all(own, ("z", "x"), split_axis=0, concat_axis=2, tiled=True)[0]
    index = a["z"]*sizes["x"]+a["x"]
    own_step = lax.dynamic_index_in_dim(timesteps, index, keepdims=False).astype(f32)
    sample_weight = 0.5+0.5*lax.dynamic_index_in_dim(weight_index, index, keepdims=False).astype(f32)
    clean, own_noise, mask = own[:IN_CH], own[IN_CH:2*IN_CH], own[2*IN_CH:]
    early = jnp.stack([
        jnp.where(jnp.arange(WIDE) == me, own_step, 0.0),
        jnp.full((WIDE,), jnp.sum(mask)),
    ] + [jnp.zeros((WIDE,), f32)]*6)
    early = add_everywhere(early, place)
    all_steps, count = early[0, :place.total], early[1, 0]
    signal, one_minus, beta, alpha, tilde = plan(own_step)
    noisy = (jnp.sqrt(signal)*clean+jnp.sqrt(one_minus)*own_noise).astype(narrow).astype(f32)
    noisy = pad_rows8(to_phases(noisy))
    noise_phases, mask_phases = pad_rows8(to_phases(own_noise)), to_phases(mask)

    whole = assemble(pieces, place).reshape(-1, WIDE)

    def rows(name, length, extra=0):
        first = ROW[name]+extra+LEAD
        return whole[first:first+length]

    stem = rows("stem_w", 14).reshape(-1)
    stem_w = taps_rows(stem[:27*C0].reshape(9, IN_CH, C0))
    stem_b = stem[27*C0:].reshape(1, C0).astype(f32)
    w1, b1 = rows("time1_w", 2*C0).reshape(C0, TEMB), rows("time1_b", 2).reshape(TEMB).astype(f32)
    w2, b2 = rows("time2_w", 2*TEMB).reshape(TEMB, TEMB), rows("time2_b", 2).reshape(TEMB).astype(f32)
    down_w, down_b = rows("down_w", 9*C0), rows("down_b", 1).astype(f32)
    vectors = whole[ROW["emb_b"]+LEAD:ROW["qkv_w"]+LEAD].astype(f32)
    res_b = rows("res_b", 4).astype(f32)
    emb_w = rows("emb_w", 4*TEMB).reshape(BLOCKS, TEMB, TEMB)

    skip, state = stem_down(noisy, stem_w, stem_b, down_w, down_b)
    embed, kept = time_forward(all_steps, w1, b1, w2, b2)
    own_embed = lax.dynamic_slice_in_dim(embed, me, 1)
    blocks = []
    for b in range(BLOCKS):
        modulate = dot(own_embed, emb_w[b]).reshape(2, CH)+vectors[2*b:2*b+2]
        vec = jnp.stack([
            res_b[2*b], res_b[2*b+1], vectors[4+2*b], vectors[8+2*b], vectors[5+2*b], vectors[9+2*b],
            1.0+modulate[0], modulate[1],
        ])
        base = RES+2*TAPS*b
        after, inner, stat = block_forward(state, whole, base, vec)
        blocks.append((state, inner, stat, base, vec))
        state = after
    before = state
    state, qkv, log, mixed_t, attn_stat, wp, wo, attn_vec = attention_forward(before, whole)

    ends = rows("head_gain", 85).reshape(-1)
    norm_u = jnp.stack([ends[:CH], ends[C0+CH:C0+2*CH]]).astype(f32)
    norm_s = jnp.stack([ends[CH:C0+CH], ends[C0+2*CH:2*(C0+CH)]]).astype(f32)
    head_size = 9*(C0+CH)*OUT_CH
    head_w = ends[2*(C0+CH):2*(C0+CH)+head_size].reshape(9, C0+CH, OUT_CH)
    head_w = jnp.transpose(head_w, (0, 2, 1))
    wu, ws = taps_rows(head_w[..., :CH]), taps_rows(head_w[..., CH:])
    head_b = ends[2*(C0+CH)+head_size:2*(C0+CH)+head_size+OUT_CH].astype(f32)
    head_b = jnp.broadcast_to(jnp.pad(head_b, (0, 8-OUT_CH))[:, None], (8, 128))
    numbers = jnp.stack([jnp.log(beta), jnp.log(tilde), beta*beta/(alpha*one_minus), sample_weight])
    grad, skip_grad, gu, gs, small_u, small_s, gb, losses = head(
        numbers, state, skip, wu, ws, norm_u, norm_s, head_b, noise_phases, mask_phases)
    grad, large, attn_small, qkv_bias = attention_back(
        grad, before, attn_stat, qkv, log, mixed_t, wp, wo, attn_vec, place.tiles)
    block_grads = [None]*BLOCKS
    for b in reversed(range(BLOCKS)):
        begin, inner, stat, base, vec = blocks[b]
        grad, large, block_grads[b] = block_back(grad, begin, inner, stat, whole, base, vec, large)
    large, d_stem, down_small, stem_small = down_stem_back(grad, skip, skip_grad, down_w, noisy, large)

    total = share_out(large, place, 2).reshape(-1, WIDE)
    total = lax.dynamic_slice_in_dim(total, spare, share)
    row = share*me+jnp.arange(share)
    dense = functools.reduce(jnp.logical_or, [
        (row >= ROW[name]) & (row < ROW[name]+length)
        for name, length in (("down_w", 9*C0), ("res_w", 4*TAPS), ("qkv_w", 3*CH), ("proj_w", CH))
    ])
    total = jnp.where(dense[:, None], total, 0.0)

    d_head = jnp.concatenate([gu[:72].reshape(9, 8, CH)[:, :OUT_CH], gs[:72].reshape(9, 8, C0)[:, :OUT_CH]], axis=-1)
    d_ends = jnp.concatenate([
        small_u[0], small_s[0], small_u[1], small_s[1], jnp.transpose(d_head, (0, 2, 1)).reshape(-1), gb[:OUT_CH, 0],
    ])
    d_ends = jnp.pad(d_ends, (0, 85*WIDE-d_ends.shape[0])).reshape(85, WIDE)
    d_stem = jnp.concatenate([d_stem[:72].reshape(9, 8, C0)[:, :IN_CH].reshape(-1), stem_small[0]]).reshape(14, WIDE)
    qkv_bias = heads_unpad(qkv_bias[0]).reshape(3, CH)
    none = jnp.zeros((4, WIDE), f32)
    s0, s1 = block_grads
    small = jnp.concatenate([
        d_stem, none, down_small[:1], s0[:2], s1[:2], none, s0[2:4], s1[2:4], s0[4:6], s1[4:6],
        attn_small[:2], qkv_bias[:1], qkv_bias[2:], attn_small[2:3], d_ends, jnp.zeros((3, WIDE), f32),
    ])
    moved = jnp.concatenate([s0[6:8], s1[6:8]])
    slots = jnp.where(jnp.arange(place.total)[:, None, None] == me, moved[None], 0.0).reshape(-1, WIDE)
    merged = add_everywhere(jnp.concatenate([small, slots]), place)
    small, moved = merged[:128], merged[128:].reshape(place.total, 4*CH)
    sinus, hidden_pre, hidden, outer_pre = kept
    embed_grad = sum(
        precise(moved[:, 2*CH*b:2*CH*(b+1)], emb_w[b].astype(f32).T) for b in range(BLOCKS))
    outer_grad = embed_grad*silu_grad(outer_pre)
    hidden_grad = precise(outer_grad, w2.astype(f32).T)*silu_grad(hidden_pre)
    filled = jnp.concatenate([
        small[:14], jnp.sum(hidden_grad, axis=0).reshape(2, WIDE), jnp.sum(outer_grad, axis=0).reshape(2, WIDE), small[18:23],
        jnp.sum(moved, axis=0).reshape(4, WIDE), small[27:],
    ])
    total = total+rank_one_share(place, kept, embed, hidden_grad, outer_grad, moved, filled)

    scaled = total/count
    sums = jnp.concatenate([losses[:2], jnp.full((1, 128), jnp.sum(scaled*scaled)), losses[3:]])
    sums = add_everywhere(sums, place)
    loss_sum, loss_vlb, grad_norm = sums[0, 0], sums[1, 0], jnp.sqrt(sums[2, 0])
    clipped = scaled*jnp.minimum(1.0, clip_limit/(grad_norm+1e-06))
    first = decay_first*moment1+(1.0-decay_first)*clipped
    second = decay_second*moment2+(1.0-decay_second)*clipped*clipped
    first_hat = first/(1.0-decay_first**STEP)
    second_hat = second/(1.0-decay_second**STEP)
    updated = params-learn_rate*(first_hat/(jnp.sqrt(second_hat)+1e-08)+weight_decay*params)
    arrays = (value.reshape(flat) for value in (updated, first, second, updated.astype(narrow)))
    return (*arrays, loss_sum, loss_vlb, count, grad_norm)


def solution(mesh):
    y = mesh.shape["batch"] // 2
    sizes = {"y": y, "c": 2, "z": mesh.shape["rows"] // y, "x": y}
    fine = Mesh(mesh.devices.reshape(tuple(sizes.values())), tuple(sizes))
    every, batch, rows = ("y", "c", "z", "x"), ("y", "c"), ("z", "x")
    return jax.shard_map(
        functools.partial(step, sizes),
        mesh=fine,
        in_specs=(P(every), P(every), P(every), P(batch, None, rows, None), P(batch, None, rows, None),
                  P(batch), P(batch, rows, None), P(batch)),
        out_specs=(P(every), P(every), P(every), P(every), P(), P(), P(), P()),
        check_vma=False,
    )
```

```python
import functools
import math

import jax
import jax.numpy as jnp
from jax import lax
from jax.experimental import pallas as pl
from jax.experimental.pallas import tpu as pltpu
from jax.sharding import Mesh
from jax.sharding import PartitionSpec as P

IN_CH = 3
C0 = 192
CH = 384
TEMB = 768
HEADS = 4
HEAD_DIM = 96
GROUPS = 32
OUT_CH = 6
DIFF_STEPS = 4000
BLOCKS = 2
STEP = 10

cosine_offset = 0.008
kl_weight = 0.001
clip_limit = 0.05
learn_rate = 0.05
decay_first = 0.9
decay_second = 0.999
weight_decay = 0.01
narrow = jnp.bfloat16
f32 = jnp.float32


def segments():
    return [
        ("stem_w", (3, 3, IN_CH, C0)),
        ("stem_b", (C0,)),
        ("time1_w", (C0, TEMB)),
        ("time1_b", (TEMB,)),
        ("time2_w", (TEMB, TEMB)),
        ("time2_b", (TEMB,)),
        ("down_w", (3, 3, C0, CH)),
        ("down_b", (CH,)),
        ("res_w", (BLOCKS, 2, 3, 3, CH, CH)),
        ("res_b", (BLOCKS, 2, CH)),
        ("emb_w", (BLOCKS, TEMB, 2 * CH)),
        ("emb_b", (BLOCKS, 2 * CH)),
        ("res_gain", (BLOCKS, 2, CH)),
        ("res_shift", (BLOCKS, 2, CH)),
        ("attn_gain", (CH,)),
        ("attn_shift", (CH,)),
        ("qkv_w", (CH, 3 * CH)),
        ("qv_b", (2 * CH,)),
        ("proj_w", (CH, CH)),
        ("proj_b", (CH,)),
        ("head_gain", (C0 + CH,)),
        ("head_shift", (C0 + CH,)),
        ("head_w", (3, 3, C0 + CH, OUT_CH)),
        ("head_b", (OUT_CH,)),
    ]


WIDE = 384
TILE = 16
LEAD = 13
ROW = {}
offset = 0
for name, shape in segments():
    ROW[name] = offset // WIDE
    offset += math.prod(shape)
RES = ROW["res_w"]+LEAD
TAIL = ROW["res_b"]


def plan(steps):
    timef = steps.astype(jnp.float32)
    angle = math.pi / 2.0 / (1.0 + cosine_offset)
    theta = (timef / DIFF_STEPS + cosine_offset) * angle
    before = ((timef - 1.0) / DIFF_STEPS + cosine_offset) * angle
    anchor = cosine_offset * angle
    base = math.cos(anchor) ** 2
    signal = jnp.cos(theta) ** 2 / base
    one_minus = jnp.sin(theta + anchor) * jnp.sin(timef / DIFF_STEPS * angle) / base
    one_prev = jnp.sin(before + anchor) * jnp.sin((timef - 1.0) / DIFF_STEPS * angle) / base
    beta = jnp.sin(theta + before) * math.sin(angle / DIFF_STEPS) / jnp.cos(before) ** 2
    alpha = 1.0 - beta
    tilde = beta * one_prev / one_minus
    return (signal, one_minus, beta, alpha, tilde)


SIDE=32; PIX=SIDE*SIDE
LIMIT=60*1024*1024
VM=pltpu.VMEM

def call(kernel, ins, outs, scratch, flops, away=(), away_out=(), alias={}, scalar=()):
    spec = pl.BlockSpec(memory_space=VM)
    places = [pl.BlockSpec(memory_space=pl.ANY if i in away else pltpu.SMEM if i in scalar else VM) for i in range(len(ins))]
    moved = sum(a.size*a.dtype.itemsize for a in ins) + sum(math.prod(o.shape)*o.dtype.itemsize for o in outs)
    return pl.pallas_call(
        kernel, out_shape=outs, in_specs=places,
        out_specs=[pl.BlockSpec(memory_space=pl.ANY) if i in away_out else spec for i in range(len(outs))],
        scratch_shapes=scratch, input_output_aliases=alias,
        compiler_params=pltpu.CompilerParams(vmem_limit_bytes=LIMIT),
        cost_estimate=pl.CostEstimate(flops=flops, bytes_accessed=moved, transcendentals=0),
    )(*ins)

def sds(shape, dtype=f32): return jax.ShapeDtypeStruct(shape, dtype)

def dot(a, b): return jnp.dot(a, b, preferred_element_type=f32)
def dot_nt(a, b): return lax.dot_general(a, b, (((1,), (1,)), ((), ())), preferred_element_type=f32)

def sigmoid(v): return 1.0 / (1.0 + jnp.exp(-v))

def membership(chans, per, first=0):
    c = lax.broadcasted_iota(jnp.int32, (chans, 128), 0) + first
    g = lax.broadcasted_iota(jnp.int32, (chans, 128), 1)
    return ((c >= g*per) & (c < (g+1)*per)).astype(f32).astype(narrow)

def three(v):
    hi = v.astype(narrow); rest = v - hi.astype(f32)
    mid = rest.astype(narrow); low = (rest - mid.astype(f32)).astype(narrow)
    return hi, mid, low

def exact(v, ones):
    return sum(dot(p, ones) for p in three(v))
def exact_nt(v, ones):
    return sum(dot_nt(p, ones) for p in three(v))

def group_totals(stats, member):
    return exact_nt(exact(stats, member), member)

def fold(v):
    return jnp.sum(v.reshape(-1, 8, v.shape[-1]), axis=0)

def rows_of(*rows):
    r = jnp.concatenate(rows, axis=0)
    return jnp.concatenate([r, jnp.zeros((8-r.shape[0], r.shape[1]), f32)], axis=0)

def norm_stats(s1, s2, member, amount):
    stats = rows_of(jnp.sum(s1, axis=0, keepdims=True), jnp.sum(s2, axis=0, keepdims=True))
    tot = group_totals(stats, member) / amount
    mean = tot[0:1]
    return mean, lax.rsqrt(tot[1:2] - mean*mean + 1e-05)

EL=128
def steps(n, body, init=None):
    return lax.fori_loop(0, n, body, init)

def pixel_column(rows, width):
    return lax.broadcasted_iota(jnp.int32, (rows, width), 0) % SIDE

def spread(pad_ref, out_ref, width, backward):
    zero = jnp.zeros((SIDE, 3*width), narrow)
    out_ref[0:SIDE, :] = zero
    out_ref[SIDE+PIX:SIDE+PIX+SIDE, :] = zero
    col = pixel_column(EL, width)
    for r in range(0, PIX, EL):
        before = jnp.where(col == 0, 0.0, pad_ref[r+7:r+7+EL, :]).astype(narrow)
        after = jnp.where(col == SIDE-1, 0.0, pad_ref[r+9:r+9+EL, :]).astype(narrow)
        mid = pad_ref[r+8:r+8+EL, :].astype(narrow)
        first, last = (after, before) if backward else (before, after)
        out_ref[r+SIDE:r+SIDE+EL, 0:width] = first
        out_ref[r+SIDE:r+SIDE+EL, width:2*width] = mid
        out_ref[r+SIDE:r+SIDE+EL, 2*width:3*width] = last

MC=1024
def conv_rows(xs_ref, w_ref, base, r):
    acc = dot(xs_ref[pl.ds(r, MC), :], w_ref[base:base+3*CH, :])
    acc += dot(xs_ref[pl.ds(r+SIDE, MC), :], w_ref[base+3*CH:base+6*CH, :])
    return acc + dot(xs_ref[pl.ds(r+2*SIDE, MC), :], w_ref[base+6*CH:base+9*CH, :])

TAPS=9*CH
class Rows:
    def __init__(self, place, first, tiles):
        starts = [place.first(d) for d in range(place.total)]
        self.tiles, self.parts, self.edges = tiles, [], []
        for d in range(place.total):
            begin = starts[d]+1 if d else 0
            end = starts[d+1]+1 if d+1 < place.total else starts[d]+place.block
            begin, end = max(begin, first), min(end, first+tiles)
            if begin < end:
                self.parts.append((d, begin-starts[d], end-starts[d], begin-first))
            if d and first <= starts[d] < first+tiles:
                self.edges.append((d, starts[d]-first))

    def scratch(self):
        return [pltpu.VMEM((self.tiles*TILE, CH), narrow), pltpu.VMEM((max(len(self.edges), 1), TILE, CH), narrow),
                pltpu.SemaphoreType.DMA((len(self.parts)+len(self.edges),))]

    def copies(self, pieces_ref, low_ref, edge_ref, sems):
        made = []
        for d, begin, end, to in self.parts:
            made.append(pltpu.make_async_copy(pieces_ref.at[d, begin*TILE:end*TILE, :],
                                              low_ref.at[to*TILE:(to+end-begin)*TILE, :], sems.at[len(made)]))
        for i, (d, to) in enumerate(self.edges):
            made.append(pltpu.make_async_copy(pieces_ref.at[d, 0:TILE, :], edge_ref.at[i], sems.at[len(made)]))
        return made

    def start(self, *refs):
        for copy in self.copies(*refs):
            copy.start()

    def finish(self, pieces_ref, low_ref, edge_ref, sems):
        for copy in self.copies(pieces_ref, low_ref, edge_ref, sems):
            copy.wait()
        for i, (d, to) in enumerate(self.edges):
            low_ref[to*TILE:(to+1)*TILE, :] = low_ref[to*TILE:(to+1)*TILE, :]+edge_ref[i]

def block_forward_kernel(rows, state_ref, pieces_ref, vec_ref, out_ref, inner_ref, stat_ref, pad_ref, xs_ref, *held):
    one, two = (pieces_ref,)+held[:3], (pieces_ref,)+held[3:]
    rows[0].start(*one)
    rows[1].start(*two)
    w1_ref, w2_ref = held[0], held[3]
    bias1, bias2, gain1, shift1, gain2, shift2, scale, offset = (vec_ref[i:i+1, :] for i in range(8))
    member = membership(CH, CH//GROUPS)
    amount = PIX*(CH//GROUPS)
    def sums(i, c):
        v = state_ref[pl.ds(pl.multiple_of(i*EL, EL), EL), :]
        return c[0]+fold(v), c[1]+fold(v*v)
    z = jnp.zeros((8, CH), f32)
    mean1, inv1 = norm_stats(*steps(PIX//EL, sums, (z, z)), member, amount)
    def act1(i, _):
        r = pl.multiple_of(i*EL, EL)
        v = (state_ref[pl.ds(r, EL), :] - mean1)*inv1*gain1 + shift1
        pad_ref[pl.ds(r+8, EL), :] = v*sigmoid(v)
        return _
    steps(PIX//EL, act1, 0)
    spread(pad_ref, xs_ref, CH, False)
    rows[0].finish(*one)
    def conv1(i, c):
        r = pl.multiple_of(i*MC, MC)
        v = conv_rows(xs_ref, w1_ref, 0, r) + bias1
        inner_ref[pl.ds(r, MC), :] = v
        return c[0]+fold(v), c[1]+fold(v*v)
    mean2, inv2 = norm_stats(*steps(PIX//MC, conv1, (z, z)), member, amount)
    def act2(i, _):
        r = pl.multiple_of(i*EL, EL)
        v = (inner_ref[pl.ds(r, EL), :] - mean2)*inv2*gain2 + shift2
        v = v*scale + offset
        pad_ref[pl.ds(r+8, EL), :] = v*sigmoid(v)
        return _
    steps(PIX//EL, act2, 0)
    spread(pad_ref, xs_ref, CH, False)
    rows[1].finish(*two)
    def conv2(i, _):
        r = pl.multiple_of(i*MC, MC)
        out_ref[pl.ds(r, MC), :] = state_ref[pl.ds(r, MC), :] + (conv_rows(xs_ref, w2_ref, 0, r) + bias2)
        return _
    steps(PIX//MC, conv2, 0)
    stat_ref[...] = rows_of(mean1, inv1, mean2, inv2)

def block_rows(place, base):
    return [Rows(place, (base+i*TAPS)//TILE, TAPS//TILE) for i in range(2)]

def block_forward(place, state, pieces, base, vectors):
    rows = block_rows(place, base)
    return call(functools.partial(block_forward_kernel, rows), [state, pieces, vectors],
        [sds((PIX, CH)), sds((PIX, CH)), sds((8, CH))],
        [pltpu.VMEM((PIX+16, CH), f32), pltpu.VMEM((PIX+2*SIDE, 3*CH), narrow)]+rows[0].scratch()+rows[1].scratch(),
        2*2*PIX*TAPS*CH, away=(1,))

def back_taps(gs_ref, w_ref, base, r):
    acc = None
    for dy in range(3):
        for dx in range(3):
            part = dot_nt(gs_ref[pl.ds(r+SIDE*(2-dy), MC), dx*CH:(dx+1)*CH],
                          w_ref[base+(3*dy+dx)*CH:base+(3*dy+dx+1)*CH, :])
            acc = part if acc is None else acc+part
    return acc

def kernel_grads(xt_ref, gs_ref, dw_ref, base):
    def body(dy, _):
        r = pl.multiple_of(SIDE*(2-dy), SIDE)
        for dx in range(3):
            at = (base+(3*dy+dx)*CH)//TILE
            value = dot(xt_ref[...], gs_ref[pl.ds(r, PIX), dx*CH:(dx+1)*CH])
            dw_ref[pl.ds(at, CH//TILE)] = value.astype(dw_ref.dtype).reshape(CH//TILE, TILE, CH)
        return _
    steps(3, body, 0)

def block_back_kernel(base, rows, grad_ref, state_ref, inner_ref, stat_ref, pieces_ref, vec_ref, large_in_ref, out_ref, large_ref, small_ref,
                      pad_ref, gs_ref, xt_ref, keep_ref, dw_ref, sems, *held):
    first_in, second_in = (pieces_ref,)+held[:3], (pieces_ref,)+held[3:]
    rows[1].start(*second_in)
    rows[0].start(*first_in)
    w1_ref, w2_ref = held[0], held[3]
    bias1, bias2, gain1, shift1, gain2, shift2, scale, offset = (vec_ref[i:i+1, :] for i in range(8))
    mean1, inv1, mean2, inv2 = (stat_ref[i:i+1, :] for i in range(4))
    member = membership(CH, CH//GROUPS)
    amount = PIX*(CH//GROUPS)
    z = jnp.zeros((8, CH), f32)
    def low(i, c):
        r = pl.multiple_of(i*EL, EL)
        g = grad_ref[pl.ds(r, EL), :].astype(narrow).astype(f32)
        pad_ref[pl.ds(r+8, EL), :] = g
        return c+fold(g)
    bias2_grad = steps(PIX//EL, low, z)
    spread(pad_ref, gs_ref, CH, True)
    for i in range(PIX//EL):
        r = i*EL
        v = (inner_ref[r:r+EL, :] - mean2)*inv2*gain2 + shift2
        v = v*scale + offset
        xt_ref[:, r:r+EL] = jnp.transpose(v*sigmoid(v)).astype(narrow)
    kernel_grads(xt_ref, gs_ref, dw_ref, TAPS)
    half = TAPS//TILE
    second_out = pltpu.make_async_copy(dw_ref.at[half:2*half], large_ref.at[base//TILE+half:base//TILE+2*half], sems.at[0])
    second_out.start()
    rows[1].finish(*second_in)
    def back2(i, c):
        r = pl.multiple_of(i*MC, MC)
        d = back_taps(gs_ref, w2_ref, 0, r)
        n = (inner_ref[pl.ds(r, MC), :] - mean2)*inv2
        nt = n*gain2 + shift2
        v = nt*scale + offset
        s = sigmoid(v)
        d = d*(s*(1.0+v*(1.0-s)))
        keep_ref[pl.ds(r, MC), :] = d
        return c[0]+fold(d*nt), c[1]+fold(d), c[2]+fold(d*n)
    mod_scale, mod_offset, dn = steps(PIX//MC, back2, (z, z, z))
    one = lambda v: jnp.sum(v, axis=0, keepdims=True)
    mod_scale, mod_offset, dn = one(mod_scale), one(mod_offset), one(dn)
    tot = group_totals(rows_of(mod_offset*scale*gain2, dn*scale*gain2), member)/amount
    first, second = tot[0:1], tot[1:2]
    def inner_back(i, c):
        r = pl.multiple_of(i*EL, EL)
        n = (inner_ref[pl.ds(r, EL), :] - mean2)*inv2
        g = (keep_ref[pl.ds(r, EL), :]*scale*gain2 - first - n*second)*inv2
        g = g.astype(narrow).astype(f32)
        pad_ref[pl.ds(r+8, EL), :] = g
        return c+fold(g)
    bias1_grad = steps(PIX//EL, inner_back, z)
    spread(pad_ref, gs_ref, CH, True)
    for i in range(PIX//EL):
        r = i*EL
        v = (state_ref[r:r+EL, :] - mean1)*inv1*gain1 + shift1
        xt_ref[:, r:r+EL] = jnp.transpose(v*sigmoid(v)).astype(narrow)
    kernel_grads(xt_ref, gs_ref, dw_ref, 0)
    first_out = pltpu.make_async_copy(dw_ref.at[0:half], large_ref.at[base//TILE:base//TILE+half], sems.at[1])
    first_out.start()
    rows[0].finish(*first_in)
    def back1(i, c):
        r = pl.multiple_of(i*MC, MC)
        d = back_taps(gs_ref, w1_ref, 0, r)
        n = (state_ref[pl.ds(r, MC), :] - mean1)*inv1
        v = n*gain1 + shift1
        s = sigmoid(v)
        d = d*(s*(1.0+v*(1.0-s)))
        keep_ref[pl.ds(r, MC), :] = d
        return c[0]+fold(d), c[1]+fold(d*n)
    shift1_grad, gain1_grad = (one(v) for v in steps(PIX//MC, back1, (z, z)))
    tot = group_totals(rows_of(shift1_grad*gain1, gain1_grad*gain1), member)/amount
    first1, second1 = tot[0:1], tot[1:2]
    def state_back(i, _):
        r = pl.multiple_of(i*EL, EL)
        n = (state_ref[pl.ds(r, EL), :] - mean1)*inv1
        out_ref[pl.ds(r, EL), :] = grad_ref[pl.ds(r, EL), :] + (keep_ref[pl.ds(r, EL), :]*gain1 - first1 - n*second1)*inv1
        return _
    steps(PIX//EL, state_back, 0)
    first_out.wait()
    second_out.wait()
    small_ref[...] = jnp.concatenate([one(bias1_grad), one(bias2_grad), gain1_grad, dn*scale, shift1_grad, mod_offset*scale, mod_scale, mod_offset], axis=0)

def block_back(place, grad, state, inner, stat, pieces, base, vectors, large):
    rows = block_rows(place, base)
    return call(functools.partial(block_back_kernel, base, rows), [grad, state, inner, stat, pieces, vectors, large],
        [sds((PIX, CH)), sds(large.shape, narrow), sds((8, CH))],
        [pltpu.VMEM((PIX+16, CH), f32), pltpu.VMEM((PIX+2*SIDE, 3*CH), narrow), pltpu.VMEM((CH, PIX), narrow),
         pltpu.VMEM((PIX, CH), f32), pltpu.VMEM((2*TAPS//TILE, TILE, CH), narrow),
         pltpu.SemaphoreType.DMA((2,))]+rows[0].scratch()+rows[1].scratch(), 2*4*PIX*TAPS*CH, away=(4, 6), away_out=(1,), alias={6: 1})

PHASES = [(0, 0), (0, 1), (1, 0), (1, 1)]
OFFSETS = [(dy, dx) for dy in (-1, 0, 1) for dx in (-1, 0, 1)]

def source(a, b, dy, dx):
    return 2*((a+dy) % 2) + (b+dx) % 2, (a+dy)//2, (b+dx)//2

def shift_lanes(v, di, dj):
    if di == 0 and dj == 0:
        return v
    moved = pltpu.roll(v, (-(SIDE*di+dj)) % PIX, 1)
    p = lax.broadcasted_iota(jnp.int32, v.shape, 1)
    i, j = p // SIDE + di, p % SIDE + dj
    return jnp.where((i >= 0) & (i < SIDE) & (j >= 0) & (j < SIDE), moved, 0.0)

def stack(phases, a, b, sign):
    rows = []
    for dy, dx in OFFSETS:
        at, di, dj = source(a, b, sign*dy, sign*dx)
        rows.append(shift_lanes(phases[at], di, dj))
    rows.append(jnp.zeros((128-72, PIX), f32))
    return jnp.concatenate(rows, axis=0)

DOWN_FIRST = (ROW["down_w"]+LEAD)//TILE
DOWN_TILES = -(-(ROW["down_b"]+1+LEAD)//TILE)-DOWN_FIRST

def stem_down_kernel(source_rows, noisy_ref, sw_ref, sb_ref, pieces_ref, skip_ref, state_ref, dw_ref, pad_ref, xs_ref, wide_ref, *held):
    source_rows.start(pieces_ref, *held)
    phases = [noisy_ref[i] for i in range(4)]
    col = pixel_column(EL, C0)
    xs_ref[:, 0:SIDE, :] = jnp.zeros((6, SIDE, C0), narrow)
    for a, b in PHASES:
        rows = jnp.transpose(stack(phases, a, b, 1)).astype(narrow)
        v = (dot(rows, sw_ref[...]) + sb_ref[...]).astype(narrow)
        skip_ref[2*a+b] = v
        if b == 0:
            xs_ref[3*a+1, SIDE:SIDE+PIX, :] = v
        else:
            xs_ref[3*a+2, SIDE:SIDE+PIX, :] = v
            pad_ref[8:8+PIX, :] = v.astype(f32)
            for r in range(0, PIX, EL):
                xs_ref[3*a, SIDE+r:SIDE+r+EL, :] = jnp.where(col == 0, 0.0, pad_ref[r+7:r+7+EL, :]).astype(narrow)
    source_rows.finish(pieces_ref, *held)
    wide_ref[...] = held[0][...].astype(f32)
    at = ROW["down_w"]+LEAD-DOWN_FIRST*TILE
    dw_ref[...] = wide_ref[at:at+9*C0, :].astype(narrow)
    acc = None
    for t, (dy, dx) in enumerate(OFFSETS):
        top = 0 if dy == -1 else SIDE
        part = dot(xs_ref[3*(dy % 2)+dx+1, top:top+PIX, :], dw_ref[t*C0:(t+1)*C0, :])
        acc = part if acc is None else acc+part
    state_ref[...] = acc + wide_ref[at+9*C0:at+9*C0+1, :]

def stem_down(place, noisy, stem_w, stem_b, pieces):
    rows = Rows(place, DOWN_FIRST, DOWN_TILES)
    return call(functools.partial(stem_down_kernel, rows), [noisy, stem_w, stem_b, pieces],
        [sds((4, PIX, C0), narrow), sds((PIX, CH)), sds((9*C0, CH), narrow)],
        [pltpu.VMEM((PIX+16, C0), f32), pltpu.VMEM((6, PIX+SIDE, C0), narrow), pltpu.VMEM((DOWN_TILES*TILE, CH), f32)]+rows.scratch(),
        2*PIX*9*C0*CH, away=(3,))

def down_stem_back_kernel(n, me_ref, grad_ref, skip_ref, more_ref, dw_ref, noisy_ref, head_ref, attn_ref, s1_ref, s0_ref,
                          large_in_ref, large_ref, small_ref,
                          pad_ref, gs_ref, ddw_ref, low_ref, sems):
    top_row = ROW["down_w"]+LEAD
    spare = top_row % TILE
    ddw_ref[0:TILE, :] = jnp.zeros((TILE, CH), f32)
    ddw_ref[9*C0:9*C0+TILE, :] = jnp.zeros((TILE, CH), f32)
    z = jnp.zeros((8, CH), f32)
    gs_ref[:, PIX:PIX+SIDE, :] = jnp.zeros((2, SIDE, CH), narrow)
    col = pixel_column(EL, CH)
    total = z
    pad_ref[PIX:PIX+16, :] = jnp.zeros((16, CH), f32)
    for r in range(0, PIX, EL):
        g = grad_ref[r:r+EL, :].astype(narrow)
        gs_ref[0, r:r+EL, :] = g
        g = g.astype(f32)
        pad_ref[r:r+EL, :] = g
        total += fold(g)
    for r in range(0, PIX, EL):
        gs_ref[1, r:r+EL, :] = jnp.where(col == SIDE-1, 0.0, pad_ref[r+1:r+1+EL, :]).astype(narrow)
    down_bias = jnp.sum(total, axis=0, keepdims=True)
    def shifted(dy, dx):
        top = SIDE if dy == -1 else 0
        return gs_ref[1 if dx == -1 else 0, top:top+PIX, :]
    phases = [noisy_ref[i] for i in range(4)]
    stem_grad, stem_bias = None, None
    for a, b in PHASES:
        turned = jnp.transpose(skip_ref[2*a+b].astype(f32)).astype(narrow)
        more = more_ref[2*a+b]
        for t, (dy, dx) in enumerate(OFFSETS):
            if (dy % 2, dx % 2) == (a, b):
                g = shifted(dy, dx)
                ddw_ref[spare+t*C0:spare+(t+1)*C0, :] = dot(turned, g)
                more += dot_nt(g, dw_ref[t*C0:(t+1)*C0, :])
        low = more.astype(narrow)
        part = dot(stack(phases, a, b, 1).astype(narrow), low)
        stem_grad = part if stem_grad is None else stem_grad+part
        part = fold(low.astype(f32))
        stem_bias = part if stem_bias is None else stem_bias+part
    for r in range(0, 9*C0+TILE, 16*TILE):
        end = min(r+16*TILE, 9*C0+TILE)
        low_ref[r//TILE:end//TILE] = ddw_ref[r:end, :].astype(narrow).reshape((end-r)//TILE, TILE, CH)
    copy = pltpu.make_async_copy(low_ref, large_ref.at[top_row//TILE:top_row//TILE+9*C0//TILE+1], sems.at[0])
    copy.start()
    copy.wait()
    small_ref[SMALL_STEM:SMALL_STEM+40, :] = jnp.concatenate(
        [stem_grad[0:40, :], jnp.concatenate([stem_grad[40:72, :], jnp.zeros((8, C0), f32)], axis=0)], axis=1)
    stem_bias = jnp.sum(stem_bias, axis=0, keepdims=True)
    small_ref[SMALL_HEAD:SMALL_HEAD+120, :] = head_ref[...]
    small_ref[SMALL_ATTN:SMALL_ATTN+8, :] = attn_ref[...]
    small_ref[SMALL_S1:SMALL_S1+8, :] = s1_ref[...]
    small_ref[SMALL_S0:SMALL_S0+8, :] = s0_ref[...]
    mine = lax.broadcasted_iota(jnp.int32, (n, CH), 0) == me_ref[0]
    for b, from_ref in enumerate((s0_ref, s1_ref)):
        for h in range(2):
            at = SMALL_MOVED+(2*b+h)*n
            small_ref[at:at+n, :] = jnp.where(mine, from_ref[6+h:7+h, :], 0.0)
    small_ref[SMALL_STEM+40:SMALL_STEM+48, :] = rows_of(down_bias, jnp.concatenate([stem_bias, jnp.zeros((1, C0), f32)], axis=1))

def down_stem_back(me, n, grad, skip, more, down_w, noisy, head_tail, attn_small, s1, s0, large):
    return call(functools.partial(down_stem_back_kernel, n),
        [me.reshape(1), grad, skip, more, down_w, noisy, head_tail, attn_small, s1, s0, large],
        [sds(large.shape, narrow), sds((SMALL_MOVED+4*n, CH))],
        [pltpu.VMEM((PIX+16, CH), f32), pltpu.VMEM((2, PIX+SIDE, CH), narrow), pltpu.VMEM((9*C0+TILE, CH), f32),
         pltpu.VMEM((9*C0//TILE+1, TILE, CH), narrow), pltpu.SemaphoreType.DMA((1,))],
        2*2*PIX*9*C0*CH, away=(10,), away_out=(0,), alias={10: 0}, scalar=(0,))

HEAD_PER = (C0+CH)//GROUPS
def silu_slope(v):
    s = sigmoid(v)
    return s*(1.0+v*(1.0-s))

KL = 0.001
def head_kernel(num_ref, state_ref, skip_ref, wu_ref, ws_ref, vu_ref, vs_ref, bias_ref, noise_ref, mask_ref,
                state_grad_ref, skip_grad_ref, tail_ref, loss_ref,
                up_ref, side_ref, q_ref):
    log_beta, log_tilde, coefficient, sample = (num_ref[i] for i in range(4))
    gain_u, shift_u = vu_ref[0:1, :], vu_ref[1:2, :]
    gain_s, shift_s = vs_ref[0:1, :], vs_ref[1:2, :]
    mu, ms = membership(CH, HEAD_PER), membership(C0, HEAD_PER, CH)
    amount = 4*PIX*HEAD_PER
    one = lambda v: jnp.sum(v, axis=0, keepdims=True)
    zu, zs = jnp.zeros((8, CH), f32), jnp.zeros((8, C0), f32)
    def sums_u(i, c):
        v = state_ref[pl.ds(pl.multiple_of(i*EL, EL), EL), :]
        return c[0]+fold(v), c[1]+fold(v*v)
    u1, u2 = steps(PIX//EL, sums_u, (zu, zu))
    s1, s2 = zs, zs
    for k in range(4):
        def sums_s(i, c):
            v = skip_ref[k, pl.ds(pl.multiple_of(i*EL, EL), EL), :].astype(f32)
            return c[0]+fold(v), c[1]+fold(v*v)
        s1, s2 = steps(PIX//EL, sums_s, (s1, s2))
    tot = (exact(rows_of(4.0*one(u1), 4.0*one(u2)), mu) + exact(rows_of(one(s1), one(s2)), ms))/amount
    tot_u, tot_s = exact_nt(tot, mu), exact_nt(tot, ms)
    mean_u, inv_u = tot_u[0:1], lax.rsqrt(tot_u[1:2]-tot_u[0:1]*tot_u[0:1]+1e-05)
    mean_s, inv_s = tot_s[0:1], lax.rsqrt(tot_s[1:2]-tot_s[0:1]*tot_s[0:1]+1e-05)
    def act_u(i, _):
        r = pl.ds(pl.multiple_of(i*EL, EL), EL)
        v = (state_ref[r, :]-mean_u)*inv_u*gain_u+shift_u
        up_ref[r, :] = (v*sigmoid(v)).astype(narrow)
        return _
    steps(PIX//EL, act_u, 0)
    for k in range(4):
        def act_s(i, _):
            r = pl.ds(pl.multiple_of(i*EL, EL), EL)
            v = (skip_ref[k, r, :].astype(f32)-mean_s)*inv_s*gain_s+shift_s
            side_ref[k, r, :] = (v*sigmoid(v)).astype(narrow)
            return _
        steps(PIX//EL, act_s, 0)
    from_up = dot_nt(wu_ref[...], up_ref[...])
    for k in range(4):
        q_ref[k] = from_up + dot_nt(ws_ref[...], side_ref[k])
    row = lax.broadcasted_iota(jnp.int32, (8, PIX), 0)
    loss, vlb, outs, bias_grad = jnp.zeros((1, PIX), f32), jnp.zeros((1, PIX), f32), [], jnp.zeros((8, PIX), f32)
    for a, b in PHASES:
        out = jnp.zeros((8, PIX), f32)
        for t, (dy, dx) in enumerate(OFFSETS):
            at, di, dj = source(a, b, dy, dx)
            out += shift_lanes(q_ref[at, 8*t:8*t+8, :], di, dj)
        out += bias_ref[:, 0:1]
        k = 2*a+b
        error = jnp.where(row < 3, out - noise_ref[k], 0.0)
        fraction = jnp.where(row < 3, (pltpu.roll(out, 5, 0)+1.0)/2.0, 0.0)
        log_var = fraction*log_beta + (1.0-fraction)*log_tilde
        inverse = jnp.exp(-log_var)
        ratio = jnp.exp(log_tilde-log_var)
        divergence = 0.5*(-1.0+log_var-log_tilde+ratio+coefficient*error*error*inverse)
        divergence = jnp.where(row < 3, divergence, 0.0)
        weight = sample*mask_ref[k]
        loss += weight*jnp.sum(error*error+KL*divergence, axis=0, keepdims=True)
        vlb += weight*KL*jnp.sum(divergence, axis=0, keepdims=True)
        predict = weight*(2.0*error+KL*coefficient*error*inverse)
        var_grad = weight*KL*0.5*(1.0-ratio-coefficient*error*error*inverse)*(log_beta-log_tilde)/2.0
        og = jnp.where(row < 3, predict, jnp.where(row < 6, pltpu.roll(var_grad, 3, 0), 0.0))
        og = og.astype(narrow).astype(f32)
        bias_grad += og
        outs.append(og)
    bias_grad = jnp.broadcast_to(jnp.sum(bias_grad, axis=1, keepdims=True), (8, CH))
    diagonal = lax.broadcasted_iota(jnp.int32, (8, CH), 0) == lax.broadcasted_iota(jnp.int32, (8, CH), 1)
    bias_grad = jnp.sum(jnp.where(diagonal, bias_grad, 0.0), axis=0, keepdims=True)
    loss_ref[...] = jnp.concatenate([jnp.broadcast_to(jnp.sum(loss, axis=1, keepdims=True), (1, 128)),
        jnp.broadcast_to(jnp.sum(vlb, axis=1, keepdims=True), (1, 128)), jnp.zeros((6, 128), f32)], axis=0)
    nine_sum, gs_total = None, None
    d1, d2 = zs, zs
    for a, b in PHASES:
        k = 2*a+b
        nine = stack(outs, a, b, -1)
        nine_sum = nine if nine_sum is None else nine_sum+nine
        part = dot(nine.astype(narrow), side_ref[k])
        gs_total = part if gs_total is None else gs_total+part
        d = dot(jnp.transpose(nine).astype(narrow), ws_ref[...])
        n = (skip_ref[k].astype(f32)-mean_s)*inv_s
        d = d*silu_slope(n*gain_s+shift_s)
        skip_grad_ref[k] = d
        d1, d2 = d1+fold(d), d2+fold(d*n)
    tail_ref[72:112, :] = jnp.concatenate(
        [gs_total[0:40, :], jnp.concatenate([gs_total[40:72, :], jnp.zeros((8, C0), f32)], axis=0)], axis=1)
    hi = nine_sum.astype(narrow); lo = (nine_sum-hi.astype(f32)).astype(narrow)
    tail_ref[0:72, :] = (dot(hi, up_ref[...])+dot(lo, up_ref[...]))[0:72, :]
    turned = jnp.transpose(nine_sum)
    hi = turned.astype(narrow); lo = (turned-hi.astype(f32)).astype(narrow)
    d = dot(hi, wu_ref[...])+dot(lo, wu_ref[...])
    n = (state_ref[...]-mean_u)*inv_u
    d = d*silu_slope(n*gain_u+shift_u)
    state_grad_ref[...] = d
    e1, e2 = one(fold(d)), one(fold(d*n))
    d1, d2 = one(d1), one(d2)
    tail_ref[112:120, :] = rows_of(e2, e1, jnp.concatenate([d2, d1], axis=1), bias_grad)
    tot = (exact(rows_of(e1*gain_u, e2*gain_u), mu)+exact(rows_of(d1*gain_s, d2*gain_s), ms))/amount
    tot_u, tot_s = exact_nt(tot, mu), exact_nt(tot, ms)
    def back_u(i, _):
        r = pl.ds(pl.multiple_of(i*EL, EL), EL)
        n = (state_ref[r, :]-mean_u)*inv_u
        state_grad_ref[r, :] = (state_grad_ref[r, :]*gain_u-4.0*tot_u[0:1]-4.0*n*tot_u[1:2])*inv_u
        return _
    steps(PIX//EL, back_u, 0)
    for k in range(4):
        def back_s(i, _):
            r = pl.ds(pl.multiple_of(i*EL, EL), EL)
            n = (skip_ref[k, r, :].astype(f32)-mean_s)*inv_s
            skip_grad_ref[k, r, :] = (skip_grad_ref[k, r, :]*gain_s-tot_s[0:1]-n*tot_s[1:2])*inv_s
            return _
        steps(PIX//EL, back_s, 0)

def head(numbers, state, skip, wu, ws, vu, vs, bias, noise, mask):
    spec = pl.BlockSpec(memory_space=VM)
    ins = [numbers, state, skip, wu, ws, vu, vs, bias, noise, mask]
    outs = [sds((PIX, CH)), sds((4, PIX, C0)), sds((120, CH)), sds((8, 128))]
    return pl.pallas_call(head_kernel, out_shape=outs,
        in_specs=[pl.BlockSpec(memory_space=pltpu.SMEM)]+[spec]*(len(ins)-1), out_specs=[spec]*len(outs),
        scratch_shapes=[pltpu.VMEM((PIX, CH), narrow), pltpu.VMEM((4, PIX, C0), narrow), pltpu.VMEM((4, 128, PIX), f32)],
        compiler_params=pltpu.CompilerParams(vmem_limit_bytes=LIMIT),
        cost_estimate=pl.CostEstimate(flops=4*2*PIX*128*(4*C0+CH), bytes_accessed=12*2**20, transcendentals=0))(*ins)

HP = 128
QW = HEADS*HP
SCALE = 1.0/math.sqrt(HEAD_DIM)
QC = 256
ATTN_FIRST = (ROW["attn_gain"]+LEAD)//TILE
ATTN_TILES = -(-(ROW["proj_b"]+LEAD+1)//TILE)-ATTN_FIRST
ATTN = {name: ROW[name]+LEAD-ATTN_FIRST*TILE for name in ("attn_gain", "attn_shift", "qkv_w", "qv_b", "proj_w", "proj_b")}

def get_rows(ref, at):
    return jnp.concatenate([ref[i, at, :] for i in range(3)], axis=1)

def put_rows(ref, at, value):
    for i in range(3):
        ref[i, at, :] = value[:, i*128:(i+1)*128]

def attention_forward_kernel(rows, state_ref, pieces_ref, out_ref, qkv_ref, log_ref, mixed_t_ref, stat_ref, wp_ref, wo_ref, vec_ref,
                             mixed_ref, vt_ref, bp_ref, wide_ref, rows_ref, edge_ref, sems):
    rows.start(pieces_ref, rows_ref, edge_ref, sems)
    rows.finish(pieces_ref, rows_ref, edge_ref, sems)
    for r in range(0, ATTN_TILES*TILE, 16*TILE):
        end = min(r+16*TILE, ATTN_TILES*TILE)
        put_rows(wide_ref, slice(r, end), rows_ref[r:end, :].astype(f32))
    one_row = lambda name, i=0: get_rows(wide_ref, slice(ATTN[name]+i, ATTN[name]+i+1))
    gain, shift, bias = one_row("attn_gain"), one_row("attn_shift"), one_row("proj_b")
    vec_ref[...] = rows_of(gain, shift)
    nothing = jnp.zeros((CH, HP-HEAD_DIM), f32)
    for j in range(3):
        third = get_rows(wide_ref, pl.ds(ATTN["qkv_w"]+j, CH, stride=3))
        third_bias = one_row("qv_b", j//2) if j != 1 else jnp.zeros((1, CH), f32)
        for h in range(HEADS):
            to = slice(j*QW+h*HP, j*QW+(h+1)*HP)
            wp_ref[:, to] = jnp.concatenate([third[:, h*HEAD_DIM:(h+1)*HEAD_DIM], nothing], axis=1).astype(narrow)
            bp_ref[:, to] = jnp.concatenate([third_bias[:, h*HEAD_DIM:(h+1)*HEAD_DIM], nothing[0:1]], axis=1)
    for h in range(HEADS):
        at = ATTN["proj_w"]+h*HEAD_DIM
        wo_ref[h*HP:h*HP+HEAD_DIM, :] = get_rows(wide_ref, slice(at, at+HEAD_DIM)).astype(narrow)
        wo_ref[h*HP+HEAD_DIM:(h+1)*HP, :] = jnp.zeros((HP-HEAD_DIM, CH), narrow)
    member = membership(CH, CH//GROUPS)
    def sums(i, c):
        v = state_ref[pl.ds(pl.multiple_of(i*EL, EL), EL), :]
        return c[0]+fold(v), c[1]+fold(v*v)
    z = jnp.zeros((8, CH), f32)
    mean, inv = norm_stats(*steps(PIX//EL, sums, (z, z)), member, PIX*(CH//GROUPS))
    stat_ref[...] = rows_of(mean, inv)
    def project(i, _):
        r = pl.ds(pl.multiple_of(i*256, 256), 256)
        n = ((state_ref[r, :]-mean)*inv*gain+shift).astype(narrow)
        qkv_ref[r, :] = (dot(n, wp_ref[...])+bp_ref[...]).astype(narrow)
        return _
    steps(PIX//256, project, 0)
    for h in range(HEADS):
        vt_ref[...] = jnp.transpose(qkv_ref[:, 2*QW+h*HP:2*QW+(h+1)*HP].astype(f32)).astype(narrow)
        for c in range(0, PIX, QC):
            s = dot_nt(qkv_ref[:, QW+h*HP:QW+(h+1)*HP], qkv_ref[c:c+QC, h*HP:(h+1)*HP])*SCALE
            top = jnp.max(s, axis=0, keepdims=True)
            e = jnp.exp(s-top)
            total = jnp.sum(e, axis=0, keepdims=True)
            log_ref[h:h+1, c:c+QC] = top+jnp.log(total)
            p = (e*(1.0/total)).astype(narrow)
            m = dot(vt_ref[...], p).astype(narrow)
            mixed_t_ref[h*HP:(h+1)*HP, c:c+QC] = m
            mixed_ref[c:c+QC, h*HP:(h+1)*HP] = jnp.transpose(m.astype(f32)).astype(narrow)
    log_ref[HEADS:8, :] = jnp.zeros((8-HEADS, PIX), f32)
    def finish(i, _):
        r = pl.ds(pl.multiple_of(i*256, 256), 256)
        out_ref[r, :] = state_ref[r, :]+(dot(mixed_ref[r, :], wo_ref[...])+bias)
        return _
    steps(PIX//256, finish, 0)

def attention_forward(place, state, pieces):
    rows = Rows(place, ATTN_FIRST, ATTN_TILES)
    return call(functools.partial(attention_forward_kernel, rows), [state, pieces],
        [sds((PIX, CH)), sds((PIX, 3*QW), narrow), sds((8, PIX)), sds((QW, PIX), narrow), sds((8, CH)),
         sds((CH, 3*QW), narrow), sds((QW, CH), narrow), sds((8, CH))],
        [pltpu.VMEM((PIX, QW), narrow), pltpu.VMEM((HP, PIX), narrow), pltpu.VMEM((1, 3*QW), f32),
         pltpu.VMEM((3, ATTN_TILES*TILE, 128), f32)]+rows.scratch(),
        2*PIX*(CH*4*QW+2*PIX*QW), away=(1,))

def attention_back_kernel(grad_ref, state_ref, stat_ref, qkv_ref, log_ref, mixed_t_ref, wp_ref, wo_ref, vec_ref,
                          out_ref, large_ref, small_ref, dm_ref, pg_ref, kt_ref, dv_ref, dk_ref, nt_ref, keep_ref,
                          wide_ref, rows_ref, sems):
    gain, shift = vec_ref[0:1, :], vec_ref[1:2, :]
    mean, inv = stat_ref[0:1, :], stat_ref[1:2, :]
    member = membership(CH, CH//GROUPS)
    z = jnp.zeros((8, CH), f32)
    one = lambda v: jnp.sum(v, axis=0, keepdims=True)
    def start(i, c):
        r = pl.ds(pl.multiple_of(i*256, 256), 256)
        g = grad_ref[r, :].astype(narrow)
        keep_ref[r, :] = g
        dm_ref[r, :] = dot_nt(g, wo_ref[...]).astype(narrow)
        return c+fold(g.astype(f32))
    proj_bias = steps(PIX//256, start, z)
    for name, after in (("attn_gain", ATTN["qkv_w"]), ("qv_b", ATTN["proj_w"]), ("proj_b", ATTN_TILES*TILE)):
        put_rows(wide_ref, slice(ATTN[name], after), jnp.zeros((after-ATTN[name], CH), f32))
    wo_grad = dot(mixed_t_ref[...], keep_ref[...])
    for h in range(HEADS):
        at = ATTN["proj_w"]+h*HEAD_DIM
        put_rows(wide_ref, slice(at, at+HEAD_DIM), wo_grad[h*HP:h*HP+HEAD_DIM, :])
    for h in range(HEADS):
        q0, k0, v0 = h*HP, QW+h*HP, 2*QW+h*HP
        kt_ref[...] = jnp.transpose(qkv_ref[:, k0:k0+HP].astype(f32)).astype(narrow)
        for c in range(0, PIX, QC):
            q, dm = qkv_ref[c:c+QC, q0:q0+HP], dm_ref[c:c+QC, h*HP:(h+1)*HP]
            s = dot_nt(qkv_ref[:, k0:k0+HP], q)*SCALE
            p = jnp.exp(s-log_ref[h:h+1, c:c+QC])
            dp = dot_nt(qkv_ref[:, v0:v0+HP], dm)
            delta = jnp.sum(dp*p, axis=0, keepdims=True)
            ds = (p*(dp-delta)).astype(narrow)
            dv = dot(p.astype(narrow), dm)
            dk = dot(ds, q)
            if c == 0:
                dv_ref[...] = dv
                dk_ref[...] = dk
            else:
                dv_ref[...] += dv
                dk_ref[...] += dk
            dq = dot(kt_ref[...], ds)
            pg_ref[c:c+QC, q0:q0+HP] = jnp.transpose(dq*SCALE).astype(narrow)
        pg_ref[:, k0:k0+HP] = (dk_ref[...]*SCALE).astype(narrow)
        pg_ref[:, v0:v0+HP] = dv_ref[...].astype(narrow)
    for r in range(0, PIX, 256):
        nt_ref[:, r:r+256] = jnp.transpose((state_ref[r:r+256, :]-mean)*inv*gain+shift).astype(narrow)
    for j in range(3):
        third = dot(nt_ref[...], pg_ref[:, j*QW:(j+1)*QW])
        third = jnp.concatenate([third[:, h*HP:h*HP+HEAD_DIM] for h in range(HEADS)], axis=1)
        put_rows(wide_ref, pl.ds(ATTN["qkv_w"]+j, CH, stride=3), third)
    for r in range(0, ATTN_TILES, 16):
        end = min(r+16, ATTN_TILES)
        rows_ref[r:end] = get_rows(wide_ref, slice(r*TILE, end*TILE)).astype(narrow).reshape(end-r, TILE, CH)
    copy = pltpu.make_async_copy(rows_ref, large_ref.at[ATTN_FIRST:ATTN_FIRST+ATTN_TILES], sems.at[0])
    copy.start()
    zb = jnp.zeros((8, 3*QW), f32)
    def norm_grad(i, c):
        r = pl.ds(pl.multiple_of(i*256, 256), 256)
        d = dot_nt(pg_ref[r, :], wp_ref[...])
        n = (state_ref[r, :]-mean)*inv
        out_ref[r, :] = d
        return c[0]+fold(d), c[1]+fold(d*n), c[2]+fold(pg_ref[r, :].astype(f32))
    shift_grad, gain_grad, bias_grad = (one(v) for v in steps(PIX//256, norm_grad, (z, z, zb)))
    compact = [jnp.concatenate([bias_grad[:, j*QW+h*HP:j*QW+h*HP+HEAD_DIM] for h in range(HEADS)], axis=1) for j in (0, 2)]
    tot = group_totals(rows_of(shift_grad*gain, gain_grad*gain), member)/(PIX*(CH//GROUPS))
    first, second = tot[0:1], tot[1:2]
    def finish(i, _):
        r = pl.ds(pl.multiple_of(i*EL, EL), EL)
        n = (state_ref[r, :]-mean)*inv
        out_ref[r, :] = grad_ref[r, :]+(out_ref[r, :]*gain-first-n*second)*inv
        return _
    steps(PIX//EL, finish, 0)
    small_ref[...] = rows_of(gain_grad, shift_grad, compact[0], compact[1], one(proj_bias))
    copy.wait()

def attention_back(grad, state, stat, qkv, log, mixed_t, wp, wo, vec, tiles):
    return call(attention_back_kernel, [grad, state, stat, qkv, log, mixed_t, wp, wo, vec],
        [sds((PIX, CH)), sds((tiles, TILE, CH), narrow), sds((8, CH))],
        [pltpu.VMEM((PIX, QW), narrow), pltpu.VMEM((PIX, 3*QW), narrow), pltpu.VMEM((HP, PIX), narrow), pltpu.VMEM((PIX, HP), f32),
         pltpu.VMEM((PIX, HP), f32), pltpu.VMEM((CH, PIX), narrow), pltpu.VMEM((PIX, CH), narrow),
         pltpu.VMEM((3, ATTN_TILES*TILE, 128), f32), pltpu.VMEM((ATTN_TILES, TILE, CH), narrow), pltpu.SemaphoreType.DMA((1,))],
        2*PIX*(CH*8*QW+5*PIX*QW), away_out=(1,))


def to_phases(v):
    c = v.shape[0]
    return jnp.transpose(v.reshape(c, SIDE, 2, SIDE, 2), (2, 4, 0, 1, 3)).reshape(4, c, PIX)


def pad_rows8(v):
    return jnp.pad(v, ((0, 0), (0, 8-v.shape[1]), (0, 0)))


def taps_rows(v):
    v = jnp.pad(v, ((0, 0), (0, 8-v.shape[1]), (0, 0))).reshape(72, v.shape[2])
    return jnp.pad(v, ((0, 128-72), (0, 0)))


class Place:
    def __init__(self, sizes, share):
        self.sizes = sizes
        self.share = share
        self.total = sizes["y"]*sizes["c"]*sizes["z"]*sizes["x"]
        firsts = [(share*d+LEAD)//TILE for d in range(self.total)]
        lasts = [-(-(share*(d+1)+LEAD)//TILE) for d in range(self.total)]
        self.block = max(last-first for first, last in zip(firsts, lasts))
        self.tiles = max(first+self.block for first in firsts)
        self.tiles = -(-self.tiles//TILE)*TILE
        self.at = {axis: lax.axis_index(axis) for axis in sizes}

    def device(self, y, c, z, x):
        s = self.sizes
        return ((y*s["c"]+c)*s["z"]+z)*s["x"]+x

    def first(self, device):
        return (self.share*device+LEAD)//TILE

    def me(self):
        a = self.at
        return self.device(a["y"], a["c"], a["z"], a["x"])


def turn(value, axis, size, distance):
    return lax.ppermute(value, axis, [(i, (i+distance) % size) for i in range(size)])


def hold_for(value, others):
    return lax.optimization_barrier((value, others))[0]


def add_everywhere(value, place):
    return add_over(value, place, ("c", "x", "y", "z"))


def add_over(value, place, axes):
    for axis in axes:
        size, step = place.sizes[axis], 1
        while step < size:
            value = value+lax.ppermute(value, axis, [(i, i ^ step) for i in range(size)])
            step *= 2
    return value


def cut_kernel(count, size, starts_ref, large_ref, out_ref, sems):
    copies = [pltpu.make_async_copy(large_ref.at[pl.ds(starts_ref[i], size)], out_ref.at[i], sems.at[i]) for i in range(count)]
    for copy in copies:
        copy.start()
    for copy in copies:
        copy.wait()


def cut(large, starts, size):
    count = starts.shape[0]
    return pl.pallas_call(
        functools.partial(cut_kernel, count, size),
        out_shape=sds((count, size, TILE, WIDE), narrow),
        in_specs=[pl.BlockSpec(memory_space=pltpu.SMEM), pl.BlockSpec(memory_space=pl.ANY)],
        out_specs=pl.BlockSpec(memory_space=VM),
        scratch_shapes=[pltpu.SemaphoreType.DMA((count,))],
        compiler_params=pltpu.CompilerParams(vmem_limit_bytes=LIMIT),
        cost_estimate=pl.CostEstimate(flops=0, bytes_accessed=1024, transcendentals=0),
    )(starts, large)


def merge_kernel(coords, sends, count, size, starts_ref, large_ref, arrived_ref, *refs):
    outs, (held_ref, sems) = refs[:-2], refs[-2:]
    copies = [pltpu.make_async_copy(large_ref.at[pl.ds(starts_ref[i], size)], held_ref.at[i], sems.at[i]) for i in range(count)]
    for copy in copies:
        copy.start()
    for i in range(count):
        copies[i].wait()
        which, at = sends[i]
        outs[which][at] = (held_ref[i].astype(f32)+arrived_ref[i].astype(f32)).astype(outs[which].dtype)


def share_out(large, small, place, parts):
    s, a, block = place.sizes, place.at, place.block
    half = (s["z"]+1)//2
    coords = [(y, z, x) for y in range(s["y"]) for z in range(s["z"]) for x in range(s["x"])]

    def starts(core):
        return jnp.stack([
            place.first(place.device((a["y"]+y) % s["y"], core, (a["z"]+z) % s["z"], (a["x"]+x) % s["x"])) for y, z, x in coords
        ]).astype(jnp.int32)

    far_starts, own_starts = starts(1-a["c"]), starts(a["c"])
    bounds = [block*i//parts for i in range(parts+1)]
    groups = [("y", [(0, z, x) for z in range(half) for x in range(s["x"])])]
    groups += [("y%d" % k, [(k, z, x) for z in range(half) for x in range(s["x"])]) for k in range(1, s["y"])]
    groups += [("x", [(y, z, 0) for z in range(half, s["z"]) for y in range(s["y"])])]
    groups += [("x%d" % k, [(y, z, k) for z in range(half, s["z"]) for y in range(s["y"])]) for k in range(1, s["x"])]
    names = [name for name, members in groups]
    sends = [None]*len(coords)
    for g, (name, members) in enumerate(groups):
        for at, member in enumerate(members):
            sends[coords.index(member)] = (g, at)
    length = small.shape[0]//2
    half_small, other_small = (lax.dynamic_slice_in_dim(small, core*length, length) for core in (a["c"], 1-a["c"]))
    arrived, merged = [], []
    for part in range(parts):
        sent = cut(large, far_starts+bounds[part], bounds[part+1]-bounds[part])
        arrived.append(turn(sent, "c", 2, 1))
        far_starts = hold_for(far_starts, sent)
    half_small = add_over(half_small+turn(other_small, "c", 2, 1), place, ("x",))
    for part in range(parts):
        size = bounds[part+1]-bounds[part]
        outs = [sds((len(members), size, TILE, WIDE), f32 if name in ("y", "x") else narrow) for name, members in groups]
        out = pl.pallas_call(
            functools.partial(merge_kernel, coords, sends, len(coords), size),
            out_shape=outs,
            in_specs=[pl.BlockSpec(memory_space=pltpu.SMEM), pl.BlockSpec(memory_space=pl.ANY), pl.BlockSpec(memory_space=VM)],
            out_specs=[pl.BlockSpec(memory_space=VM)]*len(outs),
            scratch_shapes=[pltpu.VMEM((len(coords), size, TILE, WIDE), narrow), pltpu.SemaphoreType.DMA((len(coords),))],
            compiler_params=pltpu.CompilerParams(vmem_limit_bytes=LIMIT),
            cost_estimate=pl.CostEstimate(flops=0, bytes_accessed=1024, transcendentals=0),
        )(own_starts+bounds[part], large, arrived[part])
        own_starts = hold_for(own_starts, out)
        merged.append(dict(zip(names, out)))

    def first_stage(sums):
        return ([turn(sums["y%d" % k], "y", s["y"], k) for k in range(1, s["y"])],
                [turn(sums["x%d" % k], "x", s["x"], k) for k in range(1, s["x"])])

    def first_sums(sums, came):
        near = sums["y"]+sum(value.astype(f32) for value in came[0])
        far = sums["x"]+sum(value.astype(f32) for value in came[1])
        return near.reshape((half, s["x"])+near.shape[1:]), far.reshape((s["z"]-half, s["y"])+far.shape[1:])

    def second_sums(near, far):
        near = near[:, 0]+sum(turn(near[:, k].astype(narrow), "x", s["x"], k).astype(f32) for k in range(1, s["x"]))
        far = far[:, 0]+sum(turn(far[:, k].astype(narrow), "y", s["y"], k).astype(f32) for k in range(1, s["y"]))
        return near, far

    def third_sum(near, far):
        total = near[0]
        for z in range(1, s["z"]):
            value = near[z] if z < half else far[z-half]
            total = total+turn(value.astype(narrow), "z", s["z"], z).astype(f32)
        return total

    waiting = [first_stage(merged[part]) for part in range(min(2, parts))]
    results, ready = [], None
    for part in range(parts):
        if part == 0:
            waiting[0] = hold_for(waiting[0], merged[-1])
        near, far = first_sums(merged[part], waiting[part])
        if part == 0:
            half_small = add_over(hold_for(half_small, (near, far)), place, ("y",))
        if part == min(1, parts-1):
            half_small = add_over(hold_for(half_small, (near, far)), place, ("z",))
        if part+2 < parts:
            waiting.append(first_stage(hold_for(merged[part+2], (near, far))))
        results.append(third_sum(*second_sums(near, far)))
    other_small = turn(half_small, "c", 2, 1)
    first = a["c"] == 0
    small = jnp.concatenate([jnp.where(first, half_small, other_small), jnp.where(first, other_small, half_small)])
    return jnp.concatenate(results, axis=0), small


SPOTS = (
    list(range(14))
    + [ROW["time1_b"], ROW["time1_b"]+1, ROW["time2_b"], ROW["time2_b"]+1, ROW["down_b"]]
    + [ROW["res_b"]+i for i in range(4)]
    + [ROW["emb_b"]+i for i in range(4)]
    + [ROW["res_gain"]+i for i in range(4)]
    + [ROW["res_shift"]+i for i in range(4)]
    + [ROW["attn_gain"], ROW["attn_shift"], ROW["qv_b"], ROW["qv_b"]+1, ROW["proj_b"]]
    + [ROW["head_gain"]+i for i in range(3)] + [ROW["head_b"]] + [-1]*4
    + [ROW["head_gain"]+3+9*tap+part if tap < 9 else -1 for part in range(9) for tap in range(16)]
)
SPOTS += [-1]*(256-len(SPOTS))

TIME_FIRST = (ROW["time1_w"]+LEAD)//TILE
TIME_TILES = -(-(ROW["time2_b"]+2+LEAD)//TILE)-TIME_FIRST
EMB_FIRST = (ROW["res_b"]+LEAD)//TILE
EMB_TILES = -(-(ROW["res_shift"]+4+LEAD)//TILE)-EMB_FIRST


def widen_rows(low_ref, wide_ref, count):
    for r in range(0, count, 16*TILE):
        end = min(r+16*TILE, count)
        put_rows(wide_ref, slice(r, end), low_ref[r:end, :].astype(f32))


def time_kernel(n, rows, me_ref, sinus_ref, pieces_ref, hidden_pre_ref, hidden_ref, outer_pre_ref, embed_ref, vec_ref, w2_ref, we_ref,
                time_ref, emb_ref, *held):
    one, two = (pieces_ref,)+held[:3], (pieces_ref,)+held[3:]
    rows[0].start(*one)
    rows[1].start(*two)
    rows[0].finish(*one)
    time_low_ref, emb_low_ref = held[0], held[3]
    widen_rows(time_low_ref, time_ref, TIME_TILES*TILE)

    def in_time(name, i=0):
        return ROW[name]+LEAD-TIME_FIRST*TILE+i

    def in_emb(name, i=0):
        return ROW[name]+LEAD-EMB_FIRST*TILE+i

    def row(ref, at):
        return get_rows(ref, slice(at, at+1))

    for h in range(2):
        w1 = get_rows(time_ref, pl.ds(in_time("time1_w", h), C0, stride=2)).astype(narrow)
        hidden_pre_ref[:, h*CH:(h+1)*CH] = dot(sinus_ref[...], w1)+row(time_ref, in_time("time1_b", h))
        w2_ref[h] = get_rows(time_ref, pl.ds(in_time("time2_w", h), TEMB, stride=2)).astype(narrow)
    v = hidden_pre_ref[...]
    hidden_ref[...] = (v*sigmoid(v)).astype(narrow)
    for h in range(2):
        outer_pre_ref[:, h*CH:(h+1)*CH] = dot(hidden_ref[...], w2_ref[h])+row(time_ref, in_time("time2_b", h))
    v = outer_pre_ref[...]
    embed = (v*sigmoid(v)).astype(narrow)
    embed_ref[...] = embed
    mine = lax.broadcasted_iota(jnp.int32, (n, TEMB), 0) == me_ref[0]
    own = jnp.sum(jnp.where(mine, embed.astype(f32), 0.0), axis=0, keepdims=True)
    own = jnp.broadcast_to(own, (8, TEMB)).astype(narrow)
    rows[1].finish(*two)
    widen_rows(emb_low_ref, emb_ref, EMB_TILES*TILE)
    for b in range(BLOCKS):
        modulate = []
        for h in range(2):
            we_ref[b, h] = get_rows(emb_ref, pl.ds(in_emb("emb_w", 2*TEMB*b+h), TEMB, stride=2)).astype(narrow)
            modulate.append(dot(own, we_ref[b, h])[0:1]+row(emb_ref, in_emb("emb_b", 2*b+h)))
        vec_ref[b] = jnp.concatenate([
            row(emb_ref, in_emb("res_b", 2*b)), row(emb_ref, in_emb("res_b", 2*b+1)),
            row(emb_ref, in_emb("res_gain", 2*b)), row(emb_ref, in_emb("res_shift", 2*b)),
            row(emb_ref, in_emb("res_gain", 2*b+1)), row(emb_ref, in_emb("res_shift", 2*b+1)),
            1.0+modulate[0], modulate[1],
        ], axis=0)


def time_and_modulation(place, sinus, pieces):
    rows = [Rows(place, TIME_FIRST, TIME_TILES), Rows(place, EMB_FIRST, EMB_TILES)]
    n = sinus.shape[0]
    spec = pl.BlockSpec(memory_space=VM)
    return pl.pallas_call(
        functools.partial(time_kernel, n, rows),
        out_shape=[sds((n, TEMB)), sds((n, TEMB), narrow), sds((n, TEMB)), sds((n, TEMB), narrow), sds((BLOCKS, 8, CH)),
                   sds((2, TEMB, CH), narrow), sds((BLOCKS, 2, TEMB, CH), narrow)],
        in_specs=[pl.BlockSpec(memory_space=pltpu.SMEM), spec, pl.BlockSpec(memory_space=pl.ANY)],
        out_specs=[spec]*7,
        scratch_shapes=[pltpu.VMEM((3, TIME_TILES*TILE, 128), f32), pltpu.VMEM((3, EMB_TILES*TILE, 128), f32)]
        + rows[0].scratch()+rows[1].scratch(),
        compiler_params=pltpu.CompilerParams(vmem_limit_bytes=LIMIT),
        cost_estimate=pl.CostEstimate(flops=2**27, bytes_accessed=8*2**20, transcendentals=0),
    )(place.me().reshape(1), sinus, pieces)


SMALL_HEAD, SMALL_ATTN, SMALL_S1, SMALL_STEM, SMALL_S0, SMALL_MOVED = 0, 120, 128, 136, 184, 192


def owner_kernel(share, n, me_ref, small_ref, sinus_ref, hidden_pre_ref, hidden_ref, outer_pre_ref, embed_ref, w2_ref, we_ref, spot_ref,
                 out_ref, time_ref, emb_ref, mixed_time_ref, mixed_emb_ref):
    row0 = me_ref[0]*share
    half_rows = mixed_time_ref.shape[1]//2
    one = lambda v: jnp.sum(v, axis=0, keepdims=True)
    moved = [[small_ref[SMALL_MOVED+(2*b+h)*n:SMALL_MOVED+(2*b+h+1)*n, :] for h in range(2)] for b in range(BLOCKS)]
    embed_grad = sum(exact_nt(moved[b][h], we_ref[b, h]) for b in range(BLOCKS) for h in range(2))
    outer_grad = embed_grad*silu_slope(outer_pre_ref[...])
    hidden_grad = sum(exact_nt(outer_grad[:, h*CH:(h+1)*CH], w2_ref[h]) for h in range(2))*silu_slope(hidden_pre_ref[...])

    def table(ref, values):
        ref[...] = jnp.zeros(ref.shape, f32)
        width = min(n, 128)
        for family, (value_ref, at) in enumerate(values):
            turned = jnp.transpose(value_ref[...].astype(f32))
            for first in range(0, n, width):
                group, lane = divmod(family*n+first, 128)
                ref[group, half_rows+at:half_rows+at+turned.shape[0], lane:lane+width] = turned[:, first:first+width]

    def products(ref, begin, factors, mixed_ref):
        away = row0-begin+(1 << 20)
        place = away // 2 - (1 << 19)
        start = jnp.clip(place+half_rows, 0, ref.shape[1]-half_rows)
        for h in range(2):
            right = jnp.concatenate([factors[0][h], factors[1][h]], axis=0)
            if right.shape[0] < 128:
                right = jnp.concatenate([right, jnp.zeros((128-right.shape[0], CH), f32)], axis=0)
            total = None
            for group in range(ref.shape[0]):
                left = ref[group, pl.ds(start, half_rows), :].astype(narrow)
                part = sum(dot(left, p) for p in three(right[group*128:(group+1)*128]))
                total = part if total is None else total+part
            put_rows(mixed_ref, pl.ds(h, half_rows, stride=2), total)
        odd = away-2*(away//2)
        return jnp.where(odd == 1, get_rows(mixed_ref, slice(1, 1+share)), get_rows(mixed_ref, slice(0, share)))

    halves = lambda v: [v[:, :CH], v[:, CH:]]
    table(time_ref, [(sinus_ref, 0), (hidden_ref, (ROW["time2_w"]-ROW["time1_w"])//2)])
    table(emb_ref, [(embed_ref, 0), (embed_ref, TEMB)])
    total = products(time_ref, ROW["time1_w"], [halves(hidden_grad), halves(outer_grad)], mixed_time_ref)
    total += products(emb_ref, ROW["emb_w"], moved, mixed_emb_ref)

    def small(at, count=1):
        return small_ref[at:at+count, :]

    def pairs(at):
        return jnp.concatenate([small_ref[at:at+40, :C0], small_ref[at:at+32, C0:]], axis=0)

    stem = pairs(SMALL_STEM)
    stem_rows = [stem[8*tap+c:8*tap+c+1, :] for tap in range(9) for c in range(IN_CH)]+[small(SMALL_STEM+41)[:, :C0]]
    rows = [jnp.concatenate(stem_rows[2*i:2*i+2], axis=1) for i in range(14)]
    rows += halves(one(hidden_grad))+halves(one(outer_grad))+[small(SMALL_STEM+40)]
    rows += [small(SMALL_S0, 2), small(SMALL_S1, 2)]+[one(moved[b][h]) for b in range(BLOCKS) for h in range(2)]
    rows += [small(SMALL_S0+2, 2), small(SMALL_S1+2, 2), small(SMALL_S0+4, 2), small(SMALL_S1+4, 2), small(SMALL_ATTN, 5)]
    ends = SMALL_HEAD+112
    gain_u, shift_u, side = small(ends), small(ends+1), small(ends+2)
    rows += [gain_u, jnp.concatenate([side[:, :C0], shift_u[:, :C0]], axis=1), jnp.concatenate([shift_u[:, C0:], side[:, C0:]], axis=1)]
    rows += [small(ends+3), jnp.zeros((4, CH), f32)]
    q = lax.broadcasted_iota(jnp.int32, (96, 72), 0)
    pick = (lax.broadcasted_iota(jnp.int32, (96, 72), 1) == (q % 16)*8+q//16).astype(f32).astype(narrow)
    up = sum(dot(pick, p) for p in three(small_ref[SMALL_HEAD:SMALL_HEAD+72, :]))
    side = sum(dot(pick, p) for p in three(pairs(SMALL_HEAD+72)))
    columns = [up[:, 64*i:64*i+64] for i in range(6)]+[side[:, 64*i:64*i+64] for i in range(3)]
    head_rows = None
    for o in range(OUT_CH):
        block = jnp.concatenate([column[16*o:16*o+16] for column in columns], axis=0)
        lane = lax.broadcasted_iota(jnp.int32, (64, CH), 1)
        to = (lane == 6*lax.broadcasted_iota(jnp.int32, (64, CH), 0)+o).astype(f32).astype(narrow)
        part = exact(block, to)
        head_rows = part if head_rows is None else head_rows+part
    rows = jnp.concatenate(rows+[head_rows, jnp.zeros((256-48-144, CH), f32)], axis=0)
    at = lax.broadcasted_iota(jnp.int32, (share, 256), 0)+row0
    chosen = (at == spot_ref[...]).astype(f32).astype(narrow)
    out_ref[...] = total+sum(dot(chosen, p) for p in three(rows))


def owner_rows(place, small, sinus, kept, w2, we):
    share, n = place.share, place.total
    hidden_pre, hidden, outer_pre, embed = kept
    half_rows = -(-(share+2)//16)*8
    groups = -(-2*n//128)
    spec = pl.BlockSpec(memory_space=VM)
    time_rows = (ROW["time2_b"]-ROW["time1_w"])//2
    lengths = [-(-(time_rows+2*half_rows)//8)*8, -(-(2*TEMB+2*half_rows)//8)*8]
    spots = jnp.array(SPOTS, jnp.int32)[None]
    return pl.pallas_call(
        functools.partial(owner_kernel, share, n),
        out_shape=sds((share, WIDE)),
        in_specs=[pl.BlockSpec(memory_space=pltpu.SMEM)]+[spec]*9,
        out_specs=spec,
        scratch_shapes=[pltpu.VMEM((groups, lengths[0], 128), f32), pltpu.VMEM((groups, lengths[1], 128), f32),
                        pltpu.VMEM((3, 2*half_rows, 128), f32), pltpu.VMEM((3, 2*half_rows, 128), f32)],
        compiler_params=pltpu.CompilerParams(vmem_limit_bytes=LIMIT),
        cost_estimate=pl.CostEstimate(flops=0, bytes_accessed=1024, transcendentals=0),
    )(place.me().reshape(1), small, sinus, hidden_pre, hidden, outer_pre, embed, w2, we, spots)


def step(sizes, params, moment1, moment2, images, noise, timesteps, masks, weight_index):
    flat = params.shape[0]
    share = flat // WIDE
    place = Place(sizes, share)
    a, me = place.at, place.me()
    spare = (share*me+LEAD) % TILE
    piece = jnp.zeros((place.block*TILE, WIDE), narrow)
    piece = lax.dynamic_update_slice_in_dim(piece, params.astype(narrow).reshape(share, WIDE), spare, axis=0)
    pieces = lax.all_gather(piece.reshape(place.block, TILE, WIDE), ("y", "c", "z", "x"), axis=0)

    own = jnp.concatenate([images, noise, masks.astype(f32)[:, None]], axis=1)
    own = lax.all_to_all(own, ("z", "x"), split_axis=0, concat_axis=2, tiled=True)[0]
    index = a["z"]*sizes["x"]+a["x"]
    own_step = lax.dynamic_index_in_dim(timesteps, index, keepdims=False).astype(f32)
    sample_weight = 0.5+0.5*lax.dynamic_index_in_dim(weight_index, index, keepdims=False).astype(f32)
    clean, own_noise, mask = own[:IN_CH], own[IN_CH:2*IN_CH], own[2*IN_CH:]
    early = jnp.stack([
        jnp.where(jnp.arange(WIDE) == me, own_step, 0.0),
        jnp.full((WIDE,), jnp.sum(mask)),
    ] + [jnp.zeros((WIDE,), f32)]*6)
    early = add_everywhere(early, place)
    all_steps, count = early[0, :place.total], early[1, 0]
    signal, one_minus, beta, alpha, tilde = plan(own_step)
    noisy = (jnp.sqrt(signal)*clean+jnp.sqrt(one_minus)*own_noise).astype(narrow).astype(f32)
    noisy = pad_rows8(to_phases(noisy))
    noise_phases, mask_phases = pad_rows8(to_phases(own_noise)), to_phases(mask)

    half = C0 // 2
    freqs = jnp.exp(-math.log(10000.0) * jnp.arange(half).astype(f32) / half)
    angles = all_steps[:, None] * freqs
    sinus = jnp.concatenate([jnp.cos(angles), jnp.sin(angles)], axis=-1).astype(narrow)
    pieces = pieces.reshape(place.total, place.block*TILE, WIDE)

    def rows(name, length):
        first, found = ROW[name], []
        for d in range(first//share, (first+length-1)//share+1):
            begin, end = max(first, d*share), min(first+length, (d+1)*share)
            shifted = (d*share+LEAD) % TILE-d*share
            found.append(pieces[d, begin+shifted:end+shifted])
        return found[0] if len(found) == 1 else jnp.concatenate(found)

    stem = rows("stem_w", 14).reshape(-1)
    stem_w = taps_rows(stem[:27*C0].reshape(9, IN_CH, C0))
    stem_b = stem[27*C0:].reshape(1, C0).astype(f32)
    skip, state, down_w = stem_down(place, noisy, stem_w, stem_b, pieces)
    hidden_pre, hidden, outer_pre, embed, vectors, w2, we = time_and_modulation(place, sinus, pieces)
    blocks = []
    for b in range(BLOCKS):
        vec = vectors[b]
        base = RES+2*TAPS*b
        after, inner, stat = block_forward(place, state, pieces, base, vec)
        blocks.append((state, inner, stat, base, vec))
        state = after
    before = state
    state, qkv, log, mixed_t, attn_stat, wp, wo, attn_vec = attention_forward(place, before, pieces)

    ends = rows("head_gain", 85).reshape(-1)
    norm_u = jnp.stack([ends[:CH], ends[C0+CH:C0+2*CH]]).astype(f32)
    norm_s = jnp.stack([ends[CH:C0+CH], ends[C0+2*CH:2*(C0+CH)]]).astype(f32)
    head_size = 9*(C0+CH)*OUT_CH
    head_w = ends[2*(C0+CH):2*(C0+CH)+head_size].reshape(9, C0+CH, OUT_CH)
    head_w = jnp.transpose(head_w, (0, 2, 1))
    wu, ws = taps_rows(head_w[..., :CH]), taps_rows(head_w[..., CH:])
    head_b = ends[2*(C0+CH)+head_size:2*(C0+CH)+head_size+OUT_CH].astype(f32)
    head_b = jnp.broadcast_to(jnp.pad(head_b, (0, 8-OUT_CH))[:, None], (8, 128))
    numbers = jnp.stack([jnp.log(beta), jnp.log(tilde), beta*beta/(alpha*one_minus), sample_weight])
    grad, skip_grad, head_tail, losses = head(
        numbers, state, skip, wu, ws, norm_u, norm_s, head_b, noise_phases, mask_phases)
    grad, large, attn_small = attention_back(
        grad, before, attn_stat, qkv, log, mixed_t, wp, wo, attn_vec, place.tiles)
    begin, inner, stat, base, vec = blocks[1]
    grad, large, s1 = block_back(place, grad, begin, inner, stat, pieces, base, vec, large)
    begin, inner, stat, base, vec = blocks[0]
    grad, large, s0 = block_back(place, grad, begin, inner, stat, pieces, base, vec, large)
    large, small = down_stem_back(me, place.total, grad, skip, skip_grad, down_w, noisy, head_tail, attn_small, s1, s0, large)
    total, small = share_out(large, small, place, 3)
    total = lax.dynamic_slice_in_dim(total.reshape(-1, WIDE), spare, share)
    row = share*me+jnp.arange(share)
    dense = functools.reduce(jnp.logical_or, [
        (row >= ROW[name]) & (row < ROW[name]+length)
        for name, length in (("down_w", 9*C0), ("res_w", 4*TAPS), ("qkv_w", 3*CH), ("proj_w", CH))
    ])
    total = jnp.where(dense[:, None], total, 0.0)

    total = total+owner_rows(place, small, sinus, (hidden_pre, hidden, outer_pre, embed), w2, we)

    scaled = total/count
    sums = jnp.concatenate([losses[:2], jnp.full((1, 128), jnp.sum(scaled*scaled)), losses[3:]])
    sums = add_everywhere(sums, place)
    loss_sum, loss_vlb, grad_norm = sums[0, 0], sums[1, 0], jnp.sqrt(sums[2, 0])
    scaled = scaled.reshape(flat)
    clipped = scaled*jnp.minimum(1.0, clip_limit/(grad_norm+1e-06))
    first = decay_first*moment1+(1.0-decay_first)*clipped
    second = decay_second*moment2+(1.0-decay_second)*clipped*clipped
    first_hat = first/(1.0-decay_first**STEP)
    second_hat = second/(1.0-decay_second**STEP)
    updated = params-learn_rate*(first_hat/(jnp.sqrt(second_hat)+1e-08)+weight_decay*params)
    return (updated, first, second, updated.astype(narrow), loss_sum, loss_vlb, count, grad_norm)


def solution(mesh):
    y = mesh.shape["batch"] // 2
    sizes = {"y": y, "c": 2, "z": mesh.shape["rows"] // y, "x": y}
    fine = Mesh(mesh.devices.reshape(tuple(sizes.values())), tuple(sizes))
    every, batch, rows = ("y", "c", "z", "x"), ("y", "c"), ("z", "x")
    return jax.shard_map(
        functools.partial(step, sizes),
        mesh=fine,
        in_specs=(P(every), P(every), P(every), P(batch, None, rows, None), P(batch, None, rows, None),
                  P(batch), P(batch, rows, None), P(batch)),
        out_specs=(P(every), P(every), P(every), P(every), P(), P(), P(), P()),
        check_vma=False,
    )
```

```python
import functools
import math

import jax
import jax.numpy as jnp
from jax import lax
from jax.experimental import pallas as pl
from jax.experimental.pallas import tpu as pltpu
from jax.sharding import Mesh
from jax.sharding import PartitionSpec as P

IN_CH = 3
C0 = 192
CH = 384
TEMB = 768
HEADS = 4
HEAD_DIM = 96
GROUPS = 32
OUT_CH = 6
DIFF_STEPS = 4000
BLOCKS = 2
STEP = 10

cosine_offset = 0.008
kl_weight = 0.001
clip_limit = 0.05
learn_rate = 0.05
decay_first = 0.9
decay_second = 0.999
weight_decay = 0.01
narrow = jnp.bfloat16
f32 = jnp.float32


def segments():
    return [
        ("stem_w", (3, 3, IN_CH, C0)),
        ("stem_b", (C0,)),
        ("time1_w", (C0, TEMB)),
        ("time1_b", (TEMB,)),
        ("time2_w", (TEMB, TEMB)),
        ("time2_b", (TEMB,)),
        ("down_w", (3, 3, C0, CH)),
        ("down_b", (CH,)),
        ("res_w", (BLOCKS, 2, 3, 3, CH, CH)),
        ("res_b", (BLOCKS, 2, CH)),
        ("emb_w", (BLOCKS, TEMB, 2 * CH)),
        ("emb_b", (BLOCKS, 2 * CH)),
        ("res_gain", (BLOCKS, 2, CH)),
        ("res_shift", (BLOCKS, 2, CH)),
        ("attn_gain", (CH,)),
        ("attn_shift", (CH,)),
        ("qkv_w", (CH, 3 * CH)),
        ("qv_b", (2 * CH,)),
        ("proj_w", (CH, CH)),
        ("proj_b", (CH,)),
        ("head_gain", (C0 + CH,)),
        ("head_shift", (C0 + CH,)),
        ("head_w", (3, 3, C0 + CH, OUT_CH)),
        ("head_b", (OUT_CH,)),
    ]


WIDE = 384
TILE = 16
LEAD = 13
ROW = {}
offset = 0
for name, shape in segments():
    ROW[name] = offset // WIDE
    offset += math.prod(shape)
RES = ROW["res_w"]+LEAD
TAIL = ROW["res_b"]


def plan(steps):
    timef = steps.astype(jnp.float32)
    angle = math.pi / 2.0 / (1.0 + cosine_offset)
    theta = (timef / DIFF_STEPS + cosine_offset) * angle
    before = ((timef - 1.0) / DIFF_STEPS + cosine_offset) * angle
    anchor = cosine_offset * angle
    base = math.cos(anchor) ** 2
    signal = jnp.cos(theta) ** 2 / base
    one_minus = jnp.sin(theta + anchor) * jnp.sin(timef / DIFF_STEPS * angle) / base
    one_prev = jnp.sin(before + anchor) * jnp.sin((timef - 1.0) / DIFF_STEPS * angle) / base
    beta = jnp.sin(theta + before) * math.sin(angle / DIFF_STEPS) / jnp.cos(before) ** 2
    alpha = 1.0 - beta
    tilde = beta * one_prev / one_minus
    return (signal, one_minus, beta, alpha, tilde)


SIDE=32; PIX=SIDE*SIDE
LIMIT=60*1024*1024
VM=pltpu.VMEM

def call(kernel, ins, outs, scratch, flops, away=(), away_out=(), alias={}, scalar=()):
    spec = pl.BlockSpec(memory_space=VM)
    places = [pl.BlockSpec(memory_space=pl.ANY if i in away else pltpu.SMEM if i in scalar else VM) for i in range(len(ins))]
    moved = sum(a.size*a.dtype.itemsize for a in ins) + sum(math.prod(o.shape)*o.dtype.itemsize for o in outs)
    return pl.pallas_call(
        kernel, out_shape=outs, in_specs=places,
        out_specs=[pl.BlockSpec(memory_space=pl.ANY) if i in away_out else spec for i in range(len(outs))],
        scratch_shapes=scratch, input_output_aliases=alias,
        compiler_params=pltpu.CompilerParams(vmem_limit_bytes=LIMIT),
        cost_estimate=pl.CostEstimate(flops=flops, bytes_accessed=moved, transcendentals=0),
    )(*ins)

def sds(shape, dtype=f32): return jax.ShapeDtypeStruct(shape, dtype)

def dot(a, b): return jnp.dot(a, b, preferred_element_type=f32)
def dot_nt(a, b): return lax.dot_general(a, b, (((1,), (1,)), ((), ())), preferred_element_type=f32)

def sigmoid(v): return 1.0 / (1.0 + jnp.exp(-v))

def membership(chans, per, first=0):
    c = lax.broadcasted_iota(jnp.int32, (chans, 128), 0) + first
    g = lax.broadcasted_iota(jnp.int32, (chans, 128), 1)
    return ((c >= g*per) & (c < (g+1)*per)).astype(f32).astype(narrow)

def three(v):
    hi = v.astype(narrow); rest = v - hi.astype(f32)
    mid = rest.astype(narrow); low = (rest - mid.astype(f32)).astype(narrow)
    return hi, mid, low

def exact(v, ones):
    return sum(dot(p, ones) for p in three(v))
def exact_nt(v, ones):
    return sum(dot_nt(p, ones) for p in three(v))

def group_totals(stats, member):
    return exact_nt(exact(stats, member), member)

def fold(v):
    return jnp.sum(v.reshape(-1, 8, v.shape[-1]), axis=0)

def rows_of(*rows):
    r = jnp.concatenate(rows, axis=0)
    return jnp.concatenate([r, jnp.zeros((8-r.shape[0], r.shape[1]), f32)], axis=0)

def norm_stats(s1, s2, member, amount):
    stats = rows_of(jnp.sum(s1, axis=0, keepdims=True), jnp.sum(s2, axis=0, keepdims=True))
    tot = group_totals(stats, member) / amount
    mean = tot[0:1]
    return mean, lax.rsqrt(tot[1:2] - mean*mean + 1e-05)

EL=128
def steps(n, body, init=None):
    for i in range(n):
        init = body(i, init)
    return init

def pixel_column(rows, width):
    return lax.broadcasted_iota(jnp.int32, (rows, width), 0) % SIDE

def spread(pad_ref, out_ref, width, backward):
    zero = jnp.zeros((SIDE, 3*width), narrow)
    out_ref[0:SIDE, :] = zero
    out_ref[SIDE+PIX:SIDE+PIX+SIDE, :] = zero
    col = pixel_column(EL, width)
    for r in range(0, PIX, EL):
        before = jnp.where(col == 0, 0.0, pad_ref[r+7:r+7+EL, :]).astype(narrow)
        after = jnp.where(col == SIDE-1, 0.0, pad_ref[r+9:r+9+EL, :]).astype(narrow)
        mid = pad_ref[r+8:r+8+EL, :].astype(narrow)
        first, last = (after, before) if backward else (before, after)
        out_ref[r+SIDE:r+SIDE+EL, 0:width] = first
        out_ref[r+SIDE:r+SIDE+EL, width:2*width] = mid
        out_ref[r+SIDE:r+SIDE+EL, 2*width:3*width] = last

MC=256
def conv_rows(xs_ref, w_ref, base, r):
    acc = dot(xs_ref[pl.ds(r, MC), :], w_ref[base:base+3*CH, :])
    acc += dot(xs_ref[pl.ds(r+SIDE, MC), :], w_ref[base+3*CH:base+6*CH, :])
    return acc + dot(xs_ref[pl.ds(r+2*SIDE, MC), :], w_ref[base+6*CH:base+9*CH, :])

TAPS=9*CH
class Rows:
    def __init__(self, place, first, tiles):
        starts = [place.first(d) for d in range(place.total)]
        self.tiles, self.parts, self.edges = tiles, [], []
        for d in range(place.total):
            begin = starts[d]+1 if d else 0
            end = starts[d+1]+1 if d+1 < place.total else starts[d]+place.block
            begin, end = max(begin, first), min(end, first+tiles)
            if begin < end:
                self.parts.append((d, begin-starts[d], end-starts[d], begin-first))
            if d and first <= starts[d] < first+tiles:
                self.edges.append((d, starts[d]-first))

    def scratch(self):
        return [pltpu.VMEM((self.tiles*TILE, CH), narrow), pltpu.VMEM((max(len(self.edges), 1), TILE, CH), narrow),
                pltpu.SemaphoreType.DMA((len(self.parts)+len(self.edges),))]

    def copies(self, pieces_ref, low_ref, edge_ref, sems):
        made = []
        for d, begin, end, to in self.parts:
            made.append(pltpu.make_async_copy(pieces_ref.at[d, begin*TILE:end*TILE, :],
                                              low_ref.at[to*TILE:(to+end-begin)*TILE, :], sems.at[len(made)]))
        for i, (d, to) in enumerate(self.edges):
            made.append(pltpu.make_async_copy(pieces_ref.at[d, 0:TILE, :], edge_ref.at[i], sems.at[len(made)]))
        return made

    def start(self, *refs):
        for copy in self.copies(*refs):
            copy.start()

    def finish(self, pieces_ref, low_ref, edge_ref, sems):
        for copy in self.copies(pieces_ref, low_ref, edge_ref, sems):
            copy.wait()
        for i, (d, to) in enumerate(self.edges):
            low_ref[to*TILE:(to+1)*TILE, :] = low_ref[to*TILE:(to+1)*TILE, :]+edge_ref[i]

def block_forward_kernel(rows, state_ref, pieces_ref, vec_ref, out_ref, inner_ref, stat_ref, pad_ref, xs_ref, *held):
    one, two = (pieces_ref,)+held[:3], (pieces_ref,)+held[3:]
    rows[0].start(*one)
    rows[1].start(*two)
    w1_ref, w2_ref = held[0], held[3]
    bias1, bias2, gain1, shift1, gain2, shift2, scale, offset = (vec_ref[i:i+1, :] for i in range(8))
    member = membership(CH, CH//GROUPS)
    amount = PIX*(CH//GROUPS)
    def sums(i, c):
        v = state_ref[pl.ds(i*EL, EL), :]
        return c[0]+fold(v), c[1]+fold(v*v)
    z = jnp.zeros((8, CH), f32)
    mean1, inv1 = norm_stats(*steps(PIX//EL, sums, (z, z)), member, amount)
    def act1(i, _):
        r = i*EL
        v = (state_ref[pl.ds(r, EL), :] - mean1)*inv1*gain1 + shift1
        pad_ref[pl.ds(r+8, EL), :] = v*sigmoid(v)
        return _
    steps(PIX//EL, act1, 0)
    spread(pad_ref, xs_ref, CH, False)
    rows[0].finish(*one)
    def conv1(i, c):
        r = i*MC
        v = conv_rows(xs_ref, w1_ref, 0, r) + bias1
        inner_ref[pl.ds(r, MC), :] = v
        return c[0]+fold(v), c[1]+fold(v*v)
    mean2, inv2 = norm_stats(*steps(PIX//MC, conv1, (z, z)), member, amount)
    def act2(i, _):
        r = i*EL
        v = (inner_ref[pl.ds(r, EL), :] - mean2)*inv2*gain2 + shift2
        v = v*scale + offset
        pad_ref[pl.ds(r+8, EL), :] = v*sigmoid(v)
        return _
    steps(PIX//EL, act2, 0)
    spread(pad_ref, xs_ref, CH, False)
    rows[1].finish(*two)
    def conv2(i, _):
        r = i*MC
        out_ref[pl.ds(r, MC), :] = state_ref[pl.ds(r, MC), :] + (conv_rows(xs_ref, w2_ref, 0, r) + bias2)
        return _
    steps(PIX//MC, conv2, 0)
    stat_ref[...] = rows_of(mean1, inv1, mean2, inv2)

def block_rows(place, base):
    return [Rows(place, (base+i*TAPS)//TILE, TAPS//TILE) for i in range(2)]

def block_forward(place, state, pieces, base, vectors):
    rows = block_rows(place, base)
    return call(functools.partial(block_forward_kernel, rows), [state, pieces, vectors],
        [sds((PIX, CH)), sds((PIX, CH)), sds((8, CH))],
        [pltpu.VMEM((PIX+16, CH), f32), pltpu.VMEM((PIX+2*SIDE, 3*CH), narrow)]+rows[0].scratch()+rows[1].scratch(),
        2*2*PIX*TAPS*CH, away=(1,))

def back_taps(gs_ref, w_ref, base, r):
    acc = None
    for dy in range(3):
        for dx in range(3):
            part = dot_nt(gs_ref[pl.ds(r+SIDE*(2-dy), MC), dx*CH:(dx+1)*CH],
                          w_ref[base+(3*dy+dx)*CH:base+(3*dy+dx+1)*CH, :])
            acc = part if acc is None else acc+part
    return acc

def kernel_grads(xt_ref, gs_ref, dw_ref, base):
    def body(dy, _):
        r = SIDE*(2-dy)
        value = dot(xt_ref[...], gs_ref[pl.ds(r, PIX), :]).astype(dw_ref.dtype)
        for dx in range(3):
            at = (base+(3*dy+dx)*CH)//TILE
            dw_ref[pl.ds(at, CH//TILE)] = value[:, dx*CH:(dx+1)*CH].reshape(CH//TILE, TILE, CH)
        return _
    steps(3, body, 0)

def block_back_kernel(base, rows, grad_ref, state_ref, inner_ref, stat_ref, pieces_ref, vec_ref, large_in_ref, out_ref, large_ref, small_ref,
                      pad_ref, gs_ref, xt_ref, keep_ref, dw_ref, sems, *held):
    first_in, second_in = (pieces_ref,)+held[:3], (pieces_ref,)+held[3:]
    rows[1].start(*second_in)
    rows[0].start(*first_in)
    w1_ref, w2_ref = held[0], held[3]
    bias1, bias2, gain1, shift1, gain2, shift2, scale, offset = (vec_ref[i:i+1, :] for i in range(8))
    mean1, inv1, mean2, inv2 = (stat_ref[i:i+1, :] for i in range(4))
    member = membership(CH, CH//GROUPS)
    amount = PIX*(CH//GROUPS)
    z = jnp.zeros((8, CH), f32)
    def low(i, c):
        r = i*EL
        g = grad_ref[pl.ds(r, EL), :].astype(narrow).astype(f32)
        pad_ref[pl.ds(r+8, EL), :] = g
        return c+fold(g)
    bias2_grad = steps(PIX//EL, low, z)
    spread(pad_ref, gs_ref, CH, True)
    for i in range(PIX//EL):
        r = i*EL
        v = (inner_ref[r:r+EL, :] - mean2)*inv2*gain2 + shift2
        v = v*scale + offset
        xt_ref[:, r:r+EL] = jnp.transpose(v*sigmoid(v)).astype(narrow)
    kernel_grads(xt_ref, gs_ref, dw_ref, TAPS)
    half = TAPS//TILE
    second_out = pltpu.make_async_copy(dw_ref.at[half:2*half], large_ref.at[base//TILE+half:base//TILE+2*half], sems.at[0])
    second_out.start()
    rows[1].finish(*second_in)
    def back2(i, c):
        r = i*MC
        d = back_taps(gs_ref, w2_ref, 0, r)
        n = (inner_ref[pl.ds(r, MC), :] - mean2)*inv2
        nt = n*gain2 + shift2
        v = nt*scale + offset
        s = sigmoid(v)
        d = d*(s*(1.0+v*(1.0-s)))
        keep_ref[pl.ds(r, MC), :] = d
        return c[0]+fold(d*nt), c[1]+fold(d), c[2]+fold(d*n)
    mod_scale, mod_offset, dn = steps(PIX//MC, back2, (z, z, z))
    one = lambda v: jnp.sum(v, axis=0, keepdims=True)
    mod_scale, mod_offset, dn = one(mod_scale), one(mod_offset), one(dn)
    tot = group_totals(rows_of(mod_offset*scale*gain2, dn*scale*gain2), member)/amount
    first, second = tot[0:1], tot[1:2]
    def inner_back(i, c):
        r = i*EL
        n = (inner_ref[pl.ds(r, EL), :] - mean2)*inv2
        g = (keep_ref[pl.ds(r, EL), :]*scale*gain2 - first - n*second)*inv2
        g = g.astype(narrow).astype(f32)
        pad_ref[pl.ds(r+8, EL), :] = g
        return c+fold(g)
    bias1_grad = steps(PIX//EL, inner_back, z)
    spread(pad_ref, gs_ref, CH, True)
    for i in range(PIX//EL):
        r = i*EL
        v = (state_ref[r:r+EL, :] - mean1)*inv1*gain1 + shift1
        xt_ref[:, r:r+EL] = jnp.transpose(v*sigmoid(v)).astype(narrow)
    kernel_grads(xt_ref, gs_ref, dw_ref, 0)
    first_out = pltpu.make_async_copy(dw_ref.at[0:half], large_ref.at[base//TILE:base//TILE+half], sems.at[1])
    first_out.start()
    rows[0].finish(*first_in)
    def back1(i, c):
        r = i*MC
        d = back_taps(gs_ref, w1_ref, 0, r)
        n = (state_ref[pl.ds(r, MC), :] - mean1)*inv1
        v = n*gain1 + shift1
        s = sigmoid(v)
        d = d*(s*(1.0+v*(1.0-s)))
        keep_ref[pl.ds(r, MC), :] = d
        return c[0]+fold(d), c[1]+fold(d*n)
    shift1_grad, gain1_grad = (one(v) for v in steps(PIX//MC, back1, (z, z)))
    tot = group_totals(rows_of(shift1_grad*gain1, gain1_grad*gain1), member)/amount
    first1, second1 = tot[0:1], tot[1:2]
    def state_back(i, _):
        r = i*EL
        n = (state_ref[pl.ds(r, EL), :] - mean1)*inv1
        out_ref[pl.ds(r, EL), :] = grad_ref[pl.ds(r, EL), :] + (keep_ref[pl.ds(r, EL), :]*gain1 - first1 - n*second1)*inv1
        return _
    steps(PIX//EL, state_back, 0)
    first_out.wait()
    second_out.wait()
    small_ref[...] = jnp.concatenate([one(bias1_grad), one(bias2_grad), gain1_grad, dn*scale, shift1_grad, mod_offset*scale, mod_scale, mod_offset], axis=0)

def block_back(place, grad, state, inner, stat, pieces, base, vectors, large):
    rows = block_rows(place, base)
    return call(functools.partial(block_back_kernel, base, rows), [grad, state, inner, stat, pieces, vectors, large],
        [sds((PIX, CH)), sds(large.shape, narrow), sds((8, CH))],
        [pltpu.VMEM((PIX+16, CH), f32), pltpu.VMEM((PIX+2*SIDE, 3*CH), narrow), pltpu.VMEM((CH, PIX), narrow),
         pltpu.VMEM((PIX, CH), f32), pltpu.VMEM((2*TAPS//TILE, TILE, CH), narrow),
         pltpu.SemaphoreType.DMA((2,))]+rows[0].scratch()+rows[1].scratch(), 2*4*PIX*TAPS*CH, away=(4, 6), away_out=(1,), alias={6: 1})

PHASES = [(0, 0), (0, 1), (1, 0), (1, 1)]
OFFSETS = [(dy, dx) for dy in (-1, 0, 1) for dx in (-1, 0, 1)]

def source(a, b, dy, dx):
    return 2*((a+dy) % 2) + (b+dx) % 2, (a+dy)//2, (b+dx)//2

def shift_lanes(v, di, dj):
    if di == 0 and dj == 0:
        return v
    moved = pltpu.roll(v, (-(SIDE*di+dj)) % PIX, 1)
    p = lax.broadcasted_iota(jnp.int32, v.shape, 1)
    i, j = p // SIDE + di, p % SIDE + dj
    return jnp.where((i >= 0) & (i < SIDE) & (j >= 0) & (j < SIDE), moved, 0.0)

def stack(phases, a, b, sign):
    rows = []
    for dy, dx in OFFSETS:
        at, di, dj = source(a, b, sign*dy, sign*dx)
        rows.append(shift_lanes(phases[at], di, dj))
    rows.append(jnp.zeros((128-72, PIX), f32))
    return jnp.concatenate(rows, axis=0)

DOWN_FIRST = (ROW["down_w"]+LEAD)//TILE
DOWN_TILES = -(-(ROW["down_b"]+1+LEAD)//TILE)-DOWN_FIRST

def stem_down_kernel(source_rows, noisy_ref, sw_ref, sb_ref, pieces_ref, skip_ref, state_ref, dw_ref, pad_ref, xs_ref, wide_ref, *held):
    source_rows.start(pieces_ref, *held)
    phases = [noisy_ref[i] for i in range(4)]
    col = pixel_column(EL, C0)
    xs_ref[:, 0:SIDE, :] = jnp.zeros((6, SIDE, C0), narrow)
    for a, b in PHASES:
        rows = jnp.transpose(stack(phases, a, b, 1)).astype(narrow)
        v = (dot(rows, sw_ref[...]) + sb_ref[...]).astype(narrow)
        skip_ref[2*a+b] = v
        if b == 0:
            xs_ref[3*a+1, SIDE:SIDE+PIX, :] = v
        else:
            xs_ref[3*a+2, SIDE:SIDE+PIX, :] = v
            pad_ref[8:8+PIX, :] = v.astype(f32)
            for r in range(0, PIX, EL):
                xs_ref[3*a, SIDE+r:SIDE+r+EL, :] = jnp.where(col == 0, 0.0, pad_ref[r+7:r+7+EL, :]).astype(narrow)
    source_rows.finish(pieces_ref, *held)
    wide_ref[...] = held[0][...].astype(f32)
    at = ROW["down_w"]+LEAD-DOWN_FIRST*TILE
    dw_ref[...] = wide_ref[at:at+9*C0, :].astype(narrow)
    acc = None
    for t, (dy, dx) in enumerate(OFFSETS):
        top = 0 if dy == -1 else SIDE
        part = dot(xs_ref[3*(dy % 2)+dx+1, top:top+PIX, :], dw_ref[t*C0:(t+1)*C0, :])
        acc = part if acc is None else acc+part
    state_ref[...] = acc + wide_ref[at+9*C0:at+9*C0+1, :]

def stem_down(place, noisy, stem_w, stem_b, pieces):
    rows = Rows(place, DOWN_FIRST, DOWN_TILES)
    return call(functools.partial(stem_down_kernel, rows), [noisy, stem_w, stem_b, pieces],
        [sds((4, PIX, C0), narrow), sds((PIX, CH)), sds((9*C0, CH), narrow)],
        [pltpu.VMEM((PIX+16, C0), f32), pltpu.VMEM((6, PIX+SIDE, C0), narrow), pltpu.VMEM((DOWN_TILES*TILE, CH), f32)]+rows.scratch(),
        2*PIX*9*C0*CH, away=(3,))

def down_stem_back_kernel(n, me_ref, grad_ref, skip_ref, more_ref, dw_ref, noisy_ref, head_ref, attn_ref, s1_ref, s0_ref,
                          large_in_ref, large_ref, small_ref,
                          pad_ref, gs_ref, ddw_ref, low_ref, sems):
    top_row = ROW["down_w"]+LEAD
    spare = top_row % TILE
    ddw_ref[0:TILE, :] = jnp.zeros((TILE, CH), f32)
    ddw_ref[9*C0:9*C0+TILE, :] = jnp.zeros((TILE, CH), f32)
    z = jnp.zeros((8, CH), f32)
    gs_ref[:, PIX:PIX+SIDE, :] = jnp.zeros((2, SIDE, CH), narrow)
    col = pixel_column(EL, CH)
    total = z
    pad_ref[PIX:PIX+16, :] = jnp.zeros((16, CH), f32)
    for r in range(0, PIX, EL):
        g = grad_ref[r:r+EL, :].astype(narrow)
        gs_ref[0, r:r+EL, :] = g
        g = g.astype(f32)
        pad_ref[r:r+EL, :] = g
        total += fold(g)
    for r in range(0, PIX, EL):
        gs_ref[1, r:r+EL, :] = jnp.where(col == SIDE-1, 0.0, pad_ref[r+1:r+1+EL, :]).astype(narrow)
    down_bias = jnp.sum(total, axis=0, keepdims=True)
    def shifted(dy, dx):
        top = SIDE if dy == -1 else 0
        return gs_ref[1 if dx == -1 else 0, top:top+PIX, :]
    phases = [noisy_ref[i] for i in range(4)]
    stem_grad, stem_bias = None, None
    for a, b in PHASES:
        turned = jnp.transpose(skip_ref[2*a+b].astype(f32)).astype(narrow)
        more = more_ref[2*a+b]
        for t, (dy, dx) in enumerate(OFFSETS):
            if (dy % 2, dx % 2) == (a, b):
                g = shifted(dy, dx)
                ddw_ref[spare+t*C0:spare+(t+1)*C0, :] = dot(turned, g)
                more += dot_nt(g, dw_ref[t*C0:(t+1)*C0, :])
        low = more.astype(narrow)
        part = dot(stack(phases, a, b, 1).astype(narrow), low)
        stem_grad = part if stem_grad is None else stem_grad+part
        part = fold(low.astype(f32))
        stem_bias = part if stem_bias is None else stem_bias+part
    for r in range(0, 9*C0+TILE, 16*TILE):
        end = min(r+16*TILE, 9*C0+TILE)
        low_ref[r//TILE:end//TILE] = ddw_ref[r:end, :].astype(narrow).reshape((end-r)//TILE, TILE, CH)
    copy = pltpu.make_async_copy(low_ref, large_ref.at[top_row//TILE:top_row//TILE+9*C0//TILE+1], sems.at[0])
    copy.start()
    copy.wait()
    small_ref[SMALL_STEM:SMALL_STEM+40, :] = jnp.concatenate(
        [stem_grad[0:40, :], jnp.concatenate([stem_grad[40:72, :], jnp.zeros((8, C0), f32)], axis=0)], axis=1)
    stem_bias = jnp.sum(stem_bias, axis=0, keepdims=True)
    small_ref[SMALL_HEAD:SMALL_HEAD+120, :] = head_ref[...]
    small_ref[SMALL_ATTN:SMALL_ATTN+8, :] = attn_ref[...]
    small_ref[SMALL_S1:SMALL_S1+8, :] = s1_ref[...]
    small_ref[SMALL_S0:SMALL_S0+8, :] = s0_ref[...]
    mine = lax.broadcasted_iota(jnp.int32, (n, CH), 0) == me_ref[0]
    for b, from_ref in enumerate((s0_ref, s1_ref)):
        for h in range(2):
            at = SMALL_MOVED+(2*b+h)*n
            small_ref[at:at+n, :] = jnp.where(mine, from_ref[6+h:7+h, :], 0.0)
    small_ref[SMALL_STEM+40:SMALL_STEM+48, :] = rows_of(down_bias, jnp.concatenate([stem_bias, jnp.zeros((1, C0), f32)], axis=1))

def down_stem_back(me, n, grad, skip, more, down_w, noisy, head_tail, attn_small, s1, s0, large):
    return call(functools.partial(down_stem_back_kernel, n),
        [me.reshape(1), grad, skip, more, down_w, noisy, head_tail, attn_small, s1, s0, large],
        [sds(large.shape, narrow), sds((SMALL_MOVED+4*n, CH))],
        [pltpu.VMEM((PIX+16, CH), f32), pltpu.VMEM((2, PIX+SIDE, CH), narrow), pltpu.VMEM((9*C0+TILE, CH), f32),
         pltpu.VMEM((9*C0//TILE+1, TILE, CH), narrow), pltpu.SemaphoreType.DMA((1,))],
        2*2*PIX*9*C0*CH, away=(10,), away_out=(0,), alias={10: 0}, scalar=(0,))

HEAD_PER = (C0+CH)//GROUPS
def silu_slope(v):
    s = sigmoid(v)
    return s*(1.0+v*(1.0-s))

KL = 0.001
def head_kernel(num_ref, state_ref, skip_ref, wu_ref, ws_ref, vu_ref, vs_ref, bias_ref, noise_ref, mask_ref,
                state_grad_ref, skip_grad_ref, tail_ref, loss_ref,
                up_ref, side_ref, q_ref):
    log_beta, log_tilde, coefficient, sample = (num_ref[i] for i in range(4))
    gain_u, shift_u = vu_ref[0:1, :], vu_ref[1:2, :]
    gain_s, shift_s = vs_ref[0:1, :], vs_ref[1:2, :]
    mu, ms = membership(CH, HEAD_PER), membership(C0, HEAD_PER, CH)
    amount = 4*PIX*HEAD_PER
    one = lambda v: jnp.sum(v, axis=0, keepdims=True)
    zu, zs = jnp.zeros((8, CH), f32), jnp.zeros((8, C0), f32)
    def sums_u(i, c):
        v = state_ref[pl.ds(i*EL, EL), :]
        return c[0]+fold(v), c[1]+fold(v*v)
    u1, u2 = steps(PIX//EL, sums_u, (zu, zu))
    s1, s2 = zs, zs
    for k in range(4):
        def sums_s(i, c):
            v = skip_ref[k, pl.ds(i*EL, EL), :].astype(f32)
            return c[0]+fold(v), c[1]+fold(v*v)
        s1, s2 = steps(PIX//EL, sums_s, (s1, s2))
    tot = (exact(rows_of(4.0*one(u1), 4.0*one(u2)), mu) + exact(rows_of(one(s1), one(s2)), ms))/amount
    tot_u, tot_s = exact_nt(tot, mu), exact_nt(tot, ms)
    mean_u, inv_u = tot_u[0:1], lax.rsqrt(tot_u[1:2]-tot_u[0:1]*tot_u[0:1]+1e-05)
    mean_s, inv_s = tot_s[0:1], lax.rsqrt(tot_s[1:2]-tot_s[0:1]*tot_s[0:1]+1e-05)
    def act_u(i, _):
        r = pl.ds(i*EL, EL)
        v = (state_ref[r, :]-mean_u)*inv_u*gain_u+shift_u
        up_ref[r, :] = (v*sigmoid(v)).astype(narrow)
        return _
    steps(PIX//EL, act_u, 0)
    for k in range(4):
        def act_s(i, _):
            r = pl.ds(i*EL, EL)
            v = (skip_ref[k, r, :].astype(f32)-mean_s)*inv_s*gain_s+shift_s
            side_ref[k, r, :] = (v*sigmoid(v)).astype(narrow)
            return _
        steps(PIX//EL, act_s, 0)
    from_up = dot_nt(wu_ref[...], up_ref[...])
    for k in range(4):
        q_ref[k] = from_up + dot_nt(ws_ref[...], side_ref[k])
    row = lax.broadcasted_iota(jnp.int32, (8, PIX), 0)
    loss, vlb, outs, bias_grad = jnp.zeros((1, PIX), f32), jnp.zeros((1, PIX), f32), [], jnp.zeros((8, PIX), f32)
    for a, b in PHASES:
        out = jnp.zeros((8, PIX), f32)
        for t, (dy, dx) in enumerate(OFFSETS):
            at, di, dj = source(a, b, dy, dx)
            out += shift_lanes(q_ref[at, 8*t:8*t+8, :], di, dj)
        out += bias_ref[:, 0:1]
        k = 2*a+b
        error = jnp.where(row < 3, out - noise_ref[k], 0.0)
        fraction = jnp.where(row < 3, (pltpu.roll(out, 5, 0)+1.0)/2.0, 0.0)
        log_var = fraction*log_beta + (1.0-fraction)*log_tilde
        inverse = jnp.exp(-log_var)
        ratio = jnp.exp(log_tilde-log_var)
        divergence = 0.5*(-1.0+log_var-log_tilde+ratio+coefficient*error*error*inverse)
        divergence = jnp.where(row < 3, divergence, 0.0)
        weight = sample*mask_ref[k]
        loss += weight*jnp.sum(error*error+KL*divergence, axis=0, keepdims=True)
        vlb += weight*KL*jnp.sum(divergence, axis=0, keepdims=True)
        predict = weight*(2.0*error+KL*coefficient*error*inverse)
        var_grad = weight*KL*0.5*(1.0-ratio-coefficient*error*error*inverse)*(log_beta-log_tilde)/2.0
        og = jnp.where(row < 3, predict, jnp.where(row < 6, pltpu.roll(var_grad, 3, 0), 0.0))
        og = og.astype(narrow).astype(f32)
        bias_grad += og
        outs.append(og)
    bias_grad = jnp.broadcast_to(jnp.sum(bias_grad, axis=1, keepdims=True), (8, CH))
    diagonal = lax.broadcasted_iota(jnp.int32, (8, CH), 0) == lax.broadcasted_iota(jnp.int32, (8, CH), 1)
    bias_grad = jnp.sum(jnp.where(diagonal, bias_grad, 0.0), axis=0, keepdims=True)
    loss_ref[...] = jnp.concatenate([jnp.broadcast_to(jnp.sum(loss, axis=1, keepdims=True), (1, 128)),
        jnp.broadcast_to(jnp.sum(vlb, axis=1, keepdims=True), (1, 128)), jnp.zeros((6, 128), f32)], axis=0)
    nine_sum, gs_total = None, None
    d1, d2 = zs, zs
    for a, b in PHASES:
        k = 2*a+b
        nine = stack(outs, a, b, -1)
        nine_sum = nine if nine_sum is None else nine_sum+nine
        part = dot(nine.astype(narrow), side_ref[k])
        gs_total = part if gs_total is None else gs_total+part
        d = dot(jnp.transpose(nine).astype(narrow), ws_ref[...])
        n = (skip_ref[k].astype(f32)-mean_s)*inv_s
        d = d*silu_slope(n*gain_s+shift_s)
        skip_grad_ref[k] = d
        d1, d2 = d1+fold(d), d2+fold(d*n)
    tail_ref[72:112, :] = jnp.concatenate(
        [gs_total[0:40, :], jnp.concatenate([gs_total[40:72, :], jnp.zeros((8, C0), f32)], axis=0)], axis=1)
    hi = nine_sum.astype(narrow); lo = (nine_sum-hi.astype(f32)).astype(narrow)
    tail_ref[0:72, :] = (dot(hi, up_ref[...])+dot(lo, up_ref[...]))[0:72, :]
    turned = jnp.transpose(nine_sum)
    hi = turned.astype(narrow); lo = (turned-hi.astype(f32)).astype(narrow)
    d = dot(hi, wu_ref[...])+dot(lo, wu_ref[...])
    n = (state_ref[...]-mean_u)*inv_u
    d = d*silu_slope(n*gain_u+shift_u)
    state_grad_ref[...] = d
    e1, e2 = one(fold(d)), one(fold(d*n))
    d1, d2 = one(d1), one(d2)
    tail_ref[112:120, :] = rows_of(e2, e1, jnp.concatenate([d2, d1], axis=1), bias_grad)
    tot = (exact(rows_of(e1*gain_u, e2*gain_u), mu)+exact(rows_of(d1*gain_s, d2*gain_s), ms))/amount
    tot_u, tot_s = exact_nt(tot, mu), exact_nt(tot, ms)
    def back_u(i, _):
        r = pl.ds(i*EL, EL)
        n = (state_ref[r, :]-mean_u)*inv_u
        state_grad_ref[r, :] = (state_grad_ref[r, :]*gain_u-4.0*tot_u[0:1]-4.0*n*tot_u[1:2])*inv_u
        return _
    steps(PIX//EL, back_u, 0)
    for k in range(4):
        def back_s(i, _):
            r = pl.ds(i*EL, EL)
            n = (skip_ref[k, r, :].astype(f32)-mean_s)*inv_s
            skip_grad_ref[k, r, :] = (skip_grad_ref[k, r, :]*gain_s-tot_s[0:1]-n*tot_s[1:2])*inv_s
            return _
        steps(PIX//EL, back_s, 0)

def head(numbers, state, skip, wu, ws, vu, vs, bias, noise, mask):
    spec = pl.BlockSpec(memory_space=VM)
    ins = [numbers, state, skip, wu, ws, vu, vs, bias, noise, mask]
    outs = [sds((PIX, CH)), sds((4, PIX, C0)), sds((120, CH)), sds((8, 128))]
    return pl.pallas_call(head_kernel, out_shape=outs,
        in_specs=[pl.BlockSpec(memory_space=pltpu.SMEM)]+[spec]*(len(ins)-1), out_specs=[spec]*len(outs),
        scratch_shapes=[pltpu.VMEM((PIX, CH), narrow), pltpu.VMEM((4, PIX, C0), narrow), pltpu.VMEM((4, 128, PIX), f32)],
        compiler_params=pltpu.CompilerParams(vmem_limit_bytes=LIMIT),
        cost_estimate=pl.CostEstimate(flops=4*2*PIX*128*(4*C0+CH), bytes_accessed=12*2**20, transcendentals=0))(*ins)

HP = 128
QW = HEADS*HP
SCALE = 1.0/math.sqrt(HEAD_DIM)
POWER = SCALE*math.log2(math.e)
QC = 256
ATTN_FIRST = (ROW["attn_gain"]+LEAD)//TILE
ATTN_TILES = -(-(ROW["proj_b"]+LEAD+1)//TILE)-ATTN_FIRST
ATTN = {name: ROW[name]+LEAD-ATTN_FIRST*TILE for name in ("attn_gain", "attn_shift", "qkv_w", "qv_b", "proj_w", "proj_b")}

def get_rows(ref, at):
    return jnp.concatenate([ref[i, at, :] for i in range(3)], axis=1)

def put_rows(ref, at, value):
    for i in range(3):
        ref[i, at, :] = value[:, i*128:(i+1)*128]

def attention_forward_kernel(rows, state_ref, pieces_ref, out_ref, qkv_ref, log_ref, mixed_t_ref, stat_ref, wp_ref, wo_ref, vec_ref,
                             mixed_ref, vt_ref, bp_ref, wide_ref, rows_ref, edge_ref, sems):
    rows.start(pieces_ref, rows_ref, edge_ref, sems)
    rows.finish(pieces_ref, rows_ref, edge_ref, sems)
    for r in range(0, ATTN_TILES*TILE, 16*TILE):
        end = min(r+16*TILE, ATTN_TILES*TILE)
        put_rows(wide_ref, slice(r, end), rows_ref[r:end, :].astype(f32))
    one_row = lambda name, i=0: get_rows(wide_ref, slice(ATTN[name]+i, ATTN[name]+i+1))
    gain, shift, bias = one_row("attn_gain"), one_row("attn_shift"), one_row("proj_b")
    vec_ref[...] = rows_of(gain, shift)
    nothing = jnp.zeros((CH, HP-HEAD_DIM), f32)
    for j in range(3):
        third = get_rows(wide_ref, pl.ds(ATTN["qkv_w"]+j, CH, stride=3))
        third_bias = one_row("qv_b", j//2) if j != 1 else jnp.zeros((1, CH), f32)
        for h in range(HEADS):
            to = slice(j*QW+h*HP, j*QW+(h+1)*HP)
            wp_ref[:, to] = jnp.concatenate([third[:, h*HEAD_DIM:(h+1)*HEAD_DIM], nothing], axis=1).astype(narrow)
            bp_ref[:, to] = jnp.concatenate([third_bias[:, h*HEAD_DIM:(h+1)*HEAD_DIM], nothing[0:1]], axis=1)
    for h in range(HEADS):
        at = ATTN["proj_w"]+h*HEAD_DIM
        wo_ref[h*HP:h*HP+HEAD_DIM, :] = get_rows(wide_ref, slice(at, at+HEAD_DIM)).astype(narrow)
        wo_ref[h*HP+HEAD_DIM:(h+1)*HP, :] = jnp.zeros((HP-HEAD_DIM, CH), narrow)
    member = membership(CH, CH//GROUPS)
    def sums(i, c):
        v = state_ref[pl.ds(i*EL, EL), :]
        return c[0]+fold(v), c[1]+fold(v*v)
    z = jnp.zeros((8, CH), f32)
    mean, inv = norm_stats(*steps(PIX//EL, sums, (z, z)), member, PIX*(CH//GROUPS))
    stat_ref[...] = rows_of(mean, inv)
    def project(i, _):
        r = pl.ds(i*256, 256)
        n = ((state_ref[r, :]-mean)*inv*gain+shift).astype(narrow)
        qkv_ref[r, :] = (dot(n, wp_ref[...])+bp_ref[...]).astype(narrow)
        return _
    steps(PIX//256, project, 0)
    for h in range(HEADS):
        vt_ref[...] = jnp.transpose(qkv_ref[:, 2*QW+h*HP:2*QW+(h+1)*HP].astype(f32)).astype(narrow)
        for c in range(0, PIX, QC):
            s = dot_nt(qkv_ref[:, QW+h*HP:QW+(h+1)*HP], qkv_ref[c:c+QC, h*HP:(h+1)*HP])
            top = jnp.max(s, axis=0, keepdims=True)
            e = jnp.exp2((s-top)*POWER)
            total = jnp.sum(e, axis=0, keepdims=True)
            log_ref[h:h+1, c:c+QC] = top*POWER+jnp.log2(total)
            m = (dot(vt_ref[...], e.astype(narrow))*(1.0/total)).astype(narrow)
            mixed_t_ref[h*HP:(h+1)*HP, c:c+QC] = m
            mixed_ref[c:c+QC, h*HP:(h+1)*HP] = jnp.transpose(m.astype(f32)).astype(narrow)
    log_ref[HEADS:8, :] = jnp.zeros((8-HEADS, PIX), f32)
    def finish(i, _):
        r = pl.ds(i*256, 256)
        out_ref[r, :] = state_ref[r, :]+(dot(mixed_ref[r, :], wo_ref[...])+bias)
        return _
    steps(PIX//256, finish, 0)

def attention_forward(place, state, pieces):
    rows = Rows(place, ATTN_FIRST, ATTN_TILES)
    return call(functools.partial(attention_forward_kernel, rows), [state, pieces],
        [sds((PIX, CH)), sds((PIX, 3*QW), narrow), sds((8, PIX)), sds((QW, PIX), narrow), sds((8, CH)),
         sds((CH, 3*QW), narrow), sds((QW, CH), narrow), sds((8, CH))],
        [pltpu.VMEM((PIX, QW), narrow), pltpu.VMEM((HP, PIX), narrow), pltpu.VMEM((1, 3*QW), f32),
         pltpu.VMEM((3, ATTN_TILES*TILE, 128), f32)]+rows.scratch(),
        2*PIX*(CH*4*QW+2*PIX*QW), away=(1,))

def attention_back_kernel(grad_ref, state_ref, stat_ref, qkv_ref, log_ref, mixed_t_ref, wp_ref, wo_ref, vec_ref,
                          out_ref, large_ref, small_ref, dm_ref, pg_ref, kt_ref, dv_ref, dk_ref, nt_ref, keep_ref,
                          wide_ref, rows_ref, sems):
    gain, shift = vec_ref[0:1, :], vec_ref[1:2, :]
    mean, inv = stat_ref[0:1, :], stat_ref[1:2, :]
    member = membership(CH, CH//GROUPS)
    z = jnp.zeros((8, CH), f32)
    one = lambda v: jnp.sum(v, axis=0, keepdims=True)
    def start(i, c):
        r = pl.ds(i*256, 256)
        g = grad_ref[r, :].astype(narrow)
        keep_ref[r, :] = g
        dm_ref[r, :] = dot_nt(g, wo_ref[...]).astype(narrow)
        return c+fold(g.astype(f32))
    proj_bias = steps(PIX//256, start, z)
    for name, after in (("attn_gain", ATTN["qkv_w"]), ("qv_b", ATTN["proj_w"]), ("proj_b", ATTN_TILES*TILE)):
        put_rows(wide_ref, slice(ATTN[name], after), jnp.zeros((after-ATTN[name], CH), f32))
    wo_grad = dot(mixed_t_ref[...], keep_ref[...])
    for h in range(HEADS):
        at = ATTN["proj_w"]+h*HEAD_DIM
        put_rows(wide_ref, slice(at, at+HEAD_DIM), wo_grad[h*HP:h*HP+HEAD_DIM, :])
    for h in range(HEADS):
        q0, k0, v0 = h*HP, QW+h*HP, 2*QW+h*HP
        kt_ref[...] = jnp.transpose(qkv_ref[:, k0:k0+HP].astype(f32)).astype(narrow)
        for c in range(0, PIX, QC):
            q, dm = qkv_ref[c:c+QC, q0:q0+HP], dm_ref[c:c+QC, h*HP:(h+1)*HP]
            s = dot_nt(qkv_ref[:, k0:k0+HP], q)
            p = jnp.exp2(s*POWER-log_ref[h:h+1, c:c+QC])
            dp = dot_nt(qkv_ref[:, v0:v0+HP], dm)
            dm_t = dot_nt(wo_ref[h*HP:(h+1)*HP, :], keep_ref[c:c+QC, :]).astype(narrow).astype(f32)
            delta = jnp.sum(dm_t*mixed_t_ref[h*HP:(h+1)*HP, c:c+QC].astype(f32), axis=0, keepdims=True)
            ds = (p*(dp-delta)).astype(narrow)
            dv = dot(p.astype(narrow), dm)
            dk = dot(ds, q)
            if c == 0:
                dv_ref[...] = dv
                dk_ref[...] = dk
            else:
                dv_ref[...] += dv
                dk_ref[...] += dk
            dq = dot(kt_ref[...], ds)
            pg_ref[c:c+QC, q0:q0+HP] = jnp.transpose(dq*SCALE).astype(narrow)
        pg_ref[:, k0:k0+HP] = (dk_ref[...]*SCALE).astype(narrow)
        pg_ref[:, v0:v0+HP] = dv_ref[...].astype(narrow)
    for r in range(0, PIX, 256):
        nt_ref[:, r:r+256] = jnp.transpose((state_ref[r:r+256, :]-mean)*inv*gain+shift).astype(narrow)
    for j in range(3):
        third = dot(nt_ref[...], pg_ref[:, j*QW:(j+1)*QW])
        third = jnp.concatenate([third[:, h*HP:h*HP+HEAD_DIM] for h in range(HEADS)], axis=1)
        put_rows(wide_ref, pl.ds(ATTN["qkv_w"]+j, CH, stride=3), third)
    for r in range(0, ATTN_TILES, 16):
        end = min(r+16, ATTN_TILES)
        rows_ref[r:end] = get_rows(wide_ref, slice(r*TILE, end*TILE)).astype(narrow).reshape(end-r, TILE, CH)
    copy = pltpu.make_async_copy(rows_ref, large_ref.at[ATTN_FIRST:ATTN_FIRST+ATTN_TILES], sems.at[0])
    copy.start()
    zb = jnp.zeros((8, 3*QW), f32)
    def norm_grad(i, c):
        r = pl.ds(i*256, 256)
        d = dot_nt(pg_ref[r, :], wp_ref[...])
        n = (state_ref[r, :]-mean)*inv
        out_ref[r, :] = d
        return c[0]+fold(d), c[1]+fold(d*n), c[2]+fold(pg_ref[r, :].astype(f32))
    shift_grad, gain_grad, bias_grad = (one(v) for v in steps(PIX//256, norm_grad, (z, z, zb)))
    compact = [jnp.concatenate([bias_grad[:, j*QW+h*HP:j*QW+h*HP+HEAD_DIM] for h in range(HEADS)], axis=1) for j in (0, 2)]
    tot = group_totals(rows_of(shift_grad*gain, gain_grad*gain), member)/(PIX*(CH//GROUPS))
    first, second = tot[0:1], tot[1:2]
    def finish(i, _):
        r = pl.ds(i*EL, EL)
        n = (state_ref[r, :]-mean)*inv
        out_ref[r, :] = grad_ref[r, :]+(out_ref[r, :]*gain-first-n*second)*inv
        return _
    steps(PIX//EL, finish, 0)
    small_ref[...] = rows_of(gain_grad, shift_grad, compact[0], compact[1], one(proj_bias))
    copy.wait()

def attention_back(grad, state, stat, qkv, log, mixed_t, wp, wo, vec, tiles):
    return call(attention_back_kernel, [grad, state, stat, qkv, log, mixed_t, wp, wo, vec],
        [sds((PIX, CH)), sds((tiles, TILE, CH), narrow), sds((8, CH))],
        [pltpu.VMEM((PIX, QW), narrow), pltpu.VMEM((PIX, 3*QW), narrow), pltpu.VMEM((HP, PIX), narrow), pltpu.VMEM((PIX, HP), f32),
         pltpu.VMEM((PIX, HP), f32), pltpu.VMEM((CH, PIX), narrow), pltpu.VMEM((PIX, CH), narrow),
         pltpu.VMEM((3, ATTN_TILES*TILE, 128), f32), pltpu.VMEM((ATTN_TILES, TILE, CH), narrow), pltpu.SemaphoreType.DMA((1,))],
        2*PIX*(CH*8*QW+5*PIX*QW), away_out=(1,))


def to_phases(v):
    c = v.shape[0]
    return jnp.transpose(v.reshape(c, SIDE, 2, SIDE, 2), (2, 4, 0, 1, 3)).reshape(4, c, PIX)


def pad_rows8(v):
    return jnp.pad(v, ((0, 0), (0, 8-v.shape[1]), (0, 0)))


def taps_rows(v):
    v = jnp.pad(v, ((0, 0), (0, 8-v.shape[1]), (0, 0))).reshape(72, v.shape[2])
    return jnp.pad(v, ((0, 128-72), (0, 0)))


class Place:
    def __init__(self, sizes, share):
        self.sizes = sizes
        self.share = share
        self.total = sizes["y"]*sizes["c"]*sizes["z"]*sizes["x"]
        firsts = [(share*d+LEAD)//TILE for d in range(self.total)]
        lasts = [-(-(share*(d+1)+LEAD)//TILE) for d in range(self.total)]
        self.block = max(last-first for first, last in zip(firsts, lasts))
        self.tiles = max(first+self.block for first in firsts)
        self.tiles = -(-self.tiles//TILE)*TILE
        self.at = {axis: lax.axis_index(axis) for axis in sizes}

    def device(self, y, c, z, x):
        s = self.sizes
        return ((y*s["c"]+c)*s["z"]+z)*s["x"]+x

    def first(self, device):
        return (self.share*device+LEAD)//TILE

    def me(self):
        a = self.at
        return self.device(a["y"], a["c"], a["z"], a["x"])


def turn(value, axis, size, distance):
    return lax.ppermute(value, axis, [(i, (i+distance) % size) for i in range(size)])


def hold_for(value, others):
    return lax.optimization_barrier((value, others))[0]


def add_everywhere(value, place):
    return add_over(value, place, ("c", "x", "y", "z"))


def add_over(value, place, axes):
    for axis in axes:
        size, step = place.sizes[axis], 1
        while step < size:
            value = value+lax.ppermute(value, axis, [(i, i ^ step) for i in range(size)])
            step *= 2
    return value


def cut_kernel(count, size, starts_ref, large_ref, out_ref, sems):
    copies = [pltpu.make_async_copy(large_ref.at[pl.ds(starts_ref[i], size)], out_ref.at[i], sems.at[i]) for i in range(count)]
    for copy in copies:
        copy.start()
    for copy in copies:
        copy.wait()


def cut(large, starts, size):
    count = starts.shape[0]
    return pl.pallas_call(
        functools.partial(cut_kernel, count, size),
        out_shape=sds((count, size, TILE, WIDE), narrow),
        in_specs=[pl.BlockSpec(memory_space=pltpu.SMEM), pl.BlockSpec(memory_space=pl.ANY)],
        out_specs=pl.BlockSpec(memory_space=VM),
        scratch_shapes=[pltpu.SemaphoreType.DMA((count,))],
        compiler_params=pltpu.CompilerParams(vmem_limit_bytes=LIMIT),
        cost_estimate=pl.CostEstimate(flops=0, bytes_accessed=1024, transcendentals=0),
    )(starts, large)


def merge_kernel(coords, sends, count, size, starts_ref, large_ref, arrived_ref, *refs):
    outs, (held_ref, sems) = refs[:-2], refs[-2:]
    copies = [pltpu.make_async_copy(large_ref.at[pl.ds(starts_ref[i], size)], held_ref.at[i], sems.at[i]) for i in range(count)]
    for copy in copies:
        copy.start()
    for i in range(count):
        copies[i].wait()
        which, at = sends[i]
        outs[which][at] = (held_ref[i].astype(f32)+arrived_ref[i].astype(f32)).astype(outs[which].dtype)


def share_out(large, small, place, parts):
    s, a, block = place.sizes, place.at, place.block
    half = (s["z"]+1)//2
    coords = [(y, z, x) for y in range(s["y"]) for z in range(s["z"]) for x in range(s["x"])]

    def starts(core):
        return jnp.stack([
            place.first(place.device((a["y"]+y) % s["y"], core, (a["z"]+z) % s["z"], (a["x"]+x) % s["x"])) for y, z, x in coords
        ]).astype(jnp.int32)

    far_starts, own_starts = starts(1-a["c"]), starts(a["c"])
    bounds = [block*i//parts for i in range(parts+1)]
    groups = [("y", [(0, z, x) for z in range(half) for x in range(s["x"])])]
    groups += [("y%d" % k, [(k, z, x) for z in range(half) for x in range(s["x"])]) for k in range(1, s["y"])]
    groups += [("x", [(y, z, 0) for z in range(half, s["z"]) for y in range(s["y"])])]
    groups += [("x%d" % k, [(y, z, k) for z in range(half, s["z"]) for y in range(s["y"])]) for k in range(1, s["x"])]
    names = [name for name, members in groups]
    sends = [None]*len(coords)
    for g, (name, members) in enumerate(groups):
        for at, member in enumerate(members):
            sends[coords.index(member)] = (g, at)
    length = small.shape[0]//2
    half_small, other_small = (lax.dynamic_slice_in_dim(small, core*length, length) for core in (a["c"], 1-a["c"]))
    half_small = half_small+turn(other_small, "c", 2, 1)
    far_starts = hold_for(far_starts, half_small)
    arrived, merged = [], []
    for part in range(parts):
        sent = cut(large, far_starts+bounds[part], bounds[part+1]-bounds[part])
        arrived.append(turn(sent, "c", 2, 1))
        far_starts = hold_for(far_starts, sent)
    for part in range(parts):
        size = bounds[part+1]-bounds[part]
        outs = [sds((len(members), size, TILE, WIDE), f32 if name in ("y", "x") else narrow) for name, members in groups]
        out = pl.pallas_call(
            functools.partial(merge_kernel, coords, sends, len(coords), size),
            out_shape=outs,
            in_specs=[pl.BlockSpec(memory_space=pltpu.SMEM), pl.BlockSpec(memory_space=pl.ANY), pl.BlockSpec(memory_space=VM)],
            out_specs=[pl.BlockSpec(memory_space=VM)]*len(outs),
            scratch_shapes=[pltpu.VMEM((len(coords), size, TILE, WIDE), narrow), pltpu.SemaphoreType.DMA((len(coords),))],
            compiler_params=pltpu.CompilerParams(vmem_limit_bytes=LIMIT),
            cost_estimate=pl.CostEstimate(flops=0, bytes_accessed=1024, transcendentals=0),
        )(own_starts+bounds[part], large, arrived[part])
        own_starts = hold_for(own_starts, out)
        merged.append(dict(zip(names, out)))

    def first_stage(sums):
        return ([turn(sums["y%d" % k], "y", s["y"], k) for k in range(1, s["y"])],
                [turn(sums["x%d" % k], "x", s["x"], k) for k in range(1, s["x"])])

    def first_sums(sums, came):
        near = sums["y"]+sum(value.astype(f32) for value in came[0])
        far = sums["x"]+sum(value.astype(f32) for value in came[1])
        return near.reshape((half, s["x"])+near.shape[1:]), far.reshape((s["z"]-half, s["y"])+far.shape[1:])

    def second_sums(near, far):
        near = near[:, 0]+sum(turn(near[:, k].astype(narrow), "x", s["x"], k).astype(f32) for k in range(1, s["x"]))
        far = far[:, 0]+sum(turn(far[:, k].astype(narrow), "y", s["y"], k).astype(f32) for k in range(1, s["y"]))
        return near, far

    def third_sum(near, far):
        total = near[0]
        for z in range(1, s["z"]):
            value = near[z] if z < half else far[z-half]
            total = total+turn(value.astype(narrow), "z", s["z"], z).astype(f32)
        return total

    waiting = [first_stage(merged[part]) for part in range(min(2, parts))]
    results, ready = [], None
    for part in range(parts):
        if part == 0:
            waiting[0] = hold_for(waiting[0], merged[-1])
        near, far = first_sums(merged[part], waiting[part])
        if part == 0:
            half_small = add_over(hold_for(half_small, merged[-1]), place, ("z",))
        if part == parts-1:
            half_small = add_over(hold_for(half_small, (near, far)), place, ("x", "y"))
        if part+2 < parts:
            waiting.append(first_stage(hold_for(merged[part+2], (near, far))))
        if 0 < part < parts-1:
            near, far = hold_for((near, far), waiting[part+1])
        results.append(third_sum(*second_sums(near, far)))
    other_small = turn(half_small, "c", 2, 1)
    first = a["c"] == 0
    small = jnp.concatenate([jnp.where(first, half_small, other_small), jnp.where(first, other_small, half_small)])
    return jnp.concatenate(results, axis=0), small


SPOTS = (
    list(range(14))
    + [ROW["time1_b"], ROW["time1_b"]+1, ROW["time2_b"], ROW["time2_b"]+1, ROW["down_b"]]
    + [ROW["res_b"]+i for i in range(4)]
    + [ROW["emb_b"]+i for i in range(4)]
    + [ROW["res_gain"]+i for i in range(4)]
    + [ROW["res_shift"]+i for i in range(4)]
    + [ROW["attn_gain"], ROW["attn_shift"], ROW["qv_b"], ROW["qv_b"]+1, ROW["proj_b"]]
    + [ROW["head_gain"]+i for i in range(3)] + [ROW["head_b"]] + [-1]*4
    + [ROW["head_gain"]+3+9*tap+part if tap < 9 else -1 for part in range(9) for tap in range(16)]
)
SPOTS += [-1]*(256-len(SPOTS))

TIME_FIRST = (ROW["time1_w"]+LEAD)//TILE
TIME_TILES = -(-(ROW["time2_b"]+2+LEAD)//TILE)-TIME_FIRST
EMB_FIRST = (ROW["res_b"]+LEAD)//TILE
EMB_TILES = -(-(ROW["res_shift"]+4+LEAD)//TILE)-EMB_FIRST


def widen_rows(low_ref, wide_ref, count):
    for r in range(0, count, 16*TILE):
        end = min(r+16*TILE, count)
        put_rows(wide_ref, slice(r, end), low_ref[r:end, :].astype(f32))


def time_kernel(n, rows, me_ref, sinus_ref, pieces_ref, hidden_pre_ref, hidden_ref, outer_pre_ref, embed_ref, vec_ref, w2_ref, we_ref,
                time_ref, emb_ref, *held):
    one, two = (pieces_ref,)+held[:3], (pieces_ref,)+held[3:]
    rows[0].start(*one)
    rows[1].start(*two)
    rows[0].finish(*one)
    time_low_ref, emb_low_ref = held[0], held[3]
    widen_rows(time_low_ref, time_ref, TIME_TILES*TILE)

    def in_time(name, i=0):
        return ROW[name]+LEAD-TIME_FIRST*TILE+i

    def in_emb(name, i=0):
        return ROW[name]+LEAD-EMB_FIRST*TILE+i

    def row(ref, at):
        return get_rows(ref, slice(at, at+1))

    for h in range(2):
        w1 = get_rows(time_ref, pl.ds(in_time("time1_w", h), C0, stride=2)).astype(narrow)
        hidden_pre_ref[:, h*CH:(h+1)*CH] = dot(sinus_ref[...], w1)+row(time_ref, in_time("time1_b", h))
        w2_ref[h] = get_rows(time_ref, pl.ds(in_time("time2_w", h), TEMB, stride=2)).astype(narrow)
    v = hidden_pre_ref[...]
    hidden_ref[...] = (v*sigmoid(v)).astype(narrow)
    for h in range(2):
        outer_pre_ref[:, h*CH:(h+1)*CH] = dot(hidden_ref[...], w2_ref[h])+row(time_ref, in_time("time2_b", h))
    v = outer_pre_ref[...]
    embed = (v*sigmoid(v)).astype(narrow)
    embed_ref[...] = embed
    mine = lax.broadcasted_iota(jnp.int32, (n, TEMB), 0) == me_ref[0]
    own = jnp.sum(jnp.where(mine, embed.astype(f32), 0.0), axis=0, keepdims=True)
    own = jnp.broadcast_to(own, (8, TEMB)).astype(narrow)
    rows[1].finish(*two)
    widen_rows(emb_low_ref, emb_ref, EMB_TILES*TILE)
    for b in range(BLOCKS):
        modulate = []
        for h in range(2):
            we_ref[b, h] = get_rows(emb_ref, pl.ds(in_emb("emb_w", 2*TEMB*b+h), TEMB, stride=2)).astype(narrow)
            modulate.append(dot(own, we_ref[b, h])[0:1]+row(emb_ref, in_emb("emb_b", 2*b+h)))
        vec_ref[b] = jnp.concatenate([
            row(emb_ref, in_emb("res_b", 2*b)), row(emb_ref, in_emb("res_b", 2*b+1)),
            row(emb_ref, in_emb("res_gain", 2*b)), row(emb_ref, in_emb("res_shift", 2*b)),
            row(emb_ref, in_emb("res_gain", 2*b+1)), row(emb_ref, in_emb("res_shift", 2*b+1)),
            1.0+modulate[0], modulate[1],
        ], axis=0)


def time_and_modulation(place, sinus, pieces):
    rows = [Rows(place, TIME_FIRST, TIME_TILES), Rows(place, EMB_FIRST, EMB_TILES)]
    n = sinus.shape[0]
    spec = pl.BlockSpec(memory_space=VM)
    return pl.pallas_call(
        functools.partial(time_kernel, n, rows),
        out_shape=[sds((n, TEMB)), sds((n, TEMB), narrow), sds((n, TEMB)), sds((n, TEMB), narrow), sds((BLOCKS, 8, CH)),
                   sds((2, TEMB, CH), narrow), sds((BLOCKS, 2, TEMB, CH), narrow)],
        in_specs=[pl.BlockSpec(memory_space=pltpu.SMEM), spec, pl.BlockSpec(memory_space=pl.ANY)],
        out_specs=[spec]*7,
        scratch_shapes=[pltpu.VMEM((3, TIME_TILES*TILE, 128), f32), pltpu.VMEM((3, EMB_TILES*TILE, 128), f32)]
        + rows[0].scratch()+rows[1].scratch(),
        compiler_params=pltpu.CompilerParams(vmem_limit_bytes=LIMIT),
        cost_estimate=pl.CostEstimate(flops=2**27, bytes_accessed=8*2**20, transcendentals=0),
    )(place.me().reshape(1), sinus, pieces)


SMALL_HEAD, SMALL_ATTN, SMALL_S1, SMALL_STEM, SMALL_S0, SMALL_MOVED = 0, 120, 128, 136, 184, 192


def owner_kernel(share, n, me_ref, small_ref, sinus_ref, hidden_pre_ref, hidden_ref, outer_pre_ref, embed_ref, w2_ref, we_ref, spot_ref,
                 out_ref, time_ref, emb_ref, mixed_time_ref, mixed_emb_ref):
    row0 = me_ref[0]*share
    half_rows = mixed_time_ref.shape[1]//2
    one = lambda v: jnp.sum(v, axis=0, keepdims=True)
    moved = [[small_ref[SMALL_MOVED+(2*b+h)*n:SMALL_MOVED+(2*b+h+1)*n, :] for h in range(2)] for b in range(BLOCKS)]
    embed_grad = sum(exact_nt(moved[b][h], we_ref[b, h]) for b in range(BLOCKS) for h in range(2))
    outer_grad = embed_grad*silu_slope(outer_pre_ref[...])
    hidden_grad = sum(exact_nt(outer_grad[:, h*CH:(h+1)*CH], w2_ref[h]) for h in range(2))*silu_slope(hidden_pre_ref[...])

    def table(ref, values):
        ref[...] = jnp.zeros(ref.shape, f32)
        width = min(n, 128)
        for family, (value_ref, at) in enumerate(values):
            turned = jnp.transpose(value_ref[...].astype(f32))
            for first in range(0, n, width):
                group, lane = divmod(family*n+first, 128)
                ref[group, half_rows+at:half_rows+at+turned.shape[0], lane:lane+width] = turned[:, first:first+width]

    def products(ref, begin, factors, mixed_ref):
        away = row0-begin+(1 << 20)
        place = away // 2 - (1 << 19)
        start = jnp.clip(place+half_rows, 0, ref.shape[1]-half_rows)
        for h in range(2):
            right = jnp.concatenate([factors[0][h], factors[1][h]], axis=0)
            if right.shape[0] < 128:
                right = jnp.concatenate([right, jnp.zeros((128-right.shape[0], CH), f32)], axis=0)
            total = None
            for group in range(ref.shape[0]):
                left = ref[group, pl.ds(start, half_rows), :].astype(narrow)
                part = sum(dot(left, p) for p in three(right[group*128:(group+1)*128]))
                total = part if total is None else total+part
            put_rows(mixed_ref, pl.ds(h, half_rows, stride=2), total)
        odd = away-2*(away//2)
        return jnp.where(odd == 1, get_rows(mixed_ref, slice(1, 1+share)), get_rows(mixed_ref, slice(0, share)))

    halves = lambda v: [v[:, :CH], v[:, CH:]]
    table(time_ref, [(sinus_ref, 0), (hidden_ref, (ROW["time2_w"]-ROW["time1_w"])//2)])
    table(emb_ref, [(embed_ref, 0), (embed_ref, TEMB)])
    total = products(time_ref, ROW["time1_w"], [halves(hidden_grad), halves(outer_grad)], mixed_time_ref)
    total += products(emb_ref, ROW["emb_w"], moved, mixed_emb_ref)

    def small(at, count=1):
        return small_ref[at:at+count, :]

    def pairs(at):
        return jnp.concatenate([small_ref[at:at+40, :C0], small_ref[at:at+32, C0:]], axis=0)

    stem = pairs(SMALL_STEM)
    stem_rows = [stem[8*tap+c:8*tap+c+1, :] for tap in range(9) for c in range(IN_CH)]+[small(SMALL_STEM+41)[:, :C0]]
    rows = [jnp.concatenate(stem_rows[2*i:2*i+2], axis=1) for i in range(14)]
    rows += halves(one(hidden_grad))+halves(one(outer_grad))+[small(SMALL_STEM+40)]
    rows += [small(SMALL_S0, 2), small(SMALL_S1, 2)]+[one(moved[b][h]) for b in range(BLOCKS) for h in range(2)]
    rows += [small(SMALL_S0+2, 2), small(SMALL_S1+2, 2), small(SMALL_S0+4, 2), small(SMALL_S1+4, 2), small(SMALL_ATTN, 5)]
    ends = SMALL_HEAD+112
    gain_u, shift_u, side = small(ends), small(ends+1), small(ends+2)
    rows += [gain_u, jnp.concatenate([side[:, :C0], shift_u[:, :C0]], axis=1), jnp.concatenate([shift_u[:, C0:], side[:, C0:]], axis=1)]
    rows += [small(ends+3), jnp.zeros((4, CH), f32)]
    q = lax.broadcasted_iota(jnp.int32, (96, 72), 0)
    pick = (lax.broadcasted_iota(jnp.int32, (96, 72), 1) == (q % 16)*8+q//16).astype(f32).astype(narrow)
    up = sum(dot(pick, p) for p in three(small_ref[SMALL_HEAD:SMALL_HEAD+72, :]))
    side = sum(dot(pick, p) for p in three(pairs(SMALL_HEAD+72)))
    columns = [up[:, 64*i:64*i+64] for i in range(6)]+[side[:, 64*i:64*i+64] for i in range(3)]
    head_rows = None
    for o in range(OUT_CH):
        block = jnp.concatenate([column[16*o:16*o+16] for column in columns], axis=0)
        lane = lax.broadcasted_iota(jnp.int32, (64, CH), 1)
        to = (lane == 6*lax.broadcasted_iota(jnp.int32, (64, CH), 0)+o).astype(f32).astype(narrow)
        part = exact(block, to)
        head_rows = part if head_rows is None else head_rows+part
    rows = jnp.concatenate(rows+[head_rows, jnp.zeros((256-48-144, CH), f32)], axis=0)
    at = lax.broadcasted_iota(jnp.int32, (share, 256), 0)+row0
    chosen = (at == spot_ref[...]).astype(f32).astype(narrow)
    out_ref[...] = total+sum(dot(chosen, p) for p in three(rows))


def owner_rows(place, small, sinus, kept, w2, we):
    share, n = place.share, place.total
    hidden_pre, hidden, outer_pre, embed = kept
    half_rows = -(-(share+2)//16)*8
    groups = -(-2*n//128)
    spec = pl.BlockSpec(memory_space=VM)
    time_rows = (ROW["time2_b"]-ROW["time1_w"])//2
    lengths = [-(-(time_rows+2*half_rows)//8)*8, -(-(2*TEMB+2*half_rows)//8)*8]
    spots = jnp.array(SPOTS, jnp.int32)[None]
    return pl.pallas_call(
        functools.partial(owner_kernel, share, n),
        out_shape=sds((share, WIDE)),
        in_specs=[pl.BlockSpec(memory_space=pltpu.SMEM)]+[spec]*9,
        out_specs=spec,
        scratch_shapes=[pltpu.VMEM((groups, lengths[0], 128), f32), pltpu.VMEM((groups, lengths[1], 128), f32),
                        pltpu.VMEM((3, 2*half_rows, 128), f32), pltpu.VMEM((3, 2*half_rows, 128), f32)],
        compiler_params=pltpu.CompilerParams(vmem_limit_bytes=LIMIT),
        cost_estimate=pl.CostEstimate(flops=0, bytes_accessed=1024, transcendentals=0),
    )(place.me().reshape(1), small, sinus, hidden_pre, hidden, outer_pre, embed, w2, we, spots)


def step(sizes, params, moment1, moment2, images, noise, timesteps, masks, weight_index):
    flat = params.shape[0]
    share = flat // WIDE
    place = Place(sizes, share)
    a, me = place.at, place.me()
    spare = (share*me+LEAD) % TILE
    piece = jnp.zeros((place.block*TILE, WIDE), narrow)
    piece = lax.dynamic_update_slice_in_dim(piece, params.astype(narrow).reshape(share, WIDE), spare, axis=0)
    pieces = lax.all_gather(piece.reshape(place.block, TILE, WIDE), ("y", "c", "z", "x"), axis=0)

    own = jnp.concatenate([images, noise, masks.astype(f32)[:, None]], axis=1)
    own = lax.all_to_all(own, ("z", "x"), split_axis=0, concat_axis=2, tiled=True)[0]
    index = a["z"]*sizes["x"]+a["x"]
    own_step = lax.dynamic_index_in_dim(timesteps, index, keepdims=False).astype(f32)
    sample_weight = 0.5+0.5*lax.dynamic_index_in_dim(weight_index, index, keepdims=False).astype(f32)
    clean, own_noise, mask = own[:IN_CH], own[IN_CH:2*IN_CH], own[2*IN_CH:]
    early = jnp.stack([
        jnp.where(jnp.arange(WIDE) == me, own_step, 0.0),
        jnp.full((WIDE,), jnp.sum(mask)),
    ] + [jnp.zeros((WIDE,), f32)]*6)
    early = add_everywhere(early, place)
    all_steps, count = early[0, :place.total], early[1, 0]
    signal, one_minus, beta, alpha, tilde = plan(own_step)
    noisy = (jnp.sqrt(signal)*clean+jnp.sqrt(one_minus)*own_noise).astype(narrow).astype(f32)
    noisy = pad_rows8(to_phases(noisy))
    noise_phases, mask_phases = pad_rows8(to_phases(own_noise)), to_phases(mask)

    half = C0 // 2
    freqs = jnp.exp(-math.log(10000.0) * jnp.arange(half).astype(f32) / half)
    angles = all_steps[:, None] * freqs
    sinus = jnp.concatenate([jnp.cos(angles), jnp.sin(angles)], axis=-1).astype(narrow)
    pieces = pieces.reshape(place.total, place.block*TILE, WIDE)

    def rows(name, length):
        first, found = ROW[name], []
        for d in range(first//share, (first+length-1)//share+1):
            begin, end = max(first, d*share), min(first+length, (d+1)*share)
            shifted = (d*share+LEAD) % TILE-d*share
            found.append(pieces[d, begin+shifted:end+shifted])
        return found[0] if len(found) == 1 else jnp.concatenate(found)

    stem = rows("stem_w", 14).reshape(-1)
    stem_w = taps_rows(stem[:27*C0].reshape(9, IN_CH, C0))
    stem_b = stem[27*C0:].reshape(1, C0).astype(f32)
    skip, state, down_w = stem_down(place, noisy, stem_w, stem_b, pieces)
    hidden_pre, hidden, outer_pre, embed, vectors, w2, we = time_and_modulation(place, sinus, pieces)
    blocks = []
    for b in range(BLOCKS):
        vec = vectors[b]
        base = RES+2*TAPS*b
        after, inner, stat = block_forward(place, state, pieces, base, vec)
        blocks.append((state, inner, stat, base, vec))
        state = after
    before = state
    state, qkv, log, mixed_t, attn_stat, wp, wo, attn_vec = attention_forward(place, before, pieces)

    ends = rows("head_gain", 85).reshape(-1)
    norm_u = jnp.stack([ends[:CH], ends[C0+CH:C0+2*CH]]).astype(f32)
    norm_s = jnp.stack([ends[CH:C0+CH], ends[C0+2*CH:2*(C0+CH)]]).astype(f32)
    head_size = 9*(C0+CH)*OUT_CH
    head_w = ends[2*(C0+CH):2*(C0+CH)+head_size].reshape(9, C0+CH, OUT_CH)
    head_w = jnp.transpose(head_w, (0, 2, 1))
    wu, ws = taps_rows(head_w[..., :CH]), taps_rows(head_w[..., CH:])
    head_b = ends[2*(C0+CH)+head_size:2*(C0+CH)+head_size+OUT_CH].astype(f32)
    head_b = jnp.broadcast_to(jnp.pad(head_b, (0, 8-OUT_CH))[:, None], (8, 128))
    numbers = jnp.stack([jnp.log(beta), jnp.log(tilde), beta*beta/(alpha*one_minus), sample_weight])
    grad, skip_grad, head_tail, losses = head(
        numbers, state, skip, wu, ws, norm_u, norm_s, head_b, noise_phases, mask_phases)
    grad, large, attn_small = attention_back(
        grad, before, attn_stat, qkv, log, mixed_t, wp, wo, attn_vec, place.tiles)
    begin, inner, stat, base, vec = blocks[1]
    grad, large, s1 = block_back(place, grad, begin, inner, stat, pieces, base, vec, large)
    begin, inner, stat, base, vec = blocks[0]
    grad, large, s0 = block_back(place, grad, begin, inner, stat, pieces, base, vec, large)
    large, small = down_stem_back(me, place.total, grad, skip, skip_grad, down_w, noisy, head_tail, attn_small, s1, s0, large)
    total, small = share_out(large, small, place, 2)
    total = lax.dynamic_slice_in_dim(total.reshape(-1, WIDE), spare, share)
    row = share*me+jnp.arange(share)
    dense = functools.reduce(jnp.logical_or, [
        (row >= ROW[name]) & (row < ROW[name]+length)
        for name, length in (("down_w", 9*C0), ("res_w", 4*TAPS), ("qkv_w", 3*CH), ("proj_w", CH))
    ])
    total = jnp.where(dense[:, None], total, 0.0)

    total = total+owner_rows(place, small, sinus, (hidden_pre, hidden, outer_pre, embed), w2, we)

    scaled = total/count
    sums = jnp.concatenate([losses[:2], jnp.full((1, 128), jnp.sum(scaled*scaled)), losses[3:]])
    sums = add_everywhere(sums, place)
    loss_sum, loss_vlb, grad_norm = sums[0, 0], sums[1, 0], jnp.sqrt(sums[2, 0])
    scaled = scaled.reshape(flat)
    clipped = scaled*jnp.minimum(1.0, clip_limit/(grad_norm+1e-06))
    first = decay_first*moment1+(1.0-decay_first)*clipped
    second = decay_second*moment2+(1.0-decay_second)*clipped*clipped
    first_hat = first/(1.0-decay_first**STEP)
    second_hat = second/(1.0-decay_second**STEP)
    updated = params-learn_rate*(first_hat/(jnp.sqrt(second_hat)+1e-08)+weight_decay*params)
    return (updated, first, second, updated.astype(narrow), loss_sum, loss_vlb, count, grad_norm)


def solution(mesh):
    y = mesh.shape["batch"] // 2
    sizes = {"y": y, "c": 2, "z": mesh.shape["rows"] // y, "x": y}
    fine = Mesh(mesh.devices.reshape(tuple(sizes.values())), tuple(sizes))
    every, batch, rows = ("y", "c", "z", "x"), ("y", "c"), ("z", "x")
    return jax.shard_map(
        functools.partial(step, sizes),
        mesh=fine,
        in_specs=(P(every), P(every), P(every), P(batch, None, rows, None), P(batch, None, rows, None),
                  P(batch), P(batch, rows, None), P(batch)),
        out_specs=(P(every), P(every), P(every), P(every), P(), P(), P(), P()),
        check_vma=False,
    )
```

```python
import functools
import math

import jax
import jax.numpy as jnp
from jax import lax
from jax.experimental import pallas as pl
from jax.experimental.pallas import tpu as pltpu
from jax.sharding import Mesh
from jax.sharding import PartitionSpec as P

IN_CH = 3
C0 = 192
CH = 384
TEMB = 768
HEADS = 4
HEAD_DIM = 96
GROUPS = 32
OUT_CH = 6
DIFF_STEPS = 4000
BLOCKS = 2
STEP = 10

cosine_offset = 0.008
kl_weight = 0.001
clip_limit = 0.05
learn_rate = 0.05
decay_first = 0.9
decay_second = 0.999
weight_decay = 0.01
narrow = jnp.bfloat16
f32 = jnp.float32


def segments():
    return [
        ("stem_w", (3, 3, IN_CH, C0)),
        ("stem_b", (C0,)),
        ("time1_w", (C0, TEMB)),
        ("time1_b", (TEMB,)),
        ("time2_w", (TEMB, TEMB)),
        ("time2_b", (TEMB,)),
        ("down_w", (3, 3, C0, CH)),
        ("down_b", (CH,)),
        ("res_w", (BLOCKS, 2, 3, 3, CH, CH)),
        ("res_b", (BLOCKS, 2, CH)),
        ("emb_w", (BLOCKS, TEMB, 2 * CH)),
        ("emb_b", (BLOCKS, 2 * CH)),
        ("res_gain", (BLOCKS, 2, CH)),
        ("res_shift", (BLOCKS, 2, CH)),
        ("attn_gain", (CH,)),
        ("attn_shift", (CH,)),
        ("qkv_w", (CH, 3 * CH)),
        ("qv_b", (2 * CH,)),
        ("proj_w", (CH, CH)),
        ("proj_b", (CH,)),
        ("head_gain", (C0 + CH,)),
        ("head_shift", (C0 + CH,)),
        ("head_w", (3, 3, C0 + CH, OUT_CH)),
        ("head_b", (OUT_CH,)),
    ]


WIDE = 384
TILE = 16
LEAD = 13
ROW = {}
offset = 0
for name, shape in segments():
    ROW[name] = offset // WIDE
    offset += math.prod(shape)
RES = ROW["res_w"]+LEAD
TAIL = ROW["res_b"]


def plan(steps):
    timef = steps.astype(jnp.float32)
    angle = math.pi / 2.0 / (1.0 + cosine_offset)
    theta = (timef / DIFF_STEPS + cosine_offset) * angle
    before = ((timef - 1.0) / DIFF_STEPS + cosine_offset) * angle
    anchor = cosine_offset * angle
    base = math.cos(anchor) ** 2
    signal = jnp.cos(theta) ** 2 / base
    one_minus = jnp.sin(theta + anchor) * jnp.sin(timef / DIFF_STEPS * angle) / base
    one_prev = jnp.sin(before + anchor) * jnp.sin((timef - 1.0) / DIFF_STEPS * angle) / base
    beta = jnp.sin(theta + before) * math.sin(angle / DIFF_STEPS) / jnp.cos(before) ** 2
    alpha = 1.0 - beta
    tilde = beta * one_prev / one_minus
    return (signal, one_minus, beta, alpha, tilde)


SIDE=32; PIX=SIDE*SIDE
MIB=1024*1024
VM=pltpu.VMEM

def call(kernel, ins, outs, scratch, flops, away=(), away_out=(), alias={}, scalar=(), room=32):
    spec = pl.BlockSpec(memory_space=VM)
    places = [pl.BlockSpec(memory_space=pl.ANY if i in away else pltpu.SMEM if i in scalar else VM) for i in range(len(ins))]
    moved = sum(a.size*a.dtype.itemsize for a in ins) + sum(math.prod(o.shape)*o.dtype.itemsize for o in outs)
    return pl.pallas_call(
        kernel, out_shape=outs, in_specs=places,
        out_specs=[pl.BlockSpec(memory_space=pl.ANY) if i in away_out else spec for i in range(len(outs))],
        scratch_shapes=scratch, input_output_aliases=alias,
        compiler_params=pltpu.CompilerParams(vmem_limit_bytes=room*MIB),
        cost_estimate=pl.CostEstimate(flops=flops, bytes_accessed=moved, transcendentals=0),
    )(*ins)

def sds(shape, dtype=f32): return jax.ShapeDtypeStruct(shape, dtype)

def dot(a, b): return jnp.dot(a, b, preferred_element_type=f32)
def dot_nt(a, b): return lax.dot_general(a, b, (((1,), (1,)), ((), ())), preferred_element_type=f32)

def sigmoid(v): return 0.5*jnp.tanh(0.5*v) + 0.5

def membership(chans, per, first=0):
    c = lax.broadcasted_iota(jnp.int32, (chans, 128), 0) + first
    g = lax.broadcasted_iota(jnp.int32, (chans, 128), 1)
    return ((c >= g*per) & (c < (g+1)*per)).astype(f32).astype(narrow)

def three(v):
    hi = v.astype(narrow); rest = v - hi.astype(f32)
    mid = rest.astype(narrow); low = (rest - mid.astype(f32)).astype(narrow)
    return hi, mid, low

def exact(v, ones):
    return sum(dot(p, ones) for p in three(v))
def exact_nt(v, ones):
    return sum(dot_nt(p, ones) for p in three(v))

def group_totals(stats, member):
    return exact_nt(exact(stats, member), member)

def fold(v):
    return jnp.sum(v.reshape(-1, 8, v.shape[-1]), axis=0)

def rows_of(*rows):
    r = jnp.concatenate(rows, axis=0)
    return jnp.concatenate([r, jnp.zeros((8-r.shape[0], r.shape[1]), f32)], axis=0)

def norm_stats(s1, s2, member, amount):
    stats = rows_of(jnp.sum(s1, axis=0, keepdims=True), jnp.sum(s2, axis=0, keepdims=True))
    tot = group_totals(stats, member) / amount
    mean = tot[0:1]
    return mean, lax.rsqrt(tot[1:2] - mean*mean + 1e-05)

EL=128
def steps(n, body, init=None):
    for i in range(n):
        init = body(i, init)
    return init

def pixel_column(rows, width):
    return lax.broadcasted_iota(jnp.int32, (rows, width), 0) % SIDE

def clear_edges(out_ref, width):
    zero = jnp.zeros((SIDE, 3*width), narrow)
    out_ref[0:SIDE, :] = zero
    out_ref[SIDE+PIX:SIDE+PIX+SIDE, :] = zero

def put_spread(out_ref, r, v, backward):
    count, width = v.shape
    col = pixel_column(count, width)
    before = jnp.where(col == 0, 0.0, pltpu.roll(v, 1, 0)).astype(narrow)
    after = jnp.where(col == SIDE-1, 0.0, pltpu.roll(v, count-1, 0)).astype(narrow)
    first, last = (after, before) if backward else (before, after)
    out_ref[SIDE+r:SIDE+r+count, 0:width] = first
    out_ref[SIDE+r:SIDE+r+count, width:2*width] = v.astype(narrow)
    out_ref[SIDE+r:SIDE+r+count, 2*width:3*width] = last

MC=256
def conv_rows(xs_ref, w_ref, base, r):
    acc = dot(xs_ref[pl.ds(r, MC), :], w_ref[base:base+3*CH, :])
    acc += dot(xs_ref[pl.ds(r+SIDE, MC), :], w_ref[base+3*CH:base+6*CH, :])
    return acc + dot(xs_ref[pl.ds(r+2*SIDE, MC), :], w_ref[base+6*CH:base+9*CH, :])

TAPS=9*CH
class Rows:
    def __init__(self, place, first, tiles):
        starts = [place.first(d) for d in range(place.total)]
        self.tiles, self.parts, self.edges = tiles, [], []
        for d in range(place.total):
            begin = starts[d]+1 if d else 0
            end = starts[d+1]+1 if d+1 < place.total else starts[d]+place.block
            begin, end = max(begin, first), min(end, first+tiles)
            if begin < end:
                self.parts.append((d, begin-starts[d], end-starts[d], begin-first))
            if d and first <= starts[d] < first+tiles:
                self.edges.append((d, starts[d]-first))

    def scratch(self):
        return [pltpu.VMEM((self.tiles*TILE, CH), narrow), pltpu.VMEM((max(len(self.edges), 1), TILE, CH), narrow),
                pltpu.SemaphoreType.DMA((len(self.parts)+len(self.edges),))]

    def copies(self, pieces_ref, low_ref, edge_ref, sems):
        made = []
        for d, begin, end, to in self.parts:
            made.append(pltpu.make_async_copy(pieces_ref.at[d, begin*TILE:end*TILE, :],
                                              low_ref.at[to*TILE:(to+end-begin)*TILE, :], sems.at[len(made)]))
        for i, (d, to) in enumerate(self.edges):
            made.append(pltpu.make_async_copy(pieces_ref.at[d, 0:TILE, :], edge_ref.at[i], sems.at[len(made)]))
        return made

    def start(self, *refs):
        for copy in self.copies(*refs):
            copy.start()

    def finish(self, pieces_ref, low_ref, edge_ref, sems):
        for copy in self.copies(pieces_ref, low_ref, edge_ref, sems):
            copy.wait()
        for i, (d, to) in enumerate(self.edges):
            low_ref[to*TILE:(to+1)*TILE, :] = low_ref[to*TILE:(to+1)*TILE, :]+edge_ref[i]

def block_forward_kernel(rows, state_ref, pieces_ref, vec_ref, out_ref, inner_ref, stat_ref, xs_ref, *held):
    one, two = (pieces_ref,)+held[:3], (pieces_ref,)+held[3:]
    rows[0].start(*one)
    rows[1].start(*two)
    w1_ref, w2_ref = held[0], held[3]
    bias1, bias2, gain1, shift1, gain2, shift2, scale, offset = (vec_ref[i:i+1, :] for i in range(8))
    member = membership(CH, CH//GROUPS)
    amount = PIX*(CH//GROUPS)
    def sums(i, c):
        v = state_ref[pl.ds(i*EL, EL), :]
        return c[0]+fold(v), c[1]+fold(v*v)
    z = jnp.zeros((8, CH), f32)
    mean1, inv1 = norm_stats(*steps(PIX//EL, sums, (z, z)), member, amount)
    clear_edges(xs_ref, CH)
    factor, term = inv1*gain1, shift1 - mean1*inv1*gain1
    for r in range(0, PIX, EL):
        v = state_ref[r:r+EL, :]*factor + term
        put_spread(xs_ref, r, v*sigmoid(v), False)
    rows[0].finish(*one)
    def conv1(i, c):
        r = i*MC
        v = conv_rows(xs_ref, w1_ref, 0, r) + bias1
        inner_ref[pl.ds(r, MC), :] = v
        return c[0]+fold(v), c[1]+fold(v*v)
    mean2, inv2 = norm_stats(*steps(PIX//MC, conv1, (z, z)), member, amount)
    factor, term = inv2*gain2*scale, (shift2 - mean2*inv2*gain2)*scale + offset
    for r in range(0, PIX, EL):
        v = inner_ref[r:r+EL, :]*factor + term
        put_spread(xs_ref, r, v*sigmoid(v), False)
    rows[1].finish(*two)
    def conv2(i, _):
        r = i*MC
        out_ref[pl.ds(r, MC), :] = state_ref[pl.ds(r, MC), :] + (conv_rows(xs_ref, w2_ref, 0, r) + bias2)
        return _
    steps(PIX//MC, conv2, 0)
    stat_ref[...] = rows_of(mean1, inv1, mean2, inv2)

def block_rows(place, base):
    return [Rows(place, (base+i*TAPS)//TILE, TAPS//TILE) for i in range(2)]

def block_forward(place, state, pieces, base, vectors):
    rows = block_rows(place, base)
    return call(functools.partial(block_forward_kernel, rows), [state, pieces, vectors],
        [sds((PIX, CH)), sds((PIX, CH)), sds((8, CH))],
        [pltpu.VMEM((PIX+2*SIDE, 3*CH), narrow)]+rows[0].scratch()+rows[1].scratch(),
        2*2*PIX*TAPS*CH, away=(1,), room=39)

def back_taps(gs_ref, w_ref, base, r):
    acc = None
    for dy in range(3):
        for dx in range(3):
            part = dot_nt(gs_ref[pl.ds(r+SIDE*(2-dy), MC), dx*CH:(dx+1)*CH],
                          w_ref[base+(3*dy+dx)*CH:base+(3*dy+dx+1)*CH, :])
            acc = part if acc is None else acc+part
    return acc

def kernel_grads(xt_ref, gs_ref, dw_ref, base):
    def body(dy, _):
        r = SIDE*(2-dy)
        value = dot(xt_ref[...], gs_ref[pl.ds(r, PIX), :]).astype(dw_ref.dtype)
        for dx in range(3):
            at = (base+(3*dy+dx)*CH)//TILE
            dw_ref[pl.ds(at, CH//TILE)] = value[:, dx*CH:(dx+1)*CH].reshape(CH//TILE, TILE, CH)
        return _
    steps(3, body, 0)

def block_back_kernel(base, rows, grad_ref, state_ref, inner_ref, stat_ref, pieces_ref, vec_ref, large_in_ref, out_ref, large_ref, small_ref,
                      gs_ref, xt_ref, keep_ref, dw_ref, sems, *held):
    first_in, second_in = (pieces_ref,)+held[:3], (pieces_ref,)+held[3:]
    rows[1].start(*second_in)
    rows[0].start(*first_in)
    w1_ref, w2_ref = held[0], held[3]
    bias1, bias2, gain1, shift1, gain2, shift2, scale, offset = (vec_ref[i:i+1, :] for i in range(8))
    mean1, inv1, mean2, inv2 = (stat_ref[i:i+1, :] for i in range(4))
    member = membership(CH, CH//GROUPS)
    amount = PIX*(CH//GROUPS)
    z = jnp.zeros((8, CH), f32)
    one = lambda v: jnp.sum(v, axis=0, keepdims=True)
    clear_edges(gs_ref, CH)
    factor2, term2 = inv2*gain2*scale, (shift2 - mean2*inv2*gain2)*scale + offset
    bias2_grad = z
    for r in range(0, PIX, EL):
        g = grad_ref[r:r+EL, :].astype(narrow).astype(f32)
        put_spread(gs_ref, r, g, True)
        bias2_grad += fold(g)
        v = inner_ref[r:r+EL, :]*factor2 + term2
        xt_ref[:, r:r+EL] = jnp.transpose(v*sigmoid(v)).astype(narrow)
    kernel_grads(xt_ref, gs_ref, dw_ref, TAPS)
    half = TAPS//TILE
    second_out = pltpu.make_async_copy(dw_ref.at[half:2*half], large_ref.at[base//TILE+half:base//TILE+2*half], sems.at[0])
    second_out.start()
    rows[1].finish(*second_in)
    d_sum, dn_sum = z, z
    for r in range(0, PIX, MC):
        d = back_taps(gs_ref, w2_ref, 0, r)
        x = inner_ref[r:r+MC, :]
        d = d*silu_slope(x*factor2 + term2)
        keep_ref[r:r+MC, :] = d
        d_sum += fold(d)
        dn_sum += fold(d*(x*inv2 - mean2*inv2))
    mod_offset, dn = one(d_sum), one(dn_sum)
    mod_scale = gain2*dn + shift2*mod_offset
    tot = group_totals(rows_of(mod_offset*scale*gain2, dn*scale*gain2), member)/amount
    first, second = tot[0:1]*inv2, tot[1:2]*inv2*inv2
    by_keep, by_term = scale*gain2*inv2, second*mean2 - first
    bias1_grad = z
    factor1, term1 = inv1*gain1, shift1 - mean1*inv1*gain1
    for r in range(0, PIX, EL):
        g = keep_ref[r:r+EL, :]*by_keep - inner_ref[r:r+EL, :]*second + by_term
        g = g.astype(narrow).astype(f32)
        put_spread(gs_ref, r, g, True)
        bias1_grad += fold(g)
        v = state_ref[r:r+EL, :]*factor1 + term1
        xt_ref[:, r:r+EL] = jnp.transpose(v*sigmoid(v)).astype(narrow)
    kernel_grads(xt_ref, gs_ref, dw_ref, 0)
    first_out = pltpu.make_async_copy(dw_ref.at[0:half], large_ref.at[base//TILE:base//TILE+half], sems.at[1])
    first_out.start()
    rows[0].finish(*first_in)
    d_sum, dn_sum = z, z
    for r in range(0, PIX, MC):
        d = back_taps(gs_ref, w1_ref, 0, r)
        x = state_ref[r:r+MC, :]
        d = d*silu_slope(x*factor1 + term1)
        keep_ref[r:r+MC, :] = d
        d_sum += fold(d)
        dn_sum += fold(d*(x*inv1 - mean1*inv1))
    shift1_grad, gain1_grad = one(d_sum), one(dn_sum)
    tot = group_totals(rows_of(shift1_grad*gain1, gain1_grad*gain1), member)/amount
    first1, second1 = tot[0:1]*inv1, tot[1:2]*inv1*inv1
    by_keep1, by_term1 = gain1*inv1, second1*mean1 - first1
    for r in range(0, PIX, EL):
        out_ref[r:r+EL, :] = grad_ref[r:r+EL, :] + (keep_ref[r:r+EL, :]*by_keep1 - state_ref[r:r+EL, :]*second1 + by_term1)
    first_out.wait()
    second_out.wait()
    small_ref[...] = jnp.concatenate([one(bias1_grad), one(bias2_grad), gain1_grad, dn*scale, shift1_grad, mod_offset*scale, mod_scale, mod_offset], axis=0)

def block_back(place, grad, state, inner, stat, pieces, base, vectors, large):
    rows = block_rows(place, base)
    return call(functools.partial(block_back_kernel, base, rows), [grad, state, inner, stat, pieces, vectors, large],
        [sds((PIX, CH)), sds(large.shape, narrow), sds((8, CH))],
        [pltpu.VMEM((PIX+2*SIDE, 3*CH), narrow), pltpu.VMEM((CH, PIX), narrow),
         pltpu.VMEM((PIX, CH), f32), pltpu.VMEM((2*TAPS//TILE, TILE, CH), narrow),
         pltpu.SemaphoreType.DMA((2,))]+rows[0].scratch()+rows[1].scratch(), 2*4*PIX*TAPS*CH, away=(4, 6), away_out=(1,), alias={6: 1}, room=39)

PHASES = [(0, 0), (0, 1), (1, 0), (1, 1)]
OFFSETS = [(dy, dx) for dy in (-1, 0, 1) for dx in (-1, 0, 1)]

def source(a, b, dy, dx):
    return 2*((a+dy) % 2) + (b+dx) % 2, (a+dy)//2, (b+dx)//2

def shift_lanes(v, di, dj):
    if di == 0 and dj == 0:
        return v
    moved = pltpu.roll(v, (-(SIDE*di+dj)) % PIX, 1)
    p = lax.broadcasted_iota(jnp.int32, v.shape, 1)
    i, j = p // SIDE + di, p % SIDE + dj
    return jnp.where((i >= 0) & (i < SIDE) & (j >= 0) & (j < SIDE), moved, 0.0)

def stack(phases, a, b, sign):
    rows = []
    for dy, dx in OFFSETS:
        at, di, dj = source(a, b, sign*dy, sign*dx)
        rows.append(shift_lanes(phases[at], di, dj))
    rows.append(jnp.zeros((128-72, PIX), f32))
    return jnp.concatenate(rows, axis=0)

DOWN_FIRST = (ROW["down_w"]+LEAD)//TILE
DOWN_TILES = -(-(ROW["down_b"]+1+LEAD)//TILE)-DOWN_FIRST

def stem_down_kernel(source_rows, noisy_ref, sw_ref, sb_ref, pieces_ref, skip_ref, state_ref, dw_ref, pad_ref, xs_ref, wide_ref, *held):
    source_rows.start(pieces_ref, *held)
    phases = [noisy_ref[i] for i in range(4)]
    col = pixel_column(EL, C0)
    xs_ref[:, 0:SIDE, :] = jnp.zeros((6, SIDE, C0), narrow)
    for a, b in PHASES:
        rows = jnp.transpose(stack(phases, a, b, 1)).astype(narrow)
        v = (dot(rows, sw_ref[...]) + sb_ref[...]).astype(narrow)
        skip_ref[2*a+b] = v
        if b == 0:
            xs_ref[3*a+1, SIDE:SIDE+PIX, :] = v
        else:
            xs_ref[3*a+2, SIDE:SIDE+PIX, :] = v
            pad_ref[8:8+PIX, :] = v.astype(f32)
            for r in range(0, PIX, EL):
                xs_ref[3*a, SIDE+r:SIDE+r+EL, :] = jnp.where(col == 0, 0.0, pad_ref[r+7:r+7+EL, :]).astype(narrow)
    source_rows.finish(pieces_ref, *held)
    wide_ref[...] = held[0][...].astype(f32)
    at = ROW["down_w"]+LEAD-DOWN_FIRST*TILE
    dw_ref[...] = wide_ref[at:at+9*C0, :].astype(narrow)
    acc = None
    for t, (dy, dx) in enumerate(OFFSETS):
        top = 0 if dy == -1 else SIDE
        part = dot(xs_ref[3*(dy % 2)+dx+1, top:top+PIX, :], dw_ref[t*C0:(t+1)*C0, :])
        acc = part if acc is None else acc+part
    state_ref[...] = acc + wide_ref[at+9*C0:at+9*C0+1, :]

def stem_down(place, noisy, stem_w, stem_b, pieces):
    rows = Rows(place, DOWN_FIRST, DOWN_TILES)
    return call(functools.partial(stem_down_kernel, rows), [noisy, stem_w, stem_b, pieces],
        [sds((4, PIX, C0), narrow), sds((PIX, CH)), sds((9*C0, CH), narrow)],
        [pltpu.VMEM((PIX+16, C0), f32), pltpu.VMEM((6, PIX+SIDE, C0), narrow), pltpu.VMEM((DOWN_TILES*TILE, CH), f32)]+rows.scratch(),
        2*PIX*9*C0*CH, away=(3,), room=39)

def down_stem_back_kernel(n, me_ref, grad_ref, skip_ref, more_ref, dw_ref, noisy_ref, head_ref, attn_ref, s1_ref, s0_ref,
                          large_in_ref, large_ref, small_ref,
                          pad_ref, gs_ref, ddw_ref, low_ref, sems):
    top_row = ROW["down_w"]+LEAD
    spare = top_row % TILE
    ddw_ref[0:TILE, :] = jnp.zeros((TILE, CH), f32)
    ddw_ref[9*C0:9*C0+TILE, :] = jnp.zeros((TILE, CH), f32)
    z = jnp.zeros((8, CH), f32)
    gs_ref[:, PIX:PIX+SIDE, :] = jnp.zeros((2, SIDE, CH), narrow)
    col = pixel_column(EL, CH)
    total = z
    pad_ref[PIX:PIX+16, :] = jnp.zeros((16, CH), f32)
    for r in range(0, PIX, EL):
        g = grad_ref[r:r+EL, :].astype(narrow)
        gs_ref[0, r:r+EL, :] = g
        g = g.astype(f32)
        pad_ref[r:r+EL, :] = g
        total += fold(g)
    for r in range(0, PIX, EL):
        gs_ref[1, r:r+EL, :] = jnp.where(col == SIDE-1, 0.0, pad_ref[r+1:r+1+EL, :]).astype(narrow)
    down_bias = jnp.sum(total, axis=0, keepdims=True)
    def shifted(dy, dx):
        top = SIDE if dy == -1 else 0
        return gs_ref[1 if dx == -1 else 0, top:top+PIX, :]
    phases = [noisy_ref[i] for i in range(4)]
    stem_grad, stem_bias = None, None
    for a, b in PHASES:
        turned = jnp.transpose(skip_ref[2*a+b].astype(f32)).astype(narrow)
        more = more_ref[2*a+b]
        for t, (dy, dx) in enumerate(OFFSETS):
            if (dy % 2, dx % 2) == (a, b):
                g = shifted(dy, dx)
                ddw_ref[spare+t*C0:spare+(t+1)*C0, :] = dot(turned, g)
                more += dot_nt(g, dw_ref[t*C0:(t+1)*C0, :])
        low = more.astype(narrow)
        part = dot(stack(phases, a, b, 1).astype(narrow), low)
        stem_grad = part if stem_grad is None else stem_grad+part
        part = fold(low.astype(f32))
        stem_bias = part if stem_bias is None else stem_bias+part
    for r in range(0, 9*C0+TILE, 16*TILE):
        end = min(r+16*TILE, 9*C0+TILE)
        low_ref[r//TILE:end//TILE] = ddw_ref[r:end, :].astype(narrow).reshape((end-r)//TILE, TILE, CH)
    copy = pltpu.make_async_copy(low_ref, large_ref.at[top_row//TILE:top_row//TILE+9*C0//TILE+1], sems.at[0])
    copy.start()
    copy.wait()
    small_ref[SMALL_STEM:SMALL_STEM+40, :] = jnp.concatenate(
        [stem_grad[0:40, :], jnp.concatenate([stem_grad[40:72, :], jnp.zeros((8, C0), f32)], axis=0)], axis=1)
    stem_bias = jnp.sum(stem_bias, axis=0, keepdims=True)
    small_ref[SMALL_HEAD:SMALL_HEAD+120, :] = head_ref[...]
    small_ref[SMALL_ATTN:SMALL_ATTN+8, :] = attn_ref[...]
    small_ref[SMALL_S1:SMALL_S1+8, :] = s1_ref[...]
    small_ref[SMALL_S0:SMALL_S0+8, :] = s0_ref[...]
    mine = lax.broadcasted_iota(jnp.int32, (n, CH), 0) == me_ref[0]
    for b, from_ref in enumerate((s0_ref, s1_ref)):
        for h in range(2):
            at = SMALL_MOVED+(2*b+h)*n
            small_ref[at:at+n, :] = jnp.where(mine, from_ref[6+h:7+h, :], 0.0)
    small_ref[SMALL_STEM+40:SMALL_STEM+48, :] = rows_of(down_bias, jnp.concatenate([stem_bias, jnp.zeros((1, C0), f32)], axis=1))

def down_stem_back(me, n, grad, skip, more, down_w, noisy, head_tail, attn_small, s1, s0, large):
    return call(functools.partial(down_stem_back_kernel, n),
        [me.reshape(1), grad, skip, more, down_w, noisy, head_tail, attn_small, s1, s0, large],
        [sds(large.shape, narrow), sds((SMALL_MOVED+4*n, CH))],
        [pltpu.VMEM((PIX+16, CH), f32), pltpu.VMEM((2, PIX+SIDE, CH), narrow), pltpu.VMEM((9*C0+TILE, CH), f32),
         pltpu.VMEM((9*C0//TILE+1, TILE, CH), narrow), pltpu.SemaphoreType.DMA((1,))],
        2*2*PIX*9*C0*CH, away=(10,), away_out=(0,), alias={10: 0}, scalar=(0,), room=39)

HEAD_PER = (C0+CH)//GROUPS
def silu_slope(v):
    s = sigmoid(v)
    return s*(1.0+v*(1.0-s))

KL = 0.001
def head_kernel(num_ref, state_ref, skip_ref, wu_ref, ws_ref, vu_ref, vs_ref, bias_ref, noise_ref, mask_ref,
                state_grad_ref, skip_grad_ref, tail_ref, loss_ref,
                up_ref, side_ref, q_ref):
    log_beta, log_tilde, coefficient, sample = (num_ref[i] for i in range(4))
    gain_u, shift_u = vu_ref[0:1, :], vu_ref[1:2, :]
    gain_s, shift_s = vs_ref[0:1, :], vs_ref[1:2, :]
    mu, ms = membership(CH, HEAD_PER), membership(C0, HEAD_PER, CH)
    amount = 4*PIX*HEAD_PER
    one = lambda v: jnp.sum(v, axis=0, keepdims=True)
    zu, zs = jnp.zeros((8, CH), f32), jnp.zeros((8, C0), f32)
    def sums_u(i, c):
        v = state_ref[pl.ds(i*EL, EL), :]
        return c[0]+fold(v), c[1]+fold(v*v)
    u1, u2 = steps(PIX//EL, sums_u, (zu, zu))
    s1, s2 = zs, zs
    for k in range(4):
        def sums_s(i, c):
            v = skip_ref[k, pl.ds(i*EL, EL), :].astype(f32)
            return c[0]+fold(v), c[1]+fold(v*v)
        s1, s2 = steps(PIX//EL, sums_s, (s1, s2))
    tot = (exact(rows_of(4.0*one(u1), 4.0*one(u2)), mu) + exact(rows_of(one(s1), one(s2)), ms))/amount
    tot_u, tot_s = exact_nt(tot, mu), exact_nt(tot, ms)
    mean_u, inv_u = tot_u[0:1], lax.rsqrt(tot_u[1:2]-tot_u[0:1]*tot_u[0:1]+1e-05)
    mean_s, inv_s = tot_s[0:1], lax.rsqrt(tot_s[1:2]-tot_s[0:1]*tot_s[0:1]+1e-05)
    factor_u, term_u = inv_u*gain_u, shift_u-mean_u*inv_u*gain_u
    factor_s, term_s = inv_s*gain_s, shift_s-mean_s*inv_s*gain_s
    def act_u(i, _):
        r = pl.ds(i*EL, EL)
        v = state_ref[r, :]*factor_u+term_u
        up_ref[r, :] = (v*sigmoid(v)).astype(narrow)
        return _
    steps(PIX//EL, act_u, 0)
    for k in range(4):
        def act_s(i, _):
            r = pl.ds(i*EL, EL)
            v = skip_ref[k, r, :].astype(f32)*factor_s+term_s
            side_ref[k, r, :] = (v*sigmoid(v)).astype(narrow)
            return _
        steps(PIX//EL, act_s, 0)
    from_up = dot_nt(wu_ref[...], up_ref[...])
    for k in range(4):
        q_ref[k] = from_up + dot_nt(ws_ref[...], side_ref[k])
    row = lax.broadcasted_iota(jnp.int32, (8, PIX), 0)
    loss, vlb, outs, bias_grad = jnp.zeros((1, PIX), f32), jnp.zeros((1, PIX), f32), [], jnp.zeros((8, PIX), f32)
    for a, b in PHASES:
        out = jnp.zeros((8, PIX), f32)
        for t, (dy, dx) in enumerate(OFFSETS):
            at, di, dj = source(a, b, dy, dx)
            out += shift_lanes(q_ref[at, 8*t:8*t+8, :], di, dj)
        out += bias_ref[:, 0:1]
        k = 2*a+b
        error = jnp.where(row < 3, out - noise_ref[k], 0.0)
        fraction = jnp.where(row < 3, (pltpu.roll(out, 5, 0)+1.0)/2.0, 0.0)
        log_var = fraction*log_beta + (1.0-fraction)*log_tilde
        inverse = jnp.exp(-log_var)
        ratio = jnp.exp(log_tilde-log_var)
        divergence = 0.5*(-1.0+log_var-log_tilde+ratio+coefficient*error*error*inverse)
        divergence = jnp.where(row < 3, divergence, 0.0)
        weight = sample*mask_ref[k]
        loss += weight*jnp.sum(error*error+KL*divergence, axis=0, keepdims=True)
        vlb += weight*KL*jnp.sum(divergence, axis=0, keepdims=True)
        predict = weight*(2.0*error+KL*coefficient*error*inverse)
        var_grad = weight*KL*0.5*(1.0-ratio-coefficient*error*error*inverse)*(log_beta-log_tilde)/2.0
        og = jnp.where(row < 3, predict, jnp.where(row < 6, pltpu.roll(var_grad, 3, 0), 0.0))
        og = og.astype(narrow).astype(f32)
        bias_grad += og
        outs.append(og)
    bias_grad = jnp.broadcast_to(jnp.sum(bias_grad, axis=1, keepdims=True), (8, CH))
    diagonal = lax.broadcasted_iota(jnp.int32, (8, CH), 0) == lax.broadcasted_iota(jnp.int32, (8, CH), 1)
    bias_grad = jnp.sum(jnp.where(diagonal, bias_grad, 0.0), axis=0, keepdims=True)
    loss_ref[...] = jnp.concatenate([jnp.broadcast_to(jnp.sum(loss, axis=1, keepdims=True), (1, 128)),
        jnp.broadcast_to(jnp.sum(vlb, axis=1, keepdims=True), (1, 128)), jnp.zeros((6, 128), f32)], axis=0)
    nine_sum, gs_total = None, None
    d1, d2 = zs, zs
    for a, b in PHASES:
        k = 2*a+b
        nine = stack(outs, a, b, -1)
        nine_sum = nine if nine_sum is None else nine_sum+nine
        part = dot(nine.astype(narrow), side_ref[k])
        gs_total = part if gs_total is None else gs_total+part
        d = dot(jnp.transpose(nine).astype(narrow), ws_ref[...])
        x = skip_ref[k].astype(f32)
        n = x*inv_s-mean_s*inv_s
        d = d*silu_slope(x*factor_s+term_s)
        skip_grad_ref[k] = d
        d1, d2 = d1+fold(d), d2+fold(d*n)
    tail_ref[72:112, :] = jnp.concatenate(
        [gs_total[0:40, :], jnp.concatenate([gs_total[40:72, :], jnp.zeros((8, C0), f32)], axis=0)], axis=1)
    hi = nine_sum.astype(narrow); lo = (nine_sum-hi.astype(f32)).astype(narrow)
    tail_ref[0:72, :] = (dot(hi, up_ref[...])+dot(lo, up_ref[...]))[0:72, :]
    turned = jnp.transpose(nine_sum)
    hi = turned.astype(narrow); lo = (turned-hi.astype(f32)).astype(narrow)
    d = dot(hi, wu_ref[...])+dot(lo, wu_ref[...])
    n = (state_ref[...]-mean_u)*inv_u
    d = d*silu_slope(n*gain_u+shift_u)
    state_grad_ref[...] = d
    e1, e2 = one(fold(d)), one(fold(d*n))
    d1, d2 = one(d1), one(d2)
    tail_ref[112:120, :] = rows_of(e2, e1, jnp.concatenate([d2, d1], axis=1), bias_grad)
    tot = (exact(rows_of(e1*gain_u, e2*gain_u), mu)+exact(rows_of(d1*gain_s, d2*gain_s), ms))/amount
    tot_u, tot_s = exact_nt(tot, mu), exact_nt(tot, ms)
    second_u, second_s = 4.0*tot_u[1:2]*inv_u*inv_u, tot_s[1:2]*inv_s*inv_s
    by_term_u, by_term_s = second_u*mean_u-4.0*tot_u[0:1]*inv_u, second_s*mean_s-tot_s[0:1]*inv_s
    def back_u(i, _):
        r = pl.ds(i*EL, EL)
        state_grad_ref[r, :] = state_grad_ref[r, :]*factor_u-state_ref[r, :]*second_u+by_term_u
        return _
    steps(PIX//EL, back_u, 0)
    for k in range(4):
        def back_s(i, _):
            r = pl.ds(i*EL, EL)
            skip_grad_ref[k, r, :] = skip_grad_ref[k, r, :]*factor_s-skip_ref[k, r, :].astype(f32)*second_s+by_term_s
            return _
        steps(PIX//EL, back_s, 0)

def head(numbers, state, skip, wu, ws, vu, vs, bias, noise, mask):
    spec = pl.BlockSpec(memory_space=VM)
    ins = [numbers, state, skip, wu, ws, vu, vs, bias, noise, mask]
    outs = [sds((PIX, CH)), sds((4, PIX, C0)), sds((120, CH)), sds((8, 128))]
    return pl.pallas_call(head_kernel, out_shape=outs,
        in_specs=[pl.BlockSpec(memory_space=pltpu.SMEM)]+[spec]*(len(ins)-1), out_specs=[spec]*len(outs),
        scratch_shapes=[pltpu.VMEM((PIX, CH), narrow), pltpu.VMEM((4, PIX, C0), narrow), pltpu.VMEM((4, 128, PIX), f32)],
        compiler_params=pltpu.CompilerParams(vmem_limit_bytes=26*MIB),
        cost_estimate=pl.CostEstimate(flops=4*2*PIX*128*(4*C0+CH), bytes_accessed=12*2**20, transcendentals=0))(*ins)

HP = 128
QW = HEADS*HP
SCALE = 1.0/math.sqrt(HEAD_DIM)
POWER = SCALE*math.log2(math.e)
QC = 256
ATTN_FIRST = (ROW["attn_gain"]+LEAD)//TILE
ATTN_TILES = -(-(ROW["proj_b"]+LEAD+1)//TILE)-ATTN_FIRST
ATTN = {name: ROW[name]+LEAD-ATTN_FIRST*TILE for name in ("attn_gain", "attn_shift", "qkv_w", "qv_b", "proj_w", "proj_b")}

def get_rows(ref, at):
    return jnp.concatenate([ref[i, at, :] for i in range(3)], axis=1)

def put_rows(ref, at, value):
    for i in range(3):
        ref[i, at, :] = value[:, i*128:(i+1)*128]

def attention_forward_kernel(rows, state_ref, pieces_ref, out_ref, qkv_ref, log_ref, mixed_t_ref, stat_ref, wp_ref, wo_ref, vec_ref,
                             mixed_ref, vt_ref, bp_ref, wide_ref, rows_ref, edge_ref, sems):
    rows.start(pieces_ref, rows_ref, edge_ref, sems)
    rows.finish(pieces_ref, rows_ref, edge_ref, sems)
    for r in range(0, ATTN_TILES*TILE, 16*TILE):
        end = min(r+16*TILE, ATTN_TILES*TILE)
        put_rows(wide_ref, slice(r, end), rows_ref[r:end, :].astype(f32))
    one_row = lambda name, i=0: get_rows(wide_ref, slice(ATTN[name]+i, ATTN[name]+i+1))
    gain, shift, bias = one_row("attn_gain"), one_row("attn_shift"), one_row("proj_b")
    vec_ref[...] = rows_of(gain, shift)
    nothing = jnp.zeros((CH, HP-HEAD_DIM), f32)
    for j in range(3):
        third = get_rows(wide_ref, pl.ds(ATTN["qkv_w"]+j, CH, stride=3))
        third_bias = one_row("qv_b", j//2) if j != 1 else jnp.zeros((1, CH), f32)
        for h in range(HEADS):
            to = slice(j*QW+h*HP, j*QW+(h+1)*HP)
            wp_ref[:, to] = jnp.concatenate([third[:, h*HEAD_DIM:(h+1)*HEAD_DIM], nothing], axis=1).astype(narrow)
            bp_ref[:, to] = jnp.concatenate([third_bias[:, h*HEAD_DIM:(h+1)*HEAD_DIM], nothing[0:1]], axis=1)
    for h in range(HEADS):
        at = ATTN["proj_w"]+h*HEAD_DIM
        wo_ref[h*HP:h*HP+HEAD_DIM, :] = get_rows(wide_ref, slice(at, at+HEAD_DIM)).astype(narrow)
        wo_ref[h*HP+HEAD_DIM:(h+1)*HP, :] = jnp.zeros((HP-HEAD_DIM, CH), narrow)
    member = membership(CH, CH//GROUPS)
    def sums(i, c):
        v = state_ref[pl.ds(i*EL, EL), :]
        return c[0]+fold(v), c[1]+fold(v*v)
    z = jnp.zeros((8, CH), f32)
    mean, inv = norm_stats(*steps(PIX//EL, sums, (z, z)), member, PIX*(CH//GROUPS))
    stat_ref[...] = rows_of(mean, inv)
    factor, term = inv*gain, shift-mean*inv*gain
    def project(i, _):
        r = pl.ds(i*256, 256)
        n = (state_ref[r, :]*factor+term).astype(narrow)
        qkv_ref[r, :] = (dot(n, wp_ref[...])+bp_ref[...]).astype(narrow)
        return _
    steps(PIX//256, project, 0)
    for h in range(HEADS):
        vt_ref[...] = jnp.transpose(qkv_ref[:, 2*QW+h*HP:2*QW+(h+1)*HP].astype(f32)).astype(narrow)
        for c in range(0, PIX, QC):
            s = dot_nt(qkv_ref[:, QW+h*HP:QW+(h+1)*HP], qkv_ref[c:c+QC, h*HP:(h+1)*HP])
            top = jnp.max(s, axis=0, keepdims=True)
            e = jnp.exp2((s-top)*POWER)
            total = jnp.sum(e, axis=0, keepdims=True)
            log_ref[h:h+1, c:c+QC] = top*POWER+jnp.log2(total)
            m = (dot(vt_ref[...], e.astype(narrow))*(1.0/total)).astype(narrow)
            mixed_t_ref[h*HP:(h+1)*HP, c:c+QC] = m
            mixed_ref[c:c+QC, h*HP:(h+1)*HP] = jnp.transpose(m.astype(f32)).astype(narrow)
    log_ref[HEADS:8, :] = jnp.zeros((8-HEADS, PIX), f32)
    def finish(i, _):
        r = pl.ds(i*256, 256)
        out_ref[r, :] = state_ref[r, :]+(dot(mixed_ref[r, :], wo_ref[...])+bias)
        return _
    steps(PIX//256, finish, 0)

def attention_forward(place, state, pieces):
    rows = Rows(place, ATTN_FIRST, ATTN_TILES)
    return call(functools.partial(attention_forward_kernel, rows), [state, pieces],
        [sds((PIX, CH)), sds((PIX, 3*QW), narrow), sds((8, PIX)), sds((QW, PIX), narrow), sds((8, CH)),
         sds((CH, 3*QW), narrow), sds((QW, CH), narrow), sds((8, CH))],
        [pltpu.VMEM((PIX, QW), narrow), pltpu.VMEM((HP, PIX), narrow), pltpu.VMEM((1, 3*QW), f32),
         pltpu.VMEM((3, ATTN_TILES*TILE, 128), f32)]+rows.scratch(),
        2*PIX*(CH*4*QW+2*PIX*QW), away=(1,), room=39)

def attention_back_kernel(grad_ref, state_ref, stat_ref, qkv_ref, log_ref, mixed_t_ref, wp_ref, wo_ref, vec_ref,
                          out_ref, large_ref, small_ref, dm_ref, pg_ref, kt_ref, dv_ref, dk_ref, nt_ref, keep_ref,
                          wide_ref, rows_ref, sems):
    gain, shift = vec_ref[0:1, :], vec_ref[1:2, :]
    mean, inv = stat_ref[0:1, :], stat_ref[1:2, :]
    member = membership(CH, CH//GROUPS)
    z = jnp.zeros((8, CH), f32)
    one = lambda v: jnp.sum(v, axis=0, keepdims=True)
    def start(i, c):
        r = pl.ds(i*256, 256)
        g = grad_ref[r, :].astype(narrow)
        keep_ref[r, :] = g
        dm_ref[r, :] = dot_nt(g, wo_ref[...]).astype(narrow)
        return c+fold(g.astype(f32))
    proj_bias = steps(PIX//256, start, z)
    for name, after in (("attn_gain", ATTN["qkv_w"]), ("qv_b", ATTN["proj_w"]), ("proj_b", ATTN_TILES*TILE)):
        put_rows(wide_ref, slice(ATTN[name], after), jnp.zeros((after-ATTN[name], CH), f32))
    wo_grad = dot(mixed_t_ref[...], keep_ref[...])
    for h in range(HEADS):
        at = ATTN["proj_w"]+h*HEAD_DIM
        put_rows(wide_ref, slice(at, at+HEAD_DIM), wo_grad[h*HP:h*HP+HEAD_DIM, :])
    for h in range(HEADS):
        q0, k0, v0 = h*HP, QW+h*HP, 2*QW+h*HP
        kt_ref[...] = jnp.transpose(qkv_ref[:, k0:k0+HP].astype(f32)).astype(narrow)
        for c in range(0, PIX, QC):
            q, dm = qkv_ref[c:c+QC, q0:q0+HP], dm_ref[c:c+QC, h*HP:(h+1)*HP]
            s = dot_nt(qkv_ref[:, k0:k0+HP], q)
            p = jnp.exp2(s*POWER-log_ref[h:h+1, c:c+QC])
            dp = dot_nt(qkv_ref[:, v0:v0+HP], dm)
            dm_t = dot_nt(wo_ref[h*HP:(h+1)*HP, :], keep_ref[c:c+QC, :]).astype(narrow).astype(f32)
            delta = jnp.sum(dm_t*mixed_t_ref[h*HP:(h+1)*HP, c:c+QC].astype(f32), axis=0, keepdims=True)
            ds = (p*(dp-delta)).astype(narrow)
            dv = dot(p.astype(narrow), dm)
            dk = dot(ds, q)
            if c == 0:
                dv_ref[...] = dv
                dk_ref[...] = dk
            else:
                dv_ref[...] += dv
                dk_ref[...] += dk
            dq = dot(kt_ref[...], ds)
            pg_ref[c:c+QC, q0:q0+HP] = jnp.transpose(dq*SCALE).astype(narrow)
        pg_ref[:, k0:k0+HP] = (dk_ref[...]*SCALE).astype(narrow)
        pg_ref[:, v0:v0+HP] = dv_ref[...].astype(narrow)
    factor, term = inv*gain, shift-mean*inv*gain
    for r in range(0, PIX, 256):
        nt_ref[:, r:r+256] = jnp.transpose(state_ref[r:r+256, :]*factor+term).astype(narrow)
    for j in range(3):
        third = dot(nt_ref[...], pg_ref[:, j*QW:(j+1)*QW])
        third = jnp.concatenate([third[:, h*HP:h*HP+HEAD_DIM] for h in range(HEADS)], axis=1)
        put_rows(wide_ref, pl.ds(ATTN["qkv_w"]+j, CH, stride=3), third)
    for r in range(0, ATTN_TILES, 16):
        end = min(r+16, ATTN_TILES)
        rows_ref[r:end] = get_rows(wide_ref, slice(r*TILE, end*TILE)).astype(narrow).reshape(end-r, TILE, CH)
    copy = pltpu.make_async_copy(rows_ref, large_ref.at[ATTN_FIRST:ATTN_FIRST+ATTN_TILES], sems.at[0])
    copy.start()
    zb = jnp.zeros((8, 3*QW), f32)
    def norm_grad(i, c):
        r = pl.ds(i*256, 256)
        d = dot_nt(pg_ref[r, :], wp_ref[...])
        n = state_ref[r, :]*inv-mean*inv
        out_ref[r, :] = d
        return c[0]+fold(d), c[1]+fold(d*n), c[2]+fold(pg_ref[r, :].astype(f32))
    shift_grad, gain_grad, bias_grad = (one(v) for v in steps(PIX//256, norm_grad, (z, z, zb)))
    compact = [jnp.concatenate([bias_grad[:, j*QW+h*HP:j*QW+h*HP+HEAD_DIM] for h in range(HEADS)], axis=1) for j in (0, 2)]
    tot = group_totals(rows_of(shift_grad*gain, gain_grad*gain), member)/(PIX*(CH//GROUPS))
    second = tot[1:2]*inv*inv
    by_term = second*mean-tot[0:1]*inv
    def finish(i, _):
        r = pl.ds(i*EL, EL)
        out_ref[r, :] = grad_ref[r, :]+(out_ref[r, :]*factor-state_ref[r, :]*second+by_term)
        return _
    steps(PIX//EL, finish, 0)
    small_ref[...] = rows_of(gain_grad, shift_grad, compact[0], compact[1], one(proj_bias))
    copy.wait()

def attention_back(grad, state, stat, qkv, log, mixed_t, wp, wo, vec, tiles):
    return call(attention_back_kernel, [grad, state, stat, qkv, log, mixed_t, wp, wo, vec],
        [sds((PIX, CH)), sds((tiles, TILE, CH), narrow), sds((8, CH))],
        [pltpu.VMEM((PIX, QW), narrow), pltpu.VMEM((PIX, 3*QW), narrow), pltpu.VMEM((HP, PIX), narrow), pltpu.VMEM((PIX, HP), f32),
         pltpu.VMEM((PIX, HP), f32), pltpu.VMEM((CH, PIX), narrow), pltpu.VMEM((PIX, CH), narrow),
         pltpu.VMEM((3, ATTN_TILES*TILE, 128), f32), pltpu.VMEM((ATTN_TILES, TILE, CH), narrow), pltpu.SemaphoreType.DMA((1,))],
        2*PIX*(CH*8*QW+5*PIX*QW), away_out=(1,), room=39)


def to_phases(v):
    c = v.shape[0]
    return jnp.transpose(v.reshape(c, SIDE, 2, SIDE, 2), (2, 4, 0, 1, 3)).reshape(4, c, PIX)


def pad_rows8(v):
    return jnp.pad(v, ((0, 0), (0, 8-v.shape[1]), (0, 0)))


def taps_rows(v):
    v = jnp.pad(v, ((0, 0), (0, 8-v.shape[1]), (0, 0))).reshape(72, v.shape[2])
    return jnp.pad(v, ((0, 128-72), (0, 0)))


class Place:
    def __init__(self, sizes, share):
        self.sizes = sizes
        self.share = share
        self.total = sizes["y"]*sizes["c"]*sizes["z"]*sizes["x"]
        firsts = [(share*d+LEAD)//TILE for d in range(self.total)]
        lasts = [-(-(share*(d+1)+LEAD)//TILE) for d in range(self.total)]
        self.block = max(last-first for first, last in zip(firsts, lasts))
        self.tiles = max(first+self.block for first in firsts)
        self.tiles = -(-self.tiles//TILE)*TILE
        self.at = {axis: lax.axis_index(axis) for axis in sizes}

    def device(self, y, c, z, x):
        s = self.sizes
        return ((y*s["c"]+c)*s["z"]+z)*s["x"]+x

    def first(self, device):
        return (self.share*device+LEAD)//TILE

    def me(self):
        a = self.at
        return self.device(a["y"], a["c"], a["z"], a["x"])


def turn(value, axis, size, distance):
    return lax.ppermute(value, axis, [(i, (i+distance) % size) for i in range(size)])


def hold_for(value, others):
    return lax.optimization_barrier((value, others))[0]


def add_everywhere(value, place):
    return add_over(value, place, ("c", "x", "y", "z"))


def add_over(value, place, axes):
    for axis in axes:
        size, step = place.sizes[axis], 1
        while step < size:
            value = value+lax.ppermute(value, axis, [(i, i ^ step) for i in range(size)])
            step *= 2
    return value


def cut_kernel(count, size, starts_ref, large_ref, out_ref, sems):
    copies = [pltpu.make_async_copy(large_ref.at[pl.ds(starts_ref[i], size)], out_ref.at[i], sems.at[i]) for i in range(count)]
    for copy in copies:
        copy.start()
    for copy in copies:
        copy.wait()


def cut(large, starts, size):
    count = starts.shape[0]
    return pl.pallas_call(
        functools.partial(cut_kernel, count, size),
        out_shape=sds((count, size, TILE, WIDE), narrow),
        in_specs=[pl.BlockSpec(memory_space=pltpu.SMEM), pl.BlockSpec(memory_space=pl.ANY)],
        out_specs=pl.BlockSpec(memory_space=VM),
        scratch_shapes=[pltpu.SemaphoreType.DMA((count,))],
        compiler_params=pltpu.CompilerParams(vmem_limit_bytes=39*MIB),
        cost_estimate=pl.CostEstimate(flops=0, bytes_accessed=1024, transcendentals=0),
    )(starts, large)


def merge_kernel(coords, sends, count, size, starts_ref, large_ref, arrived_ref, *refs):
    outs, (held_ref, sems) = refs[:-2], refs[-2:]
    copies = [pltpu.make_async_copy(large_ref.at[pl.ds(starts_ref[i], size)], held_ref.at[i], sems.at[i]) for i in range(count)]
    for copy in copies:
        copy.start()
    for i in range(count):
        copies[i].wait()
        which, at = sends[i]
        outs[which][at] = (held_ref[i].astype(f32)+arrived_ref[i].astype(f32)).astype(outs[which].dtype)


def share_out(large, small, place, parts):
    s, a, block = place.sizes, place.at, place.block
    half = (s["z"]+1)//2
    coords = [(y, z, x) for y in range(s["y"]) for z in range(s["z"]) for x in range(s["x"])]

    def starts(core):
        return jnp.stack([
            place.first(place.device((a["y"]+y) % s["y"], core, (a["z"]+z) % s["z"], (a["x"]+x) % s["x"])) for y, z, x in coords
        ]).astype(jnp.int32)

    far_starts, own_starts = starts(1-a["c"]), starts(a["c"])
    bounds = [block*i//parts for i in range(parts+1)]
    groups = [("y", [(0, z, x) for z in range(half) for x in range(s["x"])])]
    groups += [("y%d" % k, [(k, z, x) for z in range(half) for x in range(s["x"])]) for k in range(1, s["y"])]
    groups += [("x", [(y, z, 0) for z in range(half, s["z"]) for y in range(s["y"])])]
    groups += [("x%d" % k, [(y, z, k) for z in range(half, s["z"]) for y in range(s["y"])]) for k in range(1, s["x"])]
    names = [name for name, members in groups]
    sends = [None]*len(coords)
    for g, (name, members) in enumerate(groups):
        for at, member in enumerate(members):
            sends[coords.index(member)] = (g, at)
    length = small.shape[0]//2
    half_small, other_small = (lax.dynamic_slice_in_dim(small, core*length, length) for core in (a["c"], 1-a["c"]))
    half_small = half_small+turn(other_small, "c", 2, 1)
    far_starts = hold_for(far_starts, half_small)
    arrived, merged = [], []
    for part in range(parts):
        sent = cut(large, far_starts+bounds[part], bounds[part+1]-bounds[part])
        arrived.append(turn(sent, "c", 2, 1))
        far_starts = hold_for(far_starts, sent)
    for part in range(parts):
        size = bounds[part+1]-bounds[part]
        outs = [sds((len(members), size, TILE, WIDE), f32 if name in ("y", "x") else narrow) for name, members in groups]
        out = pl.pallas_call(
            functools.partial(merge_kernel, coords, sends, len(coords), size),
            out_shape=outs,
            in_specs=[pl.BlockSpec(memory_space=pltpu.SMEM), pl.BlockSpec(memory_space=pl.ANY), pl.BlockSpec(memory_space=VM)],
            out_specs=[pl.BlockSpec(memory_space=VM)]*len(outs),
            scratch_shapes=[pltpu.VMEM((len(coords), size, TILE, WIDE), narrow), pltpu.SemaphoreType.DMA((len(coords),))],
            compiler_params=pltpu.CompilerParams(vmem_limit_bytes=39*MIB),
            cost_estimate=pl.CostEstimate(flops=0, bytes_accessed=1024, transcendentals=0),
        )(own_starts+bounds[part], large, arrived[part])
        own_starts = hold_for(own_starts, out)
        merged.append(dict(zip(names, out)))

    def first_stage(sums):
        return ([turn(sums["y%d" % k], "y", s["y"], k) for k in range(1, s["y"])],
                [turn(sums["x%d" % k], "x", s["x"], k) for k in range(1, s["x"])])

    def first_sums(sums, came):
        near = sums["y"]+sum(value.astype(f32) for value in came[0])
        far = sums["x"]+sum(value.astype(f32) for value in came[1])
        return near.reshape((half, s["x"])+near.shape[1:]), far.reshape((s["z"]-half, s["y"])+far.shape[1:])

    def second_sums(near, far):
        near = near[:, 0]+sum(turn(near[:, k].astype(narrow), "x", s["x"], k).astype(f32) for k in range(1, s["x"]))
        far = far[:, 0]+sum(turn(far[:, k].astype(narrow), "y", s["y"], k).astype(f32) for k in range(1, s["y"]))
        return near, far

    def third_sum(near, far):
        total = near[0]
        for z in range(1, s["z"]):
            value = near[z] if z < half else far[z-half]
            total = total+turn(value.astype(narrow), "z", s["z"], z).astype(f32)
        return total

    waiting = [first_stage(merged[part]) for part in range(min(2, parts))]
    results, ready = [], None
    for part in range(parts):
        if part == 0:
            waiting[0] = hold_for(waiting[0], merged[-1])
        near, far = first_sums(merged[part], waiting[part])
        if part == 0:
            half_small = add_over(hold_for(half_small, merged[-1]), place, ("z",))
        if part == parts-1:
            half_small = add_over(hold_for(half_small, (near, far)), place, ("x", "y"))
        if part+2 < parts:
            waiting.append(first_stage(hold_for(merged[part+2], (near, far))))
        if 0 < part < parts-1:
            near, far = hold_for((near, far), waiting[part+1])
        results.append(third_sum(*second_sums(near, far)))
    other_small = turn(half_small, "c", 2, 1)
    first = a["c"] == 0
    small = jnp.concatenate([jnp.where(first, half_small, other_small), jnp.where(first, other_small, half_small)])
    return jnp.concatenate(results, axis=0), small


SPOTS = (
    list(range(14))
    + [ROW["time1_b"], ROW["time1_b"]+1, ROW["time2_b"], ROW["time2_b"]+1, ROW["down_b"]]
    + [ROW["res_b"]+i for i in range(4)]
    + [ROW["emb_b"]+i for i in range(4)]
    + [ROW["res_gain"]+i for i in range(4)]
    + [ROW["res_shift"]+i for i in range(4)]
    + [ROW["attn_gain"], ROW["attn_shift"], ROW["qv_b"], ROW["qv_b"]+1, ROW["proj_b"]]
    + [ROW["head_gain"]+i for i in range(3)] + [ROW["head_b"]] + [-1]*4
    + [ROW["head_gain"]+3+9*tap+part if tap < 9 else -1 for part in range(9) for tap in range(16)]
)
SPOTS += [-1]*(256-len(SPOTS))

TIME_FIRST = (ROW["time1_w"]+LEAD)//TILE
TIME_TILES = -(-(ROW["time2_b"]+2+LEAD)//TILE)-TIME_FIRST
EMB_FIRST = (ROW["res_b"]+LEAD)//TILE
EMB_TILES = -(-(ROW["res_shift"]+4+LEAD)//TILE)-EMB_FIRST


def widen_rows(low_ref, wide_ref, count):
    for r in range(0, count, 16*TILE):
        end = min(r+16*TILE, count)
        put_rows(wide_ref, slice(r, end), low_ref[r:end, :].astype(f32))


def time_kernel(n, rows, me_ref, sinus_ref, pieces_ref, hidden_pre_ref, hidden_ref, outer_pre_ref, embed_ref, vec_ref, w2_ref, we_ref,
                time_ref, emb_ref, *held):
    one, two = (pieces_ref,)+held[:3], (pieces_ref,)+held[3:]
    rows[0].start(*one)
    rows[1].start(*two)
    rows[0].finish(*one)
    time_low_ref, emb_low_ref = held[0], held[3]
    widen_rows(time_low_ref, time_ref, TIME_TILES*TILE)

    def in_time(name, i=0):
        return ROW[name]+LEAD-TIME_FIRST*TILE+i

    def in_emb(name, i=0):
        return ROW[name]+LEAD-EMB_FIRST*TILE+i

    def row(ref, at):
        return get_rows(ref, slice(at, at+1))

    for h in range(2):
        w1 = get_rows(time_ref, pl.ds(in_time("time1_w", h), C0, stride=2)).astype(narrow)
        hidden_pre_ref[:, h*CH:(h+1)*CH] = dot(sinus_ref[...], w1)+row(time_ref, in_time("time1_b", h))
        w2_ref[h] = get_rows(time_ref, pl.ds(in_time("time2_w", h), TEMB, stride=2)).astype(narrow)
    v = hidden_pre_ref[...]
    hidden_ref[...] = (v*sigmoid(v)).astype(narrow)
    for h in range(2):
        outer_pre_ref[:, h*CH:(h+1)*CH] = dot(hidden_ref[...], w2_ref[h])+row(time_ref, in_time("time2_b", h))
    v = outer_pre_ref[...]
    embed = (v*sigmoid(v)).astype(narrow)
    embed_ref[...] = embed
    mine = lax.broadcasted_iota(jnp.int32, (n, TEMB), 0) == me_ref[0]
    own = jnp.sum(jnp.where(mine, embed.astype(f32), 0.0), axis=0, keepdims=True)
    own = jnp.broadcast_to(own, (8, TEMB)).astype(narrow)
    rows[1].finish(*two)
    widen_rows(emb_low_ref, emb_ref, EMB_TILES*TILE)
    for b in range(BLOCKS):
        modulate = []
        for h in range(2):
            we_ref[b, h] = get_rows(emb_ref, pl.ds(in_emb("emb_w", 2*TEMB*b+h), TEMB, stride=2)).astype(narrow)
            modulate.append(dot(own, we_ref[b, h])[0:1]+row(emb_ref, in_emb("emb_b", 2*b+h)))
        vec_ref[b] = jnp.concatenate([
            row(emb_ref, in_emb("res_b", 2*b)), row(emb_ref, in_emb("res_b", 2*b+1)),
            row(emb_ref, in_emb("res_gain", 2*b)), row(emb_ref, in_emb("res_shift", 2*b)),
            row(emb_ref, in_emb("res_gain", 2*b+1)), row(emb_ref, in_emb("res_shift", 2*b+1)),
            1.0+modulate[0], modulate[1],
        ], axis=0)


def time_and_modulation(place, sinus, pieces):
    rows = [Rows(place, TIME_FIRST, TIME_TILES), Rows(place, EMB_FIRST, EMB_TILES)]
    n = sinus.shape[0]
    spec = pl.BlockSpec(memory_space=VM)
    return pl.pallas_call(
        functools.partial(time_kernel, n, rows),
        out_shape=[sds((n, TEMB)), sds((n, TEMB), narrow), sds((n, TEMB)), sds((n, TEMB), narrow), sds((BLOCKS, 8, CH)),
                   sds((2, TEMB, CH), narrow), sds((BLOCKS, 2, TEMB, CH), narrow)],
        in_specs=[pl.BlockSpec(memory_space=pltpu.SMEM), spec, pl.BlockSpec(memory_space=pl.ANY)],
        out_specs=[spec]*7,
        scratch_shapes=[pltpu.VMEM((3, TIME_TILES*TILE, 128), f32), pltpu.VMEM((3, EMB_TILES*TILE, 128), f32)]
        + rows[0].scratch()+rows[1].scratch(),
        compiler_params=pltpu.CompilerParams(vmem_limit_bytes=39*MIB),
        cost_estimate=pl.CostEstimate(flops=2**27, bytes_accessed=8*2**20, transcendentals=0),
    )(place.me().reshape(1), sinus, pieces)


SMALL_HEAD, SMALL_ATTN, SMALL_S1, SMALL_STEM, SMALL_S0, SMALL_MOVED = 0, 120, 128, 136, 184, 192


def owner_kernel(share, n, me_ref, small_ref, sinus_ref, hidden_pre_ref, hidden_ref, outer_pre_ref, embed_ref, w2_ref, we_ref, spot_ref,
                 out_ref, time_ref, emb_ref, mixed_time_ref, mixed_emb_ref):
    row0 = me_ref[0]*share
    half_rows = mixed_time_ref.shape[1]//2
    one = lambda v: jnp.sum(v, axis=0, keepdims=True)
    moved = [[small_ref[SMALL_MOVED+(2*b+h)*n:SMALL_MOVED+(2*b+h+1)*n, :] for h in range(2)] for b in range(BLOCKS)]
    embed_grad = sum(exact_nt(moved[b][h], we_ref[b, h]) for b in range(BLOCKS) for h in range(2))
    outer_grad = embed_grad*silu_slope(outer_pre_ref[...])
    hidden_grad = sum(exact_nt(outer_grad[:, h*CH:(h+1)*CH], w2_ref[h]) for h in range(2))*silu_slope(hidden_pre_ref[...])

    def table(ref, values):
        ref[...] = jnp.zeros(ref.shape, f32)
        width = min(n, 128)
        for family, (value_ref, at) in enumerate(values):
            turned = jnp.transpose(value_ref[...].astype(f32))
            for first in range(0, n, width):
                group, lane = divmod(family*n+first, 128)
                ref[group, half_rows+at:half_rows+at+turned.shape[0], lane:lane+width] = turned[:, first:first+width]

    def products(ref, begin, factors, mixed_ref):
        away = row0-begin+(1 << 20)
        place = away // 2 - (1 << 19)
        start = jnp.clip(place+half_rows, 0, ref.shape[1]-half_rows)
        for h in range(2):
            right = jnp.concatenate([factors[0][h], factors[1][h]], axis=0)
            if right.shape[0] < 128:
                right = jnp.concatenate([right, jnp.zeros((128-right.shape[0], CH), f32)], axis=0)
            total = None
            for group in range(ref.shape[0]):
                left = ref[group, pl.ds(start, half_rows), :].astype(narrow)
                part = sum(dot(left, p) for p in three(right[group*128:(group+1)*128]))
                total = part if total is None else total+part
            put_rows(mixed_ref, pl.ds(h, half_rows, stride=2), total)
        odd = away-2*(away//2)
        return jnp.where(odd == 1, get_rows(mixed_ref, slice(1, 1+share)), get_rows(mixed_ref, slice(0, share)))

    halves = lambda v: [v[:, :CH], v[:, CH:]]
    table(time_ref, [(sinus_ref, 0), (hidden_ref, (ROW["time2_w"]-ROW["time1_w"])//2)])
    table(emb_ref, [(embed_ref, 0), (embed_ref, TEMB)])
    total = products(time_ref, ROW["time1_w"], [halves(hidden_grad), halves(outer_grad)], mixed_time_ref)
    total += products(emb_ref, ROW["emb_w"], moved, mixed_emb_ref)

    def small(at, count=1):
        return small_ref[at:at+count, :]

    def pairs(at):
        return jnp.concatenate([small_ref[at:at+40, :C0], small_ref[at:at+32, C0:]], axis=0)

    stem = pairs(SMALL_STEM)
    stem_rows = [stem[8*tap+c:8*tap+c+1, :] for tap in range(9) for c in range(IN_CH)]+[small(SMALL_STEM+41)[:, :C0]]
    rows = [jnp.concatenate(stem_rows[2*i:2*i+2], axis=1) for i in range(14)]
    rows += halves(one(hidden_grad))+halves(one(outer_grad))+[small(SMALL_STEM+40)]
    rows += [small(SMALL_S0, 2), small(SMALL_S1, 2)]+[one(moved[b][h]) for b in range(BLOCKS) for h in range(2)]
    rows += [small(SMALL_S0+2, 2), small(SMALL_S1+2, 2), small(SMALL_S0+4, 2), small(SMALL_S1+4, 2), small(SMALL_ATTN, 5)]
    ends = SMALL_HEAD+112
    gain_u, shift_u, side = small(ends), small(ends+1), small(ends+2)
    rows += [gain_u, jnp.concatenate([side[:, :C0], shift_u[:, :C0]], axis=1), jnp.concatenate([shift_u[:, C0:], side[:, C0:]], axis=1)]
    rows += [small(ends+3), jnp.zeros((4, CH), f32)]
    q = lax.broadcasted_iota(jnp.int32, (96, 72), 0)
    pick = (lax.broadcasted_iota(jnp.int32, (96, 72), 1) == (q % 16)*8+q//16).astype(f32).astype(narrow)
    up = sum(dot(pick, p) for p in three(small_ref[SMALL_HEAD:SMALL_HEAD+72, :]))
    side = sum(dot(pick, p) for p in three(pairs(SMALL_HEAD+72)))
    columns = [up[:, 64*i:64*i+64] for i in range(6)]+[side[:, 64*i:64*i+64] for i in range(3)]
    head_rows = None
    for o in range(OUT_CH):
        block = jnp.concatenate([column[16*o:16*o+16] for column in columns], axis=0)
        lane = lax.broadcasted_iota(jnp.int32, (64, CH), 1)
        to = (lane == 6*lax.broadcasted_iota(jnp.int32, (64, CH), 0)+o).astype(f32).astype(narrow)
        part = exact(block, to)
        head_rows = part if head_rows is None else head_rows+part
    rows = jnp.concatenate(rows+[head_rows, jnp.zeros((256-48-144, CH), f32)], axis=0)
    at = lax.broadcasted_iota(jnp.int32, (share, 256), 0)+row0
    chosen = (at == spot_ref[...]).astype(f32).astype(narrow)
    out_ref[...] = total+sum(dot(chosen, p) for p in three(rows))


def owner_rows(place, small, sinus, kept, w2, we):
    share, n = place.share, place.total
    hidden_pre, hidden, outer_pre, embed = kept
    half_rows = -(-(share+2)//16)*8
    groups = -(-2*n//128)
    spec = pl.BlockSpec(memory_space=VM)
    time_rows = (ROW["time2_b"]-ROW["time1_w"])//2
    lengths = [-(-(time_rows+2*half_rows)//8)*8, -(-(2*TEMB+2*half_rows)//8)*8]
    spots = jnp.array(SPOTS, jnp.int32)[None]
    return pl.pallas_call(
        functools.partial(owner_kernel, share, n),
        out_shape=sds((share, WIDE)),
        in_specs=[pl.BlockSpec(memory_space=pltpu.SMEM)]+[spec]*9,
        out_specs=spec,
        scratch_shapes=[pltpu.VMEM((groups, lengths[0], 128), f32), pltpu.VMEM((groups, lengths[1], 128), f32),
                        pltpu.VMEM((3, 2*half_rows, 128), f32), pltpu.VMEM((3, 2*half_rows, 128), f32)],
        compiler_params=pltpu.CompilerParams(vmem_limit_bytes=26*MIB),
        cost_estimate=pl.CostEstimate(flops=0, bytes_accessed=1024, transcendentals=0),
    )(place.me().reshape(1), small, sinus, hidden_pre, hidden, outer_pre, embed, w2, we, spots)


def step(sizes, params, moment1, moment2, images, noise, timesteps, masks, weight_index):
    flat = params.shape[0]
    share = flat // WIDE
    place = Place(sizes, share)
    a, me = place.at, place.me()
    spare = (share*me+LEAD) % TILE
    piece = jnp.zeros((place.block*TILE, WIDE), narrow)
    piece = lax.dynamic_update_slice_in_dim(piece, params.astype(narrow).reshape(share, WIDE), spare, axis=0)
    pieces = lax.all_gather(piece.reshape(place.block, TILE, WIDE), ("y", "c", "z", "x"), axis=0)

    own = jnp.concatenate([images, noise, masks.astype(f32)[:, None]], axis=1)
    own = lax.all_to_all(own, ("z", "x"), split_axis=0, concat_axis=2, tiled=True)[0]
    index = a["z"]*sizes["x"]+a["x"]
    own_step = lax.dynamic_index_in_dim(timesteps, index, keepdims=False).astype(f32)
    sample_weight = 0.5+0.5*lax.dynamic_index_in_dim(weight_index, index, keepdims=False).astype(f32)
    clean, own_noise, mask = own[:IN_CH], own[IN_CH:2*IN_CH], own[2*IN_CH:]
    early = jnp.stack([
        jnp.where(jnp.arange(WIDE) == me, own_step, 0.0),
        jnp.full((WIDE,), jnp.sum(mask)),
    ] + [jnp.zeros((WIDE,), f32)]*6)
    early = add_everywhere(early, place)
    all_steps, count = early[0, :place.total], early[1, 0]
    signal, one_minus, beta, alpha, tilde = plan(own_step)
    noisy = (jnp.sqrt(signal)*clean+jnp.sqrt(one_minus)*own_noise).astype(narrow).astype(f32)
    noisy = pad_rows8(to_phases(noisy))
    noise_phases, mask_phases = pad_rows8(to_phases(own_noise)), to_phases(mask)

    half = C0 // 2
    freqs = jnp.exp(-math.log(10000.0) * jnp.arange(half).astype(f32) / half)
    angles = all_steps[:, None] * freqs
    sinus = jnp.concatenate([jnp.cos(angles), jnp.sin(angles)], axis=-1).astype(narrow)
    pieces = pieces.reshape(place.total, place.block*TILE, WIDE)

    def rows(name, length):
        first, found = ROW[name], []
        for d in range(first//share, (first+length-1)//share+1):
            begin, end = max(first, d*share), min(first+length, (d+1)*share)
            shifted = (d*share+LEAD) % TILE-d*share
            found.append(pieces[d, begin+shifted:end+shifted])
        return found[0] if len(found) == 1 else jnp.concatenate(found)

    stem = rows("stem_w", 14).reshape(-1)
    stem_w = taps_rows(stem[:27*C0].reshape(9, IN_CH, C0))
    stem_b = stem[27*C0:].reshape(1, C0).astype(f32)
    skip, state, down_w = stem_down(place, noisy, stem_w, stem_b, pieces)
    hidden_pre, hidden, outer_pre, embed, vectors, w2, we = time_and_modulation(place, sinus, pieces)
    blocks = []
    for b in range(BLOCKS):
        vec = vectors[b]
        base = RES+2*TAPS*b
        after, inner, stat = block_forward(place, state, pieces, base, vec)
        blocks.append((state, inner, stat, base, vec))
        state = after
    before = state
    state, qkv, log, mixed_t, attn_stat, wp, wo, attn_vec = attention_forward(place, before, pieces)

    ends = rows("head_gain", 85).reshape(-1)
    norm_u = jnp.stack([ends[:CH], ends[C0+CH:C0+2*CH]]).astype(f32)
    norm_s = jnp.stack([ends[CH:C0+CH], ends[C0+2*CH:2*(C0+CH)]]).astype(f32)
    head_size = 9*(C0+CH)*OUT_CH
    head_w = ends[2*(C0+CH):2*(C0+CH)+head_size].reshape(9, C0+CH, OUT_CH)
    head_w = jnp.transpose(head_w, (0, 2, 1))
    wu, ws = taps_rows(head_w[..., :CH]), taps_rows(head_w[..., CH:])
    head_b = ends[2*(C0+CH)+head_size:2*(C0+CH)+head_size+OUT_CH].astype(f32)
    head_b = jnp.broadcast_to(jnp.pad(head_b, (0, 8-OUT_CH))[:, None], (8, 128))
    numbers = jnp.stack([jnp.log(beta), jnp.log(tilde), beta*beta/(alpha*one_minus), sample_weight])
    grad, skip_grad, head_tail, losses = head(
        numbers, state, skip, wu, ws, norm_u, norm_s, head_b, noise_phases, mask_phases)
    grad, large, attn_small = attention_back(
        grad, before, attn_stat, qkv, log, mixed_t, wp, wo, attn_vec, place.tiles)
    begin, inner, stat, base, vec = blocks[1]
    grad, large, s1 = block_back(place, grad, begin, inner, stat, pieces, base, vec, large)
    begin, inner, stat, base, vec = blocks[0]
    grad, large, s0 = block_back(place, grad, begin, inner, stat, pieces, base, vec, large)
    large, small = down_stem_back(me, place.total, grad, skip, skip_grad, down_w, noisy, head_tail, attn_small, s1, s0, large)
    total, small = share_out(large, small, place, 2)
    total = lax.dynamic_slice_in_dim(total.reshape(-1, WIDE), spare, share)
    row = share*me+jnp.arange(share)
    dense = functools.reduce(jnp.logical_or, [
        (row >= ROW[name]) & (row < ROW[name]+length)
        for name, length in (("down_w", 9*C0), ("res_w", 4*TAPS), ("qkv_w", 3*CH), ("proj_w", CH))
    ])
    total = jnp.where(dense[:, None], total, 0.0)

    total = total+owner_rows(place, small, sinus, (hidden_pre, hidden, outer_pre, embed), w2, we)

    scaled = total/count
    sums = jnp.concatenate([losses[:2], jnp.full((1, 128), jnp.sum(scaled*scaled)), losses[3:]])
    sums = add_everywhere(sums, place)
    loss_sum, loss_vlb, grad_norm = sums[0, 0], sums[1, 0], jnp.sqrt(sums[2, 0])
    scaled = scaled.reshape(flat)
    clipped = scaled*jnp.minimum(1.0, clip_limit/(grad_norm+1e-06))
    first = decay_first*moment1+(1.0-decay_first)*clipped
    second = decay_second*moment2+(1.0-decay_second)*clipped*clipped
    first_hat = first/(1.0-decay_first**STEP)
    second_hat = second/(1.0-decay_second**STEP)
    updated = params-learn_rate*(first_hat/(jnp.sqrt(second_hat)+1e-08)+weight_decay*params)
    return (updated, first, second, updated.astype(narrow), loss_sum, loss_vlb, count, grad_norm)


def solution(mesh):
    y = mesh.shape["batch"] // 2
    sizes = {"y": y, "c": 2, "z": mesh.shape["rows"] // y, "x": y}
    fine = Mesh(mesh.devices.reshape(tuple(sizes.values())), tuple(sizes))
    every, batch, rows = ("y", "c", "z", "x"), ("y", "c"), ("z", "x")
    return jax.shard_map(
        functools.partial(step, sizes),
        mesh=fine,
        in_specs=(P(every), P(every), P(every), P(batch, None, rows, None), P(batch, None, rows, None),
                  P(batch), P(batch, rows, None), P(batch)),
        out_specs=(P(every), P(every), P(every), P(every), P(), P(), P(), P()),
        check_vma=False,
    )
```

```python
import functools
import math

import jax
import jax.numpy as jnp
from jax import lax
from jax.experimental import pallas as pl
from jax.experimental.pallas import tpu as pltpu
from jax.sharding import Mesh
from jax.sharding import PartitionSpec as P

IN_CH = 3
C0 = 192
CH = 384
TEMB = 768
HEADS = 4
HEAD_DIM = 96
GROUPS = 32
OUT_CH = 6
DIFF_STEPS = 4000
BLOCKS = 2
STEP = 10

cosine_offset = 0.008
kl_weight = 0.001
clip_limit = 0.05
learn_rate = 0.05
decay_first = 0.9
decay_second = 0.999
weight_decay = 0.01
narrow = jnp.bfloat16
f32 = jnp.float32


def segments():
    return [
        ("stem_w", (3, 3, IN_CH, C0)),
        ("stem_b", (C0,)),
        ("time1_w", (C0, TEMB)),
        ("time1_b", (TEMB,)),
        ("time2_w", (TEMB, TEMB)),
        ("time2_b", (TEMB,)),
        ("down_w", (3, 3, C0, CH)),
        ("down_b", (CH,)),
        ("res_w", (BLOCKS, 2, 3, 3, CH, CH)),
        ("res_b", (BLOCKS, 2, CH)),
        ("emb_w", (BLOCKS, TEMB, 2 * CH)),
        ("emb_b", (BLOCKS, 2 * CH)),
        ("res_gain", (BLOCKS, 2, CH)),
        ("res_shift", (BLOCKS, 2, CH)),
        ("attn_gain", (CH,)),
        ("attn_shift", (CH,)),
        ("qkv_w", (CH, 3 * CH)),
        ("qv_b", (2 * CH,)),
        ("proj_w", (CH, CH)),
        ("proj_b", (CH,)),
        ("head_gain", (C0 + CH,)),
        ("head_shift", (C0 + CH,)),
        ("head_w", (3, 3, C0 + CH, OUT_CH)),
        ("head_b", (OUT_CH,)),
    ]


WIDE = 384
TILE = 16
LEAD = 13
ROW = {}
offset = 0
for name, shape in segments():
    ROW[name] = offset // WIDE
    offset += math.prod(shape)
RES = ROW["res_w"]+LEAD
TAIL = ROW["res_b"]


def plan(steps):
    timef = steps.astype(jnp.float32)
    angle = math.pi / 2.0 / (1.0 + cosine_offset)
    theta = (timef / DIFF_STEPS + cosine_offset) * angle
    before = ((timef - 1.0) / DIFF_STEPS + cosine_offset) * angle
    anchor = cosine_offset * angle
    base = math.cos(anchor) ** 2
    signal = jnp.cos(theta) ** 2 / base
    one_minus = jnp.sin(theta + anchor) * jnp.sin(timef / DIFF_STEPS * angle) / base
    one_prev = jnp.sin(before + anchor) * jnp.sin((timef - 1.0) / DIFF_STEPS * angle) / base
    beta = jnp.sin(theta + before) * math.sin(angle / DIFF_STEPS) / jnp.cos(before) ** 2
    alpha = 1.0 - beta
    tilde = beta * one_prev / one_minus
    return (signal, one_minus, beta, alpha, tilde)


SIDE=32; PIX=SIDE*SIDE
MIB=1024*1024
VM=pltpu.VMEM

def call(kernel, ins, outs, scratch, flops, away=(), away_out=(), alias={}, scalar=(), room=32):
    spec = pl.BlockSpec(memory_space=VM)
    places = [pl.BlockSpec(memory_space=pl.ANY if i in away else pltpu.SMEM if i in scalar else VM) for i in range(len(ins))]
    moved = sum(a.size*a.dtype.itemsize for a in ins) + sum(math.prod(o.shape)*o.dtype.itemsize for o in outs)
    return pl.pallas_call(
        kernel, out_shape=outs, in_specs=places,
        out_specs=[pl.BlockSpec(memory_space=pl.ANY) if i in away_out else spec for i in range(len(outs))],
        scratch_shapes=scratch, input_output_aliases=alias,
        compiler_params=pltpu.CompilerParams(vmem_limit_bytes=room*MIB),
        cost_estimate=pl.CostEstimate(flops=flops, bytes_accessed=moved, transcendentals=0),
    )(*ins)

def sds(shape, dtype=f32): return jax.ShapeDtypeStruct(shape, dtype)

def dot(a, b): return jnp.dot(a, b, preferred_element_type=f32)
def dot_nt(a, b): return lax.dot_general(a, b, (((1,), (1,)), ((), ())), preferred_element_type=f32)

def sigmoid(v): return 0.5*jnp.tanh(0.5*v) + 0.5

def membership(chans, per, first=0):
    c = lax.broadcasted_iota(jnp.int32, (chans, 128), 0) + first
    g = lax.broadcasted_iota(jnp.int32, (chans, 128), 1)
    return ((c >= g*per) & (c < (g+1)*per)).astype(f32).astype(narrow)

def three(v):
    hi = v.astype(narrow); rest = v - hi.astype(f32)
    mid = rest.astype(narrow); low = (rest - mid.astype(f32)).astype(narrow)
    return hi, mid, low

def exact(v, ones):
    return sum(dot(p, ones) for p in three(v))
def exact_nt(v, ones):
    return sum(dot_nt(p, ones) for p in three(v))

def group_totals(stats, member):
    return exact_nt(exact(stats, member), member)

def fold(v):
    return jnp.sum(v.reshape(-1, 8, v.shape[-1]), axis=0)

def rows_of(*rows):
    r = jnp.concatenate(rows, axis=0)
    return jnp.concatenate([r, jnp.zeros((8-r.shape[0], r.shape[1]), f32)], axis=0)

def norm_stats(s1, s2, member, amount):
    stats = rows_of(jnp.sum(s1, axis=0, keepdims=True), jnp.sum(s2, axis=0, keepdims=True))
    tot = group_totals(stats, member) / amount
    mean = tot[0:1]
    return mean, lax.rsqrt(tot[1:2] - mean*mean + 1e-05)

EL=128
def steps(n, body, init=None):
    for i in range(n):
        init = body(i, init)
    return init

def pixel_column(rows, width):
    return lax.broadcasted_iota(jnp.int32, (rows, width), 0) % SIDE

def clear_edges(out_ref, width):
    zero = jnp.zeros((SIDE, 3*width), narrow)
    out_ref[0:SIDE, :] = zero
    out_ref[SIDE+PIX:SIDE+PIX+SIDE, :] = zero

def put_spread(out_ref, r, v, backward):
    count, width = v.shape
    col = pixel_column(count, width)
    before = jnp.where(col == 0, 0.0, pltpu.roll(v, 1, 0)).astype(narrow)
    after = jnp.where(col == SIDE-1, 0.0, pltpu.roll(v, count-1, 0)).astype(narrow)
    first, last = (after, before) if backward else (before, after)
    out_ref[SIDE+r:SIDE+r+count, 0:width] = first
    out_ref[SIDE+r:SIDE+r+count, width:2*width] = v.astype(narrow)
    out_ref[SIDE+r:SIDE+r+count, 2*width:3*width] = last

MC=256
def conv_rows(xs_ref, w_ref, base, r):
    acc = dot(xs_ref[pl.ds(r, MC), :], w_ref[base:base+3*CH, :])
    acc += dot(xs_ref[pl.ds(r+SIDE, MC), :], w_ref[base+3*CH:base+6*CH, :])
    return acc + dot(xs_ref[pl.ds(r+2*SIDE, MC), :], w_ref[base+6*CH:base+9*CH, :])

TAPS=9*CH
class Rows:
    def __init__(self, place, first, tiles):
        starts = [place.first(d) for d in range(place.total)]
        self.tiles, self.parts, self.edges = tiles, [], []
        for d in range(place.total):
            begin = starts[d]+1 if d else 0
            end = starts[d+1]+1 if d+1 < place.total else starts[d]+place.block
            begin, end = max(begin, first), min(end, first+tiles)
            if begin < end:
                self.parts.append((d, begin-starts[d], end-starts[d], begin-first))
            if d and first <= starts[d] < first+tiles:
                self.edges.append((d, starts[d]-first))

    def scratch(self):
        return [pltpu.VMEM((self.tiles*TILE, CH), narrow), pltpu.VMEM((max(len(self.edges), 1), TILE, CH), narrow),
                pltpu.SemaphoreType.DMA((len(self.parts)+len(self.edges),))]

    def copies(self, pieces_ref, low_ref, edge_ref, sems):
        made = []
        for d, begin, end, to in self.parts:
            made.append(pltpu.make_async_copy(pieces_ref.at[d, begin*TILE:end*TILE, :],
                                              low_ref.at[to*TILE:(to+end-begin)*TILE, :], sems.at[len(made)]))
        for i, (d, to) in enumerate(self.edges):
            made.append(pltpu.make_async_copy(pieces_ref.at[d, 0:TILE, :], edge_ref.at[i], sems.at[len(made)]))
        return made

    def start(self, *refs):
        for copy in self.copies(*refs):
            copy.start()

    def finish(self, pieces_ref, low_ref, edge_ref, sems):
        for copy in self.copies(pieces_ref, low_ref, edge_ref, sems):
            copy.wait()
        for i, (d, to) in enumerate(self.edges):
            low_ref[to*TILE:(to+1)*TILE, :] = low_ref[to*TILE:(to+1)*TILE, :]+edge_ref[i]

def block_forward_kernel(rows, state_ref, pieces_ref, vec_ref, out_ref, inner_ref, stat_ref, xs_ref, *held):
    one, two = (pieces_ref,)+held[:3], (pieces_ref,)+held[3:]
    rows[0].start(*one)
    rows[1].start(*two)
    w1_ref, w2_ref = held[0], held[3]
    bias1, bias2, gain1, shift1, gain2, shift2, scale, offset = (vec_ref[i:i+1, :] for i in range(8))
    member = membership(CH, CH//GROUPS)
    amount = PIX*(CH//GROUPS)
    def sums(i, c):
        v = state_ref[pl.ds(i*EL, EL), :]
        return c[0]+fold(v), c[1]+fold(v*v)
    z = jnp.zeros((8, CH), f32)
    mean1, inv1 = norm_stats(*steps(PIX//EL, sums, (z, z)), member, amount)
    clear_edges(xs_ref, CH)
    factor, term = inv1*gain1, shift1 - mean1*inv1*gain1
    for r in range(0, PIX, EL):
        v = state_ref[r:r+EL, :]*factor + term
        put_spread(xs_ref, r, v*sigmoid(v), False)
    rows[0].finish(*one)
    def conv1(i, c):
        r = i*MC
        v = conv_rows(xs_ref, w1_ref, 0, r) + bias1
        inner_ref[pl.ds(r, MC), :] = v
        return c[0]+fold(v), c[1]+fold(v*v)
    mean2, inv2 = norm_stats(*steps(PIX//MC, conv1, (z, z)), member, amount)
    factor, term = inv2*gain2*scale, (shift2 - mean2*inv2*gain2)*scale + offset
    for r in range(0, PIX, EL):
        v = inner_ref[r:r+EL, :]*factor + term
        put_spread(xs_ref, r, v*sigmoid(v), False)
    rows[1].finish(*two)
    def conv2(i, _):
        r = i*MC
        out_ref[pl.ds(r, MC), :] = state_ref[pl.ds(r, MC), :] + (conv_rows(xs_ref, w2_ref, 0, r) + bias2)
        return _
    steps(PIX//MC, conv2, 0)
    stat_ref[...] = rows_of(mean1, inv1, mean2, inv2)

def block_rows(place, base):
    return [Rows(place, (base+i*TAPS)//TILE, TAPS//TILE) for i in range(2)]

def block_forward(place, state, pieces, base, vectors):
    rows = block_rows(place, base)
    return call(functools.partial(block_forward_kernel, rows), [state, pieces, vectors],
        [sds((PIX, CH)), sds((PIX, CH)), sds((8, CH))],
        [pltpu.VMEM((PIX+2*SIDE, 3*CH), narrow)]+rows[0].scratch()+rows[1].scratch(),
        2*2*PIX*TAPS*CH, away=(1,), room=39)

def back_taps(gs_ref, w_ref, base, r):
    acc = None
    for dy in range(3):
        for dx in range(3):
            part = dot_nt(gs_ref[pl.ds(r+SIDE*(2-dy), MC), dx*CH:(dx+1)*CH],
                          w_ref[base+(3*dy+dx)*CH:base+(3*dy+dx+1)*CH, :])
            acc = part if acc is None else acc+part
    return acc

def kernel_grads(xt_ref, gs_ref, dw_ref, base):
    def body(dy, _):
        r = SIDE*(2-dy)
        value = dot(xt_ref[...], gs_ref[pl.ds(r, PIX), :]).astype(dw_ref.dtype)
        for dx in range(3):
            at = (base+(3*dy+dx)*CH)//TILE
            dw_ref[pl.ds(at, CH//TILE)] = value[:, dx*CH:(dx+1)*CH].reshape(CH//TILE, TILE, CH)
        return _
    steps(3, body, 0)

def block_back_kernel(base, rows, grad_ref, state_ref, inner_ref, stat_ref, pieces_ref, vec_ref, large_in_ref, out_ref, large_ref, small_ref,
                      gs_ref, xt_ref, keep_ref, dw_ref, sems, *held):
    first_in, second_in = (pieces_ref,)+held[:3], (pieces_ref,)+held[3:]
    rows[1].start(*second_in)
    rows[0].start(*first_in)
    w1_ref, w2_ref = held[0], held[3]
    bias1, bias2, gain1, shift1, gain2, shift2, scale, offset = (vec_ref[i:i+1, :] for i in range(8))
    mean1, inv1, mean2, inv2 = (stat_ref[i:i+1, :] for i in range(4))
    member = membership(CH, CH//GROUPS)
    amount = PIX*(CH//GROUPS)
    z = jnp.zeros((8, CH), f32)
    one = lambda v: jnp.sum(v, axis=0, keepdims=True)
    clear_edges(gs_ref, CH)
    factor2, term2 = inv2*gain2*scale, (shift2 - mean2*inv2*gain2)*scale + offset
    bias2_grad = z
    for r in range(0, PIX, EL):
        g = grad_ref[r:r+EL, :].astype(narrow).astype(f32)
        put_spread(gs_ref, r, g, True)
        bias2_grad += fold(g)
        v = inner_ref[r:r+EL, :]*factor2 + term2
        xt_ref[:, r:r+EL] = jnp.transpose(v*sigmoid(v)).astype(narrow)
    kernel_grads(xt_ref, gs_ref, dw_ref, TAPS)
    half = TAPS//TILE
    second_out = pltpu.make_async_copy(dw_ref.at[half:2*half], large_ref.at[base//TILE+half:base//TILE+2*half], sems.at[0])
    second_out.start()
    rows[1].finish(*second_in)
    d_sum, dn_sum = z, z
    for r in range(0, PIX, MC):
        d = back_taps(gs_ref, w2_ref, 0, r)
        x = inner_ref[r:r+MC, :]
        d = d*silu_slope(x*factor2 + term2)
        keep_ref[r:r+MC, :] = d
        d_sum += fold(d)
        dn_sum += fold(d*(x*inv2 - mean2*inv2))
    mod_offset, dn = one(d_sum), one(dn_sum)
    mod_scale = gain2*dn + shift2*mod_offset
    tot = group_totals(rows_of(mod_offset*scale*gain2, dn*scale*gain2), member)/amount
    first, second = tot[0:1]*inv2, tot[1:2]*inv2*inv2
    by_keep, by_term = scale*gain2*inv2, second*mean2 - first
    bias1_grad = z
    factor1, term1 = inv1*gain1, shift1 - mean1*inv1*gain1
    for r in range(0, PIX, EL):
        g = keep_ref[r:r+EL, :]*by_keep - inner_ref[r:r+EL, :]*second + by_term
        g = g.astype(narrow).astype(f32)
        put_spread(gs_ref, r, g, True)
        bias1_grad += fold(g)
        v = state_ref[r:r+EL, :]*factor1 + term1
        xt_ref[:, r:r+EL] = jnp.transpose(v*sigmoid(v)).astype(narrow)
    kernel_grads(xt_ref, gs_ref, dw_ref, 0)
    first_out = pltpu.make_async_copy(dw_ref.at[0:half], large_ref.at[base//TILE:base//TILE+half], sems.at[1])
    first_out.start()
    rows[0].finish(*first_in)
    d_sum, dn_sum = z, z
    for r in range(0, PIX, MC):
        d = back_taps(gs_ref, w1_ref, 0, r)
        x = state_ref[r:r+MC, :]
        d = d*silu_slope(x*factor1 + term1)
        keep_ref[r:r+MC, :] = d
        d_sum += fold(d)
        dn_sum += fold(d*(x*inv1 - mean1*inv1))
    shift1_grad, gain1_grad = one(d_sum), one(dn_sum)
    tot = group_totals(rows_of(shift1_grad*gain1, gain1_grad*gain1), member)/amount
    first1, second1 = tot[0:1]*inv1, tot[1:2]*inv1*inv1
    by_keep1, by_term1 = gain1*inv1, second1*mean1 - first1
    for r in range(0, PIX, EL):
        out_ref[r:r+EL, :] = grad_ref[r:r+EL, :] + (keep_ref[r:r+EL, :]*by_keep1 - state_ref[r:r+EL, :]*second1 + by_term1)
    first_out.wait()
    second_out.wait()
    small_ref[...] = jnp.concatenate([one(bias1_grad), one(bias2_grad), gain1_grad, dn*scale, shift1_grad, mod_offset*scale, mod_scale, mod_offset], axis=0)

def block_back(place, grad, state, inner, stat, pieces, base, vectors, large):
    rows = block_rows(place, base)
    return call(functools.partial(block_back_kernel, base, rows), [grad, state, inner, stat, pieces, vectors, large],
        [sds((PIX, CH)), sds(large.shape, narrow), sds((8, CH))],
        [pltpu.VMEM((PIX+2*SIDE, 3*CH), narrow), pltpu.VMEM((CH, PIX), narrow),
         pltpu.VMEM((PIX, CH), f32), pltpu.VMEM((2*TAPS//TILE, TILE, CH), narrow),
         pltpu.SemaphoreType.DMA((2,))]+rows[0].scratch()+rows[1].scratch(), 2*4*PIX*TAPS*CH, away=(4, 6), away_out=(1,), alias={6: 1}, room=39)

PHASES = [(0, 0), (0, 1), (1, 0), (1, 1)]
OFFSETS = [(dy, dx) for dy in (-1, 0, 1) for dx in (-1, 0, 1)]

def source(a, b, dy, dx):
    return 2*((a+dy) % 2) + (b+dx) % 2, (a+dy)//2, (b+dx)//2

def shift_lanes(v, di, dj):
    if di == 0 and dj == 0:
        return v
    moved = pltpu.roll(v, (-(SIDE*di+dj)) % PIX, 1)
    p = lax.broadcasted_iota(jnp.int32, v.shape, 1)
    i, j = p // SIDE + di, p % SIDE + dj
    return jnp.where((i >= 0) & (i < SIDE) & (j >= 0) & (j < SIDE), moved, 0.0)

def stack(phases, a, b, sign):
    rows = []
    for dy, dx in OFFSETS:
        at, di, dj = source(a, b, sign*dy, sign*dx)
        rows.append(shift_lanes(phases[at], di, dj))
    rows.append(jnp.zeros((128-72, PIX), f32))
    return jnp.concatenate(rows, axis=0)

DOWN_FIRST = (ROW["down_w"]+LEAD)//TILE
DOWN_TILES = -(-(ROW["down_b"]+1+LEAD)//TILE)-DOWN_FIRST

def stem_down_kernel(source_rows, noisy_ref, sw_ref, sb_ref, pieces_ref, skip_ref, state_ref, dw_ref, pad_ref, xs_ref, wide_ref, *held):
    source_rows.start(pieces_ref, *held)
    phases = [noisy_ref[i] for i in range(4)]
    col = pixel_column(EL, C0)
    xs_ref[:, 0:SIDE, :] = jnp.zeros((6, SIDE, C0), narrow)
    for a, b in PHASES:
        rows = jnp.transpose(stack(phases, a, b, 1)).astype(narrow)
        v = (dot(rows, sw_ref[...]) + sb_ref[...]).astype(narrow)
        skip_ref[2*a+b] = v
        if b == 0:
            xs_ref[3*a+1, SIDE:SIDE+PIX, :] = v
        else:
            xs_ref[3*a+2, SIDE:SIDE+PIX, :] = v
            pad_ref[8:8+PIX, :] = v.astype(f32)
            for r in range(0, PIX, EL):
                xs_ref[3*a, SIDE+r:SIDE+r+EL, :] = jnp.where(col == 0, 0.0, pad_ref[r+7:r+7+EL, :]).astype(narrow)
    source_rows.finish(pieces_ref, *held)
    wide_ref[...] = held[0][...].astype(f32)
    at = ROW["down_w"]+LEAD-DOWN_FIRST*TILE
    dw_ref[...] = wide_ref[at:at+9*C0, :].astype(narrow)
    acc = None
    for t, (dy, dx) in enumerate(OFFSETS):
        top = 0 if dy == -1 else SIDE
        part = dot(xs_ref[3*(dy % 2)+dx+1, top:top+PIX, :], dw_ref[t*C0:(t+1)*C0, :])
        acc = part if acc is None else acc+part
    state_ref[...] = acc + wide_ref[at+9*C0:at+9*C0+1, :]

def stem_down(place, noisy, stem_w, stem_b, pieces):
    rows = Rows(place, DOWN_FIRST, DOWN_TILES)
    return call(functools.partial(stem_down_kernel, rows), [noisy, stem_w, stem_b, pieces],
        [sds((4, PIX, C0), narrow), sds((PIX, CH)), sds((9*C0, CH), narrow)],
        [pltpu.VMEM((PIX+16, C0), f32), pltpu.VMEM((6, PIX+SIDE, C0), narrow), pltpu.VMEM((DOWN_TILES*TILE, CH), f32)]+rows.scratch(),
        2*PIX*9*C0*CH, away=(3,), room=39)

def down_stem_back_kernel(n, me_ref, grad_ref, skip_ref, more_ref, dw_ref, noisy_ref, head_ref, attn_ref, s1_ref, s0_ref,
                          large_in_ref, large_ref, small_ref,
                          pad_ref, gs_ref, ddw_ref, low_ref, sems):
    top_row = ROW["down_w"]+LEAD
    spare = top_row % TILE
    ddw_ref[0:TILE, :] = jnp.zeros((TILE, CH), f32)
    ddw_ref[9*C0:9*C0+TILE, :] = jnp.zeros((TILE, CH), f32)
    z = jnp.zeros((8, CH), f32)
    gs_ref[:, PIX:PIX+SIDE, :] = jnp.zeros((2, SIDE, CH), narrow)
    col = pixel_column(EL, CH)
    total = z
    pad_ref[PIX:PIX+16, :] = jnp.zeros((16, CH), f32)
    for r in range(0, PIX, EL):
        g = grad_ref[r:r+EL, :].astype(narrow)
        gs_ref[0, r:r+EL, :] = g
        g = g.astype(f32)
        pad_ref[r:r+EL, :] = g
        total += fold(g)
    for r in range(0, PIX, EL):
        gs_ref[1, r:r+EL, :] = jnp.where(col == SIDE-1, 0.0, pad_ref[r+1:r+1+EL, :]).astype(narrow)
    down_bias = jnp.sum(total, axis=0, keepdims=True)
    def shifted(dy, dx):
        top = SIDE if dy == -1 else 0
        return gs_ref[1 if dx == -1 else 0, top:top+PIX, :]
    phases = [noisy_ref[i] for i in range(4)]
    stem_grad, stem_bias = None, None
    for a, b in PHASES:
        turned = jnp.transpose(skip_ref[2*a+b].astype(f32)).astype(narrow)
        more = more_ref[2*a+b]
        for t, (dy, dx) in enumerate(OFFSETS):
            if (dy % 2, dx % 2) == (a, b):
                g = shifted(dy, dx)
                ddw_ref[spare+t*C0:spare+(t+1)*C0, :] = dot(turned, g)
                more += dot_nt(g, dw_ref[t*C0:(t+1)*C0, :])
        low = more.astype(narrow)
        part = dot(stack(phases, a, b, 1).astype(narrow), low)
        stem_grad = part if stem_grad is None else stem_grad+part
        part = fold(low.astype(f32))
        stem_bias = part if stem_bias is None else stem_bias+part
    for r in range(0, 9*C0+TILE, 16*TILE):
        end = min(r+16*TILE, 9*C0+TILE)
        low_ref[r//TILE:end//TILE] = ddw_ref[r:end, :].astype(narrow).reshape((end-r)//TILE, TILE, CH)
    copy = pltpu.make_async_copy(low_ref, large_ref.at[top_row//TILE:top_row//TILE+9*C0//TILE+1], sems.at[0])
    copy.start()
    copy.wait()
    small_ref[SMALL_STEM:SMALL_STEM+40, :] = jnp.concatenate(
        [stem_grad[0:40, :], jnp.concatenate([stem_grad[40:72, :], jnp.zeros((8, C0), f32)], axis=0)], axis=1)
    stem_bias = jnp.sum(stem_bias, axis=0, keepdims=True)
    small_ref[SMALL_HEAD:SMALL_HEAD+120, :] = head_ref[...]
    small_ref[SMALL_ATTN:SMALL_ATTN+8, :] = attn_ref[...]
    small_ref[SMALL_S1:SMALL_S1+8, :] = s1_ref[...]
    small_ref[SMALL_S0:SMALL_S0+8, :] = s0_ref[...]
    mine = lax.broadcasted_iota(jnp.int32, (n, CH), 0) == me_ref[0]
    for b, from_ref in enumerate((s0_ref, s1_ref)):
        for h in range(2):
            at = SMALL_MOVED+(2*b+h)*n
            small_ref[at:at+n, :] = jnp.where(mine, from_ref[6+h:7+h, :], 0.0)
    small_ref[SMALL_STEM+40:SMALL_STEM+48, :] = rows_of(down_bias, jnp.concatenate([stem_bias, jnp.zeros((1, C0), f32)], axis=1))

def down_stem_back(me, n, grad, skip, more, down_w, noisy, head_tail, attn_small, s1, s0, large):
    return call(functools.partial(down_stem_back_kernel, n),
        [me.reshape(1), grad, skip, more, down_w, noisy, head_tail, attn_small, s1, s0, large],
        [sds(large.shape, narrow), sds((SMALL_MOVED+4*n, CH))],
        [pltpu.VMEM((PIX+16, CH), f32), pltpu.VMEM((2, PIX+SIDE, CH), narrow), pltpu.VMEM((9*C0+TILE, CH), f32),
         pltpu.VMEM((9*C0//TILE+1, TILE, CH), narrow), pltpu.SemaphoreType.DMA((1,))],
        2*2*PIX*9*C0*CH, away=(10,), away_out=(0,), alias={10: 0}, scalar=(0,), room=39)

HEAD_PER = (C0+CH)//GROUPS
def silu_slope(v):
    s = sigmoid(v)
    return s*(1.0+v*(1.0-s))

KL = 0.001
HEAD_FIRST = (ROW["head_gain"]+LEAD)//TILE
HEAD_TILES = -(-(ROW["head_b"]+1+LEAD)//TILE)-HEAD_FIRST
HEAD_AT = ROW["head_gain"]+LEAD-HEAD_FIRST*TILE

def head_weights(low, wu_ref, ws_ref):
    count = HEAD_TILES*TILE
    blocks = []
    for o in range(OUT_CH):
        lane = lax.broadcasted_iota(jnp.int32, (64, CH), 1)
        take = (lane == 6*lax.broadcasted_iota(jnp.int32, (64, CH), 0)+o).astype(f32).astype(narrow)
        blocks.append(dot_nt(low, take).astype(narrow))
    blocks = jnp.concatenate(blocks, axis=0)
    row = lax.broadcasted_iota(jnp.int32, (128, OUT_CH*count), 0)
    column = lax.broadcasted_iota(jnp.int32, (128, OUT_CH*count), 1)
    valid = (row % 8 < OUT_CH) & (row < 72)
    made = []
    for part in range(9):
        put = valid & (column == (row % 8)*count+HEAD_AT+3+9*(row//8)+part)
        made.append(dot(put.astype(f32).astype(narrow), blocks))
    wu_ref[...] = jnp.concatenate(made[:6], axis=1).astype(narrow)
    ws_ref[...] = jnp.concatenate(made[6:], axis=1).astype(narrow)

def head_kernel(rows, num_ref, state_ref, skip_ref, pieces_ref, noise_ref, mask_ref,
                state_grad_ref, skip_grad_ref, tail_ref, loss_ref,
                up_ref, side_ref, q_ref, wu_ref, ws_ref, *held):
    rows.start(pieces_ref, *held)
    rows.finish(pieces_ref, *held)
    log_beta, log_tilde, coefficient, sample = (num_ref[i] for i in range(4))
    low = held[0][...]
    head_weights(low, wu_ref, ws_ref)
    wide = low.astype(f32)
    line = lambda i: wide[HEAD_AT+i:HEAD_AT+i+1, :]
    gain_u, gain_s = line(0), line(1)[:, :C0]
    shift_u, shift_s = jnp.concatenate([line(1)[:, C0:], line(2)[:, :C0]], axis=1), line(2)[:, C0:]
    own = lax.broadcasted_iota(jnp.int32, (8, CH), 0)
    own = (own == lax.broadcasted_iota(jnp.int32, (8, CH), 1)) & (own < OUT_CH)
    bias = jnp.sum(jnp.where(own, jnp.broadcast_to(line(ROW["head_b"]-ROW["head_gain"]), (8, CH)), 0.0), axis=1, keepdims=True)
    mu, ms = membership(CH, HEAD_PER), membership(C0, HEAD_PER, CH)
    amount = 4*PIX*HEAD_PER
    one = lambda v: jnp.sum(v, axis=0, keepdims=True)
    zu, zs = jnp.zeros((8, CH), f32), jnp.zeros((8, C0), f32)
    def sums_u(i, c):
        v = state_ref[pl.ds(i*EL, EL), :]
        return c[0]+fold(v), c[1]+fold(v*v)
    u1, u2 = steps(PIX//EL, sums_u, (zu, zu))
    s1, s2 = zs, zs
    for k in range(4):
        def sums_s(i, c):
            v = skip_ref[k, pl.ds(i*EL, EL), :].astype(f32)
            return c[0]+fold(v), c[1]+fold(v*v)
        s1, s2 = steps(PIX//EL, sums_s, (s1, s2))
    tot = (exact(rows_of(4.0*one(u1), 4.0*one(u2)), mu) + exact(rows_of(one(s1), one(s2)), ms))/amount
    tot_u, tot_s = exact_nt(tot, mu), exact_nt(tot, ms)
    mean_u, inv_u = tot_u[0:1], lax.rsqrt(tot_u[1:2]-tot_u[0:1]*tot_u[0:1]+1e-05)
    mean_s, inv_s = tot_s[0:1], lax.rsqrt(tot_s[1:2]-tot_s[0:1]*tot_s[0:1]+1e-05)
    factor_u, term_u = inv_u*gain_u, shift_u-mean_u*inv_u*gain_u
    factor_s, term_s = inv_s*gain_s, shift_s-mean_s*inv_s*gain_s
    def act_u(i, _):
        r = pl.ds(i*EL, EL)
        v = state_ref[r, :]*factor_u+term_u
        up_ref[r, :] = (v*sigmoid(v)).astype(narrow)
        return _
    steps(PIX//EL, act_u, 0)
    for k in range(4):
        def act_s(i, _):
            r = pl.ds(i*EL, EL)
            v = skip_ref[k, r, :].astype(f32)*factor_s+term_s
            side_ref[k, r, :] = (v*sigmoid(v)).astype(narrow)
            return _
        steps(PIX//EL, act_s, 0)
    from_up = dot_nt(wu_ref[...], up_ref[...])
    for k in range(4):
        q_ref[k] = from_up + dot_nt(ws_ref[...], side_ref[k])
    row = lax.broadcasted_iota(jnp.int32, (8, PIX), 0)
    loss, vlb, outs, bias_grad = jnp.zeros((1, PIX), f32), jnp.zeros((1, PIX), f32), [], jnp.zeros((8, PIX), f32)
    for a, b in PHASES:
        out = jnp.zeros((8, PIX), f32)
        for t, (dy, dx) in enumerate(OFFSETS):
            at, di, dj = source(a, b, dy, dx)
            out += shift_lanes(q_ref[at, 8*t:8*t+8, :], di, dj)
        out += bias
        k = 2*a+b
        error = jnp.where(row < 3, out - noise_ref[k], 0.0)
        fraction = jnp.where(row < 3, (pltpu.roll(out, 5, 0)+1.0)/2.0, 0.0)
        log_var = fraction*log_beta + (1.0-fraction)*log_tilde
        inverse = jnp.exp(-log_var)
        ratio = jnp.exp(log_tilde-log_var)
        divergence = 0.5*(-1.0+log_var-log_tilde+ratio+coefficient*error*error*inverse)
        divergence = jnp.where(row < 3, divergence, 0.0)
        weight = sample*mask_ref[k]
        loss += weight*jnp.sum(error*error+KL*divergence, axis=0, keepdims=True)
        vlb += weight*KL*jnp.sum(divergence, axis=0, keepdims=True)
        predict = weight*(2.0*error+KL*coefficient*error*inverse)
        var_grad = weight*KL*0.5*(1.0-ratio-coefficient*error*error*inverse)*(log_beta-log_tilde)/2.0
        og = jnp.where(row < 3, predict, jnp.where(row < 6, pltpu.roll(var_grad, 3, 0), 0.0))
        og = og.astype(narrow).astype(f32)
        bias_grad += og
        outs.append(og)
    bias_grad = jnp.broadcast_to(jnp.sum(bias_grad, axis=1, keepdims=True), (8, CH))
    diagonal = lax.broadcasted_iota(jnp.int32, (8, CH), 0) == lax.broadcasted_iota(jnp.int32, (8, CH), 1)
    bias_grad = jnp.sum(jnp.where(diagonal, bias_grad, 0.0), axis=0, keepdims=True)
    loss_ref[...] = jnp.concatenate([jnp.broadcast_to(jnp.sum(loss, axis=1, keepdims=True), (1, 128)),
        jnp.broadcast_to(jnp.sum(vlb, axis=1, keepdims=True), (1, 128)), jnp.zeros((6, 128), f32)], axis=0)
    nine_sum, gs_total = None, None
    d1, d2 = zs, zs
    for a, b in PHASES:
        k = 2*a+b
        nine = stack(outs, a, b, -1)
        nine_sum = nine if nine_sum is None else nine_sum+nine
        part = dot(nine.astype(narrow), side_ref[k])
        gs_total = part if gs_total is None else gs_total+part
        d = dot(jnp.transpose(nine).astype(narrow), ws_ref[...])
        x = skip_ref[k].astype(f32)
        n = x*inv_s-mean_s*inv_s
        d = d*silu_slope(x*factor_s+term_s)
        skip_grad_ref[k] = d
        d1, d2 = d1+fold(d), d2+fold(d*n)
    tail_ref[72:112, :] = jnp.concatenate(
        [gs_total[0:40, :], jnp.concatenate([gs_total[40:72, :], jnp.zeros((8, C0), f32)], axis=0)], axis=1)
    hi = nine_sum.astype(narrow); lo = (nine_sum-hi.astype(f32)).astype(narrow)
    tail_ref[0:72, :] = (dot(hi, up_ref[...])+dot(lo, up_ref[...]))[0:72, :]
    turned = jnp.transpose(nine_sum)
    hi = turned.astype(narrow); lo = (turned-hi.astype(f32)).astype(narrow)
    d = dot(hi, wu_ref[...])+dot(lo, wu_ref[...])
    n = (state_ref[...]-mean_u)*inv_u
    d = d*silu_slope(n*gain_u+shift_u)
    state_grad_ref[...] = d
    e1, e2 = one(fold(d)), one(fold(d*n))
    d1, d2 = one(d1), one(d2)
    tail_ref[112:120, :] = rows_of(e2, e1, jnp.concatenate([d2, d1], axis=1), bias_grad)
    tot = (exact(rows_of(e1*gain_u, e2*gain_u), mu)+exact(rows_of(d1*gain_s, d2*gain_s), ms))/amount
    tot_u, tot_s = exact_nt(tot, mu), exact_nt(tot, ms)
    second_u, second_s = 4.0*tot_u[1:2]*inv_u*inv_u, tot_s[1:2]*inv_s*inv_s
    by_term_u, by_term_s = second_u*mean_u-4.0*tot_u[0:1]*inv_u, second_s*mean_s-tot_s[0:1]*inv_s
    def back_u(i, _):
        r = pl.ds(i*EL, EL)
        state_grad_ref[r, :] = state_grad_ref[r, :]*factor_u-state_ref[r, :]*second_u+by_term_u
        return _
    steps(PIX//EL, back_u, 0)
    for k in range(4):
        def back_s(i, _):
            r = pl.ds(i*EL, EL)
            skip_grad_ref[k, r, :] = skip_grad_ref[k, r, :]*factor_s-skip_ref[k, r, :].astype(f32)*second_s+by_term_s
            return _
        steps(PIX//EL, back_s, 0)

def head(place, numbers, state, skip, pieces, noise, mask):
    rows = Rows(place, HEAD_FIRST, HEAD_TILES)
    spec = pl.BlockSpec(memory_space=VM)
    ins = [numbers, state, skip, pieces, noise, mask]
    outs = [sds((PIX, CH)), sds((4, PIX, C0)), sds((120, CH)), sds((8, 128))]
    return pl.pallas_call(functools.partial(head_kernel, rows), out_shape=outs,
        in_specs=[pl.BlockSpec(memory_space=pltpu.SMEM), spec, spec, pl.BlockSpec(memory_space=pl.ANY), spec, spec], out_specs=[spec]*len(outs),
        scratch_shapes=[pltpu.VMEM((PIX, CH), narrow), pltpu.VMEM((4, PIX, C0), narrow), pltpu.VMEM((4, 128, PIX), f32),
                        pltpu.VMEM((128, CH), narrow), pltpu.VMEM((128, C0), narrow)]+rows.scratch(),
        compiler_params=pltpu.CompilerParams(vmem_limit_bytes=39*MIB),
        cost_estimate=pl.CostEstimate(flops=4*2*PIX*128*(4*C0+CH), bytes_accessed=12*2**20, transcendentals=0))(*ins)

HP = 128
QW = HEADS*HP
SCALE = 1.0/math.sqrt(HEAD_DIM)
POWER = SCALE*math.log2(math.e)
QC = 256
ATTN_FIRST = (ROW["attn_gain"]+LEAD)//TILE
ATTN_TILES = -(-(ROW["proj_b"]+LEAD+1)//TILE)-ATTN_FIRST
ATTN = {name: ROW[name]+LEAD-ATTN_FIRST*TILE for name in ("attn_gain", "attn_shift", "qkv_w", "qv_b", "proj_w", "proj_b")}

def get_rows(ref, at):
    return jnp.concatenate([ref[i, at, :] for i in range(3)], axis=1)

def put_rows(ref, at, value):
    for i in range(3):
        ref[i, at, :] = value[:, i*128:(i+1)*128]

def attention_forward_kernel(rows, state_ref, pieces_ref, out_ref, qkv_ref, log_ref, mixed_t_ref, stat_ref, wp_ref, wo_ref, vec_ref,
                             mixed_ref, vt_ref, bp_ref, wide_ref, rows_ref, edge_ref, sems):
    rows.start(pieces_ref, rows_ref, edge_ref, sems)
    rows.finish(pieces_ref, rows_ref, edge_ref, sems)
    for r in range(0, ATTN_TILES*TILE, 16*TILE):
        end = min(r+16*TILE, ATTN_TILES*TILE)
        put_rows(wide_ref, slice(r, end), rows_ref[r:end, :].astype(f32))
    one_row = lambda name, i=0: get_rows(wide_ref, slice(ATTN[name]+i, ATTN[name]+i+1))
    gain, shift, bias = one_row("attn_gain"), one_row("attn_shift"), one_row("proj_b")
    vec_ref[...] = rows_of(gain, shift)
    nothing = jnp.zeros((CH, HP-HEAD_DIM), f32)
    for j in range(3):
        third = get_rows(wide_ref, pl.ds(ATTN["qkv_w"]+j, CH, stride=3))
        third_bias = one_row("qv_b", j//2) if j != 1 else jnp.zeros((1, CH), f32)
        for h in range(HEADS):
            to = slice(j*QW+h*HP, j*QW+(h+1)*HP)
            wp_ref[:, to] = jnp.concatenate([third[:, h*HEAD_DIM:(h+1)*HEAD_DIM], nothing], axis=1).astype(narrow)
            bp_ref[:, to] = jnp.concatenate([third_bias[:, h*HEAD_DIM:(h+1)*HEAD_DIM], nothing[0:1]], axis=1)
    for h in range(HEADS):
        at = ATTN["proj_w"]+h*HEAD_DIM
        wo_ref[h*HP:h*HP+HEAD_DIM, :] = get_rows(wide_ref, slice(at, at+HEAD_DIM)).astype(narrow)
        wo_ref[h*HP+HEAD_DIM:(h+1)*HP, :] = jnp.zeros((HP-HEAD_DIM, CH), narrow)
    member = membership(CH, CH//GROUPS)
    def sums(i, c):
        v = state_ref[pl.ds(i*EL, EL), :]
        return c[0]+fold(v), c[1]+fold(v*v)
    z = jnp.zeros((8, CH), f32)
    mean, inv = norm_stats(*steps(PIX//EL, sums, (z, z)), member, PIX*(CH//GROUPS))
    stat_ref[...] = rows_of(mean, inv)
    factor, term = inv*gain, shift-mean*inv*gain
    def project(i, _):
        r = pl.ds(i*256, 256)
        n = (state_ref[r, :]*factor+term).astype(narrow)
        qkv_ref[r, :] = (dot(n, wp_ref[...])+bp_ref[...]).astype(narrow)
        return _
    steps(PIX//256, project, 0)
    for h in range(HEADS):
        vt_ref[...] = jnp.transpose(qkv_ref[:, 2*QW+h*HP:2*QW+(h+1)*HP].astype(f32)).astype(narrow)
        for c in range(0, PIX, QC):
            s = dot_nt(qkv_ref[:, QW+h*HP:QW+(h+1)*HP], qkv_ref[c:c+QC, h*HP:(h+1)*HP])
            top = jnp.max(s, axis=0, keepdims=True)
            e = jnp.exp2((s-top)*POWER)
            total = jnp.sum(e, axis=0, keepdims=True)
            log_ref[h:h+1, c:c+QC] = top*POWER+jnp.log2(total)
            m = (dot(vt_ref[...], e.astype(narrow))*(1.0/total)).astype(narrow)
            mixed_t_ref[h*HP:(h+1)*HP, c:c+QC] = m
            mixed_ref[c:c+QC, h*HP:(h+1)*HP] = jnp.transpose(m.astype(f32)).astype(narrow)
    log_ref[HEADS:8, :] = jnp.zeros((8-HEADS, PIX), f32)
    def finish(i, _):
        r = pl.ds(i*256, 256)
        out_ref[r, :] = state_ref[r, :]+(dot(mixed_ref[r, :], wo_ref[...])+bias)
        return _
    steps(PIX//256, finish, 0)

def attention_forward(place, state, pieces):
    rows = Rows(place, ATTN_FIRST, ATTN_TILES)
    return call(functools.partial(attention_forward_kernel, rows), [state, pieces],
        [sds((PIX, CH)), sds((PIX, 3*QW), narrow), sds((8, PIX)), sds((QW, PIX), narrow), sds((8, CH)),
         sds((CH, 3*QW), narrow), sds((QW, CH), narrow), sds((8, CH))],
        [pltpu.VMEM((PIX, QW), narrow), pltpu.VMEM((HP, PIX), narrow), pltpu.VMEM((1, 3*QW), f32),
         pltpu.VMEM((3, ATTN_TILES*TILE, 128), f32)]+rows.scratch(),
        2*PIX*(CH*4*QW+2*PIX*QW), away=(1,), room=39)

def attention_back_kernel(grad_ref, state_ref, stat_ref, qkv_ref, log_ref, mixed_t_ref, wp_ref, wo_ref, vec_ref,
                          out_ref, large_ref, small_ref, dm_ref, pg_ref, kt_ref, dv_ref, dk_ref, nt_ref, keep_ref,
                          wide_ref, rows_ref, sems):
    gain, shift = vec_ref[0:1, :], vec_ref[1:2, :]
    mean, inv = stat_ref[0:1, :], stat_ref[1:2, :]
    member = membership(CH, CH//GROUPS)
    z = jnp.zeros((8, CH), f32)
    one = lambda v: jnp.sum(v, axis=0, keepdims=True)
    def start(i, c):
        r = pl.ds(i*256, 256)
        g = grad_ref[r, :].astype(narrow)
        keep_ref[r, :] = g
        dm_ref[r, :] = dot_nt(g, wo_ref[...]).astype(narrow)
        return c+fold(g.astype(f32))
    proj_bias = steps(PIX//256, start, z)
    for name, after in (("attn_gain", ATTN["qkv_w"]), ("qv_b", ATTN["proj_w"]), ("proj_b", ATTN_TILES*TILE)):
        put_rows(wide_ref, slice(ATTN[name], after), jnp.zeros((after-ATTN[name], CH), f32))
    wo_grad = dot(mixed_t_ref[...], keep_ref[...])
    for h in range(HEADS):
        at = ATTN["proj_w"]+h*HEAD_DIM
        put_rows(wide_ref, slice(at, at+HEAD_DIM), wo_grad[h*HP:h*HP+HEAD_DIM, :])
    for h in range(HEADS):
        q0, k0, v0 = h*HP, QW+h*HP, 2*QW+h*HP
        kt_ref[...] = jnp.transpose(qkv_ref[:, k0:k0+HP].astype(f32)).astype(narrow)
        for c in range(0, PIX, QC):
            q, dm = qkv_ref[c:c+QC, q0:q0+HP], dm_ref[c:c+QC, h*HP:(h+1)*HP]
            s = dot_nt(qkv_ref[:, k0:k0+HP], q)
            p = jnp.exp2(s*POWER-log_ref[h:h+1, c:c+QC])
            dp = dot_nt(qkv_ref[:, v0:v0+HP], dm)
            dm_t = dot_nt(wo_ref[h*HP:(h+1)*HP, :], keep_ref[c:c+QC, :]).astype(narrow).astype(f32)
            delta = jnp.sum(dm_t*mixed_t_ref[h*HP:(h+1)*HP, c:c+QC].astype(f32), axis=0, keepdims=True)
            ds = (p*(dp-delta)).astype(narrow)
            dv = dot(p.astype(narrow), dm)
            dk = dot(ds, q)
            if c == 0:
                dv_ref[...] = dv
                dk_ref[...] = dk
            else:
                dv_ref[...] += dv
                dk_ref[...] += dk
            dq = dot(kt_ref[...], ds)
            pg_ref[c:c+QC, q0:q0+HP] = jnp.transpose(dq*SCALE).astype(narrow)
        pg_ref[:, k0:k0+HP] = (dk_ref[...]*SCALE).astype(narrow)
        pg_ref[:, v0:v0+HP] = dv_ref[...].astype(narrow)
    factor, term = inv*gain, shift-mean*inv*gain
    for r in range(0, PIX, 256):
        nt_ref[:, r:r+256] = jnp.transpose(state_ref[r:r+256, :]*factor+term).astype(narrow)
    for j in range(3):
        third = dot(nt_ref[...], pg_ref[:, j*QW:(j+1)*QW])
        third = jnp.concatenate([third[:, h*HP:h*HP+HEAD_DIM] for h in range(HEADS)], axis=1)
        put_rows(wide_ref, pl.ds(ATTN["qkv_w"]+j, CH, stride=3), third)
    for r in range(0, ATTN_TILES, 16):
        end = min(r+16, ATTN_TILES)
        rows_ref[r:end] = get_rows(wide_ref, slice(r*TILE, end*TILE)).astype(narrow).reshape(end-r, TILE, CH)
    copy = pltpu.make_async_copy(rows_ref, large_ref.at[ATTN_FIRST:ATTN_FIRST+ATTN_TILES], sems.at[0])
    copy.start()
    zb = jnp.zeros((8, 3*QW), f32)
    def norm_grad(i, c):
        r = pl.ds(i*256, 256)
        d = dot_nt(pg_ref[r, :], wp_ref[...])
        n = state_ref[r, :]*inv-mean*inv
        out_ref[r, :] = d
        return c[0]+fold(d), c[1]+fold(d*n), c[2]+fold(pg_ref[r, :].astype(f32))
    shift_grad, gain_grad, bias_grad = (one(v) for v in steps(PIX//256, norm_grad, (z, z, zb)))
    compact = [jnp.concatenate([bias_grad[:, j*QW+h*HP:j*QW+h*HP+HEAD_DIM] for h in range(HEADS)], axis=1) for j in (0, 2)]
    tot = group_totals(rows_of(shift_grad*gain, gain_grad*gain), member)/(PIX*(CH//GROUPS))
    second = tot[1:2]*inv*inv
    by_term = second*mean-tot[0:1]*inv
    def finish(i, _):
        r = pl.ds(i*EL, EL)
        out_ref[r, :] = grad_ref[r, :]+(out_ref[r, :]*factor-state_ref[r, :]*second+by_term)
        return _
    steps(PIX//EL, finish, 0)
    small_ref[...] = rows_of(gain_grad, shift_grad, compact[0], compact[1], one(proj_bias))
    copy.wait()

def attention_back(grad, state, stat, qkv, log, mixed_t, wp, wo, vec, tiles):
    return call(attention_back_kernel, [grad, state, stat, qkv, log, mixed_t, wp, wo, vec],
        [sds((PIX, CH)), sds((tiles, TILE, CH), narrow), sds((8, CH))],
        [pltpu.VMEM((PIX, QW), narrow), pltpu.VMEM((PIX, 3*QW), narrow), pltpu.VMEM((HP, PIX), narrow), pltpu.VMEM((PIX, HP), f32),
         pltpu.VMEM((PIX, HP), f32), pltpu.VMEM((CH, PIX), narrow), pltpu.VMEM((PIX, CH), narrow),
         pltpu.VMEM((3, ATTN_TILES*TILE, 128), f32), pltpu.VMEM((ATTN_TILES, TILE, CH), narrow), pltpu.SemaphoreType.DMA((1,))],
        2*PIX*(CH*8*QW+5*PIX*QW), away_out=(1,), room=39)


def to_phases(v):
    c = v.shape[0]
    return jnp.transpose(v.reshape(c, SIDE, 2, SIDE, 2), (2, 4, 0, 1, 3)).reshape(4, c, PIX)


def pad_rows8(v):
    return jnp.pad(v, ((0, 0), (0, 8-v.shape[1]), (0, 0)))


def taps_rows(v):
    v = jnp.pad(v, ((0, 0), (0, 8-v.shape[1]), (0, 0))).reshape(72, v.shape[2])
    return jnp.pad(v, ((0, 128-72), (0, 0)))


class Place:
    def __init__(self, sizes, share):
        self.sizes = sizes
        self.share = share
        self.total = sizes["y"]*sizes["c"]*sizes["z"]*sizes["x"]
        firsts = [(share*d+LEAD)//TILE for d in range(self.total)]
        lasts = [-(-(share*(d+1)+LEAD)//TILE) for d in range(self.total)]
        self.block = max(last-first for first, last in zip(firsts, lasts))
        self.tiles = max(first+self.block for first in firsts)
        self.tiles = -(-self.tiles//TILE)*TILE
        self.at = {axis: lax.axis_index(axis) for axis in sizes}

    def device(self, y, c, z, x):
        s = self.sizes
        return ((y*s["c"]+c)*s["z"]+z)*s["x"]+x

    def first(self, device):
        return (self.share*device+LEAD)//TILE

    def me(self):
        a = self.at
        return self.device(a["y"], a["c"], a["z"], a["x"])


def turn(value, axis, size, distance):
    return lax.ppermute(value, axis, [(i, (i+distance) % size) for i in range(size)])


def hold_for(value, others):
    return lax.optimization_barrier((value, others))[0]


def add_everywhere(value, place):
    return add_over(value, place, ("c", "x", "y", "z"))


def add_over(value, place, axes):
    for axis in axes:
        size, step = place.sizes[axis], 1
        while step < size:
            value = value+lax.ppermute(value, axis, [(i, i ^ step) for i in range(size)])
            step *= 2
    return value


def cut_kernel(count, size, starts_ref, large_ref, out_ref, sems):
    copies = [pltpu.make_async_copy(large_ref.at[pl.ds(starts_ref[i], size)], out_ref.at[i], sems.at[i]) for i in range(count)]
    for copy in copies:
        copy.start()
    for copy in copies:
        copy.wait()


def cut(large, starts, size):
    count = starts.shape[0]
    return pl.pallas_call(
        functools.partial(cut_kernel, count, size),
        out_shape=sds((count, size, TILE, WIDE), narrow),
        in_specs=[pl.BlockSpec(memory_space=pltpu.SMEM), pl.BlockSpec(memory_space=pl.ANY)],
        out_specs=pl.BlockSpec(memory_space=VM),
        scratch_shapes=[pltpu.SemaphoreType.DMA((count,))],
        compiler_params=pltpu.CompilerParams(vmem_limit_bytes=39*MIB),
        cost_estimate=pl.CostEstimate(flops=0, bytes_accessed=1024, transcendentals=0),
    )(starts, large)


def merge_kernel(coords, sends, count, size, starts_ref, large_ref, arrived_ref, *refs):
    outs, (held_ref, sems) = refs[:-2], refs[-2:]
    copies = [pltpu.make_async_copy(large_ref.at[pl.ds(starts_ref[i], size)], held_ref.at[i], sems.at[i]) for i in range(count)]
    for copy in copies:
        copy.start()
    for i in range(count):
        copies[i].wait()
        which, at = sends[i]
        outs[which][at] = (held_ref[i].astype(f32)+arrived_ref[i].astype(f32)).astype(outs[which].dtype)


def share_out(large, small, place, parts):
    s, a, block = place.sizes, place.at, place.block
    half = (s["z"]+1)//2
    coords = [(y, z, x) for y in range(s["y"]) for z in range(s["z"]) for x in range(s["x"])]

    def starts(core):
        return jnp.stack([
            place.first(place.device((a["y"]+y) % s["y"], core, (a["z"]+z) % s["z"], (a["x"]+x) % s["x"])) for y, z, x in coords
        ]).astype(jnp.int32)

    far_starts, own_starts = starts(1-a["c"]), starts(a["c"])
    bounds = [block*i//parts for i in range(parts+1)]
    groups = [("y", [(0, z, x) for z in range(half) for x in range(s["x"])])]
    groups += [("y%d" % k, [(k, z, x) for z in range(half) for x in range(s["x"])]) for k in range(1, s["y"])]
    groups += [("x", [(y, z, 0) for z in range(half, s["z"]) for y in range(s["y"])])]
    groups += [("x%d" % k, [(y, z, k) for z in range(half, s["z"]) for y in range(s["y"])]) for k in range(1, s["x"])]
    names = [name for name, members in groups]
    sends = [None]*len(coords)
    for g, (name, members) in enumerate(groups):
        for at, member in enumerate(members):
            sends[coords.index(member)] = (g, at)
    length = small.shape[0]//2
    half_small, other_small = (lax.dynamic_slice_in_dim(small, core*length, length) for core in (a["c"], 1-a["c"]))
    half_small = half_small+turn(other_small, "c", 2, 1)
    far_starts = hold_for(far_starts, half_small)
    arrived, merged = [], []
    for part in range(parts):
        sent = cut(large, far_starts+bounds[part], bounds[part+1]-bounds[part])
        arrived.append(turn(sent, "c", 2, 1))
        far_starts = hold_for(far_starts, sent)
    for part in range(parts):
        size = bounds[part+1]-bounds[part]
        outs = [sds((len(members), size, TILE, WIDE), f32 if name in ("y", "x") else narrow) for name, members in groups]
        out = pl.pallas_call(
            functools.partial(merge_kernel, coords, sends, len(coords), size),
            out_shape=outs,
            in_specs=[pl.BlockSpec(memory_space=pltpu.SMEM), pl.BlockSpec(memory_space=pl.ANY), pl.BlockSpec(memory_space=VM)],
            out_specs=[pl.BlockSpec(memory_space=VM)]*len(outs),
            scratch_shapes=[pltpu.VMEM((len(coords), size, TILE, WIDE), narrow), pltpu.SemaphoreType.DMA((len(coords),))],
            compiler_params=pltpu.CompilerParams(vmem_limit_bytes=39*MIB),
            cost_estimate=pl.CostEstimate(flops=0, bytes_accessed=1024, transcendentals=0),
        )(own_starts+bounds[part], large, arrived[part])
        own_starts = hold_for(own_starts, out)
        merged.append(dict(zip(names, out)))

    def first_stage(sums):
        return ([turn(sums["y%d" % k], "y", s["y"], k) for k in range(1, s["y"])],
                [turn(sums["x%d" % k], "x", s["x"], k) for k in range(1, s["x"])])

    def first_sums(sums, came):
        near = sums["y"]+sum(value.astype(f32) for value in came[0])
        far = sums["x"]+sum(value.astype(f32) for value in came[1])
        return near.reshape((half, s["x"])+near.shape[1:]), far.reshape((s["z"]-half, s["y"])+far.shape[1:])

    def second_sums(near, far):
        near = near[:, 0]+sum(turn(near[:, k].astype(narrow), "x", s["x"], k).astype(f32) for k in range(1, s["x"]))
        far = far[:, 0]+sum(turn(far[:, k].astype(narrow), "y", s["y"], k).astype(f32) for k in range(1, s["y"]))
        return near, far

    def third_sum(near, far):
        total = near[0]
        for z in range(1, s["z"]):
            value = near[z] if z < half else far[z-half]
            total = total+turn(value.astype(narrow), "z", s["z"], z).astype(f32)
        return total

    waiting = [first_stage(merged[part]) for part in range(min(2, parts))]
    results, ready = [], None
    for part in range(parts):
        if part == 0:
            waiting[0] = hold_for(waiting[0], merged[-1])
        near, far = first_sums(merged[part], waiting[part])
        if part == 0:
            half_small = add_over(hold_for(half_small, merged[-1]), place, ("z",))
        if part == parts-1:
            half_small = add_over(hold_for(half_small, (near, far)), place, ("x", "y"))
        if part+2 < parts:
            waiting.append(first_stage(hold_for(merged[part+2], (near, far))))
        if 0 < part < parts-1:
            near, far = hold_for((near, far), waiting[part+1])
        results.append(third_sum(*second_sums(near, far)))
    other_small = turn(half_small, "c", 2, 1)
    first = a["c"] == 0
    small = jnp.concatenate([jnp.where(first, half_small, other_small), jnp.where(first, other_small, half_small)])
    return jnp.concatenate(results, axis=0), small


SPOTS = (
    list(range(14))
    + [ROW["time1_b"], ROW["time1_b"]+1, ROW["time2_b"], ROW["time2_b"]+1, ROW["down_b"]]
    + [ROW["res_b"]+i for i in range(4)]
    + [ROW["emb_b"]+i for i in range(4)]
    + [ROW["res_gain"]+i for i in range(4)]
    + [ROW["res_shift"]+i for i in range(4)]
    + [ROW["attn_gain"], ROW["attn_shift"], ROW["qv_b"], ROW["qv_b"]+1, ROW["proj_b"]]
    + [ROW["head_gain"]+i for i in range(3)] + [ROW["head_b"]] + [-1]*4
    + [ROW["head_gain"]+3+9*tap+part if tap < 9 else -1 for part in range(9) for tap in range(16)]
)
SPOTS += [-1]*(256-len(SPOTS))

TIME_FIRST = (ROW["time1_w"]+LEAD)//TILE
TIME_TILES = -(-(ROW["time2_b"]+2+LEAD)//TILE)-TIME_FIRST
EMB_FIRST = (ROW["res_b"]+LEAD)//TILE
EMB_TILES = -(-(ROW["res_shift"]+4+LEAD)//TILE)-EMB_FIRST


def widen_rows(low_ref, wide_ref, count):
    for r in range(0, count, 16*TILE):
        end = min(r+16*TILE, count)
        put_rows(wide_ref, slice(r, end), low_ref[r:end, :].astype(f32))


def time_kernel(n, rows, me_ref, sinus_ref, pieces_ref, hidden_pre_ref, hidden_ref, outer_pre_ref, embed_ref, vec_ref, w2_ref, we_ref,
                time_ref, emb_ref, *held):
    one, two = (pieces_ref,)+held[:3], (pieces_ref,)+held[3:]
    rows[0].start(*one)
    rows[1].start(*two)
    rows[0].finish(*one)
    time_low_ref, emb_low_ref = held[0], held[3]
    widen_rows(time_low_ref, time_ref, TIME_TILES*TILE)

    def in_time(name, i=0):
        return ROW[name]+LEAD-TIME_FIRST*TILE+i

    def in_emb(name, i=0):
        return ROW[name]+LEAD-EMB_FIRST*TILE+i

    def row(ref, at):
        return get_rows(ref, slice(at, at+1))

    for h in range(2):
        w1 = get_rows(time_ref, pl.ds(in_time("time1_w", h), C0, stride=2)).astype(narrow)
        hidden_pre_ref[:, h*CH:(h+1)*CH] = dot(sinus_ref[...], w1)+row(time_ref, in_time("time1_b", h))
        w2_ref[h] = get_rows(time_ref, pl.ds(in_time("time2_w", h), TEMB, stride=2)).astype(narrow)
    v = hidden_pre_ref[...]
    hidden_ref[...] = (v*sigmoid(v)).astype(narrow)
    for h in range(2):
        outer_pre_ref[:, h*CH:(h+1)*CH] = dot(hidden_ref[...], w2_ref[h])+row(time_ref, in_time("time2_b", h))
    v = outer_pre_ref[...]
    embed = (v*sigmoid(v)).astype(narrow)
    embed_ref[...] = embed
    mine = lax.broadcasted_iota(jnp.int32, (n, TEMB), 0) == me_ref[0]
    own = jnp.sum(jnp.where(mine, embed.astype(f32), 0.0), axis=0, keepdims=True)
    own = jnp.broadcast_to(own, (8, TEMB)).astype(narrow)
    rows[1].finish(*two)
    widen_rows(emb_low_ref, emb_ref, EMB_TILES*TILE)
    for b in range(BLOCKS):
        modulate = []
        for h in range(2):
            we_ref[b, h] = get_rows(emb_ref, pl.ds(in_emb("emb_w", 2*TEMB*b+h), TEMB, stride=2)).astype(narrow)
            modulate.append(dot(own, we_ref[b, h])[0:1]+row(emb_ref, in_emb("emb_b", 2*b+h)))
        vec_ref[b] = jnp.concatenate([
            row(emb_ref, in_emb("res_b", 2*b)), row(emb_ref, in_emb("res_b", 2*b+1)),
            row(emb_ref, in_emb("res_gain", 2*b)), row(emb_ref, in_emb("res_shift", 2*b)),
            row(emb_ref, in_emb("res_gain", 2*b+1)), row(emb_ref, in_emb("res_shift", 2*b+1)),
            1.0+modulate[0], modulate[1],
        ], axis=0)


def time_and_modulation(place, sinus, pieces):
    rows = [Rows(place, TIME_FIRST, TIME_TILES), Rows(place, EMB_FIRST, EMB_TILES)]
    n = sinus.shape[0]
    spec = pl.BlockSpec(memory_space=VM)
    return pl.pallas_call(
        functools.partial(time_kernel, n, rows),
        out_shape=[sds((n, TEMB)), sds((n, TEMB), narrow), sds((n, TEMB)), sds((n, TEMB), narrow), sds((BLOCKS, 8, CH)),
                   sds((2, TEMB, CH), narrow), sds((BLOCKS, 2, TEMB, CH), narrow)],
        in_specs=[pl.BlockSpec(memory_space=pltpu.SMEM), spec, pl.BlockSpec(memory_space=pl.ANY)],
        out_specs=[spec]*7,
        scratch_shapes=[pltpu.VMEM((3, TIME_TILES*TILE, 128), f32), pltpu.VMEM((3, EMB_TILES*TILE, 128), f32)]
        + rows[0].scratch()+rows[1].scratch(),
        compiler_params=pltpu.CompilerParams(vmem_limit_bytes=39*MIB),
        cost_estimate=pl.CostEstimate(flops=2**27, bytes_accessed=8*2**20, transcendentals=0),
    )(place.me().reshape(1), sinus, pieces)


SMALL_HEAD, SMALL_ATTN, SMALL_S1, SMALL_STEM, SMALL_S0, SMALL_MOVED = 0, 120, 128, 136, 184, 192


def owner_kernel(share, n, me_ref, small_ref, sinus_ref, hidden_pre_ref, hidden_ref, outer_pre_ref, embed_ref, w2_ref, we_ref, spot_ref,
                 out_ref, time_ref, emb_ref, mixed_time_ref, mixed_emb_ref):
    row0 = me_ref[0]*share
    half_rows = mixed_time_ref.shape[1]//2
    one = lambda v: jnp.sum(v, axis=0, keepdims=True)
    moved = [[small_ref[SMALL_MOVED+(2*b+h)*n:SMALL_MOVED+(2*b+h+1)*n, :] for h in range(2)] for b in range(BLOCKS)]
    embed_grad = sum(exact_nt(moved[b][h], we_ref[b, h]) for b in range(BLOCKS) for h in range(2))
    outer_grad = embed_grad*silu_slope(outer_pre_ref[...])
    hidden_grad = sum(exact_nt(outer_grad[:, h*CH:(h+1)*CH], w2_ref[h]) for h in range(2))*silu_slope(hidden_pre_ref[...])

    def table(ref, values):
        ref[...] = jnp.zeros(ref.shape, f32)
        width = min(n, 128)
        for family, (value_ref, at) in enumerate(values):
            turned = jnp.transpose(value_ref[...].astype(f32))
            for first in range(0, n, width):
                group, lane = divmod(family*n+first, 128)
                ref[group, half_rows+at:half_rows+at+turned.shape[0], lane:lane+width] = turned[:, first:first+width]

    def products(ref, begin, factors, mixed_ref):
        away = row0-begin+(1 << 20)
        place = away // 2 - (1 << 19)
        start = jnp.clip(place+half_rows, 0, ref.shape[1]-half_rows)
        for h in range(2):
            right = jnp.concatenate([factors[0][h], factors[1][h]], axis=0)
            if right.shape[0] < 128:
                right = jnp.concatenate([right, jnp.zeros((128-right.shape[0], CH), f32)], axis=0)
            total = None
            for group in range(ref.shape[0]):
                left = ref[group, pl.ds(start, half_rows), :].astype(narrow)
                part = sum(dot(left, p) for p in three(right[group*128:(group+1)*128]))
                total = part if total is None else total+part
            put_rows(mixed_ref, pl.ds(h, half_rows, stride=2), total)
        odd = away-2*(away//2)
        return jnp.where(odd == 1, get_rows(mixed_ref, slice(1, 1+share)), get_rows(mixed_ref, slice(0, share)))

    halves = lambda v: [v[:, :CH], v[:, CH:]]
    table(time_ref, [(sinus_ref, 0), (hidden_ref, (ROW["time2_w"]-ROW["time1_w"])//2)])
    table(emb_ref, [(embed_ref, 0), (embed_ref, TEMB)])
    total = products(time_ref, ROW["time1_w"], [halves(hidden_grad), halves(outer_grad)], mixed_time_ref)
    total += products(emb_ref, ROW["emb_w"], moved, mixed_emb_ref)

    def small(at, count=1):
        return small_ref[at:at+count, :]

    def pairs(at):
        return jnp.concatenate([small_ref[at:at+40, :C0], small_ref[at:at+32, C0:]], axis=0)

    stem = pairs(SMALL_STEM)
    stem_rows = [stem[8*tap+c:8*tap+c+1, :] for tap in range(9) for c in range(IN_CH)]+[small(SMALL_STEM+41)[:, :C0]]
    rows = [jnp.concatenate(stem_rows[2*i:2*i+2], axis=1) for i in range(14)]
    rows += halves(one(hidden_grad))+halves(one(outer_grad))+[small(SMALL_STEM+40)]
    rows += [small(SMALL_S0, 2), small(SMALL_S1, 2)]+[one(moved[b][h]) for b in range(BLOCKS) for h in range(2)]
    rows += [small(SMALL_S0+2, 2), small(SMALL_S1+2, 2), small(SMALL_S0+4, 2), small(SMALL_S1+4, 2), small(SMALL_ATTN, 5)]
    ends = SMALL_HEAD+112
    gain_u, shift_u, side = small(ends), small(ends+1), small(ends+2)
    rows += [gain_u, jnp.concatenate([side[:, :C0], shift_u[:, :C0]], axis=1), jnp.concatenate([shift_u[:, C0:], side[:, C0:]], axis=1)]
    rows += [small(ends+3), jnp.zeros((4, CH), f32)]
    q = lax.broadcasted_iota(jnp.int32, (96, 72), 0)
    pick = (lax.broadcasted_iota(jnp.int32, (96, 72), 1) == (q % 16)*8+q//16).astype(f32).astype(narrow)
    up = sum(dot(pick, p) for p in three(small_ref[SMALL_HEAD:SMALL_HEAD+72, :]))
    side = sum(dot(pick, p) for p in three(pairs(SMALL_HEAD+72)))
    columns = [up[:, 64*i:64*i+64] for i in range(6)]+[side[:, 64*i:64*i+64] for i in range(3)]
    head_rows = None
    for o in range(OUT_CH):
        block = jnp.concatenate([column[16*o:16*o+16] for column in columns], axis=0)
        lane = lax.broadcasted_iota(jnp.int32, (64, CH), 1)
        to = (lane == 6*lax.broadcasted_iota(jnp.int32, (64, CH), 0)+o).astype(f32).astype(narrow)
        part = exact(block, to)
        head_rows = part if head_rows is None else head_rows+part
    rows = jnp.concatenate(rows+[head_rows, jnp.zeros((256-48-144, CH), f32)], axis=0)
    at = lax.broadcasted_iota(jnp.int32, (share, 256), 0)+row0
    chosen = (at == spot_ref[...]).astype(f32).astype(narrow)
    out_ref[...] = total+sum(dot(chosen, p) for p in three(rows))


def owner_rows(place, small, sinus, kept, w2, we):
    share, n = place.share, place.total
    hidden_pre, hidden, outer_pre, embed = kept
    half_rows = -(-(share+2)//16)*8
    groups = -(-2*n//128)
    spec = pl.BlockSpec(memory_space=VM)
    time_rows = (ROW["time2_b"]-ROW["time1_w"])//2
    lengths = [-(-(time_rows+2*half_rows)//8)*8, -(-(2*TEMB+2*half_rows)//8)*8]
    spots = jnp.array(SPOTS, jnp.int32)[None]
    return pl.pallas_call(
        functools.partial(owner_kernel, share, n),
        out_shape=sds((share, WIDE)),
        in_specs=[pl.BlockSpec(memory_space=pltpu.SMEM)]+[spec]*9,
        out_specs=spec,
        scratch_shapes=[pltpu.VMEM((groups, lengths[0], 128), f32), pltpu.VMEM((groups, lengths[1], 128), f32),
                        pltpu.VMEM((3, 2*half_rows, 128), f32), pltpu.VMEM((3, 2*half_rows, 128), f32)],
        compiler_params=pltpu.CompilerParams(vmem_limit_bytes=26*MIB),
        cost_estimate=pl.CostEstimate(flops=0, bytes_accessed=1024, transcendentals=0),
    )(place.me().reshape(1), small, sinus, hidden_pre, hidden, outer_pre, embed, w2, we, spots)


def step(sizes, params, moment1, moment2, images, noise, timesteps, masks, weight_index):
    flat = params.shape[0]
    share = flat // WIDE
    place = Place(sizes, share)
    a, me = place.at, place.me()
    spare = (share*me+LEAD) % TILE
    piece = jnp.zeros((place.block*TILE, WIDE), narrow)
    piece = lax.dynamic_update_slice_in_dim(piece, params.astype(narrow).reshape(share, WIDE), spare, axis=0)
    pieces = lax.all_gather(piece.reshape(place.block, TILE, WIDE), ("y", "c", "z", "x"), axis=0)

    own = jnp.concatenate([images, noise, masks.astype(f32)[:, None]], axis=1)
    own = lax.all_to_all(own, ("z", "x"), split_axis=0, concat_axis=2, tiled=True)[0]
    index = a["z"]*sizes["x"]+a["x"]
    own_step = lax.dynamic_index_in_dim(timesteps, index, keepdims=False).astype(f32)
    sample_weight = 0.5+0.5*lax.dynamic_index_in_dim(weight_index, index, keepdims=False).astype(f32)
    clean, own_noise, mask = own[:IN_CH], own[IN_CH:2*IN_CH], own[2*IN_CH:]
    early = jnp.stack([
        jnp.where(jnp.arange(WIDE) == me, own_step, 0.0),
        jnp.full((WIDE,), jnp.sum(mask)),
    ] + [jnp.zeros((WIDE,), f32)]*6)
    early = add_everywhere(early, place)
    all_steps, count = early[0, :place.total], early[1, 0]
    signal, one_minus, beta, alpha, tilde = plan(own_step)
    noisy = (jnp.sqrt(signal)*clean+jnp.sqrt(one_minus)*own_noise).astype(narrow).astype(f32)
    noisy = pad_rows8(to_phases(noisy))
    noise_phases, mask_phases = pad_rows8(to_phases(own_noise)), to_phases(mask)

    half = C0 // 2
    freqs = jnp.exp(-math.log(10000.0) * jnp.arange(half).astype(f32) / half)
    angles = all_steps[:, None] * freqs
    sinus = jnp.concatenate([jnp.cos(angles), jnp.sin(angles)], axis=-1).astype(narrow)
    pieces = pieces.reshape(place.total, place.block*TILE, WIDE)

    def rows(name, length):
        first, found = ROW[name], []
        for d in range(first//share, (first+length-1)//share+1):
            begin, end = max(first, d*share), min(first+length, (d+1)*share)
            shifted = (d*share+LEAD) % TILE-d*share
            found.append(pieces[d, begin+shifted:end+shifted])
        return found[0] if len(found) == 1 else jnp.concatenate(found)

    stem = rows("stem_w", 14).reshape(-1)
    stem_w = taps_rows(stem[:27*C0].reshape(9, IN_CH, C0))
    stem_b = stem[27*C0:].reshape(1, C0).astype(f32)
    skip, state, down_w = stem_down(place, noisy, stem_w, stem_b, pieces)
    hidden_pre, hidden, outer_pre, embed, vectors, w2, we = time_and_modulation(place, sinus, pieces)
    blocks = []
    for b in range(BLOCKS):
        vec = vectors[b]
        base = RES+2*TAPS*b
        after, inner, stat = block_forward(place, state, pieces, base, vec)
        blocks.append((state, inner, stat, base, vec))
        state = after
    before = state
    state, qkv, log, mixed_t, attn_stat, wp, wo, attn_vec = attention_forward(place, before, pieces)

    numbers = jnp.stack([jnp.log(beta), jnp.log(tilde), beta*beta/(alpha*one_minus), sample_weight])
    grad, skip_grad, head_tail, losses = head(
        place, numbers, state, skip, pieces, noise_phases, mask_phases)
    grad, large, attn_small = attention_back(
        grad, before, attn_stat, qkv, log, mixed_t, wp, wo, attn_vec, place.tiles)
    begin, inner, stat, base, vec = blocks[1]
    grad, large, s1 = block_back(place, grad, begin, inner, stat, pieces, base, vec, large)
    begin, inner, stat, base, vec = blocks[0]
    grad, large, s0 = block_back(place, grad, begin, inner, stat, pieces, base, vec, large)
    large, small = down_stem_back(me, place.total, grad, skip, skip_grad, down_w, noisy, head_tail, attn_small, s1, s0, large)
    total, small = share_out(large, small, place, 2)
    total = lax.dynamic_slice_in_dim(total.reshape(-1, WIDE), spare, share)
    row = share*me+jnp.arange(share)
    dense = functools.reduce(jnp.logical_or, [
        (row >= ROW[name]) & (row < ROW[name]+length)
        for name, length in (("down_w", 9*C0), ("res_w", 4*TAPS), ("qkv_w", 3*CH), ("proj_w", CH))
    ])
    total = jnp.where(dense[:, None], total, 0.0)

    total = total+owner_rows(place, small, sinus, (hidden_pre, hidden, outer_pre, embed), w2, we)

    scaled = total/count
    sums = jnp.concatenate([losses[:2], jnp.full((1, 128), jnp.sum(scaled*scaled)), losses[3:]])
    sums = add_everywhere(sums, place)
    loss_sum, loss_vlb, grad_norm = sums[0, 0], sums[1, 0], jnp.sqrt(sums[2, 0])
    scaled = scaled.reshape(flat)
    clipped = scaled*jnp.minimum(1.0, clip_limit/(grad_norm+1e-06))
    first = decay_first*moment1+(1.0-decay_first)*clipped
    second = decay_second*moment2+(1.0-decay_second)*clipped*clipped
    first_hat = first/(1.0-decay_first**STEP)
    second_hat = second/(1.0-decay_second**STEP)
    updated = params-learn_rate*(first_hat/(jnp.sqrt(second_hat)+1e-08)+weight_decay*params)
    return (updated, first, second, updated.astype(narrow), loss_sum, loss_vlb, count, grad_norm)


def solution(mesh):
    y = mesh.shape["batch"] // 2
    sizes = {"y": y, "c": 2, "z": mesh.shape["rows"] // y, "x": y}
    fine = Mesh(mesh.devices.reshape(tuple(sizes.values())), tuple(sizes))
    every, batch, rows = ("y", "c", "z", "x"), ("y", "c"), ("z", "x")
    return jax.shard_map(
        functools.partial(step, sizes),
        mesh=fine,
        in_specs=(P(every), P(every), P(every), P(batch, None, rows, None), P(batch, None, rows, None),
                  P(batch), P(batch, rows, None), P(batch)),
        out_specs=(P(every), P(every), P(every), P(every), P(), P(), P(), P()),
        check_vma=False,
    )
```
